32 devices in a mesh: state: 4 (over y, core), domain: 8 (over z, x).
Axes of the slice: x: 2, y: 2, z: 4, core: 2. Of those that a mesh axis runs over, the one named last changes fastest.
Arguments:
- orbitals: float32 [2, 4, 56, 25600], P(None, 'state', 'domain'), may hold values from -6 to 6
- occupation: float32 [4], P('state'), may hold values from 8e-07 to 3.2e-06
- potential: float32 [56, 25600], P('domain'), may hold values from 0 to 2
- background: float32 [56, 25600], P('domain'), may hold values from 0.005 to 270, as said below
- layer_start: int32 [9], replicated, may hold values from 0 to 40, as said below
Outputs:
- orbitals_next: float32 [2, 4, 56, 25600], P(None, 'state', 'domain')
- potential_next: float32 [56, 25600], P('domain')
The draws below stay inside these ranges and needn't reach their ends.
Inputs may be any that keep to these rules, and one draw needn't show every extreme that they name: layer_start[d] - 5 d lies in 0..2, is 0 for the first and the last entry and 2 for the last domain's start, so each domain owns 3 to 7 layers and some domain owns exactly 7. `background`: positive.
All inputs are finite; a program needn't handle non-finite values.
Results may differ from the reference program's by a relative error of at most 0.000071.
Values sent between devices are 32-bit elements; how exact they have to be, the bound alone decides.
No kernel may reach another device: no remote copies, remote signals or barrier semaphores. Data moves between devices by JAX's collectives and lax.ppermute only.
A program may use at most 128 MiB of HBM per device.

```python
import math
import jax
import jax.numpy as jnp
from jax import lax

SIDE = 160
SLAB = 5
TERMS = 4
LAYERS = 7
ORBITALS = 4
ROWS = 56
PLANE = 25600
N_DOMAIN = 8


ion_spacing = 8


def draw_layer_start(key, part):
    jitter_key, pick_key = jax.random.split(jax.random.fold_in(key, 7))
    jitter = jax.random.randint(jitter_key, (N_DOMAIN + 1,), 0, 3).astype(jnp.int32)
    widest = jax.random.randint(pick_key, (), 0, N_DOMAIN - 1).astype(jnp.int32)
    slot_ids = jnp.arange(N_DOMAIN + 1, dtype=jnp.int32)
    jitter = jnp.where(slot_ids == widest, 0, jitter)
    jitter = jnp.where(slot_ids == widest + 1, 2, jitter)
    jitter = jnp.where(slot_ids == N_DOMAIN - 1, 2, jitter)
    jitter = jnp.where((slot_ids == 0) | (slot_ids == N_DOMAIN), 0, jitter)
    return (SLAB * slot_ids + jitter).astype(jnp.int32)


def draw_background(key, part):
    starts = draw_layer_start(key, part)
    place_key, charge_key, floor_key = jax.random.split(jax.random.fold_in(key, 11), 3)
    length_cells = SLAB * N_DOMAIN
    slot_ids = jnp.arange(N_DOMAIN * LAYERS, dtype=jnp.int32)
    slot_domain = slot_ids // LAYERS
    slot_x = jnp.minimum(starts[slot_domain] + slot_ids - slot_domain * LAYERS, length_cells - 1).astype(jnp.int32)
    side_cells = jnp.arange(SIDE, dtype=jnp.int32)
    x_blocks = (length_cells + ion_spacing - 1) // ion_spacing
    side_blocks = (SIDE + ion_spacing - 1) // ion_spacing
    offsets = jax.random.randint(place_key, (3, x_blocks, side_blocks, side_blocks), 0, ion_spacing).astype(jnp.int32)
    charges = jax.random.uniform(charge_key, (x_blocks, side_blocks, side_blocks), jnp.float32, 0.5, 1.5)
    block_x = (slot_x // ion_spacing)[:, None, None]
    block_y = (side_cells // ion_spacing)[None, :, None]
    block_z = (side_cells // ion_spacing)[None, None, :]
    ion_cell = offsets[0][block_x, block_y, block_z] == (slot_x % ion_spacing)[:, None, None]
    ion_cell = ion_cell & (offsets[1][block_x, block_y, block_z] == (side_cells % ion_spacing)[None, :, None])
    ion_cell = ion_cell & (offsets[2][block_x, block_y, block_z] == (side_cells % ion_spacing)[None, None, :])
    ion_charge = charges[block_x, block_y, block_z]
    rising = slot_x.astype(jnp.float32) / length_cells
    uniform_floor = jax.random.uniform(floor_key, (N_DOMAIN * LAYERS, SIDE, SIDE), jnp.float32, 0.5, 1.5)
    gradient = 1.0 + 2.0 * rising
    floor_part = 0.01 * uniform_floor
    ion_part = jnp.where(ion_cell, 20.0 * ion_charge, 0.0)
    values = (floor_part + ion_part) * gradient[:, None, None]
    return values.reshape(N_DOMAIN * LAYERS, SIDE * SIDE).astype(jnp.float32)


def shard_levels(own_key, dims, cuts, smallest, high):
    def one(axis_at, blocks):
        steps = jax.random.uniform(jax.random.fold_in(jax.random.fold_in(own_key, 6), axis_at), (blocks,), jnp.float32, smallest / len(cuts), high / len(cuts))
        return jnp.repeat(jnp.exp(steps), dims[axis_at] // blocks).reshape((-1,) + (1,) * (len(dims) - axis_at - 1))

    gain = one(*cuts[0])
    for cut in cuts[1:]:
        gain = gain * one(*cut)
    return gain


def normal_values(rng, dims, spread, reach, pieces=(), kind=jnp.bfloat16):
    entries = spread * jax.random.normal(rng, dims, jnp.float32)
    if pieces:
        entries = entries * shard_levels(rng, dims, pieces, -0.22, 0.18)
    return jnp.clip(entries, -reach, reach).astype(kind)


def setup_inputs(seed: int = 0) -> dict:
    key_of = jax.random.split(jax.random.key(seed), 6)
    orbitals = normal_values(key_of[0], (2, ORBITALS, ROWS, PLANE), 1.0, 6.0, ((1, 4), (2, 8)), jnp.float32)
    occupation = jnp.clip(8.000000093488779e-07 + 2.400000028046634e-06 * jax.random.uniform(key_of[1], (ORBITALS,), jnp.float32) ** shard_levels(key_of[1], (ORBITALS,), ((0, 4),), -0.2, 0.2), 8.000000093488779e-07, 3.2000000373955118e-06)
    potential = jnp.clip(2.0 * jax.random.uniform(key_of[2], (ROWS, PLANE), jnp.float32) ** shard_levels(key_of[2], (ROWS, PLANE), ((0, 8),), -0.2, 0.2), 0.0, 2.0)
    background = draw_background(jax.random.fold_in(key_of[5], 71), 0)
    layer_start = draw_layer_start(jax.random.fold_in(key_of[5], 71), 0)
    return {"orbitals": orbitals, "occupation": occupation, "potential": potential, "background": background, "layer_start": layer_start}


time_step = 0.3
four_pi = 4.0 * math.pi
two_pi = 2.0 * math.pi


def inside_mask(x_rows, edge_cells, length_cells):
    along_x = (2 * x_rows - (length_cells - 1)) ** 2 * ((edge_cells - 2) ** 2)
    across = 2 * jnp.arange(edge_cells, dtype=jnp.int32) - (edge_cells - 1)
    circle = (across[:, None] ** 2 + across[None, :] ** 2) * ((length_cells - 2) ** 2)
    return along_x[:, None, None] + circle[None] <= (length_cells - 2) ** 2 * (edge_cells - 2) ** 2


def wave_squared(count_cells):
    index_run = jnp.arange(count_cells, dtype=jnp.int32)
    folded = jnp.where(2 * index_run <= count_cells, index_run, index_run - count_cells)
    wave_number = folded.astype(jnp.float32) * (two_pi / count_cells)
    return wave_number * wave_number


def hamilton(grid_field, local_potential):
    padded = jnp.pad(grid_field, 1)
    beside = padded[:-2, 1:-1, 1:-1] + padded[2:, 1:-1, 1:-1]
    beside = beside + padded[1:-1, :-2, 1:-1] + padded[1:-1, 2:, 1:-1]
    beside = beside + padded[1:-1, 1:-1, :-2] + padded[1:-1, 1:-1, 2:]
    return 0.5 * (6.0 * grid_field - beside) + local_potential * grid_field


def reference(orbitals, occupation, potential, background, layer_start):
    length_cells = SLAB * N_DOMAIN
    x_cells = jnp.arange(length_cells, dtype=jnp.int32)
    owner_domain = jnp.sum((layer_start[None, 1:N_DOMAIN] <= x_cells[:, None]).astype(jnp.int32), axis=1).astype(jnp.int32)
    row_of_x = (owner_domain * LAYERS + x_cells - layer_start[owner_domain]).astype(jnp.int32)
    slot_ids = jnp.arange(N_DOMAIN * LAYERS, dtype=jnp.int32)
    slot_domain = slot_ids // LAYERS
    slot_x = layer_start[slot_domain] + slot_ids - slot_domain * LAYERS
    slot_valid = slot_x < layer_start[slot_domain + 1]
    slot_clip = jnp.minimum(slot_x, length_cells - 1).astype(jnp.int32)
    sphere_mask = inside_mask(x_cells, SIDE, length_cells).astype(jnp.float32)
    cube_potential = jnp.take(potential, row_of_x, axis=0).reshape(length_cells, SIDE, SIDE)

    def to_cube(stored):
        return jnp.take(stored, row_of_x, axis=0).reshape(length_cells, SIDE, SIDE) * sphere_mask

    def to_slots(cube_values):
        flattened = cube_values.reshape(length_cells, SIDE * SIDE)
        return jnp.where(slot_valid[:, None], jnp.take(flattened, slot_clip, axis=0), 0.0)

    def propagate(density, inputs):
        orbital_pair, weight = inputs
        current = jnp.stack([to_cube(orbital_pair[0]), to_cube(orbital_pair[1])])
        summed = current
        for term_order in range(1, TERMS + 1):
            factor = time_step / term_order
            applied_real = hamilton(current[0], cube_potential) * sphere_mask
            applied_imag = hamilton(current[1], cube_potential) * sphere_mask
            current = jnp.stack([factor * applied_imag, -factor * applied_real])
            summed = summed + current
        density = density + weight * (summed[0] * summed[0] + summed[1] * summed[1])
        return density, jnp.stack([to_slots(summed[0]), to_slots(summed[1])])

    empty_density = jnp.zeros((length_cells, SIDE, SIDE), jnp.float32)
    density, propagated = lax.scan(propagate, empty_density, (jnp.swapaxes(orbitals, 0, 1), occupation))
    ion_cube = to_cube(background)
    neutral_scale = jnp.sum(density) / jnp.sum(ion_cube)
    charge = density - neutral_scale * ion_cube
    squared = wave_squared(length_cells)[:, None, None] + wave_squared(SIDE)[None, :, None] + wave_squared(SIDE)[None, None, :]
    kernel_values = jnp.where(squared > 0, four_pi / jnp.where(squared > 0, squared, 1.0), 0.0)
    hartree = jnp.real(jnp.fft.ifftn(jnp.fft.fftn(charge) * kernel_values))
    field_cube = (hartree - jnp.cbrt(3.0 * density / math.pi)) * sphere_mask
    return jnp.swapaxes(propagated, 0, 1), to_slots(field_cube)
```

```python
import functools
import math

import jax
import jax.numpy as jnp
import numpy as np
from jax import lax
from jax.experimental import pallas as pl
from jax.experimental.pallas import tpu as pltpu
from jax.sharding import PartitionSpec as P

SIDE = 160
SLAB = 5
TERMS = 4

SLOTS = 8
WIDE = 16
LANES = 128
RIM = 256
CHUNK = 1280
GROUP = 4

time_step = 0.3
four_pi = 4.0 * math.pi
two_pi = 2.0 * math.pi
highest = lax.Precision.HIGHEST
VMEM_BYTES = 56 * 1024 * 1024


def hartley_table(count_cells):
    index_run = np.arange(count_cells)
    angles = (index_run[:, None] * index_run[None, :] % count_cells) * (2.0 * np.pi / count_cells)
    return (np.cos(angles) + np.sin(angles)).astype(np.float32)


def padded_table(count_cells, size):
    table = np.zeros((size, size), np.float32)
    table[:count_cells, :count_cells] = hartley_table(count_cells)
    return table


def circle_row(length_cells):
    across = 2 * np.arange(SIDE, dtype=np.int64) - (SIDE - 1)
    circle = (across[:, None] ** 2 + across[None, :] ** 2) * (length_cells - 2) ** 2
    return circle.reshape(1, SIDE * SIDE).astype(np.int32)


def mesh_points(x_rows, circle, length_cells):
    along_x = (2 * x_rows - (length_cells - 1)) ** 2 * (SIDE - 2) ** 2
    return along_x + circle <= (length_cells - 2) ** 2 * (SIDE - 2) ** 2


def column_pieces(first, count):
    pieces = []
    column = first
    while column < first + count:
        row = column // SIDE
        stop = min((row + 1) * SIDE, first + count)
        pieces.append((row, column - row * SIDE, stop - row * SIDE))
        column = stop
    return pieces


def rows_of(shape):
    return lax.broadcasted_iota(jnp.int32, shape, 0)


def eight(values):
    missing = jnp.zeros((SLOTS - values.shape[0], values.shape[1]), values.dtype)
    return jnp.concatenate([values, missing], axis=0)


def twice(values):
    return jnp.concatenate([values, values], axis=0)


def pack_kernel(place_ref, orbitals_ref, potential_ref, up_ref, down_ref, up_far_ref, down_far_ref,
                v_up_ref, v_down_ref):
    thickness = place_ref[1]
    state = place_ref[4]
    plane = orbitals_ref.shape[-1]

    @pl.loop(0, plane // CHUNK)
    def _(step):
        lanes = pl.ds(pl.multiple_of(step * CHUNK, CHUNK), CHUNK)
        real = eight(orbitals_ref[0, 0, :, lanes])
        imag = eight(orbitals_ref[1, 0, :, lanes])
        row = rows_of(real.shape)
        up_ref[:, lanes] = jnp.where(
            row < 4,
            pltpu.roll(real, (12 - thickness) % 8, 0),
            pltpu.roll(imag, (16 - thickness) % 8, 0),
        )
        down_ref[:, lanes] = jnp.where(row < 4, real, pltpu.roll(imag, 4, 0))
        up_far_ref[:, lanes] = jnp.where(
            row < 1,
            pltpu.roll(real, (9 - thickness) % 8, 0),
            pltpu.roll(imag, (10 - thickness) % 8, 0),
        )[:2]
        down_far_ref[:, lanes] = jnp.where(row < 1, real, pltpu.roll(imag, 1, 0))[:2]
        local = eight(potential_ref[:, lanes])
        v_up_ref[:, lanes] = pltpu.roll(local, (11 - thickness - state) % 8, 0)[:1]
        v_down_ref[:, lanes] = pltpu.roll(local, (8 - state) % 8, 0)[:1]


def planes_of_flat(flat_ref, low_ref, high_ref):
    @pl.loop(0, SIDE // GROUP)
    def _(step):
        width = GROUP * SIDE
        lanes = pl.ds(pl.multiple_of(step * width, width), width)
        values = flat_ref[:, lanes]
        for part in range(GROUP):
            row = values[:, part * SIDE:(part + 1) * SIDE]
            at = pl.ds(step * GROUP + part, SLOTS, stride=SIDE)
            low_ref[at, :] = row[:, :LANES]
            high_ref[at, :] = jnp.concatenate(
                [row[:, LANES:], jnp.zeros((SLOTS, 2 * LANES - SIDE), jnp.float32)], axis=1
            )


def rotate_planes(low_ref, high_ref, table_y, table_z, out_low_ref, out_high_ref, slots):
    @pl.loop(0, slots)
    def _(slot):
        rows = pl.ds(pl.multiple_of(slot * SIDE, SIDE), SIDE)
        plane = jnp.concatenate([low_ref[rows, :], high_ref[rows, :]], axis=1)
        plane = jnp.dot(plane, table_z, precision=highest, preferred_element_type=jnp.float32)
        plane = jnp.dot(table_y, plane, precision=highest, preferred_element_type=jnp.float32)
        out_low_ref[rows, :] = plane[:, :LANES]
        out_high_ref[rows, :] = plane[:, LANES:]


def chunk_of(low_ref, high_ref, pieces, height):
    parts = []
    for row, start, stop in pieces:
        at = pl.ds(row, SLOTS, stride=height)
        values = jnp.concatenate([low_ref[at, :], high_ref[at, :]], axis=1)
        parts.append(values[:, start:stop])
    return parts


def ions_kernel(count, states, place_ref, background_ref, circle_ref, table_y_ref, table_z_ref, out_ref,
                flat_ref, low_ref, high_ref, low_out_ref, high_out_ref):
    own_start = place_ref[0]
    thickness = place_ref[1]
    state = place_ref[4]
    length_cells = place_ref[5]
    plane = background_ref.shape[-1]
    groups, _, width = out_ref.shape

    def body(step, total):
        lanes = pl.ds(pl.multiple_of(step * CHUNK, CHUNK), CHUNK)
        values = eight(background_ref[:, lanes])
        row = rows_of(values.shape)
        inside = mesh_points(own_start + row, circle_ref[:, lanes], length_cells) & (row < thickness)
        values = jnp.where(inside, values, 0.0)
        flat_ref[:, lanes] = values
        return total + jnp.sum(values.reshape(SLOTS, CHUNK // LANES, LANES), axis=1)

    total = lax.fori_loop(0, plane // CHUNK, body, jnp.zeros((SLOTS, LANES), jnp.float32))
    whole = jnp.broadcast_to(jnp.sum(total, keepdims=True), (SLOTS, LANES))
    planes_of_flat(flat_ref, low_ref, high_ref)
    rotate_planes(low_ref, high_ref, table_y_ref[...], table_z_ref[...], low_out_ref, high_out_ref, SLOTS)
    spare = width - count
    for chosen in range(states):

        @pl.when(state == chosen)
        def _():
            for group in range(groups):
                pieces = column_pieces((chosen * groups + group) * count, count)
                parts = chunk_of(low_out_ref, high_out_ref, pieces, SIDE)
                out_ref[group] = jnp.concatenate(parts + [whole[:, :spare]], axis=1)


def propagate_kernel(count, place_ref, weight_ref, orbitals_ref, potential_ref, low_ref, high_ref,
                     low_far_ref, high_far_ref, v_low_ref, v_high_ref, circle_ref, table_y_ref,
                     table_z_ref, next_ref, density_ref, out_ref, real_ref, imag_ref, centre_ref,
                     beside_ref, flat_ref, plane_low_ref, plane_high_ref, plane_low_out_ref,
                     plane_high_out_ref):
    own_start = place_ref[0]
    thickness = place_ref[1]
    short_below = place_ref[2]
    short_above = place_ref[3]
    length_cells = place_ref[5]
    weight = weight_ref[0]
    plane = orbitals_ref.shape[-1]
    slots = orbitals_ref.shape[2]
    devices, _, width = out_ref.shape

    for term in range(TERMS):
        for field_ref in (real_ref, imag_ref):
            field_ref[term, :, :RIM] = jnp.zeros((WIDE, RIM), jnp.float32)
            field_ref[term, :, RIM + plane:] = jnp.zeros((WIDE, RIM), jnp.float32)

    @pl.loop(0, plane // CHUNK)
    def _(step):
        lanes = pl.ds(pl.multiple_of(step * CHUNK, CHUNK), CHUNK)
        inner = pl.ds(pl.multiple_of(step * CHUNK + RIM, LANES), CHUNK)
        row = rows_of((WIDE, CHUNK))
        slot = rows_of((SLOTS, CHUNK))
        x_rows = own_start - 4 + row
        inside = mesh_points(x_rows, circle_ref[:, lanes], length_cells) & (row < thickness + 8)
        local = jnp.where(
            row < 4,
            twice(pltpu.roll(eight(v_low_ref[:, lanes]), 1, 0)),
            jnp.where(
                row < 4 + thickness,
                twice(pltpu.roll(eight(potential_ref[:, lanes]), 4, 0)),
                twice(pltpu.roll(eight(v_high_ref[:, lanes]), (4 + thickness) % 8, 0)),
            ),
        )
        centre_ref[:, lanes] = jnp.where(inside, 3.0 + local, 0.0)
        beside_ref[:, lanes] = jnp.where(inside, 0.5, 0.0)
        low = low_ref[:, lanes]
        high = high_ref[:, lanes]
        low_far = eight(low_far_ref[:, lanes])
        high_far = eight(high_far_ref[:, lanes])
        low = jnp.where(
            (short_below > 0) & (slot % 4 == 0),
            jnp.where(slot < 4, low_far, pltpu.roll(low_far, 3, 0)),
            low,
        )
        high = jnp.where(
            (short_above > 0) & (slot % 4 == 3),
            jnp.where(slot < 4, pltpu.roll(high_far, 3, 0), pltpu.roll(high_far, 6, 0)),
            high,
        )
        for part, field_ref in enumerate((real_ref, imag_ref)):
            own = pltpu.roll(eight(orbitals_ref[part, 0, :, lanes]), 4, 0)
            below = low if part == 0 else pltpu.roll(low, 4, 0)
            above = pltpu.roll(high, (4 + thickness) % 8 if part == 0 else thickness % 8, 0)
            field = jnp.where(
                row < 4, twice(below), jnp.where(row < 4 + thickness, twice(own), twice(above))
            )
            field_ref[0, :, inner] = jnp.where(inside, field, 0.0)

    def hamilton(field_ref, term, step, centre, beside):
        window = field_ref[term, :, pl.ds(pl.multiple_of(step * CHUNK, LANES), CHUNK + 2 * RIM)]
        size = CHUNK + 2 * RIM
        pair = window + pltpu.roll(window, size - (SIDE + 1), 1)
        pair = pair[:, :CHUNK + RIM]
        four = pair + pltpu.roll(pair, SIDE - 1, 1)
        four = four[:, LANES:]
        four = pltpu.roll(four, 1, 1)[:, LANES:]
        field = window[:, RIM:RIM + CHUNK]
        around = four + (pltpu.roll(field, 1, 0) + pltpu.roll(field, WIDE - 1, 0))
        return centre * field - beside * around, field

    for term in range(1, TERMS):
        factor = time_step / term

        @pl.loop(0, plane // CHUNK)
        def _(step, term=term, factor=factor):
            lanes = pl.ds(pl.multiple_of(step * CHUNK, CHUNK), CHUNK)
            inner = pl.ds(pl.multiple_of(step * CHUNK + RIM, LANES), CHUNK)
            centre = centre_ref[:, lanes]
            beside = beside_ref[:, lanes]
            real_ref[term, :, inner] = factor * hamilton(imag_ref, term - 1, step, centre, beside)[0]
            imag_ref[term, :, inner] = -factor * hamilton(real_ref, term - 1, step, centre, beside)[0]

    def finish(step, total):
        factor = time_step / TERMS
        lanes = pl.ds(pl.multiple_of(step * CHUNK, CHUNK), CHUNK)
        inner = pl.ds(pl.multiple_of(step * CHUNK + RIM, LANES), CHUNK)
        centre = centre_ref[:, lanes]
        beside = beside_ref[:, lanes]
        slot = rows_of((SLOTS, CHUNK))
        density = jnp.zeros((SLOTS, CHUNK), jnp.float32)
        for part, (field_ref, other_ref, sign) in enumerate(
            ((real_ref, imag_ref, 1.0), (imag_ref, real_ref, -1.0))
        ):
            last = (sign * factor) * hamilton(other_ref, TERMS - 1, step, centre, beside)[0]
            summed = field_ref[0, :, inner]
            for term in range(1, TERMS):
                summed = summed + field_ref[term, :, inner]
            summed = summed + last
            summed = jnp.where(slot < 4, pltpu.roll(summed[:8], 4, 0), pltpu.roll(summed[8:], 4, 0))
            summed = jnp.where(slot < thickness, summed, 0.0)
            next_ref[part, 0, :, lanes] = summed[:slots]
            density = density + summed * summed
        density = weight * density
        flat_ref[:, lanes] = density
        density_ref[:, lanes] = density[:slots]
        return total + jnp.sum(density.reshape(SLOTS, CHUNK // LANES, LANES), axis=1)

    total = lax.fori_loop(0, plane // CHUNK, finish, jnp.zeros((SLOTS, LANES), jnp.float32))
    whole = jnp.broadcast_to(jnp.sum(total, keepdims=True), (SLOTS, LANES))
    planes_of_flat(flat_ref, plane_low_ref, plane_high_ref)
    rotate_planes(plane_low_ref, plane_high_ref, table_y_ref[...], table_z_ref[...],
                  plane_low_out_ref, plane_high_out_ref, SLOTS)
    spare = width - count
    for device in range(devices):
        parts = chunk_of(plane_low_out_ref, plane_high_out_ref,
                         column_pieces(device * count, count), SIDE)
        out_ref[device] = jnp.concatenate(parts + [whole[:, :spare]], axis=1)


def wave_squared(index, count_cells):
    folded = jnp.where(2 * index <= count_cells, index, index - count_cells)
    wave_number = folded.astype(jnp.float32) * (two_pi / count_cells)
    return wave_number * wave_number


def coulomb_kernel(count, length_cells, place_ref, start_ref, charge_ref, ions_ref, table_ref, out_ref):
    domains, _, width = ions_ref.shape
    states = charge_ref.shape[0] // domains
    charge = charge_ref[:domains]
    for state in range(1, states):
        charge = charge + charge_ref[state * domains:(state + 1) * domains]
    charge = charge.reshape(domains * SLOTS, width)
    ions = ions_ref[...].reshape(domains * SLOTS, width)
    first = lax.broadcasted_iota(jnp.int32, (domains * SLOTS, width), 0) % SLOTS == 0
    lane = lax.broadcasted_iota(jnp.int32, (domains * SLOTS, width), 1)
    chosen = first & (lane == count)
    electrons = jnp.sum(jnp.where(chosen, charge, 0.0), keepdims=True)
    ionic = jnp.sum(jnp.where(chosen, ions, 0.0), keepdims=True)
    charge = charge - (electrons / ionic) * ions
    layer = lax.broadcasted_iota(jnp.int32, (length_cells, domains * SLOTS), 0)
    place = lax.broadcasted_iota(jnp.int32, (length_cells, domains * SLOTS), 1)
    chosen_layer = jnp.full(layer.shape, -1, jnp.int32)
    for domain in range(domains):
        slot = place - domain * SLOTS
        here = (slot >= 0) & (slot < start_ref[domain + 1] - start_ref[domain])
        chosen_layer = jnp.where(here, start_ref[domain] + slot, chosen_layer)
    pick = (layer == chosen_layer).astype(jnp.float32)
    table = jnp.dot(table_ref[...], pick, precision=highest, preferred_element_type=jnp.float32)
    waves = jnp.dot(table, charge, precision=highest, preferred_element_type=jnp.float32)
    wave_x = lax.broadcasted_iota(jnp.int32, waves.shape, 0)
    column = place_ref[6] * count + lax.broadcasted_iota(jnp.int32, waves.shape, 1)
    wave_y = ((column.astype(jnp.float32) + 0.5) * (1.0 / SIDE)).astype(jnp.int32)
    wave_z = column - wave_y * SIDE
    squared = (
        wave_squared(wave_x, length_cells) + wave_squared(wave_y, SIDE) + wave_squared(wave_z, SIDE)
    )
    gain = jnp.where(squared > 0, four_pi / jnp.where(squared > 0, squared, 1.0), 0.0)
    waves = waves * (gain * (1.0 / (length_cells * SIDE * SIDE)))
    back = lax.dot_general(
        table, waves, (((0,), (0,)), ((), ())), precision=highest, preferred_element_type=jnp.float32
    )
    back = back.reshape(domains, SLOTS, width)
    for state in range(states):
        out_ref[state * domains:(state + 1) * domains] = back


def field_kernel(count, place_ref, waves_ref, density_ref, circle_ref, table_y_ref, table_z_ref,
                 out_ref, low_ref, high_ref, low_out_ref, high_out_ref):
    own_start = place_ref[0]
    thickness = place_ref[1]
    length_cells = place_ref[5]
    devices = waves_ref.shape[0]
    slots = out_ref.shape[0]
    pieces = []
    for device in range(devices):
        column = 0
        for row, start, stop in column_pieces(device * count, count):
            values = waves_ref[device, :, column:column + stop - start]
            column += stop - start
            if start > 0:
                pieces.append(values)
                values = jnp.concatenate(pieces, axis=1)
            if stop < SIDE:
                pieces = [values]
                continue
            pieces = []
            at = pl.ds(row, SLOTS, stride=SIDE)
            low_ref[at, :] = values[:, :LANES]
            high_ref[at, :] = jnp.concatenate(
                [values[:, LANES:], jnp.zeros((SLOTS, 2 * LANES - SIDE), jnp.float32)], axis=1
            )
    rotate_planes(low_ref, high_ref, table_y_ref[...], table_z_ref[...], low_out_ref, high_out_ref, SLOTS)

    @pl.loop(0, SIDE // GROUP)
    def _(step):
        size = GROUP * SIDE
        lanes = pl.ds(pl.multiple_of(step * size, size), size)
        parts = []
        for part in range(GROUP):
            at = pl.ds(step * GROUP + part, SLOTS, stride=SIDE)
            values = jnp.concatenate([low_out_ref[at, :], high_out_ref[at, :]], axis=1)
            parts.append(values[:, :SIDE])
        hartree = jnp.concatenate(parts, axis=1)
        content = eight(density_ref[:, lanes]) * (3.0 / math.pi)
        positive = jnp.where(content > 0, content, 1.0)
        root = jnp.exp(jnp.log(positive) * (1.0 / 3.0))
        root = root - (root - positive / (root * root)) * (1.0 / 3.0)
        root = jnp.where(content > 0, root, 0.0)
        row = rows_of(root.shape)
        inside = mesh_points(own_start + row, circle_ref[:, lanes], length_cells) & (row < thickness)
        out_ref[:, lanes] = jnp.where(inside, hartree - root, 0.0)[:slots]


def from_behind(value, steps):
    count = lax.axis_size("domain")
    leading, last = (max(0, -steps), min(count, count - steps))
    return lax.ppermute(value, "domain", [(source, source + steps) for source in range(leading, last)])


def shards(orbitals, occupation, potential, background, layer_start):
    domains = lax.axis_size("domain")
    states = lax.axis_size("state")
    devices = domains * states
    position = lax.axis_index("domain")
    state = lax.axis_index("state")
    length_cells = SLAB * domains
    layer_cap, plane = potential.shape
    count = plane // devices
    width = -(-(count + 1) // LANES) * LANES
    padded = jnp.pad(layer_start, (2, 2), mode="edge")
    near = lax.dynamic_slice_in_dim(padded, position + 1, 4, 0)
    thick = near[1:] - near[:-1]
    place = jnp.stack(
        [
            near[1],
            thick[1],
            (thick[0] == SLAB - 2).astype(jnp.int32),
            (thick[2] == SLAB - 2).astype(jnp.int32),
            state,
            jnp.int32(length_cells),
            state * domains + position,
        ]
    )
    circle = jnp.asarray(circle_row(length_cells))
    table_y = jnp.asarray(hartley_table(SIDE))
    table_z = jnp.asarray(padded_table(SIDE, 2 * LANES))
    table_x = jnp.asarray(hartley_table(length_cells))

    smem = pl.BlockSpec(memory_space=pltpu.SMEM)
    vmem = pl.BlockSpec(memory_space=pltpu.VMEM)
    params = pltpu.CompilerParams(vmem_limit_bytes=VMEM_BYTES)

    def f32(*shape):
        return jax.ShapeDtypeStruct(shape, jnp.float32)

    planes = [pltpu.VMEM((SLOTS * SIDE, LANES), jnp.float32)] * 4

    up, down, up_far, down_far, v_up, v_down = pl.pallas_call(
        pack_kernel,
        out_shape=(f32(8, plane), f32(8, plane), f32(2, plane), f32(2, plane), f32(1, plane), f32(1, plane)),
        in_specs=[smem, vmem, vmem],
        out_specs=(vmem,) * 6,
        compiler_params=params,
        name="pack_halo",
    )(place, orbitals, potential)
    low = from_behind(up, 1)
    high = from_behind(down, -1)
    v_low = from_behind(v_up, 1)
    v_high = from_behind(v_down, -1)
    low_far = from_behind(up_far, 2)
    high_far = from_behind(down_far, -2)
    v_both = lax.all_gather(jnp.concatenate([v_low, v_high], axis=1), "state", axis=0, tiled=True)

    ions = pl.pallas_call(
        functools.partial(ions_kernel, count, states),
        out_shape=f32(domains, SLOTS, width),
        in_specs=[smem] + [vmem] * 4,
        out_specs=vmem,
        scratch_shapes=[pltpu.VMEM((SLOTS, plane), jnp.float32)] + planes,
        compiler_params=params,
        name="ion_waves",
    )(place, background, circle, table_y, table_z)
    ions = lax.all_to_all(ions, "domain", split_axis=0, concat_axis=0, tiled=True)

    field_shape = (TERMS, WIDE, plane + 2 * RIM)
    orbitals_next, density, waves = pl.pallas_call(
        functools.partial(propagate_kernel, count),
        out_shape=(
            f32(*orbitals.shape),
            f32(layer_cap, plane),
            f32(devices, SLOTS, width),
        ),
        in_specs=[smem, smem] + [vmem] * 11,
        out_specs=(vmem,) * 3,
        scratch_shapes=[
            pltpu.VMEM(field_shape, jnp.float32),
            pltpu.VMEM(field_shape, jnp.float32),
            pltpu.VMEM((WIDE, plane), jnp.float32),
            pltpu.VMEM((WIDE, plane), jnp.float32),
            pltpu.VMEM((SLOTS, plane), jnp.float32),
        ]
        + planes,
        compiler_params=params,
        name="propagate",
    )(place, occupation, orbitals, potential, low, high, low_far, high_far, v_both[:, :plane],
      v_both[:, plane:], circle, table_y, table_z)
    waves = lax.all_to_all(waves, ("state", "domain"), split_axis=0, concat_axis=0, tiled=True)
    density = lax.psum(density, "state")
    waves = pl.pallas_call(
        functools.partial(coulomb_kernel, count, length_cells),
        out_shape=f32(devices, SLOTS, width),
        in_specs=[smem, smem] + [vmem] * 3,
        out_specs=vmem,
        compiler_params=params,
        name="coulomb",
    )(place, layer_start, waves, ions, table_x)
    waves = lax.all_to_all(waves, ("state", "domain"), split_axis=0, concat_axis=0, tiled=True)
    potential_next = pl.pallas_call(
        functools.partial(field_kernel, count),
        out_shape=f32(layer_cap, plane),
        in_specs=[smem] + [vmem] * 5,
        out_specs=vmem,
        scratch_shapes=planes,
        compiler_params=params,
        name="field",
    )(place, waves, density, circle, table_y, table_z)
    return orbitals_next, potential_next


def solution(mesh):
    return jax.shard_map(
        shards,
        mesh=mesh,
        in_specs=(
            P(None, "state", "domain", None),
            P("state"),
            P("domain", None),
            P("domain", None),
            P(),
        ),
        out_specs=(P(None, "state", "domain", None), P("domain", None)),
        check_vma=False,
    )
```

```python
import functools
import math

import jax
import jax.numpy as jnp
import ml_dtypes
import numpy as np
from jax import lax
from jax.experimental import pallas as pl
from jax.experimental.pallas import tpu as pltpu
from jax.sharding import PartitionSpec as P

SIDE = 160
SLAB = 5
TERMS = 4

HALO = TERMS
LANES = 128
SLOTS = 8
RUN = SIDE // 8
FLAT = SIDE * SIDE // LANES
STRIDE = FLAT // 8
WIDTH = 2 * LANES
BLOCK = 40
TALL = SIDE + 16

time_step = 0.3
four_pi = 4.0 * math.pi
two_pi = 2.0 * math.pi
highest = lax.Precision.HIGHEST
VMEM_BYTES = 56 * 1024 * 1024
SMEM_SPEC = pl.BlockSpec(memory_space=pltpu.SMEM)
VMEM_SPEC = pl.BlockSpec(memory_space=pltpu.VMEM)
ANY_SPEC = pl.BlockSpec(memory_space=pl.ANY)


def hartley_table(count_cells):
    index_run = np.arange(count_cells)
    angles = (index_run[:, None] * index_run[None, :] % count_cells) * (2.0 * np.pi / count_cells)
    return np.cos(angles) + np.sin(angles)


def plane_order():
    rows = np.arange(SIDE)
    return RUN * (rows % 8) + rows // 8


def two_parts(table):
    table = table.astype(np.float32)
    high = table.astype(ml_dtypes.bfloat16)
    low = (table - high.astype(np.float32)).astype(ml_dtypes.bfloat16)
    return high, low


def tables_of_side():
    table = hartley_table(SIDE)
    along_z = np.zeros((WIDTH, WIDTH))
    along_z[:SIDE, :SIDE] = table
    high, low = two_parts(along_z)
    along_z = np.concatenate([high, high, low], axis=0)
    high, low = two_parts(table[:, plane_order()])
    into_y = np.concatenate([high, high, low], axis=1)
    high, low = two_parts(table[plane_order(), :])
    out_of_y = np.concatenate([high, high, low], axis=1)
    return along_z, into_y, out_of_y


def circle_table():
    across = 2 * np.arange(SIDE, dtype=np.int64) - (SIDE - 1)
    return (across[:, None] ** 2 + across[None, :] ** 2).astype(np.int32)


def circle_plane():
    table = np.full((SIDE, WIDTH), 4 * SIDE * SIDE, np.int32)
    table[:, :SIDE] = circle_table()[plane_order()]
    return table


def mesh_points(x_row, circle, length_cells):
    room = ((length_cells - 2) ** 2 - (2 * x_row - (length_cells - 1)) ** 2) * (SIDE - 2) ** 2
    return (circle * (length_cells - 2) ** 2 <= room) & (circle < 4 * SIDE * SIDE)


def column_pieces(first, count):
    pieces = []
    column = first
    while column < first + count:
        row = column // SIDE
        stop = min((row + 1) * SIDE, first + count)
        pieces.append((row, column - row * SIDE, stop - row * SIDE))
        column = stop
    return pieces


def eight(values):
    missing = jnp.zeros((SLOTS - values.shape[0], values.shape[1]), values.dtype)
    return jnp.concatenate([values, missing], axis=0)


def to_plane(load, store):
    lane = lax.broadcasted_iota(jnp.int32, (8, LANES), 1)
    for step in range(RUN // 4):
        rows = [load(5 * step + part) for part in range(5)]
        store(4 * step, rows[0], rows[1])
        for part in range(1, 4):
            left = pltpu.roll(rows[part], LANES - 32 * part, 1)
            right = pltpu.roll(rows[part + 1], LANES - 32 * part, 1)
            store(4 * step + part, jnp.where(lane < LANES - 32 * part, left, right), right)


def to_flat(load, store):
    lane = lax.broadcasted_iota(jnp.int32, (8, LANES), 1)
    for step in range(RUN // 4):
        turned = []
        for part in range(4):
            low, high = load(4 * step + part)
            if part:
                low = pltpu.roll(low, 32 * part, 1)
                high = pltpu.roll(high, 32 * part, 1)
            turned.append((low, high))
        store(5 * step, turned[0][0])
        for part in range(1, 4):
            ended = 32 * (part - 1)
            values = jnp.where(lane < ended + 32, turned[part - 1][1], turned[part][0])
            if ended:
                values = jnp.where(lane < ended, turned[part - 1][0], values)
            store(5 * step + part, values)
        store(5 * step + 4, jnp.where(lane < 96, turned[3][0], turned[3][1]))


def parts_of(values):
    high = values.astype(jnp.bfloat16)
    low = (values - high.astype(jnp.float32)).astype(jnp.bfloat16)
    return high, low


def turn_z(values, table):
    high, low = parts_of(values)
    return jnp.dot(
        jnp.concatenate([high, low, high], axis=1), table, preferred_element_type=jnp.float32
    )


def turn_y(table, values):
    high, low = parts_of(values)
    return jnp.dot(
        table, jnp.concatenate([high, low, high], axis=0), preferred_element_type=jnp.float32
    )


def send_columns(planes_ref, table_y, table_z, low_ref, high_ref):
    slots = planes_ref.shape[0] // SIDE
    for slot in range(slots):
        rows = slice(slot * SIDE, (slot + 1) * SIDE)
        waves = turn_y(table_y, turn_z(planes_ref[rows, :], table_z))
        low_ref[rows, :] = waves[:, :LANES]
        high_ref[rows, :] = waves[:, LANES:]
    low_ref[slots * SIDE:, :] = jnp.zeros(((SLOTS - slots) * SIDE, LANES), jnp.float32)
    high_ref[slots * SIDE:, :] = jnp.zeros(((SLOTS - slots) * SIDE, LANES), jnp.float32)


def chunk_of(low_ref, high_ref, pieces, extra):
    parts = []
    for row, start, stop in pieces:
        at = pl.ds(row, SLOTS, stride=SIDE)
        values = jnp.concatenate([low_ref[at, :], high_ref[at, :]], axis=1)
        parts.append(values[:, start:stop])
    return jnp.concatenate(parts + [extra], axis=1)


def layers_of(stored_ref, flat_ref):
    @pl.loop(0, FLAT // 8)
    def _(step):
        for part in range(8):
            lanes = pl.ds(pl.multiple_of((step * 8 + part) * LANES, LANES), LANES)
            flat_ref[pl.ds(step * 8 + part, SLOTS, stride=FLAT), :] = eight(stored_ref[:, lanes])


def place_of(start_ref):
    position = lax.axis_index("domain")
    return position, start_ref[position], start_ref[position + 1] - start_ref[position]


def pack_kernel(start_ref, potential_ref, orbitals_ref, up_ref, down_ref, up_far_ref, down_far_ref,
                tile_ref, row_ref, sems):
    _, _, thickness = place_of(start_ref)
    pick = jnp.minimum(lax.axis_index("state"), HALO - 2)
    first = jnp.maximum(thickness - HALO, 0)
    copies = []

    def copy(source, target):
        made = pltpu.make_async_copy(source, target, sems.at[len(copies)])
        made.start()
        copies.append(made)

    for part in range(2):
        rows = pl.ds(part * HALO, HALO)
        copy(orbitals_ref.at[part, pl.ds(first, HALO)], up_ref.at[rows])
        copy(orbitals_ref.at[part, pl.ds(0, HALO)], down_ref.at[rows])
        copy(orbitals_ref.at[part, pl.ds(thickness - 1, 1)], up_far_ref.at[pl.ds(part, 1)])
        copy(orbitals_ref.at[part, pl.ds(0, 1)], down_far_ref.at[pl.ds(part, 1)])

    @pl.loop(0, FLAT // 8)
    def _(step):
        for part in range(8):
            tile = step * 8 + part
            lanes = pl.ds(pl.multiple_of(tile * LANES, LANES), LANES)
            rows = pl.ds(pl.multiple_of(tile * 8, 8), 8)
            tile_ref[rows, :] = eight(potential_ref[:, lanes])

    @pl.loop(0, FLAT // 8)
    def _(step):
        rows = pl.ds(pl.multiple_of(step * 8, 8), 8)
        row_ref[0, 0, rows, :] = tile_ref[pl.ds(step * 64 + thickness - (HALO - 1) + pick, 8, stride=8), :]
        row_ref[1, 0, rows, :] = tile_ref[pl.ds(step * 64 + pick, 8, stride=8), :]

    copy(row_ref.at[0], up_ref.at[pl.ds(2 * HALO, 1)])
    copy(row_ref.at[1], down_ref.at[pl.ds(2 * HALO, 1)])
    for made in copies:
        made.wait()


def ions_kernel(count, length_cells, start_ref, background_ref, circle_ref, table_y_ref, table_z_ref,
                out_ref, flat_ref, planes_ref, low_ref, high_ref):
    _, own_start, thickness = place_of(start_ref)
    state = lax.axis_index("state")
    slots = background_ref.shape[0]
    groups, _, width = out_ref.shape
    layers_of(background_ref, flat_ref)

    def body(slot, total):
        def store(tile, low, high):
            rows = pl.ds(pl.multiple_of(slot * SIDE + tile * 8, 8), 8)
            planes_ref[rows, :LANES] = low
            planes_ref[rows, LANES:] = high

        to_plane(lambda k: flat_ref[pl.ds(slot * FLAT + k, 8, stride=STRIDE), :], store)
        rows = pl.ds(pl.multiple_of(slot * SIDE, 8), SIDE)
        inside = mesh_points(own_start + slot, circle_ref[...], length_cells) & (slot < thickness)
        values = jnp.where(inside, planes_ref[rows, :], 0.0)
        planes_ref[rows, :] = values
        return total + jnp.sum(values.reshape(RUN, 8, WIDTH), axis=0)

    total = lax.fori_loop(0, slots, body, jnp.zeros((8, WIDTH), jnp.float32))
    whole = jnp.broadcast_to(jnp.sum(total, keepdims=True), (SLOTS, LANES))[:, :width - count]
    send_columns(planes_ref, table_y_ref[...], table_z_ref[...], low_ref, high_ref)
    for chosen in range(lax.axis_size("state")):

        @pl.when(state == chosen)
        def _():
            for group in range(groups):
                pieces = column_pieces((chosen * groups + group) * count, count)
                out_ref[group] = chunk_of(low_ref, high_ref, pieces, whole)


def propagate_kernel(count, length_cells, start_ref, weight_ref, orbitals_ref, potential_ref, below_ref,
                     above_ref, below_far_ref, above_far_ref, v_ref, circle_ref, table_y_ref,
                     table_z_ref, next_ref, density_ref, out_ref, field_ref, centre_ref, beside_ref,
                     flat_ref, planes_ref, low_ref, high_ref):
    position, own_start, thickness = place_of(start_ref)
    domains = lax.axis_size("domain")
    before = start_ref[jnp.maximum(position - 1, 0)]
    after = start_ref[jnp.minimum(position + 2, domains)]
    short_below = ((position > 0) & (own_start - before < HALO)).astype(jnp.int32)
    short_above = (position < domains - 1) & (after - own_start - thickness < HALO)
    weight = weight_ref[0]
    slots = orbitals_ref.shape[1]
    layers = slots + 2 * HALO
    devices, _, width = out_ref.shape

    def field_layer(part, x_row):
        def store(tile, low, high):
            field_ref[0, part, x_row, 8 + 8 * tile:16 + 8 * tile, :LANES] = low
            field_ref[0, part, x_row, 8 + 8 * tile:16 + 8 * tile, LANES:] = high

        return store

    def potential_layer(x_row):
        def store(tile, low, high):
            centre_ref[x_row, 8 * tile:8 * tile + 8, :LANES] = low
            centre_ref[x_row, 8 * tile:8 * tile + 8, LANES:] = high

        return store

    def rows_from(ref, *at):
        return lambda k: ref[(*at, pl.ds(k, 8, stride=STRIDE), slice(None))]

    layers_of(potential_ref, flat_ref)

    @pl.loop(0, slots)
    def _(slot):
        for part in range(2):
            to_plane(rows_from(orbitals_ref, part, slot), field_layer(part, HALO + slot))
        to_plane(
            lambda k: flat_ref[pl.ds(slot * FLAT + k, 8, stride=STRIDE), :], potential_layer(HALO + slot)
        )

    @pl.loop(0, HALO - 1)
    def _(layer):
        to_plane(rows_from(v_ref, 2 * layer), potential_layer(1 + layer))
        to_plane(rows_from(v_ref, 2 * layer + 1), potential_layer(HALO + thickness + layer))
        for part in range(2):
            to_plane(
                rows_from(below_ref, part * HALO + 1 + layer - short_below), field_layer(part, 1 + layer)
            )
            to_plane(
                rows_from(above_ref, part * HALO + layer), field_layer(part, HALO + thickness + layer)
            )

    @pl.loop(0, 2)
    def _(part):
        last = 2 * HALO - 1 + thickness

        @pl.when(short_below > 0)
        def _():
            to_plane(rows_from(below_far_ref, part), field_layer(part, 0))

        @pl.when(short_below == 0)
        def _():
            to_plane(rows_from(below_ref, part * HALO), field_layer(part, 0))

        @pl.when(short_above)
        def _():
            to_plane(rows_from(above_far_ref, part), field_layer(part, last))

        @pl.when(jnp.logical_not(short_above))
        def _():
            to_plane(rows_from(above_ref, part * HALO + HALO - 1), field_layer(part, last))

    def wrap(term, part, x_row):
        first = field_ref[term, part, x_row, 8:16, :]
        final = field_ref[term, part, x_row, SIDE:SIDE + 8, :]
        field_ref[term, part, x_row, :8, :] = pltpu.roll(final, 1, 0)
        field_ref[term, part, x_row, SIDE + 8:, :] = pltpu.roll(first, 7, 0)

    @pl.loop(0, layers)
    def _(x_row):
        known = x_row < thickness + 2 * HALO
        for block in range(SIDE // BLOCK):
            rows = slice(block * BLOCK, (block + 1) * BLOCK)
            inner = slice(8 + block * BLOCK, 8 + (block + 1) * BLOCK)
            inside = mesh_points(own_start - HALO + x_row, circle_ref[rows, :], length_cells) & known
            centre_ref[x_row, rows, :] = jnp.where(
                inside, (3.0 + centre_ref[x_row, rows, :]) * time_step, 0.0
            )
            beside_ref[x_row, rows, :] = jnp.where(inside, 0.5 * time_step, 0.0)
            for part in range(2):
                field_ref[0, part, x_row, inner, :] = jnp.where(
                    inside, field_ref[0, part, x_row, inner, :], 0.0
                )
        for part in range(2):
            wrap(0, part, x_row)

    def hamilton(term, part, x_row, block, centre, beside):
        tall = field_ref[term, part, x_row, block * BLOCK:block * BLOCK + BLOCK + 16, :]
        inner = slice(8 + block * BLOCK, 8 + (block + 1) * BLOCK)
        field = tall[8:8 + BLOCK]
        around = field_ref[term, part, x_row - 1, inner, :] + field_ref[term, part, x_row + 1, inner, :]
        around = around + (tall[:BLOCK] + tall[16:])
        around = around + (pltpu.roll(field, 1, 1) + pltpu.roll(field, WIDTH - 1, 1))
        return centre * field - beside * around

    for term in range(1, TERMS):

        @pl.loop(term, layers - term)
        def _(x_row, term=term):
            for block in range(SIDE // BLOCK):
                rows = slice(block * BLOCK, (block + 1) * BLOCK)
                inner = slice(8 + block * BLOCK, 8 + (block + 1) * BLOCK)
                centre = centre_ref[x_row, rows, :]
                beside = beside_ref[x_row, rows, :]
                for part in range(2):
                    field_ref[term, part, x_row, inner, :] = hamilton(
                        term - 1, part, x_row, block, centre, beside
                    )
            for part in range(2):
                wrap(term, part, x_row)

    def finish(slot, total):
        x_row = HALO + slot
        owned = slot < thickness
        for block in range(SIDE // BLOCK):
            rows = slice(block * BLOCK, (block + 1) * BLOCK)
            inner = slice(8 + block * BLOCK, 8 + (block + 1) * BLOCK)
            centre = centre_ref[x_row, rows, :]
            beside = beside_ref[x_row, rows, :]
            density = jnp.zeros((BLOCK, WIDTH), jnp.float32)
            for part, sign in ((0, 1.0), (1, -1.0)):
                summed = field_ref[0, part, x_row, inner, :]
                summed = summed + sign * field_ref[1, 1 - part, x_row, inner, :]
                summed = summed - (1.0 / 2.0) * field_ref[2, part, x_row, inner, :]
                summed = summed - (sign / 6.0) * field_ref[3, 1 - part, x_row, inner, :]
                summed = summed + (1.0 / 24.0) * hamilton(3, part, x_row, block, centre, beside)
                summed = jnp.where(owned, summed, 0.0)
                field_ref[2, part, x_row, inner, :] = summed
                density = density + summed * summed
            density = weight * density
            planes_ref[pl.ds(pl.multiple_of(slot * SIDE + block * BLOCK, 8), BLOCK), :] = density
            total = total + jnp.sum(density.reshape(BLOCK // 8, 8, WIDTH), axis=0)

        for part in range(2):

            def load(tile, part=part):
                tall = field_ref[2, part, x_row, 8 + 8 * tile:16 + 8 * tile, :]
                return tall[:, :LANES], tall[:, LANES:]

            def store(k, values, part=part):
                next_ref[part, slot, pl.ds(k, 8, stride=STRIDE), :] = values

            to_flat(load, store)

        def load(tile):
            tall = planes_ref[pl.ds(pl.multiple_of(slot * SIDE + tile * 8, 8), 8), :]
            return tall[:, :LANES], tall[:, LANES:]

        def store(k, values):
            density_ref[slot, pl.ds(k, 8, stride=STRIDE), :] = values

        to_flat(load, store)
        return total

    total = lax.fori_loop(0, slots, finish, jnp.zeros((8, WIDTH), jnp.float32))
    whole = jnp.broadcast_to(jnp.sum(total, keepdims=True), (SLOTS, LANES))[:, :width - count]
    send_columns(planes_ref, table_y_ref[...], table_z_ref[...], low_ref, high_ref)
    for device in range(devices):
        out_ref[device] = chunk_of(low_ref, high_ref, column_pieces(device * count, count), whole)


def wave_squared(index, count_cells):
    folded = jnp.where(2 * index <= count_cells, index, index - count_cells)
    wave_number = folded.astype(jnp.float32) * (two_pi / count_cells)
    return wave_number * wave_number


def coulomb_kernel(count, length_cells, start_ref, charge_ref, ions_ref, table_ref, out_ref):
    domains, _, width = ions_ref.shape
    states = charge_ref.shape[0] // domains
    device = lax.axis_index("state") * domains + lax.axis_index("domain")
    charge = charge_ref[:domains]
    for state in range(1, states):
        charge = charge + charge_ref[state * domains:(state + 1) * domains]
    charge = charge.reshape(domains * SLOTS, width)
    ions = ions_ref[...].reshape(domains * SLOTS, width)
    first = lax.broadcasted_iota(jnp.int32, (domains * SLOTS, width), 0) % SLOTS == 0
    lane = lax.broadcasted_iota(jnp.int32, (domains * SLOTS, width), 1)
    chosen = first & (lane == count)
    electrons = jnp.sum(jnp.where(chosen, charge, 0.0), keepdims=True)
    ionic = jnp.sum(jnp.where(chosen, ions, 0.0), keepdims=True)
    charge = charge - (electrons / ionic) * ions
    layer = lax.broadcasted_iota(jnp.int32, (length_cells, domains * SLOTS), 0)
    place = lax.broadcasted_iota(jnp.int32, (length_cells, domains * SLOTS), 1)
    chosen_layer = jnp.full(layer.shape, -1, jnp.int32)
    for domain in range(domains):
        slot = place - domain * SLOTS
        here = (slot >= 0) & (slot < start_ref[domain + 1] - start_ref[domain])
        chosen_layer = jnp.where(here, start_ref[domain] + slot, chosen_layer)
    pick = (layer == chosen_layer).astype(jnp.float32)
    table = jnp.dot(table_ref[...], pick, precision=highest, preferred_element_type=jnp.float32)
    waves = jnp.dot(table, charge, precision=highest, preferred_element_type=jnp.float32)
    wave_x = lax.broadcasted_iota(jnp.int32, waves.shape, 0)
    column = device * count + lax.broadcasted_iota(jnp.int32, waves.shape, 1)
    wave_y = ((column.astype(jnp.float32) + 0.5) * (1.0 / SIDE)).astype(jnp.int32)
    wave_z = column - wave_y * SIDE
    squared = (
        wave_squared(wave_x, length_cells) + wave_squared(wave_y, SIDE) + wave_squared(wave_z, SIDE)
    )
    gain = jnp.where(squared > 0, four_pi / jnp.where(squared > 0, squared, 1.0), 0.0)
    waves = waves * (gain * (1.0 / (length_cells * SIDE * SIDE)))
    back = lax.dot_general(
        table, waves, (((0,), (0,)), ((), ())), precision=highest, preferred_element_type=jnp.float32
    )
    back = back.reshape(domains, SLOTS, width)
    for state in range(states):
        out_ref[state * domains:(state + 1) * domains] = back


def field_kernel(count, length_cells, start_ref, waves_ref, density_ref, other_ref, circle_ref,
                 table_y_ref, table_z_ref, out_ref, low_ref, high_ref, planes_ref, flat_ref):
    _, own_start, thickness = place_of(start_ref)
    devices = waves_ref.shape[0]
    slots = out_ref.shape[0]
    pieces = []
    for device in range(devices):
        column = 0
        for row, start, stop in column_pieces(device * count, count):
            values = waves_ref[device, :, column:column + stop - start]
            column += stop - start
            if start > 0:
                pieces.append(values)
                values = jnp.concatenate(pieces, axis=1)
            if stop < SIDE:
                pieces = [values]
                continue
            pieces = []
            at = pl.ds(row, SLOTS, stride=SIDE)
            low_ref[at, :] = values[:, :LANES]
            high_ref[at, :] = jnp.concatenate(
                [values[:, LANES:], jnp.zeros((SLOTS, WIDTH - SIDE), jnp.float32)], axis=1
            )
    table_y = table_y_ref[...]
    table_z = table_z_ref[...]
    for slot in range(slots):
        rows = slice(slot * SIDE, (slot + 1) * SIDE)
        waves = jnp.concatenate([low_ref[rows, :], high_ref[rows, :]], axis=1)
        planes_ref[rows, :] = turn_y(table_y, turn_z(waves, table_z))

    @pl.loop(0, slots)
    def _(slot):
        def load(tile):
            tall = planes_ref[pl.ds(pl.multiple_of(slot * SIDE + tile * 8, 8), 8), :]
            return tall[:, :LANES], tall[:, LANES:]

        def store(k, values):
            flat_ref[pl.ds(slot * FLAT + k, 8, stride=STRIDE), :] = values

        to_flat(load, store)
        rows = pl.ds(pl.multiple_of(slot * FLAT, 8), FLAT)
        content = (density_ref[slot] + other_ref[slot]) * (3.0 / math.pi)
        positive = jnp.where(content > 0, content, 1.0)
        root = jnp.exp(jnp.log(positive) * (1.0 / 3.0))
        root = root - (root - positive / (root * root)) * (1.0 / 3.0)
        root = jnp.where(content > 0, root, 0.0)
        inside = mesh_points(own_start + slot, circle_ref[...], length_cells) & (slot < thickness)
        flat_ref[rows, :] = jnp.where(inside, flat_ref[rows, :] - root, 0.0)

    @pl.loop(0, FLAT // 8)
    def _(step):
        for part in range(8):
            lanes = pl.ds(pl.multiple_of((step * 8 + part) * LANES, LANES), LANES)
            out_ref[:, lanes] = flat_ref[pl.ds(step * 8 + part, SLOTS, stride=FLAT), :][:slots]


def from_behind(value, steps):
    count = lax.axis_size("domain")
    leading, last = (max(0, -steps), min(count, count - steps))
    return lax.ppermute(value, "domain", [(source, source + steps) for source in range(leading, last)])


def shards(orbitals, occupation, potential, background, layer_start):
    domains = lax.axis_size("domain")
    states = lax.axis_size("state")
    devices = domains * states
    length_cells = SLAB * domains
    layer_cap, plane = potential.shape
    count = plane // devices
    width = -(-(count + 1) // LANES) * LANES
    circle = jnp.asarray(circle_plane())
    flat_circle = jnp.asarray(circle_table().reshape(FLAT, LANES))
    table_z, into_y, out_of_y = (jnp.asarray(table) for table in tables_of_side())
    table_x = jnp.asarray(hartley_table(length_cells).astype(np.float32))
    params = pltpu.CompilerParams(vmem_limit_bytes=VMEM_BYTES)

    def f32(*shape):
        return jax.ShapeDtypeStruct(shape, jnp.float32)

    def scratch(*shape):
        return pltpu.VMEM(shape, jnp.float32)

    layers = orbitals.reshape(2, layer_cap, FLAT, LANES)
    up, down, up_far, down_far = pl.pallas_call(
        pack_kernel,
        out_shape=(
            f32(2 * HALO + 1, FLAT, LANES),
            f32(2 * HALO + 1, FLAT, LANES),
            f32(2, FLAT, LANES),
            f32(2, FLAT, LANES),
        ),
        in_specs=[SMEM_SPEC, VMEM_SPEC, ANY_SPEC],
        out_specs=(ANY_SPEC,) * 4,
        scratch_shapes=[
            scratch(FLAT * 8, LANES),
            scratch(2, 1, FLAT, LANES),
            pltpu.SemaphoreType.DMA((10,)),
        ],
        compiler_params=params,
        name="pack_halo",
    )(layer_start, potential, layers)
    below = from_behind(up, 1)
    above = from_behind(down, -1)
    below_far = from_behind(up_far, 2)
    above_far = from_behind(down_far, -2)
    v_edges = jnp.concatenate([below[2 * HALO:], above[2 * HALO:]], axis=0)
    v_edges = lax.all_gather(v_edges, "state", axis=0, tiled=True)

    ions = pl.pallas_call(
        functools.partial(ions_kernel, count, length_cells),
        out_shape=f32(domains, SLOTS, width),
        in_specs=[SMEM_SPEC] + [VMEM_SPEC] * 4,
        out_specs=VMEM_SPEC,
        scratch_shapes=[
            scratch(SLOTS * FLAT, LANES),
            scratch(layer_cap * SIDE, WIDTH),
            scratch(SLOTS * SIDE, LANES),
            scratch(SLOTS * SIDE, LANES),
        ],
        compiler_params=params,
        name="ion_waves",
    )(layer_start, background, circle, into_y, table_z)
    ions = lax.all_to_all(ions, "domain", split_axis=0, concat_axis=0, tiled=True)

    span = layer_cap + 2 * HALO
    orbitals_next, density, waves = pl.pallas_call(
        functools.partial(propagate_kernel, count, length_cells),
        out_shape=(
            f32(2, layer_cap, FLAT, LANES),
            f32(layer_cap, FLAT, LANES),
            f32(devices, SLOTS, width),
        ),
        in_specs=[SMEM_SPEC, SMEM_SPEC] + [VMEM_SPEC] * 10,
        out_specs=(VMEM_SPEC,) * 3,
        scratch_shapes=[
            scratch(TERMS, 2, span, TALL, WIDTH),
            scratch(span, SIDE, WIDTH),
            scratch(span, SIDE, WIDTH),
            scratch(SLOTS * FLAT, LANES),
            scratch(layer_cap * SIDE, WIDTH),
            scratch(SLOTS * SIDE, LANES),
            scratch(SLOTS * SIDE, LANES),
        ],
        compiler_params=params,
        name="propagate",
    )(layer_start, occupation, layers, potential, below, above, below_far, above_far, v_edges, circle,
      into_y, table_z)
    waves = lax.all_to_all(waves, ("state", "domain"), split_axis=0, concat_axis=0, tiled=True)
    others = [lambda value, step=step: lax.ppermute(
        value, "state", [(source, source ^ step) for source in range(states)]) for step in (1, 2)]
    density = density + others[0](density)
    other_density = others[1](density)
    waves = pl.pallas_call(
        functools.partial(coulomb_kernel, count, length_cells),
        out_shape=f32(devices, SLOTS, width),
        in_specs=[SMEM_SPEC] + [VMEM_SPEC] * 3,
        out_specs=VMEM_SPEC,
        compiler_params=params,
        name="coulomb",
    )(layer_start, waves, ions, table_x)
    waves = lax.all_to_all(waves, ("state", "domain"), split_axis=0, concat_axis=0, tiled=True)
    potential_next = pl.pallas_call(
        functools.partial(field_kernel, count, length_cells),
        out_shape=f32(layer_cap, plane),
        in_specs=[SMEM_SPEC] + [VMEM_SPEC] * 6,
        out_specs=VMEM_SPEC,
        scratch_shapes=[
            scratch(SLOTS * SIDE, LANES),
            scratch(SLOTS * SIDE, LANES),
            scratch(layer_cap * SIDE, WIDTH),
            scratch(SLOTS * FLAT, LANES),
        ],
        compiler_params=params,
        name="field",
    )(layer_start, waves, density, other_density, flat_circle, out_of_y, table_z)
    return orbitals_next.reshape(orbitals.shape), potential_next


def solution(mesh):
    return jax.shard_map(
        shards,
        mesh=mesh,
        in_specs=(
            P(None, "state", "domain", None),
            P("state"),
            P("domain", None),
            P("domain", None),
            P(),
        ),
        out_specs=(P(None, "state", "domain", None), P("domain", None)),
        check_vma=False,
    )
```

```python
import functools
import math

import jax
import jax.numpy as jnp
import ml_dtypes
import numpy as np
from jax import lax
from jax.experimental import pallas as pl
from jax.experimental.pallas import tpu as pltpu
from jax.sharding import Mesh, PartitionSpec as P

SIDE = 160
SLAB = 5
TERMS = 4

HALO = TERMS
LANES = 128
SLOTS = 8
RUN = SIDE // 8
FLAT = SIDE * SIDE // LANES
STRIDE = FLAT // 8
WIDTH = 2 * LANES
BLOCK = 40
TALL = SIDE + 16

time_step = 0.3
four_pi = 4.0 * math.pi
two_pi = 2.0 * math.pi
highest = lax.Precision.HIGHEST
VMEM_BYTES = 56 * 1024 * 1024
SMEM_SPEC = pl.BlockSpec(memory_space=pltpu.SMEM)
VMEM_SPEC = pl.BlockSpec(memory_space=pltpu.VMEM)
ANY_SPEC = pl.BlockSpec(memory_space=pl.ANY)


def hartley_table(count_cells):
    index_run = np.arange(count_cells)
    angles = (index_run[:, None] * index_run[None, :] % count_cells) * (2.0 * np.pi / count_cells)
    return np.cos(angles) + np.sin(angles)


def plane_order():
    rows = np.arange(SIDE)
    return RUN * (rows % 8) + rows // 8


def two_parts(table):
    table = table.astype(np.float32)
    high = table.astype(ml_dtypes.bfloat16)
    low = (table - high.astype(np.float32)).astype(ml_dtypes.bfloat16)
    return high, low


def tables_of_side():
    table = hartley_table(SIDE)
    along_z = np.zeros((WIDTH, WIDTH))
    along_z[:SIDE, :SIDE] = table
    high, low = two_parts(along_z)
    along_z = np.concatenate([high, high, low], axis=0)
    high, low = two_parts(table[:, plane_order()])
    into_y = np.concatenate([high, high, low], axis=1)
    high, low = two_parts(table[plane_order(), :])
    out_of_y = np.concatenate([high, high, low], axis=1)
    return along_z, into_y, out_of_y


def circle_table():
    across = 2 * np.arange(SIDE, dtype=np.int64) - (SIDE - 1)
    return (across[:, None] ** 2 + across[None, :] ** 2).astype(np.int32)


def circle_plane():
    table = np.full((SIDE, WIDTH), 4 * SIDE * SIDE, np.int32)
    table[:, :SIDE] = circle_table()[plane_order()]
    return table


def mesh_points(x_row, circle, length_cells):
    room = ((length_cells - 2) ** 2 - (2 * x_row - (length_cells - 1)) ** 2) * (SIDE - 2) ** 2
    return (circle * (length_cells - 2) ** 2 <= room) & (circle < 4 * SIDE * SIDE)


def column_pieces(first, count):
    pieces = []
    column = first
    while column < first + count:
        row = column // SIDE
        stop = min((row + 1) * SIDE, first + count)
        pieces.append((row, column - row * SIDE, stop - row * SIDE))
        column = stop
    return pieces


def eight(values):
    missing = jnp.zeros((SLOTS - values.shape[0], values.shape[1]), values.dtype)
    return jnp.concatenate([values, missing], axis=0)


def to_plane(load, store):
    lane = lax.broadcasted_iota(jnp.int32, (8, LANES), 1)
    for step in range(RUN // 4):
        rows = [load(5 * step + part) for part in range(5)]
        store(4 * step, rows[0], rows[1])
        for part in range(1, 4):
            left = pltpu.roll(rows[part], LANES - 32 * part, 1)
            right = pltpu.roll(rows[part + 1], LANES - 32 * part, 1)
            store(4 * step + part, jnp.where(lane < LANES - 32 * part, left, right), right)


def to_flat(load, store):
    lane = lax.broadcasted_iota(jnp.int32, (8, LANES), 1)
    for step in range(RUN // 4):
        turned = []
        for part in range(4):
            low, high = load(4 * step + part)
            if part:
                low = pltpu.roll(low, 32 * part, 1)
                high = pltpu.roll(high, 32 * part, 1)
            turned.append((low, high))
        store(5 * step, turned[0][0])
        for part in range(1, 4):
            ended = 32 * (part - 1)
            values = jnp.where(lane < ended + 32, turned[part - 1][1], turned[part][0])
            if ended:
                values = jnp.where(lane < ended, turned[part - 1][0], values)
            store(5 * step + part, values)
        store(5 * step + 4, jnp.where(lane < 96, turned[3][0], turned[3][1]))


def parts_of(values):
    high = values.astype(jnp.bfloat16)
    low = (values - high.astype(jnp.float32)).astype(jnp.bfloat16)
    return high, low


def turn_z(values, table):
    high, low = parts_of(values)
    return jnp.dot(
        jnp.concatenate([high, low, high], axis=1), table, preferred_element_type=jnp.float32
    )


def turn_y(table, values):
    high, low = parts_of(values)
    return jnp.dot(
        table, jnp.concatenate([high, low, high], axis=0), preferred_element_type=jnp.float32
    )


def send_columns(planes_ref, table_y, table_z, low_ref, high_ref):
    slots = planes_ref.shape[0] // SIDE
    for slot in range(slots):
        rows = slice(slot * SIDE, (slot + 1) * SIDE)
        waves = turn_y(table_y, turn_z(planes_ref[rows, :], table_z))
        low_ref[rows, :] = waves[:, :LANES]
        high_ref[rows, :] = waves[:, LANES:]
    low_ref[slots * SIDE:, :] = jnp.zeros(((SLOTS - slots) * SIDE, LANES), jnp.float32)
    high_ref[slots * SIDE:, :] = jnp.zeros(((SLOTS - slots) * SIDE, LANES), jnp.float32)


def chunk_of(low_ref, high_ref, first_row, pieces, extra):
    parts = []
    for row, start, stop in pieces:
        at = pl.ds(first_row + row, SLOTS, stride=SIDE)
        values = jnp.concatenate([low_ref[at, :], high_ref[at, :]], axis=1)
        parts.append(values[:, start:stop])
    return jnp.concatenate(parts + [extra], axis=1)


def layers_of(stored_ref, flat_ref):
    @pl.loop(0, FLAT // 8)
    def _(step):
        for part in range(8):
            lanes = pl.ds(pl.multiple_of((step * 8 + part) * LANES, LANES), LANES)
            flat_ref[pl.ds(step * 8 + part, SLOTS, stride=FLAT), :] = eight(stored_ref[:, lanes])


def state_index():
    return lax.axis_index("row") * lax.axis_size("core") + lax.axis_index("core")


def place_of(start_ref):
    position = lax.axis_index("domain")
    return position, start_ref[position], start_ref[position + 1] - start_ref[position]


def pack_kernel(start_ref, potential_ref, orbitals_ref, v_up_ref, v_down_ref, up_ref, down_ref, up_far_ref,
                down_far_ref, tile_ref, sems):
    _, _, thickness = place_of(start_ref)
    pick = jnp.minimum(state_index(), HALO - 2)
    first = jnp.maximum(thickness - HALO, 0)
    copies = []

    def copy(source, target):
        made = pltpu.make_async_copy(source, target, sems.at[len(copies)])
        made.start()
        copies.append(made)

    for part in range(2):
        rows = pl.ds(part * HALO, HALO)
        copy(orbitals_ref.at[part, pl.ds(first, HALO)], up_ref.at[rows])
        copy(orbitals_ref.at[part, pl.ds(0, HALO)], down_ref.at[rows])
        copy(orbitals_ref.at[part, pl.ds(thickness - 1, 1)], up_far_ref.at[pl.ds(part, 1)])
        copy(orbitals_ref.at[part, pl.ds(0, 1)], down_far_ref.at[pl.ds(part, 1)])

    @pl.loop(0, FLAT // 8)
    def _(step):
        for part in range(8):
            tile = step * 8 + part
            lanes = pl.ds(pl.multiple_of(tile * LANES, LANES), LANES)
            rows = pl.ds(pl.multiple_of(tile * 8, 8), 8)
            tile_ref[rows, :] = eight(potential_ref[:, lanes])

    @pl.loop(0, FLAT // 8)
    def _(step):
        rows = pl.ds(pl.multiple_of(step * 8, 8), 8)
        v_up_ref[0, rows, :] = tile_ref[pl.ds(step * 64 + thickness - (HALO - 1) + pick, 8, stride=8), :]
        v_down_ref[0, rows, :] = tile_ref[pl.ds(step * 64 + pick, 8, stride=8), :]

    for made in copies:
        made.wait()


def ions_kernel(count, length_cells, start_ref, background_ref, circle_ref, table_y_ref, table_z_ref,
                out_ref, flat_ref, planes_ref, low_ref, high_ref):
    _, own_start, thickness = place_of(start_ref)
    slots = background_ref.shape[0]
    groups, _, width = out_ref.shape
    layers_of(background_ref, flat_ref)

    def body(slot, total):
        def store(tile, low, high):
            rows = pl.ds(pl.multiple_of(slot * SIDE + tile * 8, 8), 8)
            planes_ref[rows, :LANES] = low
            planes_ref[rows, LANES:] = high

        to_plane(lambda k: flat_ref[pl.ds(slot * FLAT + k, 8, stride=STRIDE), :], store)
        rows = pl.ds(pl.multiple_of(slot * SIDE, 8), SIDE)
        inside = mesh_points(own_start + slot, circle_ref[...], length_cells) & (slot < thickness)
        values = jnp.where(inside, planes_ref[rows, :], 0.0)
        planes_ref[rows, :] = values
        return total + jnp.sum(values.reshape(RUN, 8, WIDTH), axis=0)

    total = lax.fori_loop(0, slots, body, jnp.zeros((8, WIDTH), jnp.float32))
    whole = jnp.broadcast_to(jnp.sum(total, keepdims=True), (SLOTS, LANES))[:, :width - count]
    send_columns(planes_ref, table_y_ref[...], table_z_ref[...], low_ref, high_ref)
    core_rows = SIDE // lax.axis_size("core")
    first_row = lax.axis_index("core") * core_rows + lax.axis_index("row") * (core_rows // lax.axis_size("row"))
    for group in range(groups):
        out_ref[group] = chunk_of(low_ref, high_ref, first_row, column_pieces(group * count, count), whole)


def propagate_kernel(count, length_cells, start_ref, weight_ref, orbitals_ref, potential_ref, below_ref,
                     above_ref, below_far_ref, above_far_ref, v_ref, circle_ref, table_y_ref,
                     table_z_ref, next_ref, density_ref, kept_ref, sent_ref, field_ref, centre_ref, beside_ref,
                     flat_ref, planes_ref, low_ref, high_ref):
    position, own_start, thickness = place_of(start_ref)
    domains = lax.axis_size("domain")
    before = start_ref[jnp.maximum(position - 1, 0)]
    after = start_ref[jnp.minimum(position + 2, domains)]
    short_below = ((position > 0) & (own_start - before < HALO)).astype(jnp.int32)
    short_above = (position < domains - 1) & (after - own_start - thickness < HALO)
    weight = weight_ref[0]
    slots = orbitals_ref.shape[1]
    layers = slots + 2 * HALO
    devices, _, width = kept_ref.shape

    def field_layer(part, x_row):
        def store(tile, low, high):
            field_ref[0, part, x_row, 8 + 8 * tile:16 + 8 * tile, :LANES] = low
            field_ref[0, part, x_row, 8 + 8 * tile:16 + 8 * tile, LANES:] = high

        return store

    def potential_layer(x_row):
        def store(tile, low, high):
            centre_ref[x_row, 8 * tile:8 * tile + 8, :LANES] = low
            centre_ref[x_row, 8 * tile:8 * tile + 8, LANES:] = high

        return store

    def rows_from(ref, *at):
        return lambda k: ref[(*at, pl.ds(k, 8, stride=STRIDE), slice(None))]

    layers_of(potential_ref, flat_ref)

    @pl.loop(0, slots)
    def _(slot):
        for part in range(2):
            to_plane(rows_from(orbitals_ref, part, slot), field_layer(part, HALO + slot))
        to_plane(
            lambda k: flat_ref[pl.ds(slot * FLAT + k, 8, stride=STRIDE), :], potential_layer(HALO + slot)
        )

    @pl.loop(0, HALO - 1)
    def _(layer):
        to_plane(rows_from(v_ref, 2 * layer), potential_layer(1 + layer))
        to_plane(rows_from(v_ref, 2 * layer + 1), potential_layer(HALO + thickness + layer))
        for part in range(2):
            to_plane(
                rows_from(below_ref, part * HALO + 1 + layer - short_below), field_layer(part, 1 + layer)
            )
            to_plane(
                rows_from(above_ref, part * HALO + layer), field_layer(part, HALO + thickness + layer)
            )

    @pl.loop(0, 2)
    def _(part):
        last = 2 * HALO - 1 + thickness

        @pl.when(short_below > 0)
        def _():
            to_plane(rows_from(below_far_ref, part), field_layer(part, 0))

        @pl.when(short_below == 0)
        def _():
            to_plane(rows_from(below_ref, part * HALO), field_layer(part, 0))

        @pl.when(short_above)
        def _():
            to_plane(rows_from(above_far_ref, part), field_layer(part, last))

        @pl.when(jnp.logical_not(short_above))
        def _():
            to_plane(rows_from(above_ref, part * HALO + HALO - 1), field_layer(part, last))

    def wrap(term, part, x_row):
        first = field_ref[term, part, x_row, 8:16, :]
        final = field_ref[term, part, x_row, SIDE:SIDE + 8, :]
        field_ref[term, part, x_row, :8, :] = pltpu.roll(final, 1, 0)
        field_ref[term, part, x_row, SIDE + 8:, :] = pltpu.roll(first, 7, 0)

    @pl.loop(0, layers)
    def _(x_row):
        known = x_row < thickness + 2 * HALO
        for block in range(SIDE // BLOCK):
            rows = slice(block * BLOCK, (block + 1) * BLOCK)
            inner = slice(8 + block * BLOCK, 8 + (block + 1) * BLOCK)
            inside = mesh_points(own_start - HALO + x_row, circle_ref[rows, :], length_cells) & known
            centre_ref[x_row, rows, :] = jnp.where(
                inside, (3.0 + centre_ref[x_row, rows, :]) * time_step, 0.0
            )
            beside_ref[x_row, rows, :] = jnp.where(inside, 0.5 * time_step, 0.0)
            for part in range(2):
                field_ref[0, part, x_row, inner, :] = jnp.where(
                    inside, field_ref[0, part, x_row, inner, :], 0.0
                )
        for part in range(2):
            wrap(0, part, x_row)

    def hamilton(term, part, x_row, block, centre, beside):
        tall = field_ref[term, part, x_row, block * BLOCK:block * BLOCK + BLOCK + 16, :]
        inner = slice(8 + block * BLOCK, 8 + (block + 1) * BLOCK)
        field = tall[8:8 + BLOCK]
        around = field_ref[term, part, x_row - 1, inner, :] + field_ref[term, part, x_row + 1, inner, :]
        around = around + (tall[:BLOCK] + tall[16:])
        around = around + (pltpu.roll(field, 1, 1) + pltpu.roll(field, WIDTH - 1, 1))
        return centre * field - beside * around

    for term in range(1, TERMS):

        @pl.loop(term, layers - term)
        def _(x_row, term=term):
            for block in range(SIDE // BLOCK):
                rows = slice(block * BLOCK, (block + 1) * BLOCK)
                inner = slice(8 + block * BLOCK, 8 + (block + 1) * BLOCK)
                centre = centre_ref[x_row, rows, :]
                beside = beside_ref[x_row, rows, :]
                for part in range(2):
                    field_ref[term, part, x_row, inner, :] = hamilton(
                        term - 1, part, x_row, block, centre, beside
                    )
            for part in range(2):
                wrap(term, part, x_row)

    def finish(slot, total):
        x_row = HALO + slot
        owned = slot < thickness
        for block in range(SIDE // BLOCK):
            rows = slice(block * BLOCK, (block + 1) * BLOCK)
            inner = slice(8 + block * BLOCK, 8 + (block + 1) * BLOCK)
            centre = centre_ref[x_row, rows, :]
            beside = beside_ref[x_row, rows, :]
            density = jnp.zeros((BLOCK, WIDTH), jnp.float32)
            for part, sign in ((0, 1.0), (1, -1.0)):
                summed = field_ref[0, part, x_row, inner, :]
                summed = summed + sign * field_ref[1, 1 - part, x_row, inner, :]
                summed = summed - (1.0 / 2.0) * field_ref[2, part, x_row, inner, :]
                summed = summed - (sign / 6.0) * field_ref[3, 1 - part, x_row, inner, :]
                summed = summed + (1.0 / 24.0) * hamilton(3, part, x_row, block, centre, beside)
                summed = jnp.where(owned, summed, 0.0)
                field_ref[2, part, x_row, inner, :] = summed
                density = density + summed * summed
            density = weight * density
            planes_ref[pl.ds(pl.multiple_of(slot * SIDE + block * BLOCK, 8), BLOCK), :] = density
            total = total + jnp.sum(density.reshape(BLOCK // 8, 8, WIDTH), axis=0)

        for part in range(2):

            def load(tile, part=part):
                tall = field_ref[2, part, x_row, 8 + 8 * tile:16 + 8 * tile, :]
                return tall[:, :LANES], tall[:, LANES:]

            def store(k, values, part=part):
                next_ref[part, slot, pl.ds(k, 8, stride=STRIDE), :] = values

            to_flat(load, store)

        def load(tile):
            tall = planes_ref[pl.ds(pl.multiple_of(slot * SIDE + tile * 8, 8), 8), :]
            return tall[:, :LANES], tall[:, LANES:]

        def store(k, values):
            density_ref[slot, pl.ds(k, 8, stride=STRIDE), :] = values

        to_flat(load, store)
        return total

    total = lax.fori_loop(0, slots, finish, jnp.zeros((8, WIDTH), jnp.float32))
    whole = jnp.broadcast_to(jnp.sum(total, keepdims=True), (SLOTS, LANES))[:, :width - count]
    send_columns(planes_ref, table_y_ref[...], table_z_ref[...], low_ref, high_ref)
    core_rows = SIDE // 2
    first_row = lax.axis_index("core") * core_rows
    for device in range(devices):
        pieces = column_pieces(device * count, count)
        kept_ref[device] = chunk_of(low_ref, high_ref, first_row, pieces, whole)
        sent_ref[device] = chunk_of(low_ref, high_ref, core_rows - first_row, pieces, whole)


def wave_squared(index, count_cells):
    folded = jnp.where(2 * index <= count_cells, index, index - count_cells)
    wave_number = folded.astype(jnp.float32) * (two_pi / count_cells)
    return wave_number * wave_number


def coulomb_kernel(count, length_cells, start_ref, charge_ref, ions_ref, table_ref, out_ref):
    domains, _, width = ions_ref.shape
    states = charge_ref.shape[0] // domains
    device = (lax.axis_index("core") * states + lax.axis_index("row")) * domains + lax.axis_index("domain")
    charge = charge_ref[:domains]
    for state in range(1, states):
        charge = charge + charge_ref[state * domains:(state + 1) * domains]
    charge = charge.reshape(domains * SLOTS, width)
    ions = ions_ref[...].reshape(domains * SLOTS, width)
    first = lax.broadcasted_iota(jnp.int32, (domains * SLOTS, width), 0) % SLOTS == 0
    lane = lax.broadcasted_iota(jnp.int32, (domains * SLOTS, width), 1)
    chosen = first & (lane == count)
    electrons = jnp.sum(jnp.where(chosen, charge, 0.0), keepdims=True)
    ionic = jnp.sum(jnp.where(chosen, ions, 0.0), keepdims=True)
    charge = charge - (electrons / ionic) * ions
    layer = lax.broadcasted_iota(jnp.int32, (length_cells, domains * SLOTS), 0)
    place = lax.broadcasted_iota(jnp.int32, (length_cells, domains * SLOTS), 1)
    chosen_layer = jnp.full(layer.shape, -1, jnp.int32)
    for domain in range(domains):
        slot = place - domain * SLOTS
        here = (slot >= 0) & (slot < start_ref[domain + 1] - start_ref[domain])
        chosen_layer = jnp.where(here, start_ref[domain] + slot, chosen_layer)
    pick = (layer == chosen_layer).astype(jnp.float32)
    table = jnp.dot(table_ref[...], pick, precision=highest, preferred_element_type=jnp.float32)
    waves = jnp.dot(table, charge, precision=highest, preferred_element_type=jnp.float32)
    wave_x = lax.broadcasted_iota(jnp.int32, waves.shape, 0)
    column = device * count + lax.broadcasted_iota(jnp.int32, waves.shape, 1)
    wave_y = ((column.astype(jnp.float32) + 0.5) * (1.0 / SIDE)).astype(jnp.int32)
    wave_z = column - wave_y * SIDE
    squared = (
        wave_squared(wave_x, length_cells) + wave_squared(wave_y, SIDE) + wave_squared(wave_z, SIDE)
    )
    gain = jnp.where(squared > 0, four_pi / jnp.where(squared > 0, squared, 1.0), 0.0)
    waves = waves * (gain * (1.0 / (length_cells * SIDE * SIDE)))
    back = lax.dot_general(
        table, waves, (((0,), (0,)), ((), ())), precision=highest, preferred_element_type=jnp.float32
    )
    back = back.reshape(domains, SLOTS, width)
    for state in range(states):
        out_ref[state * domains:(state + 1) * domains] = back


def field_kernel(count, length_cells, start_ref, waves_ref, others_ref, density_ref, other_ref,
                 circle_ref, table_y_ref, table_z_ref, out_ref, low_ref, high_ref, planes_ref, flat_ref):
    _, own_start, thickness = place_of(start_ref)
    devices = waves_ref.shape[0]
    slots = out_ref.shape[0]
    core_rows = SIDE // 2
    first_row = lax.axis_index("core") * core_rows
    for source_ref, first in ((waves_ref, first_row), (others_ref, core_rows - first_row)):
        pieces = []
        for device in range(devices):
            column = 0
            for row, start, stop in column_pieces(device * count, count):
                values = source_ref[device, :, column:column + stop - start]
                column += stop - start
                if start > 0:
                    pieces.append(values)
                    values = jnp.concatenate(pieces, axis=1)
                if stop < SIDE:
                    pieces = [values]
                    continue
                pieces = []
                at = pl.ds(first + row, SLOTS, stride=SIDE)
                low_ref[at, :] = values[:, :LANES]
                high_ref[at, :] = jnp.concatenate(
                    [values[:, LANES:], jnp.zeros((SLOTS, WIDTH - SIDE), jnp.float32)], axis=1
                )
    table_y = table_y_ref[...]
    table_z = table_z_ref[...]
    for slot in range(slots):
        rows = slice(slot * SIDE, (slot + 1) * SIDE)
        waves = jnp.concatenate([low_ref[rows, :], high_ref[rows, :]], axis=1)
        planes_ref[rows, :] = turn_y(table_y, turn_z(waves, table_z))

    @pl.loop(0, slots)
    def _(slot):
        def load(tile):
            tall = planes_ref[pl.ds(pl.multiple_of(slot * SIDE + tile * 8, 8), 8), :]
            return tall[:, :LANES], tall[:, LANES:]

        def store(k, values):
            flat_ref[pl.ds(slot * FLAT + k, 8, stride=STRIDE), :] = values

        to_flat(load, store)
        rows = pl.ds(pl.multiple_of(slot * FLAT, 8), FLAT)
        content = (density_ref[slot] + other_ref[slot]) * (3.0 / math.pi)
        positive = jnp.where(content > 0, content, 1.0)
        root = jnp.exp(jnp.log(positive) * (1.0 / 3.0))
        root = root - (root - positive / (root * root)) * (1.0 / 3.0)
        root = jnp.where(content > 0, root, 0.0)
        inside = mesh_points(own_start + slot, circle_ref[...], length_cells) & (slot < thickness)
        flat_ref[rows, :] = jnp.where(inside, flat_ref[rows, :] - root, 0.0)

    @pl.loop(0, FLAT // 8)
    def _(step):
        for part in range(8):
            lanes = pl.ds(pl.multiple_of((step * 8 + part) * LANES, LANES), LANES)
            out_ref[:, lanes] = flat_ref[pl.ds(step * 8 + part, SLOTS, stride=FLAT), :][:slots]


def from_behind(value, steps):
    count = lax.axis_size("domain")
    leading, last = (max(0, -steps), min(count, count - steps))
    return lax.ppermute(value, "domain", [(source, source + steps) for source in range(leading, last)])


def swapped(value, axis):
    return lax.ppermute(value, axis, [(0, 1), (1, 0)])


def shards(orbitals, occupation, potential, background, layer_start):
    domains = lax.axis_size("domain")
    rows = lax.axis_size("row")
    devices = domains * rows
    length_cells = SLAB * domains
    layer_cap, plane = potential.shape
    count = plane // (2 * devices)
    width = -(-(count + 1) // LANES) * LANES
    circle = jnp.asarray(circle_plane())
    flat_circle = jnp.asarray(circle_table().reshape(FLAT, LANES))
    table_z, into_y, out_of_y = (jnp.asarray(table) for table in tables_of_side())
    table_x = jnp.asarray(hartley_table(length_cells).astype(np.float32))
    params = pltpu.CompilerParams(vmem_limit_bytes=VMEM_BYTES)

    def f32(*shape):
        return jax.ShapeDtypeStruct(shape, jnp.float32)

    def scratch(*shape):
        return pltpu.VMEM(shape, jnp.float32)

    layers = orbitals.reshape(2, layer_cap, FLAT, LANES)
    v_up, v_down, up, down, up_far, down_far = pl.pallas_call(
        pack_kernel,
        out_shape=tuple(f32(size, FLAT, LANES) for size in (1, 1, 2 * HALO, 2 * HALO, 2, 2)),
        in_specs=[SMEM_SPEC, VMEM_SPEC, ANY_SPEC],
        out_specs=(VMEM_SPEC,) * 6,
        scratch_shapes=[scratch(FLAT * 8, LANES), pltpu.SemaphoreType.DMA((8,))],
        compiler_params=params,
        name="pack_halo",
    )(layer_start, potential, layers)
    v_edges = jnp.concatenate([from_behind(v_up, 1), from_behind(v_down, -1)], axis=0)
    below = from_behind(up, 1)
    above = from_behind(down, -1)
    below_far = from_behind(up_far, 2)
    above_far = from_behind(down_far, -2)
    v_edges = lax.all_gather(v_edges, ("row", "core"), axis=0, tiled=True)

    ions = pl.pallas_call(
        functools.partial(ions_kernel, count, length_cells),
        out_shape=f32(domains, SLOTS, width),
        in_specs=[SMEM_SPEC] + [VMEM_SPEC] * 4,
        out_specs=VMEM_SPEC,
        scratch_shapes=[
            scratch(SLOTS * FLAT, LANES),
            scratch(layer_cap * SIDE, WIDTH),
            scratch(SLOTS * SIDE, LANES),
            scratch(SLOTS * SIDE, LANES),
        ],
        compiler_params=params,
        name="ion_waves",
    )(layer_start, background, circle, into_y, table_z)
    ions = lax.all_to_all(ions, "domain", split_axis=0, concat_axis=0, tiled=True)
    ions, below = lax.optimization_barrier((ions, below))

    span = layer_cap + 2 * HALO
    orbitals_next, density, kept, sent = pl.pallas_call(
        functools.partial(propagate_kernel, count, length_cells),
        out_shape=(
            f32(2, layer_cap, FLAT, LANES),
            f32(layer_cap, FLAT, LANES),
            f32(devices, SLOTS, width),
            f32(devices, SLOTS, width),
        ),
        in_specs=[SMEM_SPEC, SMEM_SPEC] + [VMEM_SPEC] * 10,
        out_specs=(VMEM_SPEC,) * 4,
        scratch_shapes=[
            scratch(TERMS, 2, span, TALL, WIDTH),
            scratch(span, SIDE, WIDTH),
            scratch(span, SIDE, WIDTH),
            scratch(SLOTS * FLAT, LANES),
            scratch(layer_cap * SIDE, WIDTH),
            scratch(SLOTS * SIDE, LANES),
            scratch(SLOTS * SIDE, LANES),
        ],
        compiler_params=params,
        name="propagate",
    )(layer_start, occupation, layers, potential, below, above, below_far, above_far, v_edges, circle,
      into_y, table_z)
    waves = kept + swapped(sent, "core")
    density = density + swapped(density, "core")
    waves, density = lax.optimization_barrier((waves, density))
    waves = lax.all_to_all(waves, ("row", "domain"), split_axis=0, concat_axis=0, tiled=True)
    other_density = swapped(density, "row")
    waves = pl.pallas_call(
        functools.partial(coulomb_kernel, count, length_cells),
        out_shape=f32(devices, SLOTS, width),
        in_specs=[SMEM_SPEC] + [VMEM_SPEC] * 3,
        out_specs=VMEM_SPEC,
        compiler_params=params,
        name="coulomb",
    )(layer_start, waves, ions, table_x)
    waves = lax.all_to_all(waves, ("row", "domain"), split_axis=0, concat_axis=0, tiled=True)
    other_waves = swapped(waves, "core")
    potential_next = pl.pallas_call(
        functools.partial(field_kernel, count, length_cells),
        out_shape=f32(layer_cap, plane),
        in_specs=[SMEM_SPEC] + [VMEM_SPEC] * 7,
        out_specs=VMEM_SPEC,
        scratch_shapes=[
            scratch(SLOTS * SIDE, LANES),
            scratch(SLOTS * SIDE, LANES),
            scratch(layer_cap * SIDE, WIDTH),
            scratch(SLOTS * FLAT, LANES),
        ],
        compiler_params=params,
        name="field",
    )(layer_start, waves, other_waves, density, other_density, flat_circle, out_of_y, table_z)
    return orbitals_next.reshape(orbitals.shape), potential_next


def solution(mesh):
    domains = mesh.shape["domain"]
    split = Mesh(mesh.devices.reshape(-1, 2, domains), ("row", "core", "domain"))
    states = ("row", "core")
    return jax.shard_map(
        shards,
        mesh=split,
        in_specs=(
            P(None, states, "domain", None),
            P(states),
            P("domain", None),
            P("domain", None),
            P(),
        ),
        out_specs=(P(None, states, "domain", None), P("domain", None)),
        check_vma=False,
    )
```

```python
import functools
import math

import jax
import jax.numpy as jnp
import ml_dtypes
import numpy as np
from jax import lax
from jax.experimental import pallas as pl
from jax.experimental.pallas import tpu as pltpu
from jax.sharding import Mesh, PartitionSpec as P

SIDE = 160
SLAB = 5
TERMS = 4

HALO = TERMS
LANES = 128
SLOTS = 8
RUN = SIDE // 8
FLAT = SIDE * SIDE // LANES
STRIDE = FLAT // 8
WIDTH = 2 * LANES
BLOCK = 16
TALL = SIDE + 16

time_step = 0.3
four_pi = 4.0 * math.pi
two_pi = 2.0 * math.pi
highest = lax.Precision.HIGHEST
VMEM_BYTES = 56 * 1024 * 1024
SMEM_SPEC = pl.BlockSpec(memory_space=pltpu.SMEM)
VMEM_SPEC = pl.BlockSpec(memory_space=pltpu.VMEM)
ANY_SPEC = pl.BlockSpec(memory_space=pl.ANY)


def hartley_table(count_cells):
    index_run = np.arange(count_cells)
    angles = (index_run[:, None] * index_run[None, :] % count_cells) * (2.0 * np.pi / count_cells)
    return np.cos(angles) + np.sin(angles)


def plane_order():
    rows = np.arange(SIDE)
    return RUN * (rows % 8) + rows // 8


def two_parts(table):
    table = table.astype(np.float32)
    high = table.astype(ml_dtypes.bfloat16)
    low = (table - high.astype(np.float32)).astype(ml_dtypes.bfloat16)
    return high, low


def tables_of_side():
    table = hartley_table(SIDE)
    along_z = np.zeros((WIDTH, WIDTH))
    along_z[:SIDE, :SIDE] = table
    high, low = two_parts(along_z)
    along_z = np.concatenate([high, high, low], axis=0)
    high, low = two_parts(table[:, plane_order()])
    into_y = np.concatenate([high, high, low], axis=1)
    high, low = two_parts(table[plane_order(), :])
    out_of_y = np.concatenate([high, high, low], axis=1)
    return along_z, into_y, out_of_y


def circle_table():
    across = 2 * np.arange(SIDE, dtype=np.int64) - (SIDE - 1)
    return (across[:, None] ** 2 + across[None, :] ** 2).astype(np.int32)


def circle_plane():
    table = np.full((SIDE, WIDTH), 4 * SIDE * SIDE, np.int32)
    table[:, :SIDE] = circle_table()[plane_order()]
    return table


def mesh_points(x_row, circle, length_cells):
    room = ((length_cells - 2) ** 2 - (2 * x_row - (length_cells - 1)) ** 2) * (SIDE - 2) ** 2
    return (circle * (length_cells - 2) ** 2 <= room) & (circle < 4 * SIDE * SIDE)


def column_pieces(first, count):
    pieces = []
    column = first
    while column < first + count:
        row = column // SIDE
        stop = min((row + 1) * SIDE, first + count)
        pieces.append((row, column - row * SIDE, stop - row * SIDE))
        column = stop
    return pieces


def eight(values):
    missing = jnp.zeros((SLOTS - values.shape[0], values.shape[1]), values.dtype)
    return jnp.concatenate([values, missing], axis=0)


def to_plane(load, store):
    lane = lax.broadcasted_iota(jnp.int32, (8, LANES), 1)
    for step in range(RUN // 4):
        rows = [load(5 * step + part) for part in range(5)]
        store(4 * step, rows[0], rows[1])
        for part in range(1, 4):
            left = pltpu.roll(rows[part], LANES - 32 * part, 1)
            right = pltpu.roll(rows[part + 1], LANES - 32 * part, 1)
            store(4 * step + part, jnp.where(lane < LANES - 32 * part, left, right), right)


def to_flat(load, store):
    lane = lax.broadcasted_iota(jnp.int32, (8, LANES), 1)
    for step in range(RUN // 4):
        turned = []
        for part in range(4):
            low, high = load(4 * step + part)
            if part:
                low = pltpu.roll(low, 32 * part, 1)
                high = pltpu.roll(high, 32 * part, 1)
            turned.append((low, high))
        store(5 * step, turned[0][0])
        for part in range(1, 4):
            ended = 32 * (part - 1)
            values = jnp.where(lane < ended + 32, turned[part - 1][1], turned[part][0])
            if ended:
                values = jnp.where(lane < ended, turned[part - 1][0], values)
            store(5 * step + part, values)
        store(5 * step + 4, jnp.where(lane < 96, turned[3][0], turned[3][1]))


def parts_of(values):
    high = values.astype(jnp.bfloat16)
    low = (values - high.astype(jnp.float32)).astype(jnp.bfloat16)
    return high, low


def turn_z(values, table):
    high, low = parts_of(values)
    return jnp.dot(
        jnp.concatenate([high, low, high], axis=1), table, preferred_element_type=jnp.float32
    )


def turn_y(table, values):
    high, low = parts_of(values)
    return jnp.dot(
        table, jnp.concatenate([high, low, high], axis=0), preferred_element_type=jnp.float32
    )


def send_columns(planes_ref, slots, table_y, table_z, low_ref, high_ref):
    along_z = turn_z(planes_ref[:slots * SIDE, :], table_z)
    for slot in range(slots):
        rows = slice(slot * SIDE, (slot + 1) * SIDE)
        waves = turn_y(table_y, along_z[rows])
        low_ref[rows, :] = waves[:, :LANES]
        high_ref[rows, :] = waves[:, LANES:]
    low_ref[slots * SIDE:, :] = jnp.zeros(((SLOTS - slots) * SIDE, LANES), jnp.float32)
    high_ref[slots * SIDE:, :] = jnp.zeros(((SLOTS - slots) * SIDE, LANES), jnp.float32)


def chunk_of(low_ref, high_ref, first_row, pieces, extra):
    parts = []
    for row, start, stop in pieces:
        at = pl.ds(first_row + row, SLOTS, stride=SIDE)
        values = jnp.concatenate([low_ref[at, :], high_ref[at, :]], axis=1)
        parts.append(values[:, start:stop])
    return jnp.concatenate(parts + [extra], axis=1)


def layers_of(stored_ref, flat_ref):
    @pl.loop(0, FLAT // 8)
    def _(step):
        for part in range(8):
            lanes = pl.ds(pl.multiple_of((step * 8 + part) * LANES, LANES), LANES)
            flat_ref[pl.ds(step * 8 + part, SLOTS, stride=FLAT), :] = eight(stored_ref[:, lanes])


def place_of(start_ref):
    position = lax.axis_index("domain")
    return position, start_ref[position], start_ref[position + 1] - start_ref[position]


def pack_kernel(start_ref, potential_ref, orbitals_ref, v_ref, up_ref, down_ref, up_far_ref, down_far_ref,
                tile_ref, sems):
    _, _, thickness = place_of(start_ref)
    v_first = jnp.where(lax.axis_index("core") == 0, thickness - (HALO - 1), 0)
    first = jnp.maximum(thickness - HALO, 0)
    copies = []

    def copy(source, target):
        made = pltpu.make_async_copy(source, target, sems.at[len(copies)])
        made.start()
        copies.append(made)

    for part in range(2):
        rows = pl.ds(part * HALO, HALO)
        copy(orbitals_ref.at[part, pl.ds(first, HALO)], up_ref.at[rows])
        copy(orbitals_ref.at[part, pl.ds(0, HALO)], down_ref.at[rows])
        copy(orbitals_ref.at[part, pl.ds(thickness - 1, 1)], up_far_ref.at[pl.ds(part, 1)])
        copy(orbitals_ref.at[part, pl.ds(0, 1)], down_far_ref.at[pl.ds(part, 1)])

    @pl.loop(0, FLAT // 8)
    def _(step):
        for part in range(8):
            tile = step * 8 + part
            lanes = pl.ds(pl.multiple_of(tile * LANES, LANES), LANES)
            rows = pl.ds(pl.multiple_of(tile * 8, 8), 8)
            tile_ref[rows, :] = eight(potential_ref[:, lanes])

    @pl.loop(0, FLAT // 8)
    def _(step):
        rows = pl.ds(pl.multiple_of(step * 8, 8), 8)
        for layer in range(HALO - 1):
            v_ref[layer, rows, :] = tile_ref[pl.ds(step * 64 + v_first + layer, 8, stride=8), :]

    for made in copies:
        made.wait()


def ions_kernel(count, length_cells, start_ref, background_ref, circle_ref, table_y_ref, table_z_ref,
                out_ref, flat_ref, planes_ref, low_ref, high_ref):
    _, own_start, thickness = place_of(start_ref)
    slots = background_ref.shape[0]
    groups, _, width = out_ref.shape
    layers_of(background_ref, flat_ref)

    def body(slot, total):
        def store(tile, low, high):
            rows = pl.ds(pl.multiple_of(slot * SIDE + tile * 8, 8), 8)
            planes_ref[rows, :LANES] = low
            planes_ref[rows, LANES:] = high

        to_plane(lambda k: flat_ref[pl.ds(slot * FLAT + k, 8, stride=STRIDE), :], store)
        rows = pl.ds(pl.multiple_of(slot * SIDE, 8), SIDE)
        inside = mesh_points(own_start + slot, circle_ref[...], length_cells) & (slot < thickness)
        values = jnp.where(inside, planes_ref[rows, :], 0.0)
        planes_ref[rows, :] = values
        return total + jnp.sum(values.reshape(RUN, 8, WIDTH), axis=0)

    total = lax.fori_loop(0, slots, body, jnp.zeros((8, WIDTH), jnp.float32))
    whole = jnp.broadcast_to(jnp.sum(total, keepdims=True), (SLOTS, LANES))[:, :width - count]
    send_columns(planes_ref, slots, table_y_ref[...], table_z_ref[...], low_ref, high_ref)
    core_rows = SIDE // lax.axis_size("core")
    first_row = lax.axis_index("core") * core_rows + lax.axis_index("row") * (core_rows // lax.axis_size("row"))
    for group in range(groups):
        out_ref[group] = chunk_of(low_ref, high_ref, first_row, column_pieces(group * count, count), whole)


def propagate_kernel(count, length_cells, start_ref, weight_ref, orbitals_ref, potential_ref, below_ref,
                     above_ref, below_far_ref, above_far_ref, v_ref, v_other_ref, circle_ref,
                     table_y_ref, table_z_ref, next_ref, density_kept_ref, density_sent_ref, kept_ref, sent_ref, field_ref, centre_ref, beside_ref,
                     flat_ref, planes_ref, low_ref, high_ref):
    position, own_start, thickness = place_of(start_ref)
    domains = lax.axis_size("domain")
    before = start_ref[jnp.maximum(position - 1, 0)]
    after = start_ref[jnp.minimum(position + 2, domains)]
    short_below = ((position > 0) & (own_start - before < HALO)).astype(jnp.int32)
    short_above = (position < domains - 1) & (after - own_start - thickness < HALO)
    weight = weight_ref[0]
    core = lax.axis_index("core")
    slots = orbitals_ref.shape[1]
    layers = slots + 2 * HALO
    devices, _, width = kept_ref.shape

    def field_layer(part, x_row):
        def store(tile, low, high):
            field_ref[0, part, x_row, 8 + 8 * tile:16 + 8 * tile, :LANES] = low
            field_ref[0, part, x_row, 8 + 8 * tile:16 + 8 * tile, LANES:] = high

        return store

    def potential_layer(x_row):
        def store(tile, low, high):
            centre_ref[x_row, 8 * tile:8 * tile + 8, :LANES] = low
            centre_ref[x_row, 8 * tile:8 * tile + 8, LANES:] = high

        return store

    def rows_from(ref, *at):
        return lambda k: ref[(*at, pl.ds(k, 8, stride=STRIDE), slice(None))]

    layers_of(potential_ref, flat_ref)

    @pl.loop(0, slots)
    def _(slot):
        for part in range(2):
            to_plane(rows_from(orbitals_ref, part, slot), field_layer(part, HALO + slot))
        to_plane(
            lambda k: flat_ref[pl.ds(slot * FLAT + k, 8, stride=STRIDE), :], potential_layer(HALO + slot)
        )

    @pl.loop(0, HALO - 1)
    def _(layer):
        lower = 1 + layer
        upper = HALO + thickness + layer
        to_plane(rows_from(v_ref, layer), potential_layer(jnp.where(core == 0, lower, upper)))
        to_plane(rows_from(v_other_ref, layer), potential_layer(jnp.where(core == 0, upper, lower)))
        for part in range(2):
            to_plane(
                rows_from(below_ref, part * HALO + 1 + layer - short_below), field_layer(part, 1 + layer)
            )
            to_plane(
                rows_from(above_ref, part * HALO + layer), field_layer(part, HALO + thickness + layer)
            )

    @pl.loop(0, 2)
    def _(part):
        last = 2 * HALO - 1 + thickness

        @pl.when(short_below > 0)
        def _():
            to_plane(rows_from(below_far_ref, part), field_layer(part, 0))

        @pl.when(short_below == 0)
        def _():
            to_plane(rows_from(below_ref, part * HALO), field_layer(part, 0))

        @pl.when(short_above)
        def _():
            to_plane(rows_from(above_far_ref, part), field_layer(part, last))

        @pl.when(jnp.logical_not(short_above))
        def _():
            to_plane(rows_from(above_ref, part * HALO + HALO - 1), field_layer(part, last))

    def wrap(term, part, x_row):
        first = field_ref[term, part, x_row, 8:16, :]
        final = field_ref[term, part, x_row, SIDE:SIDE + 8, :]
        field_ref[term, part, x_row, :8, :] = pltpu.roll(final, 1, 0)
        field_ref[term, part, x_row, SIDE + 8:, :] = pltpu.roll(first, 7, 0)

    @pl.loop(0, layers)
    def _(x_row):
        known = x_row < thickness + 2 * HALO
        for block in range(SIDE // BLOCK):
            rows = slice(block * BLOCK, (block + 1) * BLOCK)
            inner = slice(8 + block * BLOCK, 8 + (block + 1) * BLOCK)
            inside = mesh_points(own_start - HALO + x_row, circle_ref[rows, :], length_cells) & known
            centre_ref[x_row, rows, :] = jnp.where(
                inside, (3.0 + centre_ref[x_row, rows, :]) * time_step, 0.0
            )
            beside_ref[x_row, rows, :] = jnp.where(inside, 0.5 * time_step, 0.0)
            for part in range(2):
                field_ref[0, part, x_row, inner, :] = jnp.where(
                    inside, field_ref[0, part, x_row, inner, :], 0.0
                )
        for part in range(2):
            wrap(0, part, x_row)

    def hamilton(term, part, x_row, block, centre, beside):
        tall = field_ref[term, part, x_row, block * BLOCK:block * BLOCK + BLOCK + 16, :]
        inner = slice(8 + block * BLOCK, 8 + (block + 1) * BLOCK)
        field = tall[8:8 + BLOCK]
        around = field_ref[term, part, x_row - 1, inner, :] + field_ref[term, part, x_row + 1, inner, :]
        around = around + (tall[:BLOCK] + tall[16:])
        around = around + (pltpu.roll(field, 1, 1) + pltpu.roll(field, WIDTH - 1, 1))
        return centre * field - beside * around

    for term in range(1, TERMS):

        @pl.loop(term, layers - term)
        def _(x_row, term=term):
            for block in range(SIDE // BLOCK):
                rows = slice(block * BLOCK, (block + 1) * BLOCK)
                inner = slice(8 + block * BLOCK, 8 + (block + 1) * BLOCK)
                centre = centre_ref[x_row, rows, :]
                beside = beside_ref[x_row, rows, :]
                for part in range(2):
                    field_ref[term, part, x_row, inner, :] = hamilton(
                        term - 1, part, x_row, block, centre, beside
                    )
            for part in range(2):
                wrap(term, part, x_row)

    def finish(slot, total):
        x_row = HALO + slot
        owned = slot < thickness
        for block in range(SIDE // BLOCK):
            rows = slice(block * BLOCK, (block + 1) * BLOCK)
            inner = slice(8 + block * BLOCK, 8 + (block + 1) * BLOCK)
            centre = centre_ref[x_row, rows, :]
            beside = beside_ref[x_row, rows, :]
            density = jnp.zeros((BLOCK, WIDTH), jnp.float32)
            for part, sign in ((0, 1.0), (1, -1.0)):
                summed = field_ref[0, part, x_row, inner, :]
                summed = summed + sign * field_ref[1, 1 - part, x_row, inner, :]
                summed = summed - (1.0 / 2.0) * field_ref[2, part, x_row, inner, :]
                summed = summed - (sign / 6.0) * field_ref[3, 1 - part, x_row, inner, :]
                summed = summed + (1.0 / 24.0) * hamilton(3, part, x_row, block, centre, beside)
                summed = jnp.where(owned, summed, 0.0)
                field_ref[2, part, x_row, inner, :] = summed
                density = density + summed * summed
            density = weight * density
            planes_ref[pl.ds(pl.multiple_of(slot * SIDE + block * BLOCK, 8), BLOCK), :] = density
            total = total + jnp.sum(density.reshape(BLOCK // 8, 8, WIDTH), axis=0)

        for part in range(2):

            def load(tile, part=part):
                tall = field_ref[2, part, x_row, 8 + 8 * tile:16 + 8 * tile, :]
                return tall[:, :LANES], tall[:, LANES:]

            def store(k, values, part=part):
                next_ref[part, slot, pl.ds(k, 8, stride=STRIDE), :] = values

            to_flat(load, store)

        return total

    total = lax.fori_loop(0, slots, finish, jnp.zeros((8, WIDTH), jnp.float32))
    planes_ref[slots * SIDE:, :] = jnp.zeros(((SLOTS - slots) * SIDE, WIDTH), jnp.float32)

    @pl.loop(0, SLOTS // 2)
    def _(slot):
        for first, target_ref in ((core, density_kept_ref), (1 - core, density_sent_ref)):

            def load(tile, first=first):
                row = (first * (SLOTS // 2) + slot) * SIDE + tile * 8
                tall = planes_ref[pl.ds(pl.multiple_of(row, 8), 8), :]
                return tall[:, :LANES], tall[:, LANES:]

            def store(k, values, target_ref=target_ref):
                target_ref[slot, pl.ds(k, 8, stride=STRIDE), :] = values

            to_flat(load, store)

    whole = jnp.broadcast_to(jnp.sum(total, keepdims=True), (SLOTS, LANES))[:, :width - count]
    send_columns(planes_ref, slots, table_y_ref[...], table_z_ref[...], low_ref, high_ref)
    core_rows = SIDE // 2
    first_row = core * core_rows
    for device in range(devices):
        pieces = column_pieces(device * count, count)
        kept_ref[device] = chunk_of(low_ref, high_ref, first_row, pieces, whole)
        sent_ref[device] = chunk_of(low_ref, high_ref, core_rows - first_row, pieces, whole)


def wave_squared(index, count_cells):
    folded = jnp.where(2 * index <= count_cells, index, index - count_cells)
    wave_number = folded.astype(jnp.float32) * (two_pi / count_cells)
    return wave_number * wave_number


def coulomb_kernel(count, length_cells, start_ref, charge_ref, ions_ref, table_ref, out_ref):
    domains, _, width = ions_ref.shape
    states = charge_ref.shape[0] // domains
    device = (lax.axis_index("core") * states + lax.axis_index("row")) * domains + lax.axis_index("domain")
    charge = charge_ref[:domains]
    for state in range(1, states):
        charge = charge + charge_ref[state * domains:(state + 1) * domains]
    charge = charge.reshape(domains * SLOTS, width)
    ions = ions_ref[...].reshape(domains * SLOTS, width)
    first = lax.broadcasted_iota(jnp.int32, (domains * SLOTS, width), 0) % SLOTS == 0
    lane = lax.broadcasted_iota(jnp.int32, (domains * SLOTS, width), 1)
    chosen = first & (lane == count)
    electrons = jnp.sum(jnp.where(chosen, charge, 0.0), keepdims=True)
    ionic = jnp.sum(jnp.where(chosen, ions, 0.0), keepdims=True)
    charge = charge - (electrons / ionic) * ions
    layer = lax.broadcasted_iota(jnp.int32, (length_cells, domains * SLOTS), 0)
    place = lax.broadcasted_iota(jnp.int32, (length_cells, domains * SLOTS), 1)
    chosen_layer = jnp.full(layer.shape, -1, jnp.int32)
    for domain in range(domains):
        slot = place - domain * SLOTS
        here = (slot >= 0) & (slot < start_ref[domain + 1] - start_ref[domain])
        chosen_layer = jnp.where(here, start_ref[domain] + slot, chosen_layer)
    pick = (layer == chosen_layer).astype(jnp.float32)
    table = jnp.dot(table_ref[...], pick, precision=highest, preferred_element_type=jnp.float32)
    waves = jnp.dot(table, charge, precision=highest, preferred_element_type=jnp.float32)
    wave_x = lax.broadcasted_iota(jnp.int32, waves.shape, 0)
    column = device * count + lax.broadcasted_iota(jnp.int32, waves.shape, 1)
    wave_y = ((column.astype(jnp.float32) + 0.5) * (1.0 / SIDE)).astype(jnp.int32)
    wave_z = column - wave_y * SIDE
    squared = (
        wave_squared(wave_x, length_cells) + wave_squared(wave_y, SIDE) + wave_squared(wave_z, SIDE)
    )
    gain = jnp.where(squared > 0, four_pi / jnp.where(squared > 0, squared, 1.0), 0.0)
    waves = waves * (gain * (1.0 / (length_cells * SIDE * SIDE)))
    back = lax.dot_general(
        table, waves, (((0,), (0,)), ((), ())), precision=highest, preferred_element_type=jnp.float32
    )
    back = back.reshape(domains, SLOTS, width)
    for state in range(states):
        out_ref[state * domains:(state + 1) * domains] = back


def field_kernel(count, length_cells, start_ref, waves_ref, others_ref, density_ref, other_ref,
                 circle_ref, table_y_ref, table_z_ref, out_ref, low_ref, high_ref, planes_ref, flat_ref):
    _, own_start, thickness = place_of(start_ref)
    devices = waves_ref.shape[0]
    slots = out_ref.shape[0]
    core = lax.axis_index("core")
    core_rows = SIDE // 2
    first_row = core * core_rows
    for source_ref, first in ((waves_ref, first_row), (others_ref, core_rows - first_row)):
        pieces = []
        for device in range(devices):
            column = 0
            for row, start, stop in column_pieces(device * count, count):
                values = source_ref[device, :, column:column + stop - start]
                column += stop - start
                if start > 0:
                    pieces.append(values)
                    values = jnp.concatenate(pieces, axis=1)
                if stop < SIDE:
                    pieces = [values]
                    continue
                pieces = []
                at = pl.ds(first + row, SLOTS, stride=SIDE)
                low_ref[at, :] = values[:, :LANES]
                high_ref[at, :] = jnp.concatenate(
                    [values[:, LANES:], jnp.zeros((SLOTS, WIDTH - SIDE), jnp.float32)], axis=1
                )
    table_y = table_y_ref[...]
    table_z = table_z_ref[...]
    used = slice(0, slots * SIDE)
    along_z = turn_z(jnp.concatenate([low_ref[used, :], high_ref[used, :]], axis=1), table_z)
    for slot in range(slots):
        rows = slice(slot * SIDE, (slot + 1) * SIDE)
        planes_ref[rows, :] = turn_y(table_y, along_z[rows])

    @pl.loop(0, slots)
    def _(slot):
        def load(tile):
            tall = planes_ref[pl.ds(pl.multiple_of(slot * SIDE + tile * 8, 8), 8), :]
            return tall[:, :LANES], tall[:, LANES:]

        def store(k, values):
            flat_ref[pl.ds(slot * FLAT + k, 8, stride=STRIDE), :] = values

        to_flat(load, store)
        rows = pl.ds(pl.multiple_of(slot * FLAT, 8), FLAT)
        here = slot // (SLOTS // 2) == core
        kept_slot = slot % (SLOTS // 2)
        content = jnp.where(here, density_ref[kept_slot], other_ref[kept_slot]) * (3.0 / math.pi)
        positive = jnp.where(content > 0, content, 1.0)
        root = jnp.exp(jnp.log(positive) * (1.0 / 3.0))
        root = root - (root - positive / (root * root)) * (1.0 / 3.0)
        root = jnp.where(content > 0, root, 0.0)
        inside = mesh_points(own_start + slot, circle_ref[...], length_cells) & (slot < thickness)
        flat_ref[rows, :] = jnp.where(inside, flat_ref[rows, :] - root, 0.0)

    @pl.loop(0, FLAT // 8)
    def _(step):
        for part in range(8):
            lanes = pl.ds(pl.multiple_of((step * 8 + part) * LANES, LANES), LANES)
            out_ref[:, lanes] = flat_ref[pl.ds(step * 8 + part, SLOTS, stride=FLAT), :][:slots]


def from_behind(value, steps):
    count = lax.axis_size("domain")
    leading, last = (max(0, -steps), min(count, count - steps))
    return lax.ppermute(value, "domain", [(source, source + steps) for source in range(leading, last)])


def swapped(value, axis):
    return lax.ppermute(value, axis, [(0, 1), (1, 0)])


def shards(orbitals, occupation, potential, background, layer_start):
    domains = lax.axis_size("domain")
    rows = lax.axis_size("row")
    devices = domains * rows
    length_cells = SLAB * domains
    layer_cap, plane = potential.shape
    count = plane // (2 * devices)
    width = -(-(count + 1) // LANES) * LANES
    circle = jnp.asarray(circle_plane())
    flat_circle = jnp.asarray(circle_table().reshape(FLAT, LANES))
    table_z, into_y, out_of_y = (jnp.asarray(table) for table in tables_of_side())
    table_x = jnp.asarray(hartley_table(length_cells).astype(np.float32))
    params = pltpu.CompilerParams(vmem_limit_bytes=VMEM_BYTES)

    def f32(*shape):
        return jax.ShapeDtypeStruct(shape, jnp.float32)

    def scratch(*shape):
        return pltpu.VMEM(shape, jnp.float32)

    layers = orbitals.reshape(2, layer_cap, FLAT, LANES)
    v_rows, up, down, up_far, down_far = pl.pallas_call(
        pack_kernel,
        out_shape=tuple(f32(size, FLAT, LANES) for size in (HALO - 1, 2 * HALO, 2 * HALO, 2, 2)),
        in_specs=[SMEM_SPEC, VMEM_SPEC, ANY_SPEC],
        out_specs=(VMEM_SPEC,) * 5,
        scratch_shapes=[scratch(FLAT * 8, LANES), pltpu.SemaphoreType.DMA((8,))],
        compiler_params=params,
        name="pack_halo",
    )(layer_start, potential, layers)
    v_rows = lax.ppermute(
        v_rows,
        ("core", "domain"),
        [(source, source + 1) for source in range(domains - 1)]
        + [(domains + source + 1, domains + source) for source in range(domains - 1)],
    )
    below = from_behind(up, 1)
    above = from_behind(down, -1)
    below_far = from_behind(up_far, 2)
    above_far = from_behind(down_far, -2)
    v_others = swapped(v_rows, "core")

    ions = pl.pallas_call(
        functools.partial(ions_kernel, count, length_cells),
        out_shape=f32(domains, SLOTS, width),
        in_specs=[SMEM_SPEC] + [VMEM_SPEC] * 4,
        out_specs=VMEM_SPEC,
        scratch_shapes=[
            scratch(SLOTS * FLAT, LANES),
            scratch(layer_cap * SIDE, WIDTH),
            scratch(SLOTS * SIDE, LANES),
            scratch(SLOTS * SIDE, LANES),
        ],
        compiler_params=params,
        name="ion_waves",
    )(layer_start, background, circle, into_y, table_z)
    ions = lax.all_to_all(ions, "domain", split_axis=0, concat_axis=0, tiled=True)
    ions, below = lax.optimization_barrier((ions, below))

    span = layer_cap + 2 * HALO
    orbitals_next, density_kept, density_sent, kept, sent = pl.pallas_call(
        functools.partial(propagate_kernel, count, length_cells),
        out_shape=(
            f32(2, layer_cap, FLAT, LANES),
            f32(SLOTS // 2, FLAT, LANES),
            f32(SLOTS // 2, FLAT, LANES),
            f32(devices, SLOTS, width),
            f32(devices, SLOTS, width),
        ),
        in_specs=[SMEM_SPEC, SMEM_SPEC] + [VMEM_SPEC] * 11,
        out_specs=(VMEM_SPEC,) * 5,
        scratch_shapes=[
            scratch(TERMS, 2, span, TALL, WIDTH),
            scratch(span, SIDE, WIDTH),
            scratch(span, SIDE, WIDTH),
            scratch(SLOTS * FLAT, LANES),
            scratch(SLOTS * SIDE, WIDTH),
            scratch(SLOTS * SIDE, LANES),
            scratch(SLOTS * SIDE, LANES),
        ],
        compiler_params=params,
        name="propagate",
    )(layer_start, occupation, layers, potential, below, above, below_far, above_far, v_rows,
      v_others, circle, into_y, table_z)
    waves = kept + swapped(sent, "core")
    density = density_kept + swapped(density_sent, "core")
    waves, density = lax.optimization_barrier((waves, density))
    waves = lax.all_to_all(waves, ("row", "domain"), split_axis=0, concat_axis=0, tiled=True)
    other_density = swapped(density, "row")
    waves, other_density = lax.optimization_barrier((waves, other_density))
    density = density + other_density
    other_density = swapped(density, "core")
    waves = pl.pallas_call(
        functools.partial(coulomb_kernel, count, length_cells),
        out_shape=f32(devices, SLOTS, width),
        in_specs=[SMEM_SPEC] + [VMEM_SPEC] * 3,
        out_specs=VMEM_SPEC,
        compiler_params=params,
        name="coulomb",
    )(layer_start, waves, ions, table_x)
    waves = lax.all_to_all(waves, ("row", "domain"), split_axis=0, concat_axis=0, tiled=True)
    other_waves = swapped(waves, "core")
    potential_next = pl.pallas_call(
        functools.partial(field_kernel, count, length_cells),
        out_shape=f32(layer_cap, plane),
        in_specs=[SMEM_SPEC] + [VMEM_SPEC] * 7,
        out_specs=VMEM_SPEC,
        scratch_shapes=[
            scratch(SLOTS * SIDE, LANES),
            scratch(SLOTS * SIDE, LANES),
            scratch(layer_cap * SIDE, WIDTH),
            scratch(SLOTS * FLAT, LANES),
        ],
        compiler_params=params,
        name="field",
    )(layer_start, waves, other_waves, density, other_density, flat_circle, out_of_y, table_z)
    return orbitals_next.reshape(orbitals.shape), potential_next


def solution(mesh):
    domains = mesh.shape["domain"]
    split = Mesh(mesh.devices.reshape(-1, 2, domains), ("row", "core", "domain"))
    states = ("row", "core")
    return jax.shard_map(
        shards,
        mesh=split,
        in_specs=(
            P(None, states, "domain", None),
            P(states),
            P("domain", None),
            P("domain", None),
            P(),
        ),
        out_specs=(P(None, states, "domain", None), P("domain", None)),
        check_vma=False,
    )
```

```python
import functools
import math

import jax
import jax.numpy as jnp
import ml_dtypes
import numpy as np
from jax import lax
from jax.experimental import pallas as pl
from jax.experimental.pallas import tpu as pltpu
from jax.sharding import Mesh, PartitionSpec as P

SIDE = 160
SLAB = 5
TERMS = 4

HALO = TERMS
LANES = 128
SLOTS = 8
RUN = SIDE // 8
FLAT = SIDE * SIDE // LANES
STRIDE = FLAT // 8
WIDTH = 2 * LANES
BLOCK = 16
TALL = SIDE + 16

time_step = 0.3
four_pi = 4.0 * math.pi
two_pi = 2.0 * math.pi
highest = lax.Precision.HIGHEST
VMEM_BYTES = 56 * 1024 * 1024
SMEM_SPEC = pl.BlockSpec(memory_space=pltpu.SMEM)
VMEM_SPEC = pl.BlockSpec(memory_space=pltpu.VMEM)
ANY_SPEC = pl.BlockSpec(memory_space=pl.ANY)


def hartley_table(count_cells):
    index_run = np.arange(count_cells)
    angles = (index_run[:, None] * index_run[None, :] % count_cells) * (2.0 * np.pi / count_cells)
    return np.cos(angles) + np.sin(angles)


def plane_order():
    rows = np.arange(SIDE)
    return RUN * (rows % 8) + rows // 8


def two_parts(table):
    table = table.astype(np.float32)
    high = table.astype(ml_dtypes.bfloat16)
    low = (table - high.astype(np.float32)).astype(ml_dtypes.bfloat16)
    return high, low


def tables_of_side():
    table = hartley_table(SIDE)
    along_z = np.zeros((WIDTH, WIDTH))
    along_z[:SIDE, :SIDE] = table
    high, low = two_parts(along_z)
    along_z = np.concatenate([high, high, low], axis=0)
    high, low = two_parts(table[:, plane_order()])
    into_y = np.concatenate([high, high, low], axis=1)
    high, low = two_parts(table[plane_order(), :])
    out_of_y = np.concatenate([high, high, low], axis=1)
    return along_z, into_y, out_of_y


def circle_table():
    across = 2 * np.arange(SIDE, dtype=np.int64) - (SIDE - 1)
    return (across[:, None] ** 2 + across[None, :] ** 2).astype(np.int32)


def circle_plane():
    table = np.full((SIDE, WIDTH), 4 * SIDE * SIDE, np.int32)
    table[:, :SIDE] = circle_table()[plane_order()]
    return table


def mesh_points(x_row, circle, length_cells):
    room = ((length_cells - 2) ** 2 - (2 * x_row - (length_cells - 1)) ** 2) * (SIDE - 2) ** 2
    return (circle * (length_cells - 2) ** 2 <= room) & (circle < 4 * SIDE * SIDE)


def column_pieces(first, count):
    pieces = []
    column = first
    while column < first + count:
        row = column // SIDE
        stop = min((row + 1) * SIDE, first + count)
        pieces.append((row, column - row * SIDE, stop - row * SIDE))
        column = stop
    return pieces


def eight(values):
    missing = jnp.zeros((SLOTS - values.shape[0], values.shape[1]), values.dtype)
    return jnp.concatenate([values, missing], axis=0)


def to_plane(load, store):
    lane = lax.broadcasted_iota(jnp.int32, (8, LANES), 1)
    for step in range(RUN // 4):
        rows = [load(5 * step + part) for part in range(5)]
        store(4 * step, rows[0], rows[1])
        for part in range(1, 4):
            left = pltpu.roll(rows[part], LANES - 32 * part, 1)
            right = pltpu.roll(rows[part + 1], LANES - 32 * part, 1)
            store(4 * step + part, jnp.where(lane < LANES - 32 * part, left, right), right)


def to_flat(load, store):
    lane = lax.broadcasted_iota(jnp.int32, (8, LANES), 1)
    for step in range(RUN // 4):
        turned = []
        for part in range(4):
            low, high = load(4 * step + part)
            if part:
                low = pltpu.roll(low, 32 * part, 1)
                high = pltpu.roll(high, 32 * part, 1)
            turned.append((low, high))
        store(5 * step, turned[0][0])
        for part in range(1, 4):
            ended = 32 * (part - 1)
            values = jnp.where(lane < ended + 32, turned[part - 1][1], turned[part][0])
            if ended:
                values = jnp.where(lane < ended, turned[part - 1][0], values)
            store(5 * step + part, values)
        store(5 * step + 4, jnp.where(lane < 96, turned[3][0], turned[3][1]))


def parts_of(values):
    high = values.astype(jnp.bfloat16)
    low = (values - high.astype(jnp.float32)).astype(jnp.bfloat16)
    return high, low


def turn_z(values, table):
    high, low = parts_of(values)
    return jnp.dot(
        jnp.concatenate([high, low, high], axis=1), table, preferred_element_type=jnp.float32
    )


def turn_y(table, values):
    high, low = parts_of(values)
    return jnp.dot(
        table, jnp.concatenate([high, low, high], axis=0), preferred_element_type=jnp.float32
    )


def send_columns(planes_ref, slots, table_y, table_z, low_ref, high_ref):
    along_z = turn_z(planes_ref[:slots * SIDE, :], table_z)
    for slot in range(slots):
        rows = slice(slot * SIDE, (slot + 1) * SIDE)
        waves = turn_y(table_y, along_z[rows])
        low_ref[rows, :] = waves[:, :LANES]
        high_ref[rows, :] = waves[:, LANES:]
    low_ref[slots * SIDE:, :] = jnp.zeros(((SLOTS - slots) * SIDE, LANES), jnp.float32)
    high_ref[slots * SIDE:, :] = jnp.zeros(((SLOTS - slots) * SIDE, LANES), jnp.float32)


def chunk_of(low_ref, high_ref, first_row, pieces, extra):
    parts = []
    for row, start, stop in pieces:
        at = pl.ds(first_row + row, SLOTS, stride=SIDE)
        values = jnp.concatenate([low_ref[at, :], high_ref[at, :]], axis=1)
        parts.append(values[:, start:stop])
    return jnp.concatenate(parts + [extra], axis=1)


def layers_of(stored_ref, flat_ref):
    @pl.loop(0, FLAT // 8)
    def _(step):
        for part in range(8):
            lanes = pl.ds(pl.multiple_of((step * 8 + part) * LANES, LANES), LANES)
            flat_ref[pl.ds(step * 8 + part, SLOTS, stride=FLAT), :] = eight(stored_ref[:, lanes])


def place_of(start_ref):
    position = lax.axis_index("domain")
    return position, start_ref[position], start_ref[position + 1] - start_ref[position]


def pack_kernel(start_ref, potential_ref, orbitals_ref, v_ref, up_ref, down_ref, up_far_ref, down_far_ref,
                tile_ref, sems):
    _, _, thickness = place_of(start_ref)
    v_first = jnp.where(lax.axis_index("core") == 0, thickness - (HALO - 1), 0)
    first = jnp.maximum(thickness - HALO, 0)
    copies = []

    def copy(source, target):
        made = pltpu.make_async_copy(source, target, sems.at[len(copies)])
        made.start()
        copies.append(made)

    for part in range(2):
        rows = pl.ds(part * HALO, HALO)
        copy(orbitals_ref.at[part, pl.ds(first, HALO)], up_ref.at[rows])
        copy(orbitals_ref.at[part, pl.ds(0, HALO)], down_ref.at[rows])
        copy(orbitals_ref.at[part, pl.ds(thickness - 1, 1)], up_far_ref.at[pl.ds(part, 1)])
        copy(orbitals_ref.at[part, pl.ds(0, 1)], down_far_ref.at[pl.ds(part, 1)])

    @pl.loop(0, FLAT // 8)
    def _(step):
        for part in range(8):
            tile = step * 8 + part
            lanes = pl.ds(pl.multiple_of(tile * LANES, LANES), LANES)
            rows = pl.ds(pl.multiple_of(tile * 8, 8), 8)
            tile_ref[rows, :] = eight(potential_ref[:, lanes])

    @pl.loop(0, FLAT // 8)
    def _(step):
        rows = pl.ds(pl.multiple_of(step * 8, 8), 8)
        for layer in range(HALO - 1):
            v_ref[layer, rows, :] = tile_ref[pl.ds(step * 64 + v_first + layer, 8, stride=8), :]

    for made in copies:
        made.wait()


def ions_kernel(count, length_cells, start_ref, background_ref, circle_ref, table_y_ref, table_z_ref,
                out_ref, flat_ref, planes_ref, low_ref, high_ref):
    _, own_start, thickness = place_of(start_ref)
    slots = background_ref.shape[0]
    groups, _, width = out_ref.shape
    layers_of(background_ref, flat_ref)

    def body(slot, total):
        def store(tile, low, high):
            rows = pl.ds(pl.multiple_of(slot * SIDE + tile * 8, 8), 8)
            planes_ref[rows, :LANES] = low
            planes_ref[rows, LANES:] = high

        to_plane(lambda k: flat_ref[pl.ds(slot * FLAT + k, 8, stride=STRIDE), :], store)
        rows = pl.ds(pl.multiple_of(slot * SIDE, 8), SIDE)
        inside = mesh_points(own_start + slot, circle_ref[...], length_cells) & (slot < thickness)
        values = jnp.where(inside, planes_ref[rows, :], 0.0)
        planes_ref[rows, :] = values
        return total + jnp.sum(values.reshape(RUN, 8, WIDTH), axis=0)

    total = lax.fori_loop(0, slots, body, jnp.zeros((8, WIDTH), jnp.float32))
    whole = jnp.broadcast_to(jnp.sum(total, keepdims=True), (SLOTS, LANES))[:, :width - count]
    send_columns(planes_ref, slots, table_y_ref[...], table_z_ref[...], low_ref, high_ref)
    core_rows = SIDE // lax.axis_size("core")
    first_row = lax.axis_index("core") * core_rows + lax.axis_index("row") * (core_rows // lax.axis_size("row"))
    for group in range(groups):
        out_ref[group] = chunk_of(low_ref, high_ref, first_row, column_pieces(group * count, count), whole)


def propagate_kernel(count, length_cells, start_ref, weight_ref, orbitals_ref, potential_ref, below_ref,
                     above_ref, below_far_ref, above_far_ref, v_ref, v_other_ref, circle_ref,
                     table_y_ref, table_z_ref, next_ref, density_kept_ref, density_sent_ref, kept_ref, sent_ref, field_ref, centre_ref, beside_ref,
                     flat_ref, planes_ref, low_ref, high_ref):
    position, own_start, thickness = place_of(start_ref)
    domains = lax.axis_size("domain")
    before = start_ref[jnp.maximum(position - 1, 0)]
    after = start_ref[jnp.minimum(position + 2, domains)]
    short_below = ((position > 0) & (own_start - before < HALO)).astype(jnp.int32)
    short_above = (position < domains - 1) & (after - own_start - thickness < HALO)
    weight = weight_ref[0]
    core = lax.axis_index("core")
    slots = orbitals_ref.shape[1]
    layers = slots + 2 * HALO
    devices, _, width = kept_ref.shape

    def field_layer(part, x_row):
        def store(tile, low, high):
            field_ref[0, part, x_row, 8 + 8 * tile:16 + 8 * tile, :LANES] = low
            field_ref[0, part, x_row, 8 + 8 * tile:16 + 8 * tile, LANES:] = high

        return store

    def potential_layer(x_row):
        def store(tile, low, high):
            centre_ref[x_row, 8 * tile:8 * tile + 8, :LANES] = low
            centre_ref[x_row, 8 * tile:8 * tile + 8, LANES:] = high

        return store

    def rows_from(ref, *at):
        return lambda k: ref[(*at, pl.ds(k, 8, stride=STRIDE), slice(None))]

    layers_of(potential_ref, flat_ref)

    @pl.loop(0, slots)
    def _(slot):
        for part in range(2):
            to_plane(rows_from(orbitals_ref, part, slot), field_layer(part, HALO + slot))
        to_plane(
            lambda k: flat_ref[pl.ds(slot * FLAT + k, 8, stride=STRIDE), :], potential_layer(HALO + slot)
        )

    @pl.loop(0, HALO - 1)
    def _(layer):
        lower = 1 + layer
        upper = HALO + thickness + layer
        to_plane(rows_from(v_ref, layer), potential_layer(jnp.where(core == 0, lower, upper)))
        to_plane(rows_from(v_other_ref, layer), potential_layer(jnp.where(core == 0, upper, lower)))
        for part in range(2):
            to_plane(
                rows_from(below_ref, part * HALO + 1 + layer - short_below), field_layer(part, 1 + layer)
            )
            to_plane(
                rows_from(above_ref, part * HALO + layer), field_layer(part, HALO + thickness + layer)
            )

    @pl.loop(0, 2)
    def _(part):
        last = 2 * HALO - 1 + thickness

        @pl.when(short_below > 0)
        def _():
            to_plane(rows_from(below_far_ref, part), field_layer(part, 0))

        @pl.when(short_below == 0)
        def _():
            to_plane(rows_from(below_ref, part * HALO), field_layer(part, 0))

        @pl.when(short_above)
        def _():
            to_plane(rows_from(above_far_ref, part), field_layer(part, last))

        @pl.when(jnp.logical_not(short_above))
        def _():
            to_plane(rows_from(above_ref, part * HALO + HALO - 1), field_layer(part, last))

    def wrap(term, part, x_row):
        first = field_ref[term, part, x_row, 8:16, :]
        final = field_ref[term, part, x_row, SIDE:SIDE + 8, :]
        field_ref[term, part, x_row, :8, :] = pltpu.roll(final, 1, 0)
        field_ref[term, part, x_row, SIDE + 8:, :] = pltpu.roll(first, 7, 0)

    @pl.loop(0, layers)
    def _(x_row):
        known = x_row < thickness + 2 * HALO
        for block in range(SIDE // BLOCK):
            rows = slice(block * BLOCK, (block + 1) * BLOCK)
            inner = slice(8 + block * BLOCK, 8 + (block + 1) * BLOCK)
            inside = mesh_points(own_start - HALO + x_row, circle_ref[rows, :], length_cells) & known
            centre_ref[x_row, rows, :] = jnp.where(
                inside, (3.0 + centre_ref[x_row, rows, :]) * time_step, 0.0
            )
            beside_ref[x_row, rows, :] = jnp.where(inside, 0.5 * time_step, 0.0)
            for part in range(2):
                field_ref[0, part, x_row, inner, :] = jnp.where(
                    inside, field_ref[0, part, x_row, inner, :], 0.0
                )
        for part in range(2):
            wrap(0, part, x_row)

    def hamilton(term, part, x_row, block, centre, beside):
        tall = field_ref[term, part, x_row, block * BLOCK:block * BLOCK + BLOCK + 16, :]
        inner = slice(8 + block * BLOCK, 8 + (block + 1) * BLOCK)
        field = tall[8:8 + BLOCK]
        around = field_ref[term, part, x_row - 1, inner, :] + field_ref[term, part, x_row + 1, inner, :]
        around = around + (tall[:BLOCK] + tall[16:])
        around = around + (pltpu.roll(field, 1, 1) + pltpu.roll(field, WIDTH - 1, 1))
        return centre * field - beside * around

    for term in range(1, TERMS):

        @pl.loop(term, layers - term)
        def _(x_row, term=term):
            for block in range(SIDE // BLOCK):
                rows = slice(block * BLOCK, (block + 1) * BLOCK)
                inner = slice(8 + block * BLOCK, 8 + (block + 1) * BLOCK)
                centre = centre_ref[x_row, rows, :]
                beside = beside_ref[x_row, rows, :]
                for part in range(2):
                    field_ref[term, part, x_row, inner, :] = hamilton(
                        term - 1, part, x_row, block, centre, beside
                    )
            for part in range(2):
                wrap(term, part, x_row)

    def finish(slot, total):
        x_row = HALO + slot
        owned = slot < thickness
        for block in range(SIDE // BLOCK):
            rows = slice(block * BLOCK, (block + 1) * BLOCK)
            inner = slice(8 + block * BLOCK, 8 + (block + 1) * BLOCK)
            centre = centre_ref[x_row, rows, :]
            beside = beside_ref[x_row, rows, :]
            density = jnp.zeros((BLOCK, WIDTH), jnp.float32)
            for part, sign in ((0, 1.0), (1, -1.0)):
                summed = field_ref[0, part, x_row, inner, :]
                summed = summed + sign * field_ref[1, 1 - part, x_row, inner, :]
                summed = summed - (1.0 / 2.0) * field_ref[2, part, x_row, inner, :]
                summed = summed - (sign / 6.0) * field_ref[3, 1 - part, x_row, inner, :]
                summed = summed + (1.0 / 24.0) * hamilton(3, part, x_row, block, centre, beside)
                summed = jnp.where(owned, summed, 0.0)
                field_ref[2, part, x_row, inner, :] = summed
                density = density + summed * summed
            density = weight * density
            planes_ref[pl.ds(pl.multiple_of(slot * SIDE + block * BLOCK, 8), BLOCK), :] = density
            total = total + jnp.sum(density.reshape(BLOCK // 8, 8, WIDTH), axis=0)

        for part in range(2):

            def load(tile, part=part):
                tall = field_ref[2, part, x_row, 8 + 8 * tile:16 + 8 * tile, :]
                return tall[:, :LANES], tall[:, LANES:]

            def store(k, values, part=part):
                next_ref[part, slot, pl.ds(k, 8, stride=STRIDE), :] = values

            to_flat(load, store)

        return total

    total = lax.fori_loop(0, slots, finish, jnp.zeros((8, WIDTH), jnp.float32))
    planes_ref[slots * SIDE:, :] = jnp.zeros(((SLOTS - slots) * SIDE, WIDTH), jnp.float32)

    @pl.loop(0, SLOTS // 2)
    def _(slot):
        for first, target_ref in ((core, density_kept_ref), (1 - core, density_sent_ref)):

            def load(tile, first=first):
                row = (first * (SLOTS // 2) + slot) * SIDE + tile * 8
                tall = planes_ref[pl.ds(pl.multiple_of(row, 8), 8), :]
                return tall[:, :LANES], tall[:, LANES:]

            def store(k, values, target_ref=target_ref):
                target_ref[slot, pl.ds(k, 8, stride=STRIDE), :] = values

            to_flat(load, store)

    whole = jnp.broadcast_to(jnp.sum(total, keepdims=True), (SLOTS, LANES))[:, :width - count]
    send_columns(planes_ref, slots, table_y_ref[...], table_z_ref[...], low_ref, high_ref)
    core_rows = SIDE // 2
    first_row = core * core_rows
    for device in range(devices):
        pieces = column_pieces(device * count, count)
        kept_ref[device] = chunk_of(low_ref, high_ref, first_row, pieces, whole)
        sent_ref[device] = chunk_of(low_ref, high_ref, core_rows - first_row, pieces, whole)


def wave_squared(index, count_cells):
    folded = jnp.where(2 * index <= count_cells, index, index - count_cells)
    wave_number = folded.astype(jnp.float32) * (two_pi / count_cells)
    return wave_number * wave_number


def coulomb_kernel(count, length_cells, start_ref, charge_ref, ions_ref, table_ref, out_ref):
    domains, _, width = ions_ref.shape
    states = charge_ref.shape[0] // domains
    device = (lax.axis_index("core") * states + lax.axis_index("row")) * domains + lax.axis_index("domain")
    charge = charge_ref[:domains]
    for state in range(1, states):
        charge = charge + charge_ref[state * domains:(state + 1) * domains]
    charge = charge.reshape(domains * SLOTS, width)
    ions = ions_ref[...].reshape(domains * SLOTS, width)
    first = lax.broadcasted_iota(jnp.int32, (domains * SLOTS, width), 0) % SLOTS == 0
    lane = lax.broadcasted_iota(jnp.int32, (domains * SLOTS, width), 1)
    chosen = first & (lane == count)
    electrons = jnp.sum(jnp.where(chosen, charge, 0.0), keepdims=True)
    ionic = jnp.sum(jnp.where(chosen, ions, 0.0), keepdims=True)
    charge = charge - (electrons / ionic) * ions
    layer = lax.broadcasted_iota(jnp.int32, (length_cells, domains * SLOTS), 0)
    place = lax.broadcasted_iota(jnp.int32, (length_cells, domains * SLOTS), 1)
    chosen_layer = jnp.full(layer.shape, -1, jnp.int32)
    for domain in range(domains):
        slot = place - domain * SLOTS
        here = (slot >= 0) & (slot < start_ref[domain + 1] - start_ref[domain])
        chosen_layer = jnp.where(here, start_ref[domain] + slot, chosen_layer)
    pick = (layer == chosen_layer).astype(jnp.float32)
    table = jnp.dot(table_ref[...], pick, precision=highest, preferred_element_type=jnp.float32)
    waves = jnp.dot(table, charge, precision=highest, preferred_element_type=jnp.float32)
    wave_x = lax.broadcasted_iota(jnp.int32, waves.shape, 0)
    column = device * count + lax.broadcasted_iota(jnp.int32, waves.shape, 1)
    wave_y = ((column.astype(jnp.float32) + 0.5) * (1.0 / SIDE)).astype(jnp.int32)
    wave_z = column - wave_y * SIDE
    squared = (
        wave_squared(wave_x, length_cells) + wave_squared(wave_y, SIDE) + wave_squared(wave_z, SIDE)
    )
    gain = jnp.where(squared > 0, four_pi / jnp.where(squared > 0, squared, 1.0), 0.0)
    waves = waves * (gain * (1.0 / (length_cells * SIDE * SIDE)))
    back = lax.dot_general(
        table, waves, (((0,), (0,)), ((), ())), precision=highest, preferred_element_type=jnp.float32
    )
    back = back.reshape(domains, SLOTS, width)
    for state in range(states):
        out_ref[state * domains:(state + 1) * domains] = back


def field_kernel(count, length_cells, start_ref, waves_ref, others_ref, density_ref, other_ref,
                 circle_ref, table_y_ref, table_z_ref, out_ref, low_ref, high_ref, planes_ref, flat_ref):
    _, own_start, thickness = place_of(start_ref)
    devices = waves_ref.shape[0]
    slots = out_ref.shape[0]
    core = lax.axis_index("core")
    core_rows = SIDE // 2
    first_row = core * core_rows
    for source_ref, first in ((waves_ref, first_row), (others_ref, core_rows - first_row)):
        pieces = []
        for device in range(devices):
            column = 0
            for row, start, stop in column_pieces(device * count, count):
                values = source_ref[device, :, column:column + stop - start]
                column += stop - start
                if start > 0:
                    pieces.append(values)
                    values = jnp.concatenate(pieces, axis=1)
                if stop < SIDE:
                    pieces = [values]
                    continue
                pieces = []
                at = pl.ds(first + row, SLOTS, stride=SIDE)
                low_ref[at, :] = values[:, :LANES]
                high_ref[at, :] = jnp.concatenate(
                    [values[:, LANES:], jnp.zeros((SLOTS, WIDTH - SIDE), jnp.float32)], axis=1
                )
    table_y = table_y_ref[...]
    table_z = table_z_ref[...]
    used = slice(0, slots * SIDE)
    along_z = turn_z(jnp.concatenate([low_ref[used, :], high_ref[used, :]], axis=1), table_z)
    for slot in range(slots):
        rows = slice(slot * SIDE, (slot + 1) * SIDE)
        planes_ref[rows, :] = turn_y(table_y, along_z[rows])

    @pl.loop(0, slots)
    def _(slot):
        def load(tile):
            tall = planes_ref[pl.ds(pl.multiple_of(slot * SIDE + tile * 8, 8), 8), :]
            return tall[:, :LANES], tall[:, LANES:]

        def store(k, values):
            flat_ref[pl.ds(slot * FLAT + k, 8, stride=STRIDE), :] = values

        to_flat(load, store)
        rows = pl.ds(pl.multiple_of(slot * FLAT, 8), FLAT)
        here = slot // (SLOTS // 2) == core
        kept_slot = slot % (SLOTS // 2)
        content = jnp.where(here, density_ref[kept_slot], other_ref[kept_slot]) * (3.0 / math.pi)
        positive = jnp.where(content > 0, content, 1.0)
        root = jnp.exp(jnp.log(positive) * (1.0 / 3.0))
        root = root - (root - positive / (root * root)) * (1.0 / 3.0)
        root = jnp.where(content > 0, root, 0.0)
        inside = mesh_points(own_start + slot, circle_ref[...], length_cells) & (slot < thickness)
        flat_ref[rows, :] = jnp.where(inside, flat_ref[rows, :] - root, 0.0)

    @pl.loop(0, FLAT // 8)
    def _(step):
        for part in range(8):
            lanes = pl.ds(pl.multiple_of((step * 8 + part) * LANES, LANES), LANES)
            out_ref[:, lanes] = flat_ref[pl.ds(step * 8 + part, SLOTS, stride=FLAT), :][:slots]


def from_behind(value, steps):
    count = lax.axis_size("domain")
    leading, last = (max(0, -steps), min(count, count - steps))
    return lax.ppermute(value, "domain", [(source, source + steps) for source in range(leading, last)])


def swapped(value, axis):
    return lax.ppermute(value, axis, [(0, 1), (1, 0)])


def shards(orbitals, occupation, potential, background, layer_start):
    domains = lax.axis_size("domain")
    rows = lax.axis_size("row")
    devices = domains * rows
    length_cells = SLAB * domains
    layer_cap, plane = potential.shape
    count = plane // (2 * devices)
    width = -(-(count + 1) // LANES) * LANES
    circle = jnp.asarray(circle_plane())
    flat_circle = jnp.asarray(circle_table().reshape(FLAT, LANES))
    table_z, into_y, out_of_y = (jnp.asarray(table) for table in tables_of_side())
    table_x = jnp.asarray(hartley_table(length_cells).astype(np.float32))
    params = pltpu.CompilerParams(vmem_limit_bytes=VMEM_BYTES)

    def f32(*shape):
        return jax.ShapeDtypeStruct(shape, jnp.float32)

    def scratch(*shape):
        return pltpu.VMEM(shape, jnp.float32)

    layers = orbitals.reshape(2, layer_cap, FLAT, LANES)
    v_rows, up, down, up_far, down_far = pl.pallas_call(
        pack_kernel,
        out_shape=tuple(f32(size, FLAT, LANES) for size in (HALO - 1, 2 * HALO, 2 * HALO, 2, 2)),
        in_specs=[SMEM_SPEC, VMEM_SPEC, ANY_SPEC],
        out_specs=(VMEM_SPEC,) * 5,
        scratch_shapes=[scratch(FLAT * 8, LANES), pltpu.SemaphoreType.DMA((8,))],
        compiler_params=params,
        name="pack_halo",
    )(layer_start, potential, layers)
    v_rows = lax.ppermute(
        v_rows,
        ("core", "domain"),
        [(source, source + 1) for source in range(domains - 1)]
        + [(domains + source + 1, domains + source) for source in range(domains - 1)],
    )
    below = from_behind(up, 1)
    above = from_behind(down, -1)
    below_far = from_behind(up_far, 2)
    above_far = from_behind(down_far, -2)
    v_others = swapped(v_rows, "core")
    background, below_far, above_far = lax.optimization_barrier((background, below_far, above_far))

    ions = pl.pallas_call(
        functools.partial(ions_kernel, count, length_cells),
        out_shape=f32(domains, SLOTS, width),
        in_specs=[SMEM_SPEC] + [VMEM_SPEC] * 4,
        out_specs=VMEM_SPEC,
        scratch_shapes=[
            scratch(SLOTS * FLAT, LANES),
            scratch(layer_cap * SIDE, WIDTH),
            scratch(SLOTS * SIDE, LANES),
            scratch(SLOTS * SIDE, LANES),
        ],
        compiler_params=params,
        name="ion_waves",
    )(layer_start, background, circle, into_y, table_z)
    ions = lax.all_to_all(ions, "domain", split_axis=0, concat_axis=0, tiled=True)
    ions, below = lax.optimization_barrier((ions, below))

    span = layer_cap + 2 * HALO
    orbitals_next, density_kept, density_sent, kept, sent = pl.pallas_call(
        functools.partial(propagate_kernel, count, length_cells),
        out_shape=(
            f32(2, layer_cap, FLAT, LANES),
            f32(SLOTS // 2, FLAT, LANES),
            f32(SLOTS // 2, FLAT, LANES),
            f32(devices, SLOTS, width),
            f32(devices, SLOTS, width),
        ),
        in_specs=[SMEM_SPEC, SMEM_SPEC] + [VMEM_SPEC] * 11,
        out_specs=(VMEM_SPEC,) * 5,
        scratch_shapes=[
            scratch(TERMS, 2, span, TALL, WIDTH),
            scratch(span, SIDE, WIDTH),
            scratch(span, SIDE, WIDTH),
            scratch(SLOTS * FLAT, LANES),
            scratch(SLOTS * SIDE, WIDTH),
            scratch(SLOTS * SIDE, LANES),
            scratch(SLOTS * SIDE, LANES),
        ],
        compiler_params=params,
        name="propagate",
    )(layer_start, occupation, layers, potential, below, above, below_far, above_far, v_rows,
      v_others, circle, into_y, table_z)
    waves = kept + swapped(sent, "core")
    density = density_kept + swapped(density_sent, "core")
    waves, density = lax.optimization_barrier((waves, density))
    waves = lax.all_to_all(waves, ("row", "domain"), split_axis=0, concat_axis=0, tiled=True)
    other_density = swapped(density, "row")
    waves = pl.pallas_call(
        functools.partial(coulomb_kernel, count, length_cells),
        out_shape=f32(devices, SLOTS, width),
        in_specs=[SMEM_SPEC] + [VMEM_SPEC] * 3,
        out_specs=VMEM_SPEC,
        compiler_params=params,
        name="coulomb",
    )(layer_start, waves, ions, table_x)
    waves, other_density = lax.optimization_barrier((waves, other_density))
    density = density + other_density
    other_density = swapped(density, "core")
    waves = lax.all_to_all(waves, ("row", "domain"), split_axis=0, concat_axis=0, tiled=True)
    other_waves = swapped(waves, "core")
    potential_next = pl.pallas_call(
        functools.partial(field_kernel, count, length_cells),
        out_shape=f32(layer_cap, plane),
        in_specs=[SMEM_SPEC] + [VMEM_SPEC] * 7,
        out_specs=VMEM_SPEC,
        scratch_shapes=[
            scratch(SLOTS * SIDE, LANES),
            scratch(SLOTS * SIDE, LANES),
            scratch(layer_cap * SIDE, WIDTH),
            scratch(SLOTS * FLAT, LANES),
        ],
        compiler_params=params,
        name="field",
    )(layer_start, waves, other_waves, density, other_density, flat_circle, out_of_y, table_z)
    return orbitals_next.reshape(orbitals.shape), potential_next


def solution(mesh):
    domains = mesh.shape["domain"]
    split = Mesh(mesh.devices.reshape(-1, 2, domains), ("row", "core", "domain"))
    states = ("row", "core")
    return jax.shard_map(
        shards,
        mesh=split,
        in_specs=(
            P(None, states, "domain", None),
            P(states),
            P("domain", None),
            P("domain", None),
            P(),
        ),
        out_specs=(P(None, states, "domain", None), P("domain", None)),
        check_vma=False,
    )
```

```python
import functools
import math

import jax
import jax.numpy as jnp
import ml_dtypes
import numpy as np
from jax import lax
from jax.experimental import pallas as pl
from jax.experimental.pallas import tpu as pltpu
from jax.sharding import Mesh, PartitionSpec as P

SIDE = 160
SLAB = 5
TERMS = 4

HALO = TERMS
LANES = 128
SLOTS = 8
RUN = SIDE // 8
FLAT = SIDE * SIDE // LANES
STRIDE = FLAT // 8
WIDTH = 2 * LANES
BLOCK = 16
TALL = SIDE + 16

time_step = 0.3
four_pi = 4.0 * math.pi
two_pi = 2.0 * math.pi
highest = lax.Precision.HIGHEST
VMEM_BYTES = 56 * 1024 * 1024
SMEM_SPEC = pl.BlockSpec(memory_space=pltpu.SMEM)
VMEM_SPEC = pl.BlockSpec(memory_space=pltpu.VMEM)
ANY_SPEC = pl.BlockSpec(memory_space=pl.ANY)


def hartley_table(count_cells):
    index_run = np.arange(count_cells)
    angles = (index_run[:, None] * index_run[None, :] % count_cells) * (2.0 * np.pi / count_cells)
    return np.cos(angles) + np.sin(angles)


def plane_order():
    rows = np.arange(SIDE)
    return RUN * (rows % 8) + rows // 8


def two_parts(table):
    table = table.astype(np.float32)
    high = table.astype(ml_dtypes.bfloat16)
    low = (table - high.astype(np.float32)).astype(ml_dtypes.bfloat16)
    return high, low


def tables_of_side():
    table = hartley_table(SIDE)
    along_z = np.zeros((WIDTH, WIDTH))
    along_z[:SIDE, :SIDE] = table
    high, low = two_parts(along_z)
    along_z = np.concatenate([high, high, low], axis=0)
    high, low = two_parts(table[:, plane_order()])
    into_y = np.concatenate([high, high, low], axis=1)
    high, low = two_parts(table[plane_order(), :])
    out_of_y = np.concatenate([high, high, low], axis=1)
    return along_z, into_y, out_of_y


def neighbour_table():
    table = np.zeros((WIDTH, WIDTH), np.float32)
    cells = np.arange(SIDE - 1)
    table[cells, cells + 1] = 1.0
    table[cells + 1, cells] = 1.0
    return np.concatenate([table, table], axis=0).astype(ml_dtypes.bfloat16)


def circle_table():
    across = 2 * np.arange(SIDE, dtype=np.int64) - (SIDE - 1)
    return (across[:, None] ** 2 + across[None, :] ** 2).astype(np.int32)


def circle_plane():
    table = np.full((SIDE, WIDTH), 4 * SIDE * SIDE, np.int32)
    table[:, :SIDE] = circle_table()[plane_order()]
    return table


def mesh_points(x_row, circle, length_cells):
    room = ((length_cells - 2) ** 2 - (2 * x_row - (length_cells - 1)) ** 2) * (SIDE - 2) ** 2
    return (circle * (length_cells - 2) ** 2 <= room) & (circle < 4 * SIDE * SIDE)


def column_pieces(first, count):
    pieces = []
    column = first
    while column < first + count:
        row = column // SIDE
        stop = min((row + 1) * SIDE, first + count)
        pieces.append((row, column - row * SIDE, stop - row * SIDE))
        column = stop
    return pieces


def eight(values):
    missing = jnp.zeros((SLOTS - values.shape[0], values.shape[1]), values.dtype)
    return jnp.concatenate([values, missing], axis=0)


def to_plane(load, store):
    lane = lax.broadcasted_iota(jnp.int32, (8, LANES), 1)
    for step in range(RUN // 4):
        rows = [load(5 * step + part) for part in range(5)]
        store(4 * step, rows[0], rows[1])
        for part in range(1, 4):
            left = pltpu.roll(rows[part], LANES - 32 * part, 1)
            right = pltpu.roll(rows[part + 1], LANES - 32 * part, 1)
            store(4 * step + part, jnp.where(lane < LANES - 32 * part, left, right), right)


def to_flat(load, store):
    lane = lax.broadcasted_iota(jnp.int32, (8, LANES), 1)
    for step in range(RUN // 4):
        turned = []
        for part in range(4):
            low, high = load(4 * step + part)
            if part:
                low = pltpu.roll(low, 32 * part, 1)
                high = pltpu.roll(high, 32 * part, 1)
            turned.append((low, high))
        store(5 * step, turned[0][0])
        for part in range(1, 4):
            ended = 32 * (part - 1)
            values = jnp.where(lane < ended + 32, turned[part - 1][1], turned[part][0])
            if ended:
                values = jnp.where(lane < ended, turned[part - 1][0], values)
            store(5 * step + part, values)
        store(5 * step + 4, jnp.where(lane < 96, turned[3][0], turned[3][1]))


def parts_of(values):
    high = values.astype(jnp.bfloat16)
    low = (values - high.astype(jnp.float32)).astype(jnp.bfloat16)
    return high, low


def turn_z(values, table):
    high, low = parts_of(values)
    return jnp.dot(
        jnp.concatenate([high, low, high], axis=1), table, preferred_element_type=jnp.float32
    )


def turn_y(table, values):
    high, low = parts_of(values)
    return jnp.dot(
        table, jnp.concatenate([high, low, high], axis=0), preferred_element_type=jnp.float32
    )


def send_columns(planes_ref, slots, table_y, table_z, low_ref, high_ref):
    along_z = turn_z(planes_ref[:slots * SIDE, :], table_z)
    for slot in range(slots):
        rows = slice(slot * SIDE, (slot + 1) * SIDE)
        waves = turn_y(table_y, along_z[rows])
        low_ref[rows, :] = waves[:, :LANES]
        high_ref[rows, :] = waves[:, LANES:]
    low_ref[slots * SIDE:, :] = jnp.zeros(((SLOTS - slots) * SIDE, LANES), jnp.float32)
    high_ref[slots * SIDE:, :] = jnp.zeros(((SLOTS - slots) * SIDE, LANES), jnp.float32)


def chunk_of(low_ref, high_ref, first_row, pieces, extra):
    parts = []
    for row, start, stop in pieces:
        at = pl.ds(first_row + row, SLOTS, stride=SIDE)
        values = jnp.concatenate([low_ref[at, :], high_ref[at, :]], axis=1)
        parts.append(values[:, start:stop])
    return jnp.concatenate(parts + [extra], axis=1)


def layers_of(stored_ref, flat_ref):
    @pl.loop(0, FLAT // 8)
    def _(step):
        for part in range(8):
            lanes = pl.ds(pl.multiple_of((step * 8 + part) * LANES, LANES), LANES)
            flat_ref[pl.ds(step * 8 + part, SLOTS, stride=FLAT), :] = eight(stored_ref[:, lanes])


def place_of(start_ref):
    position = lax.axis_index("domain")
    return position, start_ref[position], start_ref[position + 1] - start_ref[position]


def pack_kernel(start_ref, potential_ref, orbitals_ref, v_ref, up_ref, down_ref, up_far_ref, down_far_ref,
                tile_ref, sems):
    _, _, thickness = place_of(start_ref)
    v_first = jnp.where(lax.axis_index("core") == 0, thickness - (HALO - 1), 0)
    first = jnp.maximum(thickness - HALO, 0)
    copies = []

    def copy(source, target):
        made = pltpu.make_async_copy(source, target, sems.at[len(copies)])
        made.start()
        copies.append(made)

    for part in range(2):
        rows = pl.ds(part * HALO, HALO)
        copy(orbitals_ref.at[part, pl.ds(first, HALO)], up_ref.at[rows])
        copy(orbitals_ref.at[part, pl.ds(0, HALO)], down_ref.at[rows])
        copy(orbitals_ref.at[part, pl.ds(thickness - 1, 1)], up_far_ref.at[pl.ds(part, 1)])
        copy(orbitals_ref.at[part, pl.ds(0, 1)], down_far_ref.at[pl.ds(part, 1)])

    @pl.loop(0, FLAT // 8)
    def _(step):
        for part in range(8):
            tile = step * 8 + part
            lanes = pl.ds(pl.multiple_of(tile * LANES, LANES), LANES)
            rows = pl.ds(pl.multiple_of(tile * 8, 8), 8)
            tile_ref[rows, :] = eight(potential_ref[:, lanes])

    @pl.loop(0, FLAT // 8)
    def _(step):
        rows = pl.ds(pl.multiple_of(step * 8, 8), 8)
        for layer in range(HALO - 1):
            v_ref[layer, rows, :] = tile_ref[pl.ds(step * 64 + v_first + layer, 8, stride=8), :]

    for made in copies:
        made.wait()


def ions_kernel(count, length_cells, start_ref, background_ref, circle_ref, table_y_ref, table_z_ref,
                out_ref, flat_ref, planes_ref, low_ref, high_ref):
    _, own_start, thickness = place_of(start_ref)
    slots = background_ref.shape[0]
    groups, _, width = out_ref.shape
    layers_of(background_ref, flat_ref)

    def body(slot, total):
        def store(tile, low, high):
            rows = pl.ds(pl.multiple_of(slot * SIDE + tile * 8, 8), 8)
            planes_ref[rows, :LANES] = low
            planes_ref[rows, LANES:] = high

        to_plane(lambda k: flat_ref[pl.ds(slot * FLAT + k, 8, stride=STRIDE), :], store)
        rows = pl.ds(pl.multiple_of(slot * SIDE, 8), SIDE)
        inside = mesh_points(own_start + slot, circle_ref[...], length_cells) & (slot < thickness)
        values = jnp.where(inside, planes_ref[rows, :], 0.0)
        planes_ref[rows, :] = values
        return total + jnp.sum(values.reshape(RUN, 8, WIDTH), axis=0)

    total = lax.fori_loop(0, slots, body, jnp.zeros((8, WIDTH), jnp.float32))
    whole = jnp.broadcast_to(jnp.sum(total, keepdims=True), (SLOTS, LANES))[:, :width - count]
    send_columns(planes_ref, slots, table_y_ref[...], table_z_ref[...], low_ref, high_ref)
    core_rows = SIDE // lax.axis_size("core")
    first_row = lax.axis_index("core") * core_rows + lax.axis_index("row") * (core_rows // lax.axis_size("row"))
    for group in range(groups):
        out_ref[group] = chunk_of(low_ref, high_ref, first_row, column_pieces(group * count, count), whole)


def propagate_kernel(count, length_cells, start_ref, weight_ref, orbitals_ref, potential_ref, below_ref,
                     above_ref, below_far_ref, above_far_ref, v_ref, v_other_ref, circle_ref,
                     beside_z_ref, table_y_ref, table_z_ref, next_ref, density_kept_ref, density_sent_ref, kept_ref, sent_ref, field_ref, centre_ref, beside_ref,
                     flat_ref, planes_ref, low_ref, high_ref):
    position, own_start, thickness = place_of(start_ref)
    domains = lax.axis_size("domain")
    before = start_ref[jnp.maximum(position - 1, 0)]
    after = start_ref[jnp.minimum(position + 2, domains)]
    short_below = ((position > 0) & (own_start - before < HALO)).astype(jnp.int32)
    short_above = (position < domains - 1) & (after - own_start - thickness < HALO)
    weight = weight_ref[0]
    core = lax.axis_index("core")
    slots = orbitals_ref.shape[1]
    layers = slots + 2 * HALO
    devices, _, width = kept_ref.shape

    def field_layer(part, x_row):
        def store(tile, low, high):
            field_ref[0, part, x_row, 8 + 8 * tile:16 + 8 * tile, :LANES] = low
            field_ref[0, part, x_row, 8 + 8 * tile:16 + 8 * tile, LANES:] = high

        return store

    def potential_layer(x_row):
        def store(tile, low, high):
            centre_ref[x_row, 8 * tile:8 * tile + 8, :LANES] = low
            centre_ref[x_row, 8 * tile:8 * tile + 8, LANES:] = high

        return store

    def rows_from(ref, *at):
        return lambda k: ref[(*at, pl.ds(k, 8, stride=STRIDE), slice(None))]

    layers_of(potential_ref, flat_ref)

    @pl.loop(0, slots)
    def _(slot):
        for part in range(2):
            to_plane(rows_from(orbitals_ref, part, slot), field_layer(part, HALO + slot))
        to_plane(
            lambda k: flat_ref[pl.ds(slot * FLAT + k, 8, stride=STRIDE), :], potential_layer(HALO + slot)
        )

    @pl.loop(0, HALO - 1)
    def _(layer):
        lower = 1 + layer
        upper = HALO + thickness + layer
        to_plane(rows_from(v_ref, layer), potential_layer(jnp.where(core == 0, lower, upper)))
        to_plane(rows_from(v_other_ref, layer), potential_layer(jnp.where(core == 0, upper, lower)))
        for part in range(2):
            to_plane(
                rows_from(below_ref, part * HALO + 1 + layer - short_below), field_layer(part, 1 + layer)
            )
            to_plane(
                rows_from(above_ref, part * HALO + layer), field_layer(part, HALO + thickness + layer)
            )

    @pl.loop(0, 2)
    def _(part):
        last = 2 * HALO - 1 + thickness

        @pl.when(short_below > 0)
        def _():
            to_plane(rows_from(below_far_ref, part), field_layer(part, 0))

        @pl.when(short_below == 0)
        def _():
            to_plane(rows_from(below_ref, part * HALO), field_layer(part, 0))

        @pl.when(short_above)
        def _():
            to_plane(rows_from(above_far_ref, part), field_layer(part, last))

        @pl.when(jnp.logical_not(short_above))
        def _():
            to_plane(rows_from(above_ref, part * HALO + HALO - 1), field_layer(part, last))

    def wrap(term, part, x_row):
        first = field_ref[term, part, x_row, 8:16, :]
        final = field_ref[term, part, x_row, SIDE:SIDE + 8, :]
        field_ref[term, part, x_row, :8, :] = pltpu.roll(final, 1, 0)
        field_ref[term, part, x_row, SIDE + 8:, :] = pltpu.roll(first, 7, 0)

    @pl.loop(0, layers)
    def _(x_row):
        known = x_row < thickness + 2 * HALO
        for block in range(SIDE // BLOCK):
            rows = slice(block * BLOCK, (block + 1) * BLOCK)
            inner = slice(8 + block * BLOCK, 8 + (block + 1) * BLOCK)
            inside = mesh_points(own_start - HALO + x_row, circle_ref[rows, :], length_cells) & known
            centre_ref[x_row, rows, :] = jnp.where(
                inside, (3.0 + centre_ref[x_row, rows, :]) * time_step, 0.0
            )
            beside_ref[x_row, rows, :] = jnp.where(inside, 0.5 * time_step, 0.0)
            for part in range(2):
                field_ref[0, part, x_row, inner, :] = jnp.where(
                    inside, field_ref[0, part, x_row, inner, :], 0.0
                )
        for part in range(2):
            wrap(0, part, x_row)

    def beside_z(term, x_row):
        field = jnp.concatenate(
            [field_ref[term, part, x_row, 8:8 + SIDE, :] for part in range(2)], axis=0
        )
        return jnp.dot(
            jnp.concatenate(parts_of(field), axis=1), beside_z_ref[...], preferred_element_type=jnp.float32
        )

    def hamilton(term, part, x_row, block, along_z, centre, beside):
        tall = field_ref[term, part, x_row, block * BLOCK:block * BLOCK + BLOCK + 16, :]
        inner = slice(8 + block * BLOCK, 8 + (block + 1) * BLOCK)
        field = tall[8:8 + BLOCK]
        around = field_ref[term, part, x_row - 1, inner, :] + field_ref[term, part, x_row + 1, inner, :]
        around = around + (tall[:BLOCK] + tall[16:])
        first = part * SIDE + block * BLOCK
        around = around + along_z[first:first + BLOCK]
        return centre * field - beside * around

    for term in range(1, TERMS):

        @pl.loop(term, layers - term)
        def _(x_row, term=term):
            along_z = beside_z(term - 1, x_row)
            for block in range(SIDE // BLOCK):
                rows = slice(block * BLOCK, (block + 1) * BLOCK)
                inner = slice(8 + block * BLOCK, 8 + (block + 1) * BLOCK)
                centre = centre_ref[x_row, rows, :]
                beside = beside_ref[x_row, rows, :]
                for part in range(2):
                    field_ref[term, part, x_row, inner, :] = hamilton(
                        term - 1, part, x_row, block, along_z, centre, beside
                    )
            for part in range(2):
                wrap(term, part, x_row)

    def finish(slot, total):
        x_row = HALO + slot
        owned = slot < thickness
        along_z = beside_z(TERMS - 1, x_row)
        for block in range(SIDE // BLOCK):
            rows = slice(block * BLOCK, (block + 1) * BLOCK)
            inner = slice(8 + block * BLOCK, 8 + (block + 1) * BLOCK)
            centre = centre_ref[x_row, rows, :]
            beside = beside_ref[x_row, rows, :]
            density = jnp.zeros((BLOCK, WIDTH), jnp.float32)
            for part, sign in ((0, 1.0), (1, -1.0)):
                summed = field_ref[0, part, x_row, inner, :]
                summed = summed + sign * field_ref[1, 1 - part, x_row, inner, :]
                summed = summed - (1.0 / 2.0) * field_ref[2, part, x_row, inner, :]
                summed = summed - (sign / 6.0) * field_ref[3, 1 - part, x_row, inner, :]
                summed = summed + (1.0 / 24.0) * hamilton(
                    TERMS - 1, part, x_row, block, along_z, centre, beside
                )
                summed = jnp.where(owned, summed, 0.0)
                field_ref[2, part, x_row, inner, :] = summed
                density = density + summed * summed
            density = weight * density
            planes_ref[pl.ds(pl.multiple_of(slot * SIDE + block * BLOCK, 8), BLOCK), :] = density
            total = total + jnp.sum(density.reshape(BLOCK // 8, 8, WIDTH), axis=0)

        for part in range(2):

            def load(tile, part=part):
                tall = field_ref[2, part, x_row, 8 + 8 * tile:16 + 8 * tile, :]
                return tall[:, :LANES], tall[:, LANES:]

            def store(k, values, part=part):
                next_ref[part, slot, pl.ds(k, 8, stride=STRIDE), :] = values

            to_flat(load, store)

        return total

    total = lax.fori_loop(0, slots, finish, jnp.zeros((8, WIDTH), jnp.float32))
    planes_ref[slots * SIDE:, :] = jnp.zeros(((SLOTS - slots) * SIDE, WIDTH), jnp.float32)

    @pl.loop(0, SLOTS // 2)
    def _(slot):
        for first, target_ref in ((core, density_kept_ref), (1 - core, density_sent_ref)):

            def load(tile, first=first):
                row = (first * (SLOTS // 2) + slot) * SIDE + tile * 8
                tall = planes_ref[pl.ds(pl.multiple_of(row, 8), 8), :]
                return tall[:, :LANES], tall[:, LANES:]

            def store(k, values, target_ref=target_ref):
                target_ref[slot, pl.ds(k, 8, stride=STRIDE), :] = values

            to_flat(load, store)

    whole = jnp.broadcast_to(jnp.sum(total, keepdims=True), (SLOTS, LANES))[:, :width - count]
    send_columns(planes_ref, slots, table_y_ref[...], table_z_ref[...], low_ref, high_ref)
    core_rows = SIDE // 2
    first_row = core * core_rows
    for device in range(devices):
        pieces = column_pieces(device * count, count)
        kept_ref[device] = chunk_of(low_ref, high_ref, first_row, pieces, whole)
        sent_ref[device] = chunk_of(low_ref, high_ref, core_rows - first_row, pieces, whole)


def wave_squared(index, count_cells):
    folded = jnp.where(2 * index <= count_cells, index, index - count_cells)
    wave_number = folded.astype(jnp.float32) * (two_pi / count_cells)
    return wave_number * wave_number


def coulomb_kernel(count, length_cells, start_ref, charge_ref, ions_ref, table_ref, out_ref):
    domains, _, width = ions_ref.shape
    states = charge_ref.shape[0] // domains
    device = (lax.axis_index("core") * states + lax.axis_index("row")) * domains + lax.axis_index("domain")
    charge = charge_ref[:domains]
    for state in range(1, states):
        charge = charge + charge_ref[state * domains:(state + 1) * domains]
    charge = charge.reshape(domains * SLOTS, width)
    ions = ions_ref[...].reshape(domains * SLOTS, width)
    first = lax.broadcasted_iota(jnp.int32, (domains * SLOTS, width), 0) % SLOTS == 0
    lane = lax.broadcasted_iota(jnp.int32, (domains * SLOTS, width), 1)
    chosen = first & (lane == count)
    electrons = jnp.sum(jnp.where(chosen, charge, 0.0), keepdims=True)
    ionic = jnp.sum(jnp.where(chosen, ions, 0.0), keepdims=True)
    charge = charge - (electrons / ionic) * ions
    layer = lax.broadcasted_iota(jnp.int32, (length_cells, domains * SLOTS), 0)
    place = lax.broadcasted_iota(jnp.int32, (length_cells, domains * SLOTS), 1)
    chosen_layer = jnp.full(layer.shape, -1, jnp.int32)
    for domain in range(domains):
        slot = place - domain * SLOTS
        here = (slot >= 0) & (slot < start_ref[domain + 1] - start_ref[domain])
        chosen_layer = jnp.where(here, start_ref[domain] + slot, chosen_layer)
    pick = (layer == chosen_layer).astype(jnp.float32)
    table = jnp.dot(table_ref[...], pick, precision=highest, preferred_element_type=jnp.float32)
    waves = jnp.dot(table, charge, precision=highest, preferred_element_type=jnp.float32)
    wave_x = lax.broadcasted_iota(jnp.int32, waves.shape, 0)
    column = device * count + lax.broadcasted_iota(jnp.int32, waves.shape, 1)
    wave_y = ((column.astype(jnp.float32) + 0.5) * (1.0 / SIDE)).astype(jnp.int32)
    wave_z = column - wave_y * SIDE
    squared = (
        wave_squared(wave_x, length_cells) + wave_squared(wave_y, SIDE) + wave_squared(wave_z, SIDE)
    )
    gain = jnp.where(squared > 0, four_pi / jnp.where(squared > 0, squared, 1.0), 0.0)
    waves = waves * (gain * (1.0 / (length_cells * SIDE * SIDE)))
    back = lax.dot_general(
        table, waves, (((0,), (0,)), ((), ())), precision=highest, preferred_element_type=jnp.float32
    )
    back = back.reshape(domains, SLOTS, width)
    for state in range(states):
        out_ref[state * domains:(state + 1) * domains] = back


def field_kernel(count, length_cells, start_ref, waves_ref, others_ref, density_ref, other_ref,
                 circle_ref, table_y_ref, table_z_ref, out_ref, low_ref, high_ref, planes_ref, flat_ref):
    _, own_start, thickness = place_of(start_ref)
    devices = waves_ref.shape[0]
    slots = out_ref.shape[0]
    core = lax.axis_index("core")
    core_rows = SIDE // 2
    first_row = core * core_rows
    for source_ref, first in ((waves_ref, first_row), (others_ref, core_rows - first_row)):
        pieces = []
        for device in range(devices):
            column = 0
            for row, start, stop in column_pieces(device * count, count):
                values = source_ref[device, :, column:column + stop - start]
                column += stop - start
                if start > 0:
                    pieces.append(values)
                    values = jnp.concatenate(pieces, axis=1)
                if stop < SIDE:
                    pieces = [values]
                    continue
                pieces = []
                at = pl.ds(first + row, SLOTS, stride=SIDE)
                low_ref[at, :] = values[:, :LANES]
                high_ref[at, :] = jnp.concatenate(
                    [values[:, LANES:], jnp.zeros((SLOTS, WIDTH - SIDE), jnp.float32)], axis=1
                )
    table_y = table_y_ref[...]
    table_z = table_z_ref[...]
    used = slice(0, slots * SIDE)
    along_z = turn_z(jnp.concatenate([low_ref[used, :], high_ref[used, :]], axis=1), table_z)
    for slot in range(slots):
        rows = slice(slot * SIDE, (slot + 1) * SIDE)
        planes_ref[rows, :] = turn_y(table_y, along_z[rows])

    @pl.loop(0, slots)
    def _(slot):
        def load(tile):
            tall = planes_ref[pl.ds(pl.multiple_of(slot * SIDE + tile * 8, 8), 8), :]
            return tall[:, :LANES], tall[:, LANES:]

        def store(k, values):
            flat_ref[pl.ds(slot * FLAT + k, 8, stride=STRIDE), :] = values

        to_flat(load, store)
        rows = pl.ds(pl.multiple_of(slot * FLAT, 8), FLAT)
        here = slot // (SLOTS // 2) == core
        kept_slot = slot % (SLOTS // 2)
        content = jnp.where(here, density_ref[kept_slot], other_ref[kept_slot]) * (3.0 / math.pi)
        positive = jnp.where(content > 0, content, 1.0)
        root = jnp.exp(jnp.log(positive) * (1.0 / 3.0))
        root = root - (root - positive / (root * root)) * (1.0 / 3.0)
        root = jnp.where(content > 0, root, 0.0)
        inside = mesh_points(own_start + slot, circle_ref[...], length_cells) & (slot < thickness)
        flat_ref[rows, :] = jnp.where(inside, flat_ref[rows, :] - root, 0.0)

    @pl.loop(0, FLAT // 8)
    def _(step):
        for part in range(8):
            lanes = pl.ds(pl.multiple_of((step * 8 + part) * LANES, LANES), LANES)
            out_ref[:, lanes] = flat_ref[pl.ds(step * 8 + part, SLOTS, stride=FLAT), :][:slots]


def from_behind(value, steps):
    count = lax.axis_size("domain")
    leading, last = (max(0, -steps), min(count, count - steps))
    return lax.ppermute(value, "domain", [(source, source + steps) for source in range(leading, last)])


def swapped(value, axis):
    return lax.ppermute(value, axis, [(0, 1), (1, 0)])


def shards(orbitals, occupation, potential, background, layer_start):
    domains = lax.axis_size("domain")
    rows = lax.axis_size("row")
    devices = domains * rows
    length_cells = SLAB * domains
    layer_cap, plane = potential.shape
    count = plane // (2 * devices)
    width = -(-(count + 1) // LANES) * LANES
    circle = jnp.asarray(circle_plane())
    flat_circle = jnp.asarray(circle_table().reshape(FLAT, LANES))
    table_z, into_y, out_of_y = (jnp.asarray(table) for table in tables_of_side())
    table_x = jnp.asarray(hartley_table(length_cells).astype(np.float32))
    params = pltpu.CompilerParams(vmem_limit_bytes=VMEM_BYTES)

    def f32(*shape):
        return jax.ShapeDtypeStruct(shape, jnp.float32)

    def scratch(*shape):
        return pltpu.VMEM(shape, jnp.float32)

    layers = orbitals.reshape(2, layer_cap, FLAT, LANES)
    v_rows, up, down, up_far, down_far = pl.pallas_call(
        pack_kernel,
        out_shape=tuple(f32(size, FLAT, LANES) for size in (HALO - 1, 2 * HALO, 2 * HALO, 2, 2)),
        in_specs=[SMEM_SPEC, VMEM_SPEC, ANY_SPEC],
        out_specs=(VMEM_SPEC,) * 5,
        scratch_shapes=[scratch(FLAT * 8, LANES), pltpu.SemaphoreType.DMA((8,))],
        compiler_params=params,
        name="pack_halo",
    )(layer_start, potential, layers)
    v_rows = lax.ppermute(
        v_rows,
        ("core", "domain"),
        [(source, source + 1) for source in range(domains - 1)]
        + [(domains + source + 1, domains + source) for source in range(domains - 1)],
    )
    below = from_behind(up, 1)
    above = from_behind(down, -1)
    below_far = from_behind(up_far, 2)
    above_far = from_behind(down_far, -2)
    v_others = swapped(v_rows, "core")
    background, below_far, above_far = lax.optimization_barrier((background, below_far, above_far))

    ions = pl.pallas_call(
        functools.partial(ions_kernel, count, length_cells),
        out_shape=f32(domains, SLOTS, width),
        in_specs=[SMEM_SPEC] + [VMEM_SPEC] * 4,
        out_specs=VMEM_SPEC,
        scratch_shapes=[
            scratch(SLOTS * FLAT, LANES),
            scratch(layer_cap * SIDE, WIDTH),
            scratch(SLOTS * SIDE, LANES),
            scratch(SLOTS * SIDE, LANES),
        ],
        compiler_params=params,
        name="ion_waves",
    )(layer_start, background, circle, into_y, table_z)
    ions = lax.all_to_all(ions, "domain", split_axis=0, concat_axis=0, tiled=True)
    ions, below = lax.optimization_barrier((ions, below))

    span = layer_cap + 2 * HALO
    orbitals_next, density_kept, density_sent, kept, sent = pl.pallas_call(
        functools.partial(propagate_kernel, count, length_cells),
        out_shape=(
            f32(2, layer_cap, FLAT, LANES),
            f32(SLOTS // 2, FLAT, LANES),
            f32(SLOTS // 2, FLAT, LANES),
            f32(devices, SLOTS, width),
            f32(devices, SLOTS, width),
        ),
        in_specs=[SMEM_SPEC, SMEM_SPEC] + [VMEM_SPEC] * 12,
        out_specs=(VMEM_SPEC,) * 5,
        scratch_shapes=[
            scratch(TERMS, 2, span, TALL, WIDTH),
            scratch(span, SIDE, WIDTH),
            scratch(span, SIDE, WIDTH),
            scratch(SLOTS * FLAT, LANES),
            scratch(SLOTS * SIDE, WIDTH),
            scratch(SLOTS * SIDE, LANES),
            scratch(SLOTS * SIDE, LANES),
        ],
        compiler_params=params,
        name="propagate",
    )(layer_start, occupation, layers, potential, below, above, below_far, above_far, v_rows,
      v_others, circle, jnp.asarray(neighbour_table()), into_y, table_z)
    waves = kept + swapped(sent, "core")
    density = density_kept + swapped(density_sent, "core")
    waves, density = lax.optimization_barrier((waves, density))
    waves = lax.all_to_all(waves, ("row", "domain"), split_axis=0, concat_axis=0, tiled=True)
    other_density = swapped(density, "row")
    waves = pl.pallas_call(
        functools.partial(coulomb_kernel, count, length_cells),
        out_shape=f32(devices, SLOTS, width),
        in_specs=[SMEM_SPEC] + [VMEM_SPEC] * 3,
        out_specs=VMEM_SPEC,
        compiler_params=params,
        name="coulomb",
    )(layer_start, waves, ions, table_x)
    waves, other_density = lax.optimization_barrier((waves, other_density))
    density = density + other_density
    other_density = swapped(density, "core")
    waves = lax.all_to_all(waves, ("row", "domain"), split_axis=0, concat_axis=0, tiled=True)
    other_waves = swapped(waves, "core")
    potential_next = pl.pallas_call(
        functools.partial(field_kernel, count, length_cells),
        out_shape=f32(layer_cap, plane),
        in_specs=[SMEM_SPEC] + [VMEM_SPEC] * 7,
        out_specs=VMEM_SPEC,
        scratch_shapes=[
            scratch(SLOTS * SIDE, LANES),
            scratch(SLOTS * SIDE, LANES),
            scratch(layer_cap * SIDE, WIDTH),
            scratch(SLOTS * FLAT, LANES),
        ],
        compiler_params=params,
        name="field",
    )(layer_start, waves, other_waves, density, other_density, flat_circle, out_of_y, table_z)
    return orbitals_next.reshape(orbitals.shape), potential_next


def solution(mesh):
    domains = mesh.shape["domain"]
    split = Mesh(mesh.devices.reshape(-1, 2, domains), ("row", "core", "domain"))
    states = ("row", "core")
    return jax.shard_map(
        shards,
        mesh=split,
        in_specs=(
            P(None, states, "domain", None),
            P(states),
            P("domain", None),
            P("domain", None),
            P(),
        ),
        out_specs=(P(None, states, "domain", None), P("domain", None)),
        check_vma=False,
    )
```

```python
import functools
import math

import jax
import jax.numpy as jnp
import ml_dtypes
import numpy as np
from jax import lax
from jax.experimental import pallas as pl
from jax.experimental.pallas import tpu as pltpu
from jax.sharding import Mesh, PartitionSpec as P

SIDE = 160
SLAB = 5
TERMS = 4

HALO = TERMS
LANES = 128
SLOTS = 8
RUN = SIDE // 8
FLAT = SIDE * SIDE // LANES
STRIDE = FLAT // 8
WIDTH = 2 * LANES
BLOCK = 32
TALL = SIDE + 16

time_step = 0.3
four_pi = 4.0 * math.pi
two_pi = 2.0 * math.pi
highest = lax.Precision.HIGHEST
VMEM_BYTES = 56 * 1024 * 1024
SMEM_SPEC = pl.BlockSpec(memory_space=pltpu.SMEM)
VMEM_SPEC = pl.BlockSpec(memory_space=pltpu.VMEM)
ANY_SPEC = pl.BlockSpec(memory_space=pl.ANY)


def hartley_table(count_cells):
    index_run = np.arange(count_cells)
    angles = (index_run[:, None] * index_run[None, :] % count_cells) * (2.0 * np.pi / count_cells)
    return np.cos(angles) + np.sin(angles)


def plane_order():
    rows = np.arange(SIDE)
    return RUN * (rows % 8) + rows // 8


def two_parts(table):
    table = table.astype(np.float32)
    high = table.astype(ml_dtypes.bfloat16)
    low = (table - high.astype(np.float32)).astype(ml_dtypes.bfloat16)
    return high, low


def tables_of_side():
    table = hartley_table(SIDE)
    along_z = np.zeros((WIDTH, WIDTH))
    along_z[:SIDE, :SIDE] = table
    high, low = two_parts(along_z)
    along_z = np.concatenate([high, high, low], axis=0)
    high, low = two_parts(table[:, plane_order()])
    into_y = np.concatenate([high, high, low], axis=1)
    high, low = two_parts(table[plane_order(), :])
    out_of_y = np.concatenate([high, high, low], axis=1)
    return along_z, into_y, out_of_y


def circle_table():
    across = 2 * np.arange(SIDE, dtype=np.int64) - (SIDE - 1)
    return (across[:, None] ** 2 + across[None, :] ** 2).astype(np.int32)


def circle_plane():
    table = np.full((SIDE, WIDTH), 4 * SIDE * SIDE, np.int32)
    table[:, :SIDE] = circle_table()[plane_order()]
    return table


def mesh_points(x_row, circle, length_cells):
    room = ((length_cells - 2) ** 2 - (2 * x_row - (length_cells - 1)) ** 2) * (SIDE - 2) ** 2
    return (circle * (length_cells - 2) ** 2 <= room) & (circle < 4 * SIDE * SIDE)


def column_pieces(first, count):
    pieces = []
    column = first
    while column < first + count:
        row = column // SIDE
        stop = min((row + 1) * SIDE, first + count)
        pieces.append((row, column - row * SIDE, stop - row * SIDE))
        column = stop
    return pieces


def eight(values):
    missing = jnp.zeros((SLOTS - values.shape[0], values.shape[1]), values.dtype)
    return jnp.concatenate([values, missing], axis=0)


def to_plane(load, store):
    lane = lax.broadcasted_iota(jnp.int32, (8, LANES), 1)
    for step in range(RUN // 4):
        rows = [load(5 * step + part) for part in range(5)]
        store(4 * step, rows[0], rows[1])
        for part in range(1, 4):
            left = pltpu.roll(rows[part], LANES - 32 * part, 1)
            right = pltpu.roll(rows[part + 1], LANES - 32 * part, 1)
            store(4 * step + part, jnp.where(lane < LANES - 32 * part, left, right), right)


def to_flat(load, store):
    lane = lax.broadcasted_iota(jnp.int32, (8, LANES), 1)
    for step in range(RUN // 4):
        turned = []
        for part in range(4):
            low, high = load(4 * step + part)
            if part:
                low = pltpu.roll(low, 32 * part, 1)
                high = pltpu.roll(high, 32 * part, 1)
            turned.append((low, high))
        store(5 * step, turned[0][0])
        for part in range(1, 4):
            ended = 32 * (part - 1)
            values = jnp.where(lane < ended + 32, turned[part - 1][1], turned[part][0])
            if ended:
                values = jnp.where(lane < ended, turned[part - 1][0], values)
            store(5 * step + part, values)
        store(5 * step + 4, jnp.where(lane < 96, turned[3][0], turned[3][1]))


def parts_of(values):
    high = values.astype(jnp.bfloat16)
    low = (values - high.astype(jnp.float32)).astype(jnp.bfloat16)
    return high, low


def turn_z(values, table):
    high, low = parts_of(values)
    return jnp.dot(
        jnp.concatenate([high, low, high], axis=1), table, preferred_element_type=jnp.float32
    )


def turn_y(table, values):
    high, low = parts_of(values)
    return jnp.dot(
        table, jnp.concatenate([high, low, high], axis=0), preferred_element_type=jnp.float32
    )


def send_columns(planes_ref, slots, table_y, table_z, low_ref, high_ref):
    along_z = turn_z(planes_ref[:slots * SIDE, :], table_z)
    for slot in range(slots):
        rows = slice(slot * SIDE, (slot + 1) * SIDE)
        waves = turn_y(table_y, along_z[rows])
        low_ref[rows, :] = waves[:, :LANES]
        high_ref[rows, :] = waves[:, LANES:]
    low_ref[slots * SIDE:, :] = jnp.zeros(((SLOTS - slots) * SIDE, LANES), jnp.float32)
    high_ref[slots * SIDE:, :] = jnp.zeros(((SLOTS - slots) * SIDE, LANES), jnp.float32)


def chunk_of(low_ref, high_ref, first_row, pieces, extra):
    parts = []
    for row, start, stop in pieces:
        at = pl.ds(first_row + row, SLOTS, stride=SIDE)
        values = jnp.concatenate([low_ref[at, :], high_ref[at, :]], axis=1)
        parts.append(values[:, start:stop])
    return jnp.concatenate(parts + [extra], axis=1)


def layers_of(stored_ref, flat_ref):
    @pl.loop(0, FLAT // 8)
    def _(step):
        for part in range(8):
            lanes = pl.ds(pl.multiple_of((step * 8 + part) * LANES, LANES), LANES)
            flat_ref[pl.ds(step * 8 + part, SLOTS, stride=FLAT), :] = eight(stored_ref[:, lanes])


def place_of(start_ref):
    position = lax.axis_index("domain")
    return position, start_ref[position], start_ref[position + 1] - start_ref[position]


def pack_kernel(start_ref, potential_ref, orbitals_ref, v_ref, up_ref, down_ref, up_far_ref, down_far_ref,
                tile_ref, sems):
    _, _, thickness = place_of(start_ref)
    v_first = jnp.where(lax.axis_index("core") == 0, thickness - (HALO - 1), 0)
    first = jnp.maximum(thickness - HALO, 0)
    copies = []

    def copy(source, target):
        made = pltpu.make_async_copy(source, target, sems.at[len(copies)])
        made.start()
        copies.append(made)

    for part in range(2):
        rows = pl.ds(part * HALO, HALO)
        copy(orbitals_ref.at[part, pl.ds(first, HALO)], up_ref.at[rows])
        copy(orbitals_ref.at[part, pl.ds(0, HALO)], down_ref.at[rows])
        copy(orbitals_ref.at[part, pl.ds(thickness - 1, 1)], up_far_ref.at[pl.ds(part, 1)])
        copy(orbitals_ref.at[part, pl.ds(0, 1)], down_far_ref.at[pl.ds(part, 1)])

    @pl.loop(0, FLAT // 8)
    def _(step):
        for part in range(8):
            tile = step * 8 + part
            lanes = pl.ds(pl.multiple_of(tile * LANES, LANES), LANES)
            rows = pl.ds(pl.multiple_of(tile * 8, 8), 8)
            tile_ref[rows, :] = eight(potential_ref[:, lanes])

    @pl.loop(0, FLAT // 8)
    def _(step):
        rows = pl.ds(pl.multiple_of(step * 8, 8), 8)
        for layer in range(HALO - 1):
            v_ref[layer, rows, :] = tile_ref[pl.ds(step * 64 + v_first + layer, 8, stride=8), :]

    for made in copies:
        made.wait()


def ions_kernel(count, length_cells, start_ref, background_ref, circle_ref, table_y_ref, table_z_ref,
                out_ref, flat_ref, planes_ref, low_ref, high_ref):
    _, own_start, thickness = place_of(start_ref)
    slots = background_ref.shape[0]
    groups, _, width = out_ref.shape
    layers_of(background_ref, flat_ref)

    def body(slot, total):
        def store(tile, low, high):
            rows = pl.ds(pl.multiple_of(slot * SIDE + tile * 8, 8), 8)
            planes_ref[rows, :LANES] = low
            planes_ref[rows, LANES:] = high

        to_plane(lambda k: flat_ref[pl.ds(slot * FLAT + k, 8, stride=STRIDE), :], store)
        rows = pl.ds(pl.multiple_of(slot * SIDE, 8), SIDE)
        inside = mesh_points(own_start + slot, circle_ref[...], length_cells) & (slot < thickness)
        values = jnp.where(inside, planes_ref[rows, :], 0.0)
        planes_ref[rows, :] = values
        return total + jnp.sum(values.reshape(RUN, 8, WIDTH), axis=0)

    total = lax.fori_loop(0, slots, body, jnp.zeros((8, WIDTH), jnp.float32))
    whole = jnp.broadcast_to(jnp.sum(total, keepdims=True), (SLOTS, LANES))[:, :width - count]
    send_columns(planes_ref, slots, table_y_ref[...], table_z_ref[...], low_ref, high_ref)
    core_rows = SIDE // lax.axis_size("core")
    first_row = lax.axis_index("core") * core_rows + lax.axis_index("row") * (core_rows // lax.axis_size("row"))
    for group in range(groups):
        out_ref[group] = chunk_of(low_ref, high_ref, first_row, column_pieces(group * count, count), whole)


def propagate_kernel(count, length_cells, start_ref, weight_ref, orbitals_ref, potential_ref, below_ref,
                     above_ref, below_far_ref, above_far_ref, v_ref, v_other_ref, circle_ref,
                     table_y_ref, table_z_ref, next_ref, density_kept_ref, density_sent_ref, kept_ref, sent_ref, first_ref, second_ref,
                     third_ref, fourth_ref, sum_ref, centre_ref, beside_ref, flat_ref, planes_ref, low_ref, high_ref):
    position, own_start, thickness = place_of(start_ref)
    domains = lax.axis_size("domain")
    before = start_ref[jnp.maximum(position - 1, 0)]
    after = start_ref[jnp.minimum(position + 2, domains)]
    short_below = ((position > 0) & (own_start - before < HALO)).astype(jnp.int32)
    short_above = (position < domains - 1) & (after - own_start - thickness < HALO)
    weight = weight_ref[0]
    core = lax.axis_index("core")
    slots = orbitals_ref.shape[1]
    layers = slots + 2 * HALO
    devices, _, width = kept_ref.shape
    field_refs = (first_ref, second_ref, third_ref, fourth_ref)

    def field_layer(part, x_row):
        def store(tile, low, high):
            first_ref[part, x_row, 8 + 8 * tile:16 + 8 * tile, :LANES] = low
            first_ref[part, x_row, 8 + 8 * tile:16 + 8 * tile, LANES:] = high

        return store

    def potential_layer(x_row):
        def store(tile, low, high):
            centre_ref[x_row, 8 * tile:8 * tile + 8, :LANES] = low
            centre_ref[x_row, 8 * tile:8 * tile + 8, LANES:] = high

        return store

    def rows_from(ref, *at):
        return lambda k: ref[(*at, pl.ds(k, 8, stride=STRIDE), slice(None))]

    layers_of(potential_ref, flat_ref)

    @pl.loop(0, slots)
    def _(slot):
        for part in range(2):
            to_plane(rows_from(orbitals_ref, part, slot), field_layer(part, HALO + slot))
        to_plane(
            lambda k: flat_ref[pl.ds(slot * FLAT + k, 8, stride=STRIDE), :], potential_layer(HALO + slot)
        )

    @pl.loop(0, HALO - 1)
    def _(layer):
        lower = 1 + layer
        upper = HALO + thickness + layer
        to_plane(rows_from(v_ref, layer), potential_layer(jnp.where(core == 0, lower, upper)))
        to_plane(rows_from(v_other_ref, layer), potential_layer(jnp.where(core == 0, upper, lower)))
        for part in range(2):
            to_plane(
                rows_from(below_ref, part * HALO + 1 + layer - short_below), field_layer(part, 1 + layer)
            )
            to_plane(
                rows_from(above_ref, part * HALO + layer), field_layer(part, HALO + thickness + layer)
            )

    @pl.loop(0, 2)
    def _(part):
        last = 2 * HALO - 1 + thickness

        @pl.when(short_below > 0)
        def _():
            to_plane(rows_from(below_far_ref, part), field_layer(part, 0))

        @pl.when(short_below == 0)
        def _():
            to_plane(rows_from(below_ref, part * HALO), field_layer(part, 0))

        @pl.when(short_above)
        def _():
            to_plane(rows_from(above_far_ref, part), field_layer(part, last))

        @pl.when(jnp.logical_not(short_above))
        def _():
            to_plane(rows_from(above_ref, part * HALO + HALO - 1), field_layer(part, last))

    def wrap(term, part, x_row):
        first = field_refs[term][part, x_row, 8:16, :]
        final = field_refs[term][part, x_row, SIDE:SIDE + 8, :]
        field_refs[term][part, x_row, :8, :] = pltpu.roll(final, 1, 0)
        field_refs[term][part, x_row, SIDE + 8:, :] = pltpu.roll(first, 7, 0)

    @pl.loop(0, layers)
    def _(x_row):
        known = x_row < thickness + 2 * HALO
        for block in range(SIDE // BLOCK):
            rows = slice(block * BLOCK, (block + 1) * BLOCK)
            inner = slice(8 + block * BLOCK, 8 + (block + 1) * BLOCK)
            inside = mesh_points(own_start - HALO + x_row, circle_ref[rows, :], length_cells) & known
            centre_ref[x_row, rows, :] = jnp.where(
                inside, (3.0 + centre_ref[x_row, rows, :]) * time_step, 0.0
            )
            beside_ref[x_row, rows, :] = jnp.where(inside, 0.5 * time_step, 0.0)
            for part in range(2):
                first_ref[part, x_row, inner, :] = jnp.where(
                    inside, first_ref[part, x_row, inner, :], 0.0
                )
        for part in range(2):
            wrap(0, part, x_row)

    def hamilton(term, part, x_row, block, centre, beside):
        field_ref = field_refs[term]
        tall = field_ref[part, x_row, block * BLOCK:block * BLOCK + BLOCK + 16, :]
        inner = slice(8 + block * BLOCK, 8 + (block + 1) * BLOCK)
        field = tall[8:8 + BLOCK]
        around = field_ref[part, x_row - 1, inner, :] + field_ref[part, x_row + 1, inner, :]
        around = around + (tall[:BLOCK] + tall[16:])
        around = around + (pltpu.roll(field, 1, 1) + pltpu.roll(field, WIDTH - 1, 1))
        return centre * field - beside * around

    for term in range(1, TERMS):

        @pl.loop(term, layers - term)
        def _(x_row, term=term):
            for block in range(SIDE // BLOCK):
                rows = slice(block * BLOCK, (block + 1) * BLOCK)
                inner = slice(8 + block * BLOCK, 8 + (block + 1) * BLOCK)
                centre = centre_ref[x_row, rows, :]
                beside = beside_ref[x_row, rows, :]
                for part in range(2):
                    field_refs[term][part, x_row, inner, :] = hamilton(
                        term - 1, part, x_row, block, centre, beside
                    )
            for part in range(2):
                wrap(term, part, x_row)

    def finish(slot, total):
        x_row = HALO + slot
        owned = slot < thickness
        for block in range(SIDE // BLOCK):
            rows = slice(block * BLOCK, (block + 1) * BLOCK)
            inner = slice(8 + block * BLOCK, 8 + (block + 1) * BLOCK)
            centre = centre_ref[x_row, rows, :]
            beside = beside_ref[x_row, rows, :]
            density = jnp.zeros((BLOCK, WIDTH), jnp.float32)
            for part, sign in ((0, 1.0), (1, -1.0)):
                summed = first_ref[part, x_row, inner, :]
                summed = summed + sign * second_ref[1 - part, x_row, inner, :]
                summed = summed - (1.0 / 2.0) * third_ref[part, x_row, inner, :]
                summed = summed - (sign / 6.0) * fourth_ref[1 - part, x_row, inner, :]
                summed = summed + (1.0 / 24.0) * hamilton(3, part, x_row, block, centre, beside)
                summed = jnp.where(owned, summed, 0.0)
                sum_ref[part, rows, :] = summed
                density = density + summed * summed
            density = weight * density
            planes_ref[pl.ds(pl.multiple_of(slot * SIDE + block * BLOCK, 8), BLOCK), :] = density
            total = total + jnp.sum(density.reshape(BLOCK // 8, 8, WIDTH), axis=0)

        for part in range(2):

            def load(tile, part=part):
                tall = sum_ref[part, 8 * tile:8 * tile + 8, :]
                return tall[:, :LANES], tall[:, LANES:]

            def store(k, values, part=part):
                next_ref[part, slot, pl.ds(k, 8, stride=STRIDE), :] = values

            to_flat(load, store)

        return total

    total = lax.fori_loop(0, slots, finish, jnp.zeros((8, WIDTH), jnp.float32))
    planes_ref[slots * SIDE:, :] = jnp.zeros(((SLOTS - slots) * SIDE, WIDTH), jnp.float32)

    @pl.loop(0, SLOTS // 2)
    def _(slot):
        for first, target_ref in ((core, density_kept_ref), (1 - core, density_sent_ref)):

            def load(tile, first=first):
                row = (first * (SLOTS // 2) + slot) * SIDE + tile * 8
                tall = planes_ref[pl.ds(pl.multiple_of(row, 8), 8), :]
                return tall[:, :LANES], tall[:, LANES:]

            def store(k, values, target_ref=target_ref):
                target_ref[slot, pl.ds(k, 8, stride=STRIDE), :] = values

            to_flat(load, store)

    whole = jnp.broadcast_to(jnp.sum(total, keepdims=True), (SLOTS, LANES))[:, :width - count]
    send_columns(planes_ref, slots, table_y_ref[...], table_z_ref[...], low_ref, high_ref)
    core_rows = SIDE // 2
    first_row = core * core_rows
    for device in range(devices):
        pieces = column_pieces(device * count, count)
        kept_ref[device] = chunk_of(low_ref, high_ref, first_row, pieces, whole)
        sent_ref[device] = chunk_of(low_ref, high_ref, core_rows - first_row, pieces, whole)


def wave_squared(index, count_cells):
    folded = jnp.where(2 * index <= count_cells, index, index - count_cells)
    wave_number = folded.astype(jnp.float32) * (two_pi / count_cells)
    return wave_number * wave_number


def coulomb_kernel(count, length_cells, start_ref, charge_ref, ions_ref, table_ref, out_ref):
    domains, _, width = ions_ref.shape
    states = charge_ref.shape[0] // domains
    device = (lax.axis_index("core") * states + lax.axis_index("row")) * domains + lax.axis_index("domain")
    charge = charge_ref[:domains]
    for state in range(1, states):
        charge = charge + charge_ref[state * domains:(state + 1) * domains]
    charge = charge.reshape(domains * SLOTS, width)
    ions = ions_ref[...].reshape(domains * SLOTS, width)
    first = lax.broadcasted_iota(jnp.int32, (domains * SLOTS, width), 0) % SLOTS == 0
    lane = lax.broadcasted_iota(jnp.int32, (domains * SLOTS, width), 1)
    chosen = first & (lane == count)
    electrons = jnp.sum(jnp.where(chosen, charge, 0.0), keepdims=True)
    ionic = jnp.sum(jnp.where(chosen, ions, 0.0), keepdims=True)
    charge = charge - (electrons / ionic) * ions
    layer = lax.broadcasted_iota(jnp.int32, (length_cells, domains * SLOTS), 0)
    place = lax.broadcasted_iota(jnp.int32, (length_cells, domains * SLOTS), 1)
    chosen_layer = jnp.full(layer.shape, -1, jnp.int32)
    for domain in range(domains):
        slot = place - domain * SLOTS
        here = (slot >= 0) & (slot < start_ref[domain + 1] - start_ref[domain])
        chosen_layer = jnp.where(here, start_ref[domain] + slot, chosen_layer)
    pick = (layer == chosen_layer).astype(jnp.float32)
    table = jnp.dot(table_ref[...], pick, precision=highest, preferred_element_type=jnp.float32)
    waves = jnp.dot(table, charge, precision=highest, preferred_element_type=jnp.float32)
    wave_x = lax.broadcasted_iota(jnp.int32, waves.shape, 0)
    column = device * count + lax.broadcasted_iota(jnp.int32, waves.shape, 1)
    wave_y = ((column.astype(jnp.float32) + 0.5) * (1.0 / SIDE)).astype(jnp.int32)
    wave_z = column - wave_y * SIDE
    squared = (
        wave_squared(wave_x, length_cells) + wave_squared(wave_y, SIDE) + wave_squared(wave_z, SIDE)
    )
    gain = jnp.where(squared > 0, four_pi / jnp.where(squared > 0, squared, 1.0), 0.0)
    waves = waves * (gain * (1.0 / (length_cells * SIDE * SIDE)))
    back = lax.dot_general(
        table, waves, (((0,), (0,)), ((), ())), precision=highest, preferred_element_type=jnp.float32
    )
    back = back.reshape(domains, SLOTS, width)
    for state in range(states):
        out_ref[state * domains:(state + 1) * domains] = back


def field_kernel(count, length_cells, start_ref, waves_ref, others_ref, density_ref, other_ref,
                 circle_ref, table_y_ref, table_z_ref, out_ref, low_ref, high_ref, planes_ref, flat_ref):
    _, own_start, thickness = place_of(start_ref)
    devices = waves_ref.shape[0]
    slots = out_ref.shape[0]
    core = lax.axis_index("core")
    core_rows = SIDE // 2
    first_row = core * core_rows
    for source_ref, first in ((waves_ref, first_row), (others_ref, core_rows - first_row)):
        pieces = []
        for device in range(devices):
            column = 0
            for row, start, stop in column_pieces(device * count, count):
                values = source_ref[device, :, column:column + stop - start]
                column += stop - start
                if start > 0:
                    pieces.append(values)
                    values = jnp.concatenate(pieces, axis=1)
                if stop < SIDE:
                    pieces = [values]
                    continue
                pieces = []
                at = pl.ds(first + row, SLOTS, stride=SIDE)
                low_ref[at, :] = values[:, :LANES]
                high_ref[at, :] = jnp.concatenate(
                    [values[:, LANES:], jnp.zeros((SLOTS, WIDTH - SIDE), jnp.float32)], axis=1
                )
    table_y = table_y_ref[...]
    table_z = table_z_ref[...]
    used = slice(0, slots * SIDE)
    along_z = turn_z(jnp.concatenate([low_ref[used, :], high_ref[used, :]], axis=1), table_z)
    for slot in range(slots):
        rows = slice(slot * SIDE, (slot + 1) * SIDE)
        planes_ref[rows, :] = turn_y(table_y, along_z[rows])

    @pl.loop(0, slots)
    def _(slot):
        def load(tile):
            tall = planes_ref[pl.ds(pl.multiple_of(slot * SIDE + tile * 8, 8), 8), :]
            return tall[:, :LANES], tall[:, LANES:]

        def store(k, values):
            flat_ref[pl.ds(slot * FLAT + k, 8, stride=STRIDE), :] = values

        to_flat(load, store)
        rows = pl.ds(pl.multiple_of(slot * FLAT, 8), FLAT)
        here = slot // (SLOTS // 2) == core
        kept_slot = slot % (SLOTS // 2)
        content = jnp.where(here, density_ref[kept_slot], other_ref[kept_slot]) * (3.0 / math.pi)
        positive = jnp.where(content > 0, content, 1.0)
        root = jnp.exp(jnp.log(positive) * (1.0 / 3.0))
        root = root - (root - positive / (root * root)) * (1.0 / 3.0)
        root = jnp.where(content > 0, root, 0.0)
        inside = mesh_points(own_start + slot, circle_ref[...], length_cells) & (slot < thickness)
        flat_ref[rows, :] = jnp.where(inside, flat_ref[rows, :] - root, 0.0)

    @pl.loop(0, FLAT // 8)
    def _(step):
        for part in range(8):
            lanes = pl.ds(pl.multiple_of((step * 8 + part) * LANES, LANES), LANES)
            out_ref[:, lanes] = flat_ref[pl.ds(step * 8 + part, SLOTS, stride=FLAT), :][:slots]


def from_behind(value, steps):
    count = lax.axis_size("domain")
    leading, last = (max(0, -steps), min(count, count - steps))
    return lax.ppermute(value, "domain", [(source, source + steps) for source in range(leading, last)])


def swapped(value, axis):
    return lax.ppermute(value, axis, [(0, 1), (1, 0)])


def shards(orbitals, occupation, potential, background, layer_start):
    domains = lax.axis_size("domain")
    rows = lax.axis_size("row")
    devices = domains * rows
    length_cells = SLAB * domains
    layer_cap, plane = potential.shape
    count = plane // (2 * devices)
    width = -(-(count + 1) // LANES) * LANES
    circle = jnp.asarray(circle_plane())
    flat_circle = jnp.asarray(circle_table().reshape(FLAT, LANES))
    table_z, into_y, out_of_y = (jnp.asarray(table) for table in tables_of_side())
    table_x = jnp.asarray(hartley_table(length_cells).astype(np.float32))
    params = pltpu.CompilerParams(vmem_limit_bytes=VMEM_BYTES)

    def f32(*shape):
        return jax.ShapeDtypeStruct(shape, jnp.float32)

    def scratch(*shape):
        return pltpu.VMEM(shape, jnp.float32)

    layers = orbitals.reshape(2, layer_cap, FLAT, LANES)
    v_rows, up, down, up_far, down_far = pl.pallas_call(
        pack_kernel,
        out_shape=tuple(f32(size, FLAT, LANES) for size in (HALO - 1, 2 * HALO, 2 * HALO, 2, 2)),
        in_specs=[SMEM_SPEC, VMEM_SPEC, ANY_SPEC],
        out_specs=(VMEM_SPEC,) * 5,
        scratch_shapes=[scratch(FLAT * 8, LANES), pltpu.SemaphoreType.DMA((8,))],
        compiler_params=params,
        name="pack_halo",
    )(layer_start, potential, layers)
    v_rows = lax.ppermute(
        v_rows,
        ("core", "domain"),
        [(source, source + 1) for source in range(domains - 1)]
        + [(domains + source + 1, domains + source) for source in range(domains - 1)],
    )
    below = from_behind(up, 1)
    above = from_behind(down, -1)
    below_far = from_behind(up_far, 2)
    above_far = from_behind(down_far, -2)
    v_others = swapped(v_rows, "core")
    background, below_far, above_far = lax.optimization_barrier((background, below_far, above_far))

    ions = pl.pallas_call(
        functools.partial(ions_kernel, count, length_cells),
        out_shape=f32(domains, SLOTS, width),
        in_specs=[SMEM_SPEC] + [VMEM_SPEC] * 4,
        out_specs=VMEM_SPEC,
        scratch_shapes=[
            scratch(SLOTS * FLAT, LANES),
            scratch(layer_cap * SIDE, WIDTH),
            scratch(SLOTS * SIDE, LANES),
            scratch(SLOTS * SIDE, LANES),
        ],
        compiler_params=params,
        name="ion_waves",
    )(layer_start, background, circle, into_y, table_z)
    ions = lax.all_to_all(ions, "domain", split_axis=0, concat_axis=0, tiled=True)
    ions, below = lax.optimization_barrier((ions, below))

    span = layer_cap + 2 * HALO
    orbitals_next, density_kept, density_sent, kept, sent = pl.pallas_call(
        functools.partial(propagate_kernel, count, length_cells),
        out_shape=(
            f32(2, layer_cap, FLAT, LANES),
            f32(SLOTS // 2, FLAT, LANES),
            f32(SLOTS // 2, FLAT, LANES),
            f32(devices, SLOTS, width),
            f32(devices, SLOTS, width),
        ),
        in_specs=[SMEM_SPEC, SMEM_SPEC] + [VMEM_SPEC] * 11,
        out_specs=(VMEM_SPEC,) * 5,
        scratch_shapes=[
            scratch(2, span, TALL, WIDTH),
            scratch(2, span, TALL, WIDTH),
            scratch(2, span, TALL, WIDTH),
            scratch(2, span, TALL, WIDTH),
            scratch(2, SIDE, WIDTH),
            scratch(span, SIDE, WIDTH),
            scratch(span, SIDE, WIDTH),
            scratch(SLOTS * FLAT, LANES),
            scratch(SLOTS * SIDE, WIDTH),
            scratch(SLOTS * SIDE, LANES),
            scratch(SLOTS * SIDE, LANES),
        ],
        compiler_params=params,
        name="propagate",
    )(layer_start, occupation, layers, potential, below, above, below_far, above_far, v_rows,
      v_others, circle, into_y, table_z)
    waves = kept + swapped(sent, "core")
    density = density_kept + swapped(density_sent, "core")
    waves, density = lax.optimization_barrier((waves, density))
    waves = lax.all_to_all(waves, ("row", "domain"), split_axis=0, concat_axis=0, tiled=True)
    other_density = swapped(density, "row")
    waves = pl.pallas_call(
        functools.partial(coulomb_kernel, count, length_cells),
        out_shape=f32(devices, SLOTS, width),
        in_specs=[SMEM_SPEC] + [VMEM_SPEC] * 3,
        out_specs=VMEM_SPEC,
        compiler_params=params,
        name="coulomb",
    )(layer_start, waves, ions, table_x)
    waves, other_density = lax.optimization_barrier((waves, other_density))
    density = density + other_density
    other_density = swapped(density, "core")
    waves = lax.all_to_all(waves, ("row", "domain"), split_axis=0, concat_axis=0, tiled=True)
    other_waves = swapped(waves, "core")
    potential_next = pl.pallas_call(
        functools.partial(field_kernel, count, length_cells),
        out_shape=f32(layer_cap, plane),
        in_specs=[SMEM_SPEC] + [VMEM_SPEC] * 7,
        out_specs=VMEM_SPEC,
        scratch_shapes=[
            scratch(SLOTS * SIDE, LANES),
            scratch(SLOTS * SIDE, LANES),
            scratch(layer_cap * SIDE, WIDTH),
            scratch(SLOTS * FLAT, LANES),
        ],
        compiler_params=params,
        name="field",
    )(layer_start, waves, other_waves, density, other_density, flat_circle, out_of_y, table_z)
    return orbitals_next.reshape(orbitals.shape), potential_next


def solution(mesh):
    domains = mesh.shape["domain"]
    split = Mesh(mesh.devices.reshape(-1, 2, domains), ("row", "core", "domain"))
    states = ("row", "core")
    return jax.shard_map(
        shards,
        mesh=split,
        in_specs=(
            P(None, states, "domain", None),
            P(states),
            P("domain", None),
            P("domain", None),
            P(),
        ),
        out_specs=(P(None, states, "domain", None), P("domain", None)),
        check_vma=False,
    )
```

```python
import functools
import math

import jax
import jax.numpy as jnp
import ml_dtypes
import numpy as np
from jax import lax
from jax.experimental import pallas as pl
from jax.experimental.pallas import tpu as pltpu
from jax.sharding import Mesh, PartitionSpec as P

SIDE = 160
SLAB = 5
TERMS = 4

HALO = TERMS
LANES = 128
SLOTS = 8
RUN = SIDE // 8
FLAT = SIDE * SIDE // LANES
STRIDE = FLAT // 8
WIDTH = 2 * LANES
BLOCK = 32
TALL = SIDE + 16

time_step = 0.3
four_pi = 4.0 * math.pi
two_pi = 2.0 * math.pi
highest = lax.Precision.HIGHEST
VMEM_BYTES = 56 * 1024 * 1024
SMEM_SPEC = pl.BlockSpec(memory_space=pltpu.SMEM)
VMEM_SPEC = pl.BlockSpec(memory_space=pltpu.VMEM)
ANY_SPEC = pl.BlockSpec(memory_space=pl.ANY)


def hartley_table(count_cells):
    index_run = np.arange(count_cells)
    angles = (index_run[:, None] * index_run[None, :] % count_cells) * (2.0 * np.pi / count_cells)
    return np.cos(angles) + np.sin(angles)


def plane_order():
    rows = np.arange(SIDE)
    return RUN * (rows % 8) + rows // 8


def two_parts(table):
    table = table.astype(np.float32)
    high = table.astype(ml_dtypes.bfloat16)
    low = (table - high.astype(np.float32)).astype(ml_dtypes.bfloat16)
    return high, low


def tables_of_side():
    table = hartley_table(SIDE)
    along_z = np.zeros((WIDTH, WIDTH))
    along_z[:SIDE, :SIDE] = table
    high, low = two_parts(along_z)
    along_z = np.concatenate([high, high, low], axis=0)
    high, low = two_parts(table[:, plane_order()])
    into_y = np.concatenate([high, high, low], axis=1)
    high, low = two_parts(table[plane_order(), :])
    out_of_y = np.concatenate([high, high, low], axis=1)
    return along_z, into_y, out_of_y


def circle_table():
    across = 2 * np.arange(SIDE, dtype=np.int64) - (SIDE - 1)
    return (across[:, None] ** 2 + across[None, :] ** 2).astype(np.int32)


def circle_plane():
    table = np.full((SIDE, WIDTH), 4 * SIDE * SIDE, np.int32)
    table[:, :SIDE] = circle_table()[plane_order()]
    return table


def mesh_points(x_row, circle, length_cells):
    room = ((length_cells - 2) ** 2 - (2 * x_row - (length_cells - 1)) ** 2) * (SIDE - 2) ** 2
    return (circle * (length_cells - 2) ** 2 <= room) & (circle < 4 * SIDE * SIDE)


def column_pieces(first, count):
    pieces = []
    column = first
    while column < first + count:
        row = column // SIDE
        stop = min((row + 1) * SIDE, first + count)
        pieces.append((row, column - row * SIDE, stop - row * SIDE))
        column = stop
    return pieces


def eight(values):
    missing = jnp.zeros((SLOTS - values.shape[0], values.shape[1]), values.dtype)
    return jnp.concatenate([values, missing], axis=0)


def to_plane(load, store):
    lane = lax.broadcasted_iota(jnp.int32, (8, LANES), 1)
    for step in range(RUN // 4):
        rows = [load(5 * step + part) for part in range(5)]
        store(4 * step, rows[0], rows[1])
        for part in range(1, 4):
            left = pltpu.roll(rows[part], LANES - 32 * part, 1)
            right = pltpu.roll(rows[part + 1], LANES - 32 * part, 1)
            store(4 * step + part, jnp.where(lane < LANES - 32 * part, left, right), right)


def to_flat(load, store):
    lane = lax.broadcasted_iota(jnp.int32, (8, LANES), 1)
    for step in range(RUN // 4):
        turned = []
        for part in range(4):
            low, high = load(4 * step + part)
            if part:
                low = pltpu.roll(low, 32 * part, 1)
                high = pltpu.roll(high, 32 * part, 1)
            turned.append((low, high))
        store(5 * step, turned[0][0])
        for part in range(1, 4):
            ended = 32 * (part - 1)
            values = jnp.where(lane < ended + 32, turned[part - 1][1], turned[part][0])
            if ended:
                values = jnp.where(lane < ended, turned[part - 1][0], values)
            store(5 * step + part, values)
        store(5 * step + 4, jnp.where(lane < 96, turned[3][0], turned[3][1]))


def parts_of(values):
    high = values.astype(jnp.bfloat16)
    low = (values - high.astype(jnp.float32)).astype(jnp.bfloat16)
    return high, low


def turn_z(values, table):
    high, low = parts_of(values)
    return jnp.dot(
        jnp.concatenate([high, low, high], axis=1), table, preferred_element_type=jnp.float32
    )


def turn_y(table, values):
    high, low = parts_of(values)
    return jnp.dot(
        table, jnp.concatenate([high, low, high], axis=0), preferred_element_type=jnp.float32
    )


def send_columns(planes_ref, slots, table_y, table_z, low_ref, high_ref):
    along_z = turn_z(planes_ref[:slots * SIDE, :], table_z)
    for slot in range(slots):
        rows = slice(slot * SIDE, (slot + 1) * SIDE)
        waves = turn_y(table_y, along_z[rows])
        low_ref[rows, :] = waves[:, :LANES]
        high_ref[rows, :] = waves[:, LANES:]
    low_ref[slots * SIDE:, :] = jnp.zeros(((SLOTS - slots) * SIDE, LANES), jnp.float32)
    high_ref[slots * SIDE:, :] = jnp.zeros(((SLOTS - slots) * SIDE, LANES), jnp.float32)


def chunk_of(low_ref, high_ref, first_row, pieces, extra):
    parts = []
    for row, start, stop in pieces:
        at = pl.ds(first_row + row, SLOTS, stride=SIDE)
        values = jnp.concatenate([low_ref[at, :], high_ref[at, :]], axis=1)
        parts.append(values[:, start:stop])
    return jnp.concatenate(parts + [extra], axis=1)


def layers_of(stored_ref, flat_ref):
    @pl.loop(0, FLAT // 8)
    def _(step):
        for part in range(8):
            lanes = pl.ds(pl.multiple_of((step * 8 + part) * LANES, LANES), LANES)
            flat_ref[pl.ds(step * 8 + part, SLOTS, stride=FLAT), :] = eight(stored_ref[:, lanes])


def place_of(start_ref):
    position = lax.axis_index("domain")
    return position, start_ref[position], start_ref[position + 1] - start_ref[position]


def pack_kernel(start_ref, potential_ref, orbitals_ref, v_ref, real_up_ref, real_down_ref, imag_up_ref,
                imag_down_ref, up_far_ref, down_far_ref, tile_ref, sems):
    _, _, thickness = place_of(start_ref)
    v_first = jnp.where(lax.axis_index("core") == 0, thickness - (HALO - 1), 0)
    first = jnp.maximum(thickness - HALO, 0)
    copies = []

    def copy(source, target):
        made = pltpu.make_async_copy(source, target, sems.at[len(copies)])
        made.start()
        copies.append(made)

    for part, up_ref, down_ref in ((0, real_up_ref, real_down_ref), (1, imag_up_ref, imag_down_ref)):
        copy(orbitals_ref.at[part, pl.ds(first, HALO)], up_ref)
        copy(orbitals_ref.at[part, pl.ds(0, HALO)], down_ref)
        copy(orbitals_ref.at[part, pl.ds(thickness - 1, 1)], up_far_ref.at[pl.ds(part, 1)])
        copy(orbitals_ref.at[part, pl.ds(0, 1)], down_far_ref.at[pl.ds(part, 1)])

    @pl.loop(0, FLAT // 8)
    def _(step):
        for part in range(8):
            tile = step * 8 + part
            lanes = pl.ds(pl.multiple_of(tile * LANES, LANES), LANES)
            rows = pl.ds(pl.multiple_of(tile * 8, 8), 8)
            tile_ref[rows, :] = eight(potential_ref[:, lanes])

    @pl.loop(0, FLAT // 8)
    def _(step):
        rows = pl.ds(pl.multiple_of(step * 8, 8), 8)
        for layer in range(HALO - 1):
            v_ref[layer, rows, :] = tile_ref[pl.ds(step * 64 + v_first + layer, 8, stride=8), :]

    for made in copies:
        made.wait()


def ions_kernel(count, length_cells, start_ref, background_ref, circle_ref, table_y_ref, table_z_ref,
                out_ref, flat_ref, planes_ref, low_ref, high_ref):
    _, own_start, thickness = place_of(start_ref)
    slots = background_ref.shape[0]
    groups, _, width = out_ref.shape
    layers_of(background_ref, flat_ref)

    def body(slot, total):
        def store(tile, low, high):
            rows = pl.ds(pl.multiple_of(slot * SIDE + tile * 8, 8), 8)
            planes_ref[rows, :LANES] = low
            planes_ref[rows, LANES:] = high

        to_plane(lambda k: flat_ref[pl.ds(slot * FLAT + k, 8, stride=STRIDE), :], store)
        rows = pl.ds(pl.multiple_of(slot * SIDE, 8), SIDE)
        inside = mesh_points(own_start + slot, circle_ref[...], length_cells) & (slot < thickness)
        values = jnp.where(inside, planes_ref[rows, :], 0.0)
        planes_ref[rows, :] = values
        return total + jnp.sum(values.reshape(RUN, 8, WIDTH), axis=0)

    total = lax.fori_loop(0, slots, body, jnp.zeros((8, WIDTH), jnp.float32))
    whole = jnp.broadcast_to(jnp.sum(total, keepdims=True), (SLOTS, LANES))[:, :width - count]
    send_columns(planes_ref, slots, table_y_ref[...], table_z_ref[...], low_ref, high_ref)
    core_rows = SIDE // lax.axis_size("core")
    first_row = lax.axis_index("core") * core_rows + lax.axis_index("row") * (core_rows // lax.axis_size("row"))
    for group in range(groups):
        out_ref[group] = chunk_of(low_ref, high_ref, first_row, column_pieces(group * count, count), whole)


def rows_from(ref, *at):
    return lambda k: ref[(*at, pl.ds(k, 8, stride=STRIDE), slice(None))]


def plane_at(ref, x_row, skip):
    def store(tile, low, high):
        ref[x_row, skip + 8 * tile:skip + 8 * tile + 8, :LANES] = low
        ref[x_row, skip + 8 * tile:skip + 8 * tile + 8, LANES:] = high

    return store


class Chain:
    def __init__(self, length_cells, part, start_ref, circle_ref, field_refs, centre_ref, beside_ref):
        position, self.own_start, self.thickness = place_of(start_ref)
        domains = lax.axis_size("domain")
        before = start_ref[jnp.maximum(position - 1, 0)]
        after = start_ref[jnp.minimum(position + 2, domains)]
        self.short_below = (position > 0) & (self.own_start - before < HALO)
        self.short_above = (position < domains - 1) & (after - self.own_start - self.thickness < HALO)
        self.length_cells = length_cells
        self.part = part
        self.circle_ref = circle_ref
        self.field_refs = field_refs
        self.centre_ref = centre_ref
        self.beside_ref = beside_ref
        self.layers = field_refs[0].shape[0]

    def fill(self, orbitals_ref, below_ref, above_ref, below_far_ref, above_far_ref):
        field_ref = self.field_refs[0]
        short_below = self.short_below.astype(jnp.int32)
        upper = HALO + self.thickness

        @pl.loop(0, orbitals_ref.shape[1])
        def _(slot):
            to_plane(rows_from(orbitals_ref, self.part, slot), plane_at(field_ref, HALO + slot, 8))

        @pl.loop(0, HALO - 1)
        def _(layer):
            to_plane(rows_from(below_ref, 1 + layer - short_below), plane_at(field_ref, 1 + layer, 8))
            to_plane(rows_from(above_ref, layer), plane_at(field_ref, upper + layer, 8))

        for short, near_ref, near, far_ref, x_row in (
            (self.short_below, below_ref, 0, below_far_ref, 0),
            (self.short_above, above_ref, HALO - 1, above_far_ref, upper + HALO - 1),
        ):

            @pl.when(short)
            def _(far_ref=far_ref, x_row=x_row):
                to_plane(rows_from(far_ref, self.part), plane_at(field_ref, x_row, 8))

            @pl.when(jnp.logical_not(short))
            def _(near_ref=near_ref, near=near, x_row=x_row):
                to_plane(rows_from(near_ref, near), plane_at(field_ref, x_row, 8))

    def wrap(self, term, x_row):
        field_ref = self.field_refs[term]
        first = field_ref[x_row, 8:16, :]
        final = field_ref[x_row, SIDE:SIDE + 8, :]
        field_ref[x_row, :8, :] = pltpu.roll(final, 1, 0)
        field_ref[x_row, SIDE + 8:, :] = pltpu.roll(first, 7, 0)

    def confine(self, make_centre):
        field_ref = self.field_refs[0]

        @pl.loop(0, self.layers)
        def _(x_row):
            known = x_row < self.thickness + 2 * HALO
            for block in range(SIDE // BLOCK):
                rows = slice(block * BLOCK, (block + 1) * BLOCK)
                inner = slice(8 + block * BLOCK, 8 + (block + 1) * BLOCK)
                inside = known & mesh_points(
                    self.own_start - HALO + x_row, self.circle_ref[rows, :], self.length_cells
                )
                if make_centre:
                    self.centre_ref[x_row, rows, :] = jnp.where(
                        inside, (3.0 + self.centre_ref[x_row, rows, :]) * time_step, 0.0
                    )
                self.beside_ref[x_row, rows, :] = jnp.where(inside, 0.5 * time_step, 0.0)
                field_ref[x_row, inner, :] = jnp.where(inside, field_ref[x_row, inner, :], 0.0)
            self.wrap(0, x_row)

    def hamilton(self, term, x_row, block):
        field_ref = self.field_refs[term]
        rows = slice(block * BLOCK, (block + 1) * BLOCK)
        inner = slice(8 + block * BLOCK, 8 + (block + 1) * BLOCK)
        tall = field_ref[x_row, block * BLOCK:block * BLOCK + BLOCK + 16, :]
        field = tall[8:8 + BLOCK]
        around = field_ref[x_row - 1, inner, :] + field_ref[x_row + 1, inner, :]
        around = around + (tall[:BLOCK] + tall[16:])
        around = around + (pltpu.roll(field, 1, 1) + pltpu.roll(field, WIDTH - 1, 1))
        return self.centre_ref[x_row, rows, :] * field - self.beside_ref[x_row, rows, :] * around

    def steps(self):
        for term in range(1, TERMS):

            @pl.loop(term, self.layers - term)
            def _(x_row, term=term):
                for block in range(SIDE // BLOCK):
                    inner = slice(8 + block * BLOCK, 8 + (block + 1) * BLOCK)
                    self.field_refs[term][x_row, inner, :] = self.hamilton(term - 1, x_row, block)
                self.wrap(term, x_row)

    def sums(self, x_row, block):
        inner = slice(8 + block * BLOCK, 8 + (block + 1) * BLOCK)
        terms = [ref[x_row, inner, :] for ref in self.field_refs]
        even = terms[0] - (1.0 / 2.0) * terms[2] + (1.0 / 24.0) * self.hamilton(TERMS - 1, x_row, block)
        return even, terms[1] - (1.0 / 6.0) * terms[3]


def real_kernel(length_cells, start_ref, orbitals_ref, potential_ref, below_ref, above_ref, below_far_ref,
                above_far_ref, v_ref, v_other_ref, circle_ref, even_ref, odd_ref, centre_ref, first_ref,
                second_ref, third_ref, fourth_ref, beside_ref, flat_ref):
    field_refs = (first_ref, second_ref, third_ref, fourth_ref)
    chain = Chain(length_cells, 0, start_ref, circle_ref, field_refs, centre_ref, beside_ref)
    slots = orbitals_ref.shape[1]
    core = lax.axis_index("core")
    layers_of(potential_ref, flat_ref)

    @pl.loop(0, slots)
    def _(slot):
        to_plane(
            lambda k: flat_ref[pl.ds(slot * FLAT + k, 8, stride=STRIDE), :],
            plane_at(centre_ref, HALO + slot, 0),
        )

    @pl.loop(0, HALO - 1)
    def _(layer):
        lower = 1 + layer
        upper = HALO + chain.thickness + layer
        to_plane(rows_from(v_ref, layer), plane_at(centre_ref, jnp.where(core == 0, lower, upper), 0))
        to_plane(rows_from(v_other_ref, layer), plane_at(centre_ref, jnp.where(core == 0, upper, lower), 0))

    chain.fill(orbitals_ref, below_ref, above_ref, below_far_ref, above_far_ref)
    chain.confine(True)
    chain.steps()

    @pl.loop(0, slots)
    def _(slot):
        for block in range(SIDE // BLOCK):
            rows = slice(block * BLOCK, (block + 1) * BLOCK)
            even_ref[slot, rows, :], odd_ref[slot, rows, :] = chain.sums(HALO + slot, block)


def propagate_kernel(count, length_cells, start_ref, weight_ref, orbitals_ref, below_ref, above_ref,
                     below_far_ref, above_far_ref, even_ref, odd_ref, centre_ref, circle_ref, table_y_ref,
                     table_z_ref, next_ref, density_kept_ref, density_sent_ref, kept_ref, sent_ref,
                     first_ref, second_ref, third_ref, fourth_ref, sum_ref, beside_ref, planes_ref, low_ref,
                     high_ref):
    field_refs = (first_ref, second_ref, third_ref, fourth_ref)
    chain = Chain(length_cells, 1, start_ref, circle_ref, field_refs, centre_ref, beside_ref)
    weight = weight_ref[0]
    core = lax.axis_index("core")
    slots = orbitals_ref.shape[1]
    devices, _, width = kept_ref.shape
    chain.fill(orbitals_ref, below_ref, above_ref, below_far_ref, above_far_ref)
    chain.confine(False)
    chain.steps()

    def finish(slot, total):
        owned = slot < chain.thickness
        for block in range(SIDE // BLOCK):
            rows = slice(block * BLOCK, (block + 1) * BLOCK)
            even, odd = chain.sums(HALO + slot, block)
            real = jnp.where(owned, even_ref[slot, rows, :] + odd, 0.0)
            imag = jnp.where(owned, even - odd_ref[slot, rows, :], 0.0)
            sum_ref[0, rows, :] = real
            sum_ref[1, rows, :] = imag
            density = weight * (real * real + imag * imag)
            planes_ref[pl.ds(pl.multiple_of(slot * SIDE + block * BLOCK, 8), BLOCK), :] = density
            total = total + jnp.sum(density.reshape(BLOCK // 8, 8, WIDTH), axis=0)

        for part in range(2):

            def load(tile, part=part):
                tall = sum_ref[part, 8 * tile:8 * tile + 8, :]
                return tall[:, :LANES], tall[:, LANES:]

            def store(k, values, part=part):
                next_ref[part, slot, pl.ds(k, 8, stride=STRIDE), :] = values

            to_flat(load, store)
        return total

    total = lax.fori_loop(0, slots, finish, jnp.zeros((8, WIDTH), jnp.float32))
    planes_ref[slots * SIDE:, :] = jnp.zeros(((SLOTS - slots) * SIDE, WIDTH), jnp.float32)

    @pl.loop(0, SLOTS // 2)
    def _(slot):
        for first, target_ref in ((core, density_kept_ref), (1 - core, density_sent_ref)):

            def load(tile, first=first):
                row = (first * (SLOTS // 2) + slot) * SIDE + tile * 8
                tall = planes_ref[pl.ds(pl.multiple_of(row, 8), 8), :]
                return tall[:, :LANES], tall[:, LANES:]

            def store(k, values, target_ref=target_ref):
                target_ref[slot, pl.ds(k, 8, stride=STRIDE), :] = values

            to_flat(load, store)

    whole = jnp.broadcast_to(jnp.sum(total, keepdims=True), (SLOTS, LANES))[:, :width - count]
    send_columns(planes_ref, slots, table_y_ref[...], table_z_ref[...], low_ref, high_ref)
    core_rows = SIDE // 2
    first_row = core * core_rows
    for device in range(devices):
        pieces = column_pieces(device * count, count)
        kept_ref[device] = chunk_of(low_ref, high_ref, first_row, pieces, whole)
        sent_ref[device] = chunk_of(low_ref, high_ref, core_rows - first_row, pieces, whole)


def wave_squared(index, count_cells):
    folded = jnp.where(2 * index <= count_cells, index, index - count_cells)
    wave_number = folded.astype(jnp.float32) * (two_pi / count_cells)
    return wave_number * wave_number


def coulomb_kernel(count, length_cells, start_ref, charge_ref, ions_ref, table_ref, out_ref):
    domains, _, width = ions_ref.shape
    states = charge_ref.shape[0] // domains
    device = (lax.axis_index("core") * states + lax.axis_index("row")) * domains + lax.axis_index("domain")
    charge = charge_ref[:domains]
    for state in range(1, states):
        charge = charge + charge_ref[state * domains:(state + 1) * domains]
    charge = charge.reshape(domains * SLOTS, width)
    ions = ions_ref[...].reshape(domains * SLOTS, width)
    first = lax.broadcasted_iota(jnp.int32, (domains * SLOTS, width), 0) % SLOTS == 0
    lane = lax.broadcasted_iota(jnp.int32, (domains * SLOTS, width), 1)
    chosen = first & (lane == count)
    electrons = jnp.sum(jnp.where(chosen, charge, 0.0), keepdims=True)
    ionic = jnp.sum(jnp.where(chosen, ions, 0.0), keepdims=True)
    charge = charge - (electrons / ionic) * ions
    layer = lax.broadcasted_iota(jnp.int32, (length_cells, domains * SLOTS), 0)
    place = lax.broadcasted_iota(jnp.int32, (length_cells, domains * SLOTS), 1)
    chosen_layer = jnp.full(layer.shape, -1, jnp.int32)
    for domain in range(domains):
        slot = place - domain * SLOTS
        here = (slot >= 0) & (slot < start_ref[domain + 1] - start_ref[domain])
        chosen_layer = jnp.where(here, start_ref[domain] + slot, chosen_layer)
    pick = (layer == chosen_layer).astype(jnp.float32)
    table = jnp.dot(table_ref[...], pick, precision=highest, preferred_element_type=jnp.float32)
    waves = jnp.dot(table, charge, precision=highest, preferred_element_type=jnp.float32)
    wave_x = lax.broadcasted_iota(jnp.int32, waves.shape, 0)
    column = device * count + lax.broadcasted_iota(jnp.int32, waves.shape, 1)
    wave_y = ((column.astype(jnp.float32) + 0.5) * (1.0 / SIDE)).astype(jnp.int32)
    wave_z = column - wave_y * SIDE
    squared = (
        wave_squared(wave_x, length_cells) + wave_squared(wave_y, SIDE) + wave_squared(wave_z, SIDE)
    )
    gain = jnp.where(squared > 0, four_pi / jnp.where(squared > 0, squared, 1.0), 0.0)
    waves = waves * (gain * (1.0 / (length_cells * SIDE * SIDE)))
    back = lax.dot_general(
        table, waves, (((0,), (0,)), ((), ())), precision=highest, preferred_element_type=jnp.float32
    )
    back = back.reshape(domains, SLOTS, width)
    for state in range(states):
        out_ref[state * domains:(state + 1) * domains] = back


def field_kernel(count, length_cells, start_ref, waves_ref, others_ref, density_ref, other_ref,
                 circle_ref, table_y_ref, table_z_ref, out_ref, low_ref, high_ref, planes_ref, flat_ref):
    _, own_start, thickness = place_of(start_ref)
    devices = waves_ref.shape[0]
    slots = out_ref.shape[0]
    core = lax.axis_index("core")
    core_rows = SIDE // 2
    first_row = core * core_rows
    for source_ref, first in ((waves_ref, first_row), (others_ref, core_rows - first_row)):
        pieces = []
        for device in range(devices):
            column = 0
            for row, start, stop in column_pieces(device * count, count):
                values = source_ref[device, :, column:column + stop - start]
                column += stop - start
                if start > 0:
                    pieces.append(values)
                    values = jnp.concatenate(pieces, axis=1)
                if stop < SIDE:
                    pieces = [values]
                    continue
                pieces = []
                at = pl.ds(first + row, SLOTS, stride=SIDE)
                low_ref[at, :] = values[:, :LANES]
                high_ref[at, :] = jnp.concatenate(
                    [values[:, LANES:], jnp.zeros((SLOTS, WIDTH - SIDE), jnp.float32)], axis=1
                )
    table_y = table_y_ref[...]
    table_z = table_z_ref[...]
    used = slice(0, slots * SIDE)
    along_z = turn_z(jnp.concatenate([low_ref[used, :], high_ref[used, :]], axis=1), table_z)
    for slot in range(slots):
        rows = slice(slot * SIDE, (slot + 1) * SIDE)
        planes_ref[rows, :] = turn_y(table_y, along_z[rows])

    @pl.loop(0, slots)
    def _(slot):
        def load(tile):
            tall = planes_ref[pl.ds(pl.multiple_of(slot * SIDE + tile * 8, 8), 8), :]
            return tall[:, :LANES], tall[:, LANES:]

        def store(k, values):
            flat_ref[pl.ds(slot * FLAT + k, 8, stride=STRIDE), :] = values

        to_flat(load, store)
        rows = pl.ds(pl.multiple_of(slot * FLAT, 8), FLAT)
        here = slot // (SLOTS // 2) == core
        kept_slot = slot % (SLOTS // 2)
        content = jnp.where(here, density_ref[kept_slot], other_ref[kept_slot]) * (3.0 / math.pi)
        positive = jnp.where(content > 0, content, 1.0)
        root = jnp.exp(jnp.log(positive) * (1.0 / 3.0))
        root = root - (root - positive / (root * root)) * (1.0 / 3.0)
        root = jnp.where(content > 0, root, 0.0)
        inside = mesh_points(own_start + slot, circle_ref[...], length_cells) & (slot < thickness)
        flat_ref[rows, :] = jnp.where(inside, flat_ref[rows, :] - root, 0.0)

    @pl.loop(0, FLAT // 8)
    def _(step):
        for part in range(8):
            lanes = pl.ds(pl.multiple_of((step * 8 + part) * LANES, LANES), LANES)
            out_ref[:, lanes] = flat_ref[pl.ds(step * 8 + part, SLOTS, stride=FLAT), :][:slots]


def from_behind(value, steps):
    count = lax.axis_size("domain")
    leading, last = (max(0, -steps), min(count, count - steps))
    return lax.ppermute(value, "domain", [(source, source + steps) for source in range(leading, last)])


def swapped(value, axis):
    return lax.ppermute(value, axis, [(0, 1), (1, 0)])


def shards(orbitals, occupation, potential, background, layer_start):
    domains = lax.axis_size("domain")
    rows = lax.axis_size("row")
    devices = domains * rows
    length_cells = SLAB * domains
    layer_cap, plane = potential.shape
    count = plane // (2 * devices)
    width = -(-(count + 1) // LANES) * LANES
    circle = jnp.asarray(circle_plane())
    flat_circle = jnp.asarray(circle_table().reshape(FLAT, LANES))
    table_z, into_y, out_of_y = (jnp.asarray(table) for table in tables_of_side())
    table_x = jnp.asarray(hartley_table(length_cells).astype(np.float32))
    params = pltpu.CompilerParams(vmem_limit_bytes=VMEM_BYTES)

    def f32(*shape):
        return jax.ShapeDtypeStruct(shape, jnp.float32)

    def scratch(*shape):
        return pltpu.VMEM(shape, jnp.float32)

    layers = orbitals.reshape(2, layer_cap, FLAT, LANES)
    v_rows, real_up, real_down, imag_up, imag_down, up_far, down_far = pl.pallas_call(
        pack_kernel,
        out_shape=tuple(f32(size, FLAT, LANES) for size in (HALO - 1, HALO, HALO, HALO, HALO, 2, 2)),
        in_specs=[SMEM_SPEC, VMEM_SPEC, ANY_SPEC],
        out_specs=(VMEM_SPEC,) * 7,
        scratch_shapes=[scratch(FLAT * 8, LANES), pltpu.SemaphoreType.DMA((8,))],
        compiler_params=params,
        name="pack_halo",
    )(layer_start, potential, layers)
    real_below = from_behind(real_up, 1)
    real_above = from_behind(real_down, -1)
    v_rows = lax.ppermute(
        v_rows,
        ("core", "domain"),
        [(source, source + 1) for source in range(domains - 1)]
        + [(domains + source + 1, domains + source) for source in range(domains - 1)],
    )
    below_far = from_behind(up_far, 2)
    above_far = from_behind(down_far, -2)
    v_rows, below_far, above_far = lax.optimization_barrier((v_rows, below_far, above_far))
    v_others = swapped(v_rows, "core")
    imag_below = from_behind(imag_up, 1)
    imag_above = from_behind(imag_down, -1)

    ions = pl.pallas_call(
        functools.partial(ions_kernel, count, length_cells),
        out_shape=f32(domains, SLOTS, width),
        in_specs=[SMEM_SPEC] + [VMEM_SPEC] * 4,
        out_specs=VMEM_SPEC,
        scratch_shapes=[
            scratch(SLOTS * FLAT, LANES),
            scratch(layer_cap * SIDE, WIDTH),
            scratch(SLOTS * SIDE, LANES),
            scratch(SLOTS * SIDE, LANES),
        ],
        compiler_params=params,
        name="ion_waves",
    )(layer_start, background, circle, into_y, table_z)
    ions, real_below = lax.optimization_barrier((ions, real_below))
    ions = lax.all_to_all(ions, "domain", split_axis=0, concat_axis=0, tiled=True)

    span = layer_cap + 2 * HALO
    fields = [scratch(span, TALL, WIDTH)] * TERMS
    even, odd, centre = pl.pallas_call(
        functools.partial(real_kernel, length_cells),
        out_shape=(
            f32(layer_cap, SIDE, WIDTH),
            f32(layer_cap, SIDE, WIDTH),
            f32(span, SIDE, WIDTH),
        ),
        in_specs=[SMEM_SPEC] + [VMEM_SPEC] * 9,
        out_specs=(VMEM_SPEC,) * 3,
        scratch_shapes=fields + [scratch(span, SIDE, WIDTH), scratch(SLOTS * FLAT, LANES)],
        compiler_params=params,
        name="propagate_real",
    )(layer_start, layers, potential, real_below, real_above, below_far, above_far, v_rows, v_others, circle)
    ions, imag_below = lax.optimization_barrier((ions, imag_below))
    orbitals_next, density_kept, density_sent, kept, sent = pl.pallas_call(
        functools.partial(propagate_kernel, count, length_cells),
        out_shape=(
            f32(2, layer_cap, FLAT, LANES),
            f32(SLOTS // 2, FLAT, LANES),
            f32(SLOTS // 2, FLAT, LANES),
            f32(devices, SLOTS, width),
            f32(devices, SLOTS, width),
        ),
        in_specs=[SMEM_SPEC, SMEM_SPEC] + [VMEM_SPEC] * 11,
        out_specs=(VMEM_SPEC,) * 5,
        scratch_shapes=fields
        + [
            scratch(2, SIDE, WIDTH),
            scratch(span, SIDE, WIDTH),
            scratch(SLOTS * SIDE, WIDTH),
            scratch(SLOTS * SIDE, LANES),
            scratch(SLOTS * SIDE, LANES),
        ],
        compiler_params=params,
        name="propagate",
    )(layer_start, occupation, layers, imag_below, imag_above, below_far, above_far, even, odd, centre,
      circle, into_y, table_z)
    waves = kept + swapped(sent, "core")
    density = density_kept + swapped(density_sent, "core")
    waves, density = lax.optimization_barrier((waves, density))
    waves = lax.all_to_all(waves, ("row", "domain"), split_axis=0, concat_axis=0, tiled=True)
    other_density = swapped(density, "row")
    waves = pl.pallas_call(
        functools.partial(coulomb_kernel, count, length_cells),
        out_shape=f32(devices, SLOTS, width),
        in_specs=[SMEM_SPEC] + [VMEM_SPEC] * 3,
        out_specs=VMEM_SPEC,
        compiler_params=params,
        name="coulomb",
    )(layer_start, waves, ions, table_x)
    waves, other_density = lax.optimization_barrier((waves, other_density))
    density = density + other_density
    other_density = swapped(density, "core")
    waves = lax.all_to_all(waves, ("row", "domain"), split_axis=0, concat_axis=0, tiled=True)
    other_waves = swapped(waves, "core")
    potential_next = pl.pallas_call(
        functools.partial(field_kernel, count, length_cells),
        out_shape=f32(layer_cap, plane),
        in_specs=[SMEM_SPEC] + [VMEM_SPEC] * 7,
        out_specs=VMEM_SPEC,
        scratch_shapes=[
            scratch(SLOTS * SIDE, LANES),
            scratch(SLOTS * SIDE, LANES),
            scratch(layer_cap * SIDE, WIDTH),
            scratch(SLOTS * FLAT, LANES),
        ],
        compiler_params=params,
        name="field",
    )(layer_start, waves, other_waves, density, other_density, flat_circle, out_of_y, table_z)
    return orbitals_next.reshape(orbitals.shape), potential_next


def solution(mesh):
    domains = mesh.shape["domain"]
    split = Mesh(mesh.devices.reshape(-1, 2, domains), ("row", "core", "domain"))
    states = ("row", "core")
    return jax.shard_map(
        shards,
        mesh=split,
        in_specs=(
            P(None, states, "domain", None),
            P(states),
            P("domain", None),
            P("domain", None),
            P(),
        ),
        out_specs=(P(None, states, "domain", None), P("domain", None)),
        check_vma=False,
    )
```

```python
import functools
import math

import jax
import jax.numpy as jnp
import ml_dtypes
import numpy as np
from jax import lax
from jax.experimental import pallas as pl
from jax.experimental.pallas import tpu as pltpu
from jax.sharding import Mesh, PartitionSpec as P

SIDE = 160
SLAB = 5
TERMS = 4

HALO = TERMS
LANES = 128
SLOTS = 8
RUN = SIDE // 8
FLAT = SIDE * SIDE // LANES
STRIDE = FLAT // 8
WIDTH = 2 * LANES
BLOCK = 32
TALL = SIDE + 16

time_step = 0.3
four_pi = 4.0 * math.pi
two_pi = 2.0 * math.pi
highest = lax.Precision.HIGHEST
VMEM_BYTES = 56 * 1024 * 1024
SMEM_SPEC = pl.BlockSpec(memory_space=pltpu.SMEM)
VMEM_SPEC = pl.BlockSpec(memory_space=pltpu.VMEM)
ANY_SPEC = pl.BlockSpec(memory_space=pl.ANY)


def hartley_table(count_cells):
    index_run = np.arange(count_cells)
    angles = (index_run[:, None] * index_run[None, :] % count_cells) * (2.0 * np.pi / count_cells)
    return np.cos(angles) + np.sin(angles)


def plane_order():
    rows = np.arange(SIDE)
    return RUN * (rows % 8) + rows // 8


def two_parts(table):
    table = table.astype(np.float32)
    high = table.astype(ml_dtypes.bfloat16)
    low = (table - high.astype(np.float32)).astype(ml_dtypes.bfloat16)
    return high, low


def tables_of_side():
    table = hartley_table(SIDE)
    along_z = np.zeros((WIDTH, WIDTH))
    along_z[:SIDE, :SIDE] = table
    high, low = two_parts(along_z)
    along_z = np.concatenate([high, high, low], axis=0)
    high, low = two_parts(table[:, plane_order()])
    into_y = np.concatenate([high, high, low], axis=1)
    high, low = two_parts(table[plane_order(), :])
    out_of_y = np.concatenate([high, high, low], axis=1)
    return along_z, into_y, out_of_y


def circle_table():
    across = 2 * np.arange(SIDE, dtype=np.int64) - (SIDE - 1)
    return (across[:, None] ** 2 + across[None, :] ** 2).astype(np.int32)


def circle_plane():
    table = np.full((SIDE, WIDTH), 4 * SIDE * SIDE, np.int32)
    table[:, :SIDE] = circle_table()[plane_order()]
    return table


def mesh_points(x_row, circle, length_cells):
    room = ((length_cells - 2) ** 2 - (2 * x_row - (length_cells - 1)) ** 2) * (SIDE - 2) ** 2
    return (circle * (length_cells - 2) ** 2 <= room) & (circle < 4 * SIDE * SIDE)


def column_pieces(first, count):
    pieces = []
    column = first
    while column < first + count:
        row = column // SIDE
        stop = min((row + 1) * SIDE, first + count)
        pieces.append((row, column - row * SIDE, stop - row * SIDE))
        column = stop
    return pieces


def eight(values):
    missing = jnp.zeros((SLOTS - values.shape[0], values.shape[1]), values.dtype)
    return jnp.concatenate([values, missing], axis=0)


def to_plane(load, store):
    lane = lax.broadcasted_iota(jnp.int32, (8, LANES), 1)
    for step in range(RUN // 4):
        rows = [load(5 * step + part) for part in range(5)]
        store(4 * step, rows[0], rows[1])
        for part in range(1, 4):
            left = pltpu.roll(rows[part], LANES - 32 * part, 1)
            right = pltpu.roll(rows[part + 1], LANES - 32 * part, 1)
            store(4 * step + part, jnp.where(lane < LANES - 32 * part, left, right), right)


def to_flat(load, store):
    lane = lax.broadcasted_iota(jnp.int32, (8, LANES), 1)
    for step in range(RUN // 4):
        turned = []
        for part in range(4):
            low, high = load(4 * step + part)
            if part:
                low = pltpu.roll(low, 32 * part, 1)
                high = pltpu.roll(high, 32 * part, 1)
            turned.append((low, high))
        store(5 * step, turned[0][0])
        for part in range(1, 4):
            ended = 32 * (part - 1)
            values = jnp.where(lane < ended + 32, turned[part - 1][1], turned[part][0])
            if ended:
                values = jnp.where(lane < ended, turned[part - 1][0], values)
            store(5 * step + part, values)
        store(5 * step + 4, jnp.where(lane < 96, turned[3][0], turned[3][1]))


def parts_of(values):
    high = values.astype(jnp.bfloat16)
    low = (values - high.astype(jnp.float32)).astype(jnp.bfloat16)
    return high, low


def turn_z(values, table):
    high, low = parts_of(values)
    return jnp.dot(
        jnp.concatenate([high, low, high], axis=1), table, preferred_element_type=jnp.float32
    )


def turn_y(table, values):
    high, low = parts_of(values)
    return jnp.dot(
        table, jnp.concatenate([high, low, high], axis=0), preferred_element_type=jnp.float32
    )


def send_columns(planes_ref, slots, table_y, table_z, low_ref, high_ref):
    along_z = turn_z(planes_ref[:slots * SIDE, :], table_z)
    for slot in range(slots):
        rows = slice(slot * SIDE, (slot + 1) * SIDE)
        waves = turn_y(table_y, along_z[rows])
        low_ref[rows, :] = waves[:, :LANES]
        high_ref[rows, :] = waves[:, LANES:]
    low_ref[slots * SIDE:, :] = jnp.zeros(((SLOTS - slots) * SIDE, LANES), jnp.float32)
    high_ref[slots * SIDE:, :] = jnp.zeros(((SLOTS - slots) * SIDE, LANES), jnp.float32)


def chunk_of(low_ref, high_ref, first_row, pieces, extra):
    parts = []
    for row, start, stop in pieces:
        at = pl.ds(first_row + row, SLOTS, stride=SIDE)
        values = jnp.concatenate([low_ref[at, :], high_ref[at, :]], axis=1)
        parts.append(values[:, start:stop])
    return jnp.concatenate(parts + [extra], axis=1)


def layers_of(stored_ref, flat_ref):
    @pl.loop(0, FLAT // 8)
    def _(step):
        for part in range(8):
            lanes = pl.ds(pl.multiple_of((step * 8 + part) * LANES, LANES), LANES)
            flat_ref[pl.ds(step * 8 + part, SLOTS, stride=FLAT), :] = eight(stored_ref[:, lanes])


def place_of(start_ref):
    position = lax.axis_index("domain")
    return position, start_ref[position], start_ref[position + 1] - start_ref[position]


def pack_kernel(start_ref, potential_ref, orbitals_ref, v_ref, real_up_ref, real_down_ref, imag_up_ref,
                imag_down_ref, up_far_ref, down_far_ref, tile_ref, sems):
    _, _, thickness = place_of(start_ref)
    v_first = jnp.where(lax.axis_index("core") == 0, thickness - (HALO - 1), 0)
    first = jnp.maximum(thickness - HALO, 0)
    copies = []

    def copy(source, target):
        made = pltpu.make_async_copy(source, target, sems.at[len(copies)])
        made.start()
        copies.append(made)

    for part, up_ref, down_ref in ((0, real_up_ref, real_down_ref), (1, imag_up_ref, imag_down_ref)):
        copy(orbitals_ref.at[part, pl.ds(first, HALO)], up_ref)
        copy(orbitals_ref.at[part, pl.ds(0, HALO)], down_ref)
        copy(orbitals_ref.at[part, pl.ds(thickness - 1, 1)], up_far_ref.at[pl.ds(part, 1)])
        copy(orbitals_ref.at[part, pl.ds(0, 1)], down_far_ref.at[pl.ds(part, 1)])

    @pl.loop(0, FLAT // 8)
    def _(step):
        for part in range(8):
            tile = step * 8 + part
            lanes = pl.ds(pl.multiple_of(tile * LANES, LANES), LANES)
            rows = pl.ds(pl.multiple_of(tile * 8, 8), 8)
            tile_ref[rows, :] = eight(potential_ref[:, lanes])

    @pl.loop(0, FLAT // 8)
    def _(step):
        rows = pl.ds(pl.multiple_of(step * 8, 8), 8)
        for layer in range(HALO - 1):
            v_ref[layer, rows, :] = tile_ref[pl.ds(step * 64 + v_first + layer, 8, stride=8), :]

    for made in copies:
        made.wait()


def ions_kernel(count, length_cells, start_ref, background_ref, circle_ref, table_y_ref, table_z_ref,
                out_ref, flat_ref, planes_ref, low_ref, high_ref):
    _, own_start, thickness = place_of(start_ref)
    slots = background_ref.shape[0]
    groups, _, width = out_ref.shape
    layers_of(background_ref, flat_ref)

    def body(slot, total):
        def store(tile, low, high):
            rows = pl.ds(pl.multiple_of(slot * SIDE + tile * 8, 8), 8)
            planes_ref[rows, :LANES] = low
            planes_ref[rows, LANES:] = high

        to_plane(lambda k: flat_ref[pl.ds(slot * FLAT + k, 8, stride=STRIDE), :], store)
        rows = pl.ds(pl.multiple_of(slot * SIDE, 8), SIDE)
        inside = mesh_points(own_start + slot, circle_ref[...], length_cells) & (slot < thickness)
        values = jnp.where(inside, planes_ref[rows, :], 0.0)
        planes_ref[rows, :] = values
        return total + jnp.sum(values.reshape(RUN, 8, WIDTH), axis=0)

    total = lax.fori_loop(0, slots, body, jnp.zeros((8, WIDTH), jnp.float32))
    whole = jnp.broadcast_to(jnp.sum(total, keepdims=True), (SLOTS, LANES))[:, :width - count]
    send_columns(planes_ref, slots, table_y_ref[...], table_z_ref[...], low_ref, high_ref)
    core_rows = SIDE // lax.axis_size("core")
    first_row = lax.axis_index("core") * core_rows + lax.axis_index("row") * (core_rows // lax.axis_size("row"))
    for group in range(groups):
        out_ref[group] = chunk_of(low_ref, high_ref, first_row, column_pieces(group * count, count), whole)


def rows_from(ref, *at):
    return lambda k: ref[(*at, pl.ds(k, 8, stride=STRIDE), slice(None))]


def plane_at(ref, x_row, skip):
    def store(tile, low, high):
        ref[x_row, skip + 8 * tile:skip + 8 * tile + 8, :LANES] = low
        ref[x_row, skip + 8 * tile:skip + 8 * tile + 8, LANES:] = high

    return store


class Chain:
    def __init__(self, length_cells, start_ref, circle_ref, field_refs, centre_ref, beside_ref):
        position, self.own_start, self.thickness = place_of(start_ref)
        domains = lax.axis_size("domain")
        before = start_ref[jnp.maximum(position - 1, 0)]
        after = start_ref[jnp.minimum(position + 2, domains)]
        self.short_below = (position > 0) & (self.own_start - before < HALO)
        self.short_above = (position < domains - 1) & (after - self.own_start - self.thickness < HALO)
        self.length_cells = length_cells
        self.circle_ref = circle_ref
        self.field_refs = field_refs
        self.centre_ref = centre_ref
        self.beside_ref = beside_ref
        self.layers = field_refs[0].shape[0]

    def fill(self, own_copy, own_ref, below_ref, above_ref):
        field_ref = self.field_refs[0]
        short_below = self.short_below.astype(jnp.int32)
        upper = HALO + self.thickness

        @pl.loop(0, HALO - 1)
        def _(layer):
            to_plane(rows_from(below_ref, 1 + layer - short_below), plane_at(field_ref, 1 + layer, 8))
            to_plane(rows_from(above_ref, layer), plane_at(field_ref, upper + layer, 8))

        for short, near_ref, near, x_row in (
            (self.short_below, below_ref, 0, 0),
            (self.short_above, above_ref, HALO - 1, upper + HALO - 1),
        ):

            @pl.when(short)
            def _(x_row=x_row):
                field_ref[x_row] = jnp.zeros((TALL, WIDTH), jnp.float32)

            @pl.when(jnp.logical_not(short))
            def _(near_ref=near_ref, near=near, x_row=x_row):
                to_plane(rows_from(near_ref, near), plane_at(field_ref, x_row, 8))

        own_copy.wait()

        @pl.loop(0, self.thickness)
        def _(slot):
            to_plane(rows_from(own_ref, slot), plane_at(field_ref, HALO + slot, 8))

    def add_far(self, below_far_ref, above_far_ref, spare_ref, target_refs):
        edge_above = HALO + self.thickness - 1
        for short, far_ref, edge, step in (
            (self.short_below, below_far_ref, HALO, -1),
            (self.short_above, above_far_ref, edge_above, 1),
        ):

            @pl.when(short)
            def _(far_ref=far_ref, edge=edge, step=step):
                for part in range(2):
                    to_plane(rows_from(far_ref, part), plane_at(spare_ref, part, 0))
                for block in range(SIDE // BLOCK):
                    rows = slice(block * BLOCK, (block + 1) * BLOCK)
                    inner = slice(8 + block * BLOCK, 8 + (block + 1) * BLOCK)
                    gain = self.beside_ref[edge, rows, :] * (1.0 / 24.0)
                    for hop in range(1, HALO):
                        gain = gain * self.beside_ref[edge + hop * step, rows, :]
                    inside = self.beside_ref[edge + HALO * step, rows, :] > 0
                    for part, target_ref in enumerate(target_refs):
                        far = jnp.where(inside, spare_ref[part, rows, :], 0.0)
                        target_ref[edge, inner, :] = target_ref[edge, inner, :] + gain * far

    def wrap(self, term, x_row):
        field_ref = self.field_refs[term]
        first = field_ref[x_row, 8:16, :]
        final = field_ref[x_row, SIDE:SIDE + 8, :]
        field_ref[x_row, :8, :] = pltpu.roll(final, 1, 0)
        field_ref[x_row, SIDE + 8:, :] = pltpu.roll(first, 7, 0)

    def confine(self, make_centre):
        field_ref = self.field_refs[0]

        @pl.loop(0, self.layers)
        def _(x_row):
            known = x_row < self.thickness + 2 * HALO
            for block in range(SIDE // BLOCK):
                rows = slice(block * BLOCK, (block + 1) * BLOCK)
                inner = slice(8 + block * BLOCK, 8 + (block + 1) * BLOCK)
                inside = known & mesh_points(
                    self.own_start - HALO + x_row, self.circle_ref[rows, :], self.length_cells
                )
                if make_centre:
                    self.centre_ref[x_row, rows, :] = jnp.where(
                        inside, (3.0 + self.centre_ref[x_row, rows, :]) * time_step, 0.0
                    )
                self.beside_ref[x_row, rows, :] = jnp.where(inside, 0.5 * time_step, 0.0)
                field_ref[x_row, inner, :] = jnp.where(inside, field_ref[x_row, inner, :], 0.0)
            self.wrap(0, x_row)

    def hamilton(self, term, x_row, block):
        field_ref = self.field_refs[term]
        rows = slice(block * BLOCK, (block + 1) * BLOCK)
        inner = slice(8 + block * BLOCK, 8 + (block + 1) * BLOCK)
        tall = field_ref[x_row, block * BLOCK:block * BLOCK + BLOCK + 16, :]
        field = tall[8:8 + BLOCK]
        around = field_ref[x_row - 1, inner, :] + field_ref[x_row + 1, inner, :]
        around = around + (tall[:BLOCK] + tall[16:])
        around = around + (pltpu.roll(field, 1, 1) + pltpu.roll(field, WIDTH - 1, 1))
        return self.centre_ref[x_row, rows, :] * field - self.beside_ref[x_row, rows, :] * around

    def steps(self):
        for term in range(1, TERMS):

            @pl.loop(term, self.layers - term)
            def _(x_row, term=term):
                for block in range(SIDE // BLOCK):
                    inner = slice(8 + block * BLOCK, 8 + (block + 1) * BLOCK)
                    self.field_refs[term][x_row, inner, :] = self.hamilton(term - 1, x_row, block)
                self.wrap(term, x_row)

    def sums(self, x_row, block):
        inner = slice(8 + block * BLOCK, 8 + (block + 1) * BLOCK)
        terms = [ref[x_row, inner, :] for ref in self.field_refs]
        even = terms[0] - (1.0 / 2.0) * terms[2] + (1.0 / 24.0) * self.hamilton(TERMS - 1, x_row, block)
        return even, terms[1] - (1.0 / 6.0) * terms[3]


def real_kernel(length_cells, start_ref, orbitals_ref, potential_ref, below_ref, above_ref, v_ref, v_other_ref,
                circle_ref, even_ref, odd_ref, centre_ref, first_ref,
                second_ref, third_ref, fourth_ref, beside_ref, own_ref, sem, flat_ref):
    own_copy = pltpu.make_async_copy(orbitals_ref.at[0], own_ref, sem)
    own_copy.start()
    field_refs = (first_ref, second_ref, third_ref, fourth_ref)
    chain = Chain(length_cells, start_ref, circle_ref, field_refs, centre_ref, beside_ref)
    slots = orbitals_ref.shape[1]
    core = lax.axis_index("core")
    layers_of(potential_ref, flat_ref)

    @pl.loop(0, slots)
    def _(slot):
        to_plane(
            lambda k: flat_ref[pl.ds(slot * FLAT + k, 8, stride=STRIDE), :],
            plane_at(centre_ref, HALO + slot, 0),
        )

    @pl.loop(0, HALO - 1)
    def _(layer):
        lower = 1 + layer
        upper = HALO + chain.thickness + layer
        to_plane(rows_from(v_ref, layer), plane_at(centre_ref, jnp.where(core == 0, lower, upper), 0))
        to_plane(rows_from(v_other_ref, layer), plane_at(centre_ref, jnp.where(core == 0, upper, lower), 0))

    chain.fill(own_copy, own_ref, below_ref, above_ref)
    chain.confine(True)
    chain.steps()

    @pl.loop(0, slots)
    def _(slot):
        for block in range(SIDE // BLOCK):
            rows = slice(block * BLOCK, (block + 1) * BLOCK)
            even_ref[slot, rows, :], odd_ref[slot, rows, :] = chain.sums(HALO + slot, block)


def propagate_kernel(count, length_cells, start_ref, weight_ref, orbitals_ref, below_ref, above_ref,
                     below_far_ref, above_far_ref, even_ref, odd_ref, centre_ref, circle_ref, table_y_ref,
                     table_z_ref, psi_ref, kept_ref, sent_ref, first_ref, second_ref, third_ref,
                     fourth_ref, beside_ref, own_ref, sem, spare_ref, planes_ref, low_ref, high_ref):
    own_copy = pltpu.make_async_copy(orbitals_ref.at[1], own_ref, sem)
    own_copy.start()
    field_refs = (first_ref, second_ref, third_ref, fourth_ref)
    chain = Chain(length_cells, start_ref, circle_ref, field_refs, centre_ref, beside_ref)
    weight = weight_ref[0]
    core = lax.axis_index("core")
    slots = orbitals_ref.shape[1]
    devices, _, width = kept_ref.shape
    chain.fill(own_copy, own_ref, below_ref, above_ref)
    chain.confine(False)
    chain.steps()
    chain.add_far(below_far_ref, above_far_ref, spare_ref, (second_ref, first_ref))

    def finish(slot, total):
        owned = slot < chain.thickness
        for block in range(SIDE // BLOCK):
            rows = slice(block * BLOCK, (block + 1) * BLOCK)
            even, odd = chain.sums(HALO + slot, block)
            real = jnp.where(owned, even_ref[slot, rows, :] + odd, 0.0)
            imag = jnp.where(owned, even - odd_ref[slot, rows, :], 0.0)
            psi_ref[0, slot, rows, :] = real
            psi_ref[1, slot, rows, :] = imag
            density = weight * (real * real + imag * imag)
            planes_ref[pl.ds(pl.multiple_of(slot * SIDE + block * BLOCK, 8), BLOCK), :] = density
            total = total + jnp.sum(density.reshape(BLOCK // 8, 8, WIDTH), axis=0)
        return total

    total = lax.fori_loop(0, slots, finish, jnp.zeros((8, WIDTH), jnp.float32))
    whole = jnp.broadcast_to(jnp.sum(total, keepdims=True), (SLOTS, LANES))[:, :width - count]
    send_columns(planes_ref, slots, table_y_ref[...], table_z_ref[...], low_ref, high_ref)
    core_rows = SIDE // 2
    first_row = core * core_rows
    for device in range(devices):
        pieces = column_pieces(device * count, count)
        kept_ref[device] = chunk_of(low_ref, high_ref, first_row, pieces, whole)
        sent_ref[device] = chunk_of(low_ref, high_ref, core_rows - first_row, pieces, whole)


def unpack_kernel(weight_ref, psi_ref, next_ref, density_kept_ref, density_sent_ref, density_ref):
    core = lax.axis_index("core")
    weight = weight_ref[0]
    slots = psi_ref.shape[1]

    @pl.loop(0, slots)
    def _(slot):
        for part in range(2):

            def load(tile, part=part):
                tall = psi_ref[part, slot, 8 * tile:8 * tile + 8, :]
                return tall[:, :LANES], tall[:, LANES:]

            def store(k, values, part=part):
                next_ref[part, slot, pl.ds(k, 8, stride=STRIDE), :] = values

            to_flat(load, store)
        real = next_ref[0, slot]
        imag = next_ref[1, slot]
        density_ref[slot] = weight * (real * real + imag * imag)

    for slot in range(slots, SLOTS):
        density_ref[slot] = jnp.zeros((FLAT, LANES), jnp.float32)

    @pl.loop(0, SLOTS // 2)
    def _(slot):
        density_kept_ref[slot] = density_ref[core * (SLOTS // 2) + slot]
        density_sent_ref[slot] = density_ref[(1 - core) * (SLOTS // 2) + slot]


def wave_squared(index, count_cells):
    folded = jnp.where(2 * index <= count_cells, index, index - count_cells)
    wave_number = folded.astype(jnp.float32) * (two_pi / count_cells)
    return wave_number * wave_number


def coulomb_kernel(count, length_cells, start_ref, charge_ref, ions_ref, table_ref, out_ref):
    domains, _, width = ions_ref.shape
    states = charge_ref.shape[0] // domains
    device = (lax.axis_index("core") * states + lax.axis_index("row")) * domains + lax.axis_index("domain")
    charge = charge_ref[:domains]
    for state in range(1, states):
        charge = charge + charge_ref[state * domains:(state + 1) * domains]
    charge = charge.reshape(domains * SLOTS, width)
    ions = ions_ref[...].reshape(domains * SLOTS, width)
    first = lax.broadcasted_iota(jnp.int32, (domains * SLOTS, width), 0) % SLOTS == 0
    lane = lax.broadcasted_iota(jnp.int32, (domains * SLOTS, width), 1)
    chosen = first & (lane == count)
    electrons = jnp.sum(jnp.where(chosen, charge, 0.0), keepdims=True)
    ionic = jnp.sum(jnp.where(chosen, ions, 0.0), keepdims=True)
    charge = charge - (electrons / ionic) * ions
    layer = lax.broadcasted_iota(jnp.int32, (length_cells, domains * SLOTS), 0)
    place = lax.broadcasted_iota(jnp.int32, (length_cells, domains * SLOTS), 1)
    chosen_layer = jnp.full(layer.shape, -1, jnp.int32)
    for domain in range(domains):
        slot = place - domain * SLOTS
        here = (slot >= 0) & (slot < start_ref[domain + 1] - start_ref[domain])
        chosen_layer = jnp.where(here, start_ref[domain] + slot, chosen_layer)
    pick = (layer == chosen_layer).astype(jnp.float32)
    table = jnp.dot(table_ref[...], pick, precision=highest, preferred_element_type=jnp.float32)
    waves = jnp.dot(table, charge, precision=highest, preferred_element_type=jnp.float32)
    wave_x = lax.broadcasted_iota(jnp.int32, waves.shape, 0)
    column = device * count + lax.broadcasted_iota(jnp.int32, waves.shape, 1)
    wave_y = ((column.astype(jnp.float32) + 0.5) * (1.0 / SIDE)).astype(jnp.int32)
    wave_z = column - wave_y * SIDE
    squared = (
        wave_squared(wave_x, length_cells) + wave_squared(wave_y, SIDE) + wave_squared(wave_z, SIDE)
    )
    gain = jnp.where(squared > 0, four_pi / jnp.where(squared > 0, squared, 1.0), 0.0)
    waves = waves * (gain * (1.0 / (length_cells * SIDE * SIDE)))
    back = lax.dot_general(
        table, waves, (((0,), (0,)), ((), ())), precision=highest, preferred_element_type=jnp.float32
    )
    back = back.reshape(domains, SLOTS, width)
    for state in range(states):
        out_ref[state * domains:(state + 1) * domains] = back


def field_kernel(count, length_cells, start_ref, waves_ref, others_ref, density_ref, other_ref,
                 circle_ref, table_y_ref, table_z_ref, out_ref, low_ref, high_ref, planes_ref, flat_ref):
    _, own_start, thickness = place_of(start_ref)
    devices = waves_ref.shape[0]
    slots = out_ref.shape[0]
    core = lax.axis_index("core")
    core_rows = SIDE // 2
    first_row = core * core_rows
    for source_ref, first in ((waves_ref, first_row), (others_ref, core_rows - first_row)):
        pieces = []
        for device in range(devices):
            column = 0
            for row, start, stop in column_pieces(device * count, count):
                values = source_ref[device, :, column:column + stop - start]
                column += stop - start
                if start > 0:
                    pieces.append(values)
                    values = jnp.concatenate(pieces, axis=1)
                if stop < SIDE:
                    pieces = [values]
                    continue
                pieces = []
                at = pl.ds(first + row, SLOTS, stride=SIDE)
                low_ref[at, :] = values[:, :LANES]
                high_ref[at, :] = jnp.concatenate(
                    [values[:, LANES:], jnp.zeros((SLOTS, WIDTH - SIDE), jnp.float32)], axis=1
                )
    table_y = table_y_ref[...]
    table_z = table_z_ref[...]
    used = slice(0, slots * SIDE)
    along_z = turn_z(jnp.concatenate([low_ref[used, :], high_ref[used, :]], axis=1), table_z)
    for slot in range(slots):
        rows = slice(slot * SIDE, (slot + 1) * SIDE)
        planes_ref[rows, :] = turn_y(table_y, along_z[rows])

    @pl.loop(0, slots)
    def _(slot):
        def load(tile):
            tall = planes_ref[pl.ds(pl.multiple_of(slot * SIDE + tile * 8, 8), 8), :]
            return tall[:, :LANES], tall[:, LANES:]

        def store(k, values):
            flat_ref[pl.ds(slot * FLAT + k, 8, stride=STRIDE), :] = values

        to_flat(load, store)
        rows = pl.ds(pl.multiple_of(slot * FLAT, 8), FLAT)
        here = slot // (SLOTS // 2) == core
        kept_slot = slot % (SLOTS // 2)
        content = jnp.where(here, density_ref[kept_slot], other_ref[kept_slot]) * (3.0 / math.pi)
        positive = jnp.where(content > 0, content, 1.0)
        root = jnp.exp(jnp.log(positive) * (1.0 / 3.0))
        root = root - (root - positive / (root * root)) * (1.0 / 3.0)
        root = jnp.where(content > 0, root, 0.0)
        inside = mesh_points(own_start + slot, circle_ref[...], length_cells) & (slot < thickness)
        flat_ref[rows, :] = jnp.where(inside, flat_ref[rows, :] - root, 0.0)

    @pl.loop(0, FLAT // 8)
    def _(step):
        for part in range(8):
            lanes = pl.ds(pl.multiple_of((step * 8 + part) * LANES, LANES), LANES)
            out_ref[:, lanes] = flat_ref[pl.ds(step * 8 + part, SLOTS, stride=FLAT), :][:slots]


def from_behind(value, steps):
    count = lax.axis_size("domain")
    leading, last = (max(0, -steps), min(count, count - steps))
    return lax.ppermute(value, "domain", [(source, source + steps) for source in range(leading, last)])


def swapped(value, axis):
    return lax.ppermute(value, axis, [(0, 1), (1, 0)])


def shards(orbitals, occupation, potential, background, layer_start):
    domains = lax.axis_size("domain")
    rows = lax.axis_size("row")
    devices = domains * rows
    length_cells = SLAB * domains
    layer_cap, plane = potential.shape
    count = plane // (2 * devices)
    width = -(-(count + 1) // LANES) * LANES
    circle = jnp.asarray(circle_plane())
    flat_circle = jnp.asarray(circle_table().reshape(FLAT, LANES))
    table_z, into_y, out_of_y = (jnp.asarray(table) for table in tables_of_side())
    table_x = jnp.asarray(hartley_table(length_cells).astype(np.float32))
    params = pltpu.CompilerParams(vmem_limit_bytes=VMEM_BYTES)

    def f32(*shape):
        return jax.ShapeDtypeStruct(shape, jnp.float32)

    def scratch(*shape):
        return pltpu.VMEM(shape, jnp.float32)

    def cost(duration):
        return pl.CostEstimate(flops=0, transcendentals=0, bytes_accessed=duration * 3_000_000)

    layers = orbitals.reshape(2, layer_cap, FLAT, LANES)
    v_rows, real_up, real_down, imag_up, imag_down, up_far, down_far = pl.pallas_call(
        pack_kernel,
        out_shape=tuple(f32(size, FLAT, LANES) for size in (HALO - 1, HALO, HALO, HALO, HALO, 2, 2)),
        in_specs=[SMEM_SPEC, VMEM_SPEC, ANY_SPEC],
        out_specs=(VMEM_SPEC,) * 7,
        scratch_shapes=[scratch(FLAT * 8, LANES), pltpu.SemaphoreType.DMA((8,))],
        compiler_params=params,
        cost_estimate=cost(4),
        name="pack_halo",
    )(layer_start, potential, layers)
    real_below = from_behind(real_up, 1)
    real_above = from_behind(real_down, -1)
    v_rows = lax.ppermute(
        v_rows,
        ("core", "domain"),
        [(source, source + 1) for source in range(domains - 1)]
        + [(domains + source + 1, domains + source) for source in range(domains - 1)],
    )
    v_others = swapped(v_rows, "core")
    imag_below = from_behind(imag_up, 1)
    imag_above = from_behind(imag_down, -1)
    below_far = from_behind(up_far, 2)
    above_far = from_behind(down_far, -2)

    ions = pl.pallas_call(
        functools.partial(ions_kernel, count, length_cells),
        out_shape=f32(domains, SLOTS, width),
        in_specs=[SMEM_SPEC] + [VMEM_SPEC] * 4,
        out_specs=VMEM_SPEC,
        scratch_shapes=[
            scratch(SLOTS * FLAT, LANES),
            scratch(layer_cap * SIDE, WIDTH),
            scratch(SLOTS * SIDE, LANES),
            scratch(SLOTS * SIDE, LANES),
        ],
        compiler_params=params,
        cost_estimate=cost(5),
        name="ion_waves",
    )(layer_start, background, circle, into_y, table_z)
    ions, real_below = lax.optimization_barrier((ions, real_below))
    ions = lax.all_to_all(ions, "domain", split_axis=0, concat_axis=0, tiled=True)

    span = layer_cap + 2 * HALO
    chain = [scratch(span, TALL, WIDTH)] * TERMS + [
        scratch(span, SIDE, WIDTH),
        scratch(layer_cap, FLAT, LANES),
        pltpu.SemaphoreType.DMA,
    ]
    even, odd, centre = pl.pallas_call(
        functools.partial(real_kernel, length_cells),
        out_shape=(
            f32(layer_cap, SIDE, WIDTH),
            f32(layer_cap, SIDE, WIDTH),
            f32(span, SIDE, WIDTH),
        ),
        in_specs=[SMEM_SPEC, ANY_SPEC] + [VMEM_SPEC] * 6,
        out_specs=(VMEM_SPEC,) * 3,
        scratch_shapes=chain + [scratch(SLOTS * FLAT, LANES)],
        compiler_params=params,
        cost_estimate=cost(14),
        name="propagate_real",
    )(layer_start, layers, potential, real_below, real_above, v_rows, v_others, circle)
    ions, imag_below = lax.optimization_barrier((ions, imag_below))
    psi, kept, sent = pl.pallas_call(
        functools.partial(propagate_kernel, count, length_cells),
        out_shape=(
            f32(2, layer_cap, SIDE, WIDTH),
            f32(devices, SLOTS, width),
            f32(devices, SLOTS, width),
        ),
        in_specs=[SMEM_SPEC, SMEM_SPEC, ANY_SPEC] + [VMEM_SPEC] * 10,
        out_specs=(VMEM_SPEC,) * 3,
        scratch_shapes=chain
        + [
            scratch(2, SIDE, WIDTH),
            scratch(layer_cap * SIDE, WIDTH),
            scratch(SLOTS * SIDE, LANES),
            scratch(SLOTS * SIDE, LANES),
        ],
        compiler_params=params,
        cost_estimate=cost(15),
        name="propagate",
    )(layer_start, occupation, layers, imag_below, imag_above, below_far, above_far, even, odd, centre,
      circle, into_y, table_z)
    waves = kept + swapped(sent, "core")
    waves = lax.all_to_all(waves, ("row", "domain"), split_axis=0, concat_axis=0, tiled=True)
    orbitals_next, density_kept, density_sent = pl.pallas_call(
        unpack_kernel,
        out_shape=(
            f32(2, layer_cap, FLAT, LANES),
            f32(SLOTS // 2, FLAT, LANES),
            f32(SLOTS // 2, FLAT, LANES),
        ),
        in_specs=[SMEM_SPEC, VMEM_SPEC],
        out_specs=(VMEM_SPEC,) * 3,
        scratch_shapes=[scratch(SLOTS, FLAT, LANES)],
        compiler_params=params,
        cost_estimate=cost(4),
        name="unpack",
    )(occupation, psi)
    density = density_kept + swapped(density_sent, "core")
    other_density = swapped(density, "row")
    waves = pl.pallas_call(
        functools.partial(coulomb_kernel, count, length_cells),
        out_shape=f32(devices, SLOTS, width),
        in_specs=[SMEM_SPEC] + [VMEM_SPEC] * 3,
        out_specs=VMEM_SPEC,
        compiler_params=params,
        cost_estimate=cost(3),
        name="coulomb",
    )(layer_start, waves, ions, table_x)
    waves, other_density = lax.optimization_barrier((waves, other_density))
    density = density + other_density
    other_density = swapped(density, "core")
    waves = lax.all_to_all(waves, ("row", "domain"), split_axis=0, concat_axis=0, tiled=True)
    other_waves = swapped(waves, "core")
    potential_next = pl.pallas_call(
        functools.partial(field_kernel, count, length_cells),
        out_shape=f32(layer_cap, plane),
        in_specs=[SMEM_SPEC] + [VMEM_SPEC] * 7,
        out_specs=VMEM_SPEC,
        scratch_shapes=[
            scratch(SLOTS * SIDE, LANES),
            scratch(SLOTS * SIDE, LANES),
            scratch(layer_cap * SIDE, WIDTH),
            scratch(SLOTS * FLAT, LANES),
        ],
        compiler_params=params,
        cost_estimate=cost(6),
        name="field",
    )(layer_start, waves, other_waves, density, other_density, flat_circle, out_of_y, table_z)
    return orbitals_next.reshape(orbitals.shape), potential_next


def solution(mesh):
    domains = mesh.shape["domain"]
    split = Mesh(mesh.devices.reshape(-1, 2, domains), ("row", "core", "domain"))
    states = ("row", "core")
    return jax.shard_map(
        shards,
        mesh=split,
        in_specs=(
            P(None, states, "domain", None),
            P(states),
            P("domain", None),
            P("domain", None),
            P(),
        ),
        out_specs=(P(None, states, "domain", None), P("domain", None)),
        check_vma=False,
    )
```

```python
import functools
import math

import jax
import jax.numpy as jnp
import ml_dtypes
import numpy as np
from jax import lax
from jax.experimental import pallas as pl
from jax.experimental.pallas import tpu as pltpu
from jax.sharding import Mesh, PartitionSpec as P

SIDE = 160
SLAB = 5
TERMS = 4

HALO = TERMS
LANES = 128
SLOTS = 8
RUN = SIDE // 8
FLAT = SIDE * SIDE // LANES
STRIDE = FLAT // 8
WIDTH = 2 * LANES
BLOCK = 32
TALL = SIDE + 16

time_step = 0.3
four_pi = 4.0 * math.pi
two_pi = 2.0 * math.pi
highest = lax.Precision.HIGHEST
VMEM_BYTES = 56 * 1024 * 1024
SMEM_SPEC = pl.BlockSpec(memory_space=pltpu.SMEM)
VMEM_SPEC = pl.BlockSpec(memory_space=pltpu.VMEM)
ANY_SPEC = pl.BlockSpec(memory_space=pl.ANY)


def hartley_table(count_cells):
    index_run = np.arange(count_cells)
    angles = (index_run[:, None] * index_run[None, :] % count_cells) * (2.0 * np.pi / count_cells)
    return np.cos(angles) + np.sin(angles)


def plane_order():
    rows = np.arange(SIDE)
    return RUN * (rows % 8) + rows // 8


def two_parts(table):
    table = table.astype(np.float32)
    high = table.astype(ml_dtypes.bfloat16)
    low = (table - high.astype(np.float32)).astype(ml_dtypes.bfloat16)
    return high, low


def tables_of_side():
    table = hartley_table(SIDE)
    along_z = np.zeros((WIDTH, WIDTH))
    along_z[:SIDE, :SIDE] = table
    high, low = two_parts(along_z)
    along_z = np.concatenate([high, high, low], axis=0)
    high, low = two_parts(table[:, plane_order()])
    into_y = np.concatenate([high, high, low], axis=1)
    high, low = two_parts(table[plane_order(), :])
    out_of_y = np.concatenate([high, high, low], axis=1)
    return along_z, into_y, out_of_y


def circle_table():
    across = 2 * np.arange(SIDE, dtype=np.int64) - (SIDE - 1)
    return (across[:, None] ** 2 + across[None, :] ** 2).astype(np.int32)


def circle_plane():
    table = np.full((SIDE, WIDTH), 4 * SIDE * SIDE, np.int32)
    table[:, :SIDE] = circle_table()[plane_order()]
    return table


def mesh_points(x_row, circle, length_cells):
    room = ((length_cells - 2) ** 2 - (2 * x_row - (length_cells - 1)) ** 2) * (SIDE - 2) ** 2
    return (circle * (length_cells - 2) ** 2 <= room) & (circle < 4 * SIDE * SIDE)


def column_pieces(first, count):
    pieces = []
    column = first
    while column < first + count:
        row = column // SIDE
        stop = min((row + 1) * SIDE, first + count)
        pieces.append((row, column - row * SIDE, stop - row * SIDE))
        column = stop
    return pieces


def eight(values):
    missing = jnp.zeros((SLOTS - values.shape[0], values.shape[1]), values.dtype)
    return jnp.concatenate([values, missing], axis=0)


def sublane_rows():
    return lax.broadcasted_iota(jnp.int32, (8, LANES), 0)


def by_sublane(pieces):
    row = sublane_rows()
    joined = pieces[0][1]
    for sublane, values in pieces[1:]:
        joined = jnp.where(row == sublane, values, joined)
    return joined


def rolled(values, rows):
    return pltpu.roll(values, rows % 8, 0) if rows % 8 else values


def transposed(tiles):
    turned = [rolled(tile, index) for index, tile in enumerate(tiles)]
    return [
        rolled(by_sublane([((row + index) % 8, tile) for index, tile in enumerate(turned)]), -row)
        for row in range(8)
    ]


def to_plane(load, store):
    lane = lax.broadcasted_iota(jnp.int32, (8, LANES), 1)
    tiles = [load(tile) for tile in range(STRIDE)]

    def spread(k):
        flat = [STRIDE * s + k for s in range(8)]
        return rolled(by_sublane([(row % 8, tiles[row // 8]) for row in flat]), -k)

    for step in range(RUN // 4):
        rows = [spread(5 * step + part) for part in range(5)]
        store(4 * step, rows[0], rows[1])
        for part in range(1, 4):
            left = pltpu.roll(rows[part], LANES - 32 * part, 1)
            right = pltpu.roll(rows[part + 1], LANES - 32 * part, 1)
            store(4 * step + part, jnp.where(lane < LANES - 32 * part, left, right), right)


def to_flat(load, store):
    lane = lax.broadcasted_iota(jnp.int32, (8, LANES), 1)
    spread = []
    for step in range(RUN // 4):
        turned = []
        for part in range(4):
            low, high = load(4 * step + part)
            if part:
                low = pltpu.roll(low, 32 * part, 1)
                high = pltpu.roll(high, 32 * part, 1)
            turned.append((low, high))
        rows = [turned[0][0]]
        for part in range(1, 4):
            ended = 32 * (part - 1)
            values = jnp.where(lane < ended + 32, turned[part - 1][1], turned[part][0])
            if ended:
                values = jnp.where(lane < ended, turned[part - 1][0], values)
            rows.append(values)
        rows.append(jnp.where(lane < 96, turned[3][0], turned[3][1]))
        spread += [rolled(values, 5 * step + part) for part, values in enumerate(rows)]
    for tile in range(STRIDE):
        store(tile, by_sublane([(t, spread[(8 * tile + t) % STRIDE]) for t in range(8)]))


def parts_of(values):
    high = values.astype(jnp.bfloat16)
    low = (values - high.astype(jnp.float32)).astype(jnp.bfloat16)
    return high, low


def turn_z(values, table):
    high, low = parts_of(values)
    return jnp.dot(
        jnp.concatenate([high, low, high], axis=1), table, preferred_element_type=jnp.float32
    )


def turn_y(table, values):
    high, low = parts_of(values)
    return jnp.dot(
        table, jnp.concatenate([high, low, high], axis=0), preferred_element_type=jnp.float32
    )


def tile_rows(first, count=8):
    return pl.ds(pl.multiple_of(first, 8), count)


def send_columns(planes_ref, slots, table_y, table_z, waves_ref, turned_ref):
    along_z = turn_z(planes_ref[:slots * SIDE, :], table_z)
    for slot in range(slots):
        rows = slice(slot * SIDE, (slot + 1) * SIDE)
        waves_ref[rows, :] = turn_y(table_y, along_z[rows])

    @pl.loop(0, SIDE // 8)
    def _(step):
        for lanes in (slice(0, LANES), slice(LANES, WIDTH)):
            tiles = [waves_ref[tile_rows(slot * SIDE + step * 8), lanes] for slot in range(slots)]
            tiles += [jnp.zeros((8, LANES), jnp.float32)] * (SLOTS - slots)
            for row, values in enumerate(transposed(tiles)):
                turned_ref[step * 8 + row, :, lanes] = values


def chunk_of(turned_ref, first_row, pieces, extra):
    parts = [turned_ref[first_row + row][:, start:stop] for row, start, stop in pieces]
    return jnp.concatenate(parts + [extra], axis=1)


def layers_of(stored_ref, flat_ref):
    @pl.loop(0, STRIDE)
    def _(step):
        tiles = []
        for part in range(8):
            lanes = pl.ds(pl.multiple_of((step * 8 + part) * LANES, LANES), LANES)
            tiles.append(eight(stored_ref[:, lanes]))
        for slot, values in enumerate(transposed(tiles)):
            flat_ref[slot, tile_rows(step * 8), :] = values


def place_of(start_ref):
    position = lax.axis_index("domain")
    return position, start_ref[position], start_ref[position + 1] - start_ref[position]


def pack_kernel(start_ref, potential_ref, orbitals_ref, v_ref, up_ref, down_ref, up_far_ref, down_far_ref,
                flat_ref, sems):
    _, _, thickness = place_of(start_ref)
    v_first = jnp.where(lax.axis_index("core") == 0, thickness - (HALO - 1), 0)
    first = jnp.maximum(thickness - HALO, 0)
    copies = []

    def copy(source, target):
        made = pltpu.make_async_copy(source, target, sems.at[len(copies)])
        made.start()
        copies.append(made)

    for part in range(2):
        rows = pl.ds(part * HALO, HALO)
        copy(orbitals_ref.at[part, pl.ds(first, HALO)], up_ref.at[rows])
        copy(orbitals_ref.at[part, pl.ds(0, HALO)], down_ref.at[rows])
        copy(orbitals_ref.at[part, pl.ds(thickness - 1, 1)], up_far_ref.at[pl.ds(part, 1)])
        copy(orbitals_ref.at[part, pl.ds(0, 1)], down_far_ref.at[pl.ds(part, 1)])

    layers_of(potential_ref, flat_ref)
    for layer in range(HALO - 1):
        v_ref[layer] = flat_ref[v_first + layer]
    for made in copies:
        made.wait()


def rows_from(ref, *at):
    return lambda tile: ref[(*at, slice(8 * tile, 8 * tile + 8), slice(None))]


def ions_kernel(count, length_cells, start_ref, background_ref, circle_ref, table_y_ref, table_z_ref,
                out_ref, flat_ref, planes_ref, waves_ref, turned_ref):
    _, own_start, thickness = place_of(start_ref)
    slots = background_ref.shape[0]
    groups, _, width = out_ref.shape
    layers_of(background_ref, flat_ref)

    def body(slot, total):
        def store(tile, low, high):
            rows = pl.ds(pl.multiple_of(slot * SIDE + tile * 8, 8), 8)
            planes_ref[rows, :LANES] = low
            planes_ref[rows, LANES:] = high

        to_plane(rows_from(flat_ref, slot), store)
        rows = pl.ds(pl.multiple_of(slot * SIDE, 8), SIDE)
        inside = mesh_points(own_start + slot, circle_ref[...], length_cells) & (slot < thickness)
        values = jnp.where(inside, planes_ref[rows, :], 0.0)
        planes_ref[rows, :] = values
        return total + jnp.sum(values.reshape(RUN, 8, WIDTH), axis=0)

    total = lax.fori_loop(0, slots, body, jnp.zeros((8, WIDTH), jnp.float32))
    whole = jnp.broadcast_to(jnp.sum(total, keepdims=True), (SLOTS, LANES))[:, :width - count]
    send_columns(planes_ref, slots, table_y_ref[...], table_z_ref[...], waves_ref, turned_ref)
    core_rows = SIDE // lax.axis_size("core")
    first_row = lax.axis_index("core") * core_rows + lax.axis_index("row") * (core_rows // lax.axis_size("row"))
    for group in range(groups):
        out_ref[group] = chunk_of(turned_ref, first_row, column_pieces(group * count, count), whole)


def propagate_kernel(count, length_cells, start_ref, weight_ref, orbitals_ref, potential_ref, below_ref,
                     above_ref, below_far_ref, above_far_ref, v_ref, v_other_ref, circle_ref,
                     table_y_ref, table_z_ref, next_ref, density_kept_ref, density_sent_ref, kept_ref, sent_ref, first_ref, second_ref,
                     third_ref, fourth_ref, sum_ref, centre_ref, beside_ref, flat_ref, planes_ref, waves_ref, turned_ref):
    position, own_start, thickness = place_of(start_ref)
    domains = lax.axis_size("domain")
    before = start_ref[jnp.maximum(position - 1, 0)]
    after = start_ref[jnp.minimum(position + 2, domains)]
    short_below = ((position > 0) & (own_start - before < HALO)).astype(jnp.int32)
    short_above = (position < domains - 1) & (after - own_start - thickness < HALO)
    weight = weight_ref[0]
    core = lax.axis_index("core")
    slots = orbitals_ref.shape[1]
    layers = slots + 2 * HALO
    devices, _, width = kept_ref.shape
    field_refs = (first_ref, second_ref, third_ref, fourth_ref)

    def field_layer(part, x_row):
        def store(tile, low, high):
            first_ref[part, x_row, 8 + 8 * tile:16 + 8 * tile, :LANES] = low
            first_ref[part, x_row, 8 + 8 * tile:16 + 8 * tile, LANES:] = high

        return store

    def potential_layer(x_row):
        def store(tile, low, high):
            centre_ref[x_row, 8 * tile:8 * tile + 8, :LANES] = low
            centre_ref[x_row, 8 * tile:8 * tile + 8, LANES:] = high

        return store

    layers_of(potential_ref, flat_ref)

    @pl.loop(0, slots)
    def _(slot):
        for part in range(2):
            to_plane(rows_from(orbitals_ref, part, slot), field_layer(part, HALO + slot))
        to_plane(rows_from(flat_ref, slot), potential_layer(HALO + slot))

    @pl.loop(0, HALO - 1)
    def _(layer):
        lower = 1 + layer
        upper = HALO + thickness + layer
        to_plane(rows_from(v_ref, layer), potential_layer(jnp.where(core == 0, lower, upper)))
        to_plane(rows_from(v_other_ref, layer), potential_layer(jnp.where(core == 0, upper, lower)))
        for part in range(2):
            to_plane(
                rows_from(below_ref, part * HALO + 1 + layer - short_below), field_layer(part, 1 + layer)
            )
            to_plane(
                rows_from(above_ref, part * HALO + layer), field_layer(part, HALO + thickness + layer)
            )

    @pl.loop(0, 2)
    def _(part):
        last = 2 * HALO - 1 + thickness

        @pl.when(short_below > 0)
        def _():
            to_plane(rows_from(below_far_ref, part), field_layer(part, 0))

        @pl.when(short_below == 0)
        def _():
            to_plane(rows_from(below_ref, part * HALO), field_layer(part, 0))

        @pl.when(short_above)
        def _():
            to_plane(rows_from(above_far_ref, part), field_layer(part, last))

        @pl.when(jnp.logical_not(short_above))
        def _():
            to_plane(rows_from(above_ref, part * HALO + HALO - 1), field_layer(part, last))

    def wrap(term, part, x_row):
        first = field_refs[term][part, x_row, 8:16, :]
        final = field_refs[term][part, x_row, SIDE:SIDE + 8, :]
        field_refs[term][part, x_row, :8, :] = pltpu.roll(final, 1, 0)
        field_refs[term][part, x_row, SIDE + 8:, :] = pltpu.roll(first, 7, 0)

    @pl.loop(0, layers)
    def _(x_row):
        known = x_row < thickness + 2 * HALO
        for block in range(SIDE // BLOCK):
            rows = slice(block * BLOCK, (block + 1) * BLOCK)
            inner = slice(8 + block * BLOCK, 8 + (block + 1) * BLOCK)
            inside = mesh_points(own_start - HALO + x_row, circle_ref[rows, :], length_cells) & known
            centre_ref[x_row, rows, :] = jnp.where(
                inside, (3.0 + centre_ref[x_row, rows, :]) * time_step, 0.0
            )
            beside_ref[x_row, rows, :] = jnp.where(inside, 0.5 * time_step, 0.0)
            for part in range(2):
                first_ref[part, x_row, inner, :] = jnp.where(
                    inside, first_ref[part, x_row, inner, :], 0.0
                )
        for part in range(2):
            wrap(0, part, x_row)

    def hamilton(term, part, x_row, block, centre, beside):
        field_ref = field_refs[term]
        tall = field_ref[part, x_row, block * BLOCK:block * BLOCK + BLOCK + 16, :]
        inner = slice(8 + block * BLOCK, 8 + (block + 1) * BLOCK)
        field = tall[8:8 + BLOCK]
        around = field_ref[part, x_row - 1, inner, :] + field_ref[part, x_row + 1, inner, :]
        around = around + (tall[:BLOCK] + tall[16:])
        around = around + (pltpu.roll(field, 1, 1) + pltpu.roll(field, WIDTH - 1, 1))
        return centre * field - beside * around

    for term in range(1, TERMS):

        @pl.loop(term, layers - term)
        def _(x_row, term=term):
            for block in range(SIDE // BLOCK):
                rows = slice(block * BLOCK, (block + 1) * BLOCK)
                inner = slice(8 + block * BLOCK, 8 + (block + 1) * BLOCK)
                centre = centre_ref[x_row, rows, :]
                beside = beside_ref[x_row, rows, :]
                for part in range(2):
                    field_refs[term][part, x_row, inner, :] = hamilton(
                        term - 1, part, x_row, block, centre, beside
                    )
            for part in range(2):
                wrap(term, part, x_row)

    def finish(slot, total):
        x_row = HALO + slot
        owned = slot < thickness
        for block in range(SIDE // BLOCK):
            rows = slice(block * BLOCK, (block + 1) * BLOCK)
            inner = slice(8 + block * BLOCK, 8 + (block + 1) * BLOCK)
            centre = centre_ref[x_row, rows, :]
            beside = beside_ref[x_row, rows, :]
            density = jnp.zeros((BLOCK, WIDTH), jnp.float32)
            for part, sign in ((0, 1.0), (1, -1.0)):
                summed = first_ref[part, x_row, inner, :]
                summed = summed + sign * second_ref[1 - part, x_row, inner, :]
                summed = summed - (1.0 / 2.0) * third_ref[part, x_row, inner, :]
                summed = summed - (sign / 6.0) * fourth_ref[1 - part, x_row, inner, :]
                summed = summed + (1.0 / 24.0) * hamilton(3, part, x_row, block, centre, beside)
                summed = jnp.where(owned, summed, 0.0)
                sum_ref[part, rows, :] = summed
                density = density + summed * summed
            density = weight * density
            planes_ref[pl.ds(pl.multiple_of(slot * SIDE + block * BLOCK, 8), BLOCK), :] = density
            total = total + jnp.sum(density.reshape(BLOCK // 8, 8, WIDTH), axis=0)

        for part in range(2):

            def load(tile, part=part):
                tall = sum_ref[part, 8 * tile:8 * tile + 8, :]
                return tall[:, :LANES], tall[:, LANES:]

            def store(tile, values, part=part):
                next_ref[part, slot, 8 * tile:8 * tile + 8, :] = values

            to_flat(load, store)

        return total

    total = lax.fori_loop(0, slots, finish, jnp.zeros((8, WIDTH), jnp.float32))
    planes_ref[slots * SIDE:, :] = jnp.zeros(((SLOTS - slots) * SIDE, WIDTH), jnp.float32)

    @pl.loop(0, SLOTS // 2)
    def _(slot):
        for first, target_ref in ((core, density_kept_ref), (1 - core, density_sent_ref)):

            def load(tile, first=first):
                row = (first * (SLOTS // 2) + slot) * SIDE + tile * 8
                tall = planes_ref[pl.ds(pl.multiple_of(row, 8), 8), :]
                return tall[:, :LANES], tall[:, LANES:]

            def store(tile, values, target_ref=target_ref):
                target_ref[slot, 8 * tile:8 * tile + 8, :] = values

            to_flat(load, store)

    whole = jnp.broadcast_to(jnp.sum(total, keepdims=True), (SLOTS, LANES))[:, :width - count]
    send_columns(planes_ref, slots, table_y_ref[...], table_z_ref[...], waves_ref, turned_ref)
    core_rows = SIDE // 2
    first_row = core * core_rows
    for device in range(devices):
        pieces = column_pieces(device * count, count)
        kept_ref[device] = chunk_of(turned_ref, first_row, pieces, whole)
        sent_ref[device] = chunk_of(turned_ref, core_rows - first_row, pieces, whole)


def wave_squared(index, count_cells):
    folded = jnp.where(2 * index <= count_cells, index, index - count_cells)
    wave_number = folded.astype(jnp.float32) * (two_pi / count_cells)
    return wave_number * wave_number


def coulomb_kernel(count, length_cells, start_ref, charge_ref, ions_ref, table_ref, out_ref):
    domains, _, width = ions_ref.shape
    states = charge_ref.shape[0] // domains
    device = (lax.axis_index("core") * states + lax.axis_index("row")) * domains + lax.axis_index("domain")
    charge = charge_ref[:domains]
    for state in range(1, states):
        charge = charge + charge_ref[state * domains:(state + 1) * domains]
    charge = charge.reshape(domains * SLOTS, width)
    ions = ions_ref[...].reshape(domains * SLOTS, width)
    first = lax.broadcasted_iota(jnp.int32, (domains * SLOTS, width), 0) % SLOTS == 0
    lane = lax.broadcasted_iota(jnp.int32, (domains * SLOTS, width), 1)
    chosen = first & (lane == count)
    electrons = jnp.sum(jnp.where(chosen, charge, 0.0), keepdims=True)
    ionic = jnp.sum(jnp.where(chosen, ions, 0.0), keepdims=True)
    charge = charge - (electrons / ionic) * ions
    layer = lax.broadcasted_iota(jnp.int32, (length_cells, domains * SLOTS), 0)
    place = lax.broadcasted_iota(jnp.int32, (length_cells, domains * SLOTS), 1)
    chosen_layer = jnp.full(layer.shape, -1, jnp.int32)
    for domain in range(domains):
        slot = place - domain * SLOTS
        here = (slot >= 0) & (slot < start_ref[domain + 1] - start_ref[domain])
        chosen_layer = jnp.where(here, start_ref[domain] + slot, chosen_layer)
    pick = (layer == chosen_layer).astype(jnp.float32)
    table = jnp.dot(table_ref[...], pick, precision=highest, preferred_element_type=jnp.float32)
    waves = jnp.dot(table, charge, precision=highest, preferred_element_type=jnp.float32)
    wave_x = lax.broadcasted_iota(jnp.int32, waves.shape, 0)
    column = device * count + lax.broadcasted_iota(jnp.int32, waves.shape, 1)
    wave_y = ((column.astype(jnp.float32) + 0.5) * (1.0 / SIDE)).astype(jnp.int32)
    wave_z = column - wave_y * SIDE
    squared = (
        wave_squared(wave_x, length_cells) + wave_squared(wave_y, SIDE) + wave_squared(wave_z, SIDE)
    )
    gain = jnp.where(squared > 0, four_pi / jnp.where(squared > 0, squared, 1.0), 0.0)
    waves = waves * (gain * (1.0 / (length_cells * SIDE * SIDE)))
    back = lax.dot_general(
        table, waves, (((0,), (0,)), ((), ())), precision=highest, preferred_element_type=jnp.float32
    )
    back = back.reshape(domains, SLOTS, width)
    for state in range(states):
        out_ref[state * domains:(state + 1) * domains] = back


def field_kernel(count, length_cells, start_ref, waves_ref, others_ref, density_ref, other_ref,
                 circle_ref, table_y_ref, table_z_ref, out_ref, turned_ref, plane_waves_ref, planes_ref, flat_ref):
    _, own_start, thickness = place_of(start_ref)
    devices = waves_ref.shape[0]
    slots = out_ref.shape[0]
    core = lax.axis_index("core")
    core_rows = SIDE // 2
    first_row = core * core_rows
    for source_ref, first in ((waves_ref, first_row), (others_ref, core_rows - first_row)):
        pieces = []
        for device in range(devices):
            column = 0
            for row, start, stop in column_pieces(device * count, count):
                values = source_ref[device, :, column:column + stop - start]
                column += stop - start
                if start > 0:
                    pieces.append(values)
                    values = jnp.concatenate(pieces, axis=1)
                if stop < SIDE:
                    pieces = [values]
                    continue
                pieces = []
                turned_ref[first + row, :, :LANES] = values[:, :LANES]
                turned_ref[first + row, :, LANES:] = jnp.concatenate(
                    [values[:, LANES:], jnp.zeros((SLOTS, WIDTH - SIDE), jnp.float32)], axis=1
                )

    @pl.loop(0, SIDE // 8)
    def _(step):
        for lanes in (slice(0, LANES), slice(LANES, WIDTH)):
            tiles = transposed([turned_ref[step * 8 + row, :, lanes] for row in range(8)])
            for slot in range(slots):
                plane_waves_ref[tile_rows(slot * SIDE + step * 8), lanes] = tiles[slot]

    table_y = table_y_ref[...]
    table_z = table_z_ref[...]
    along_z = turn_z(plane_waves_ref[...], table_z)
    for slot in range(slots):
        rows = slice(slot * SIDE, (slot + 1) * SIDE)
        planes_ref[rows, :] = turn_y(table_y, along_z[rows])

    @pl.loop(0, slots)
    def _(slot):
        def load(tile):
            tall = planes_ref[pl.ds(pl.multiple_of(slot * SIDE + tile * 8, 8), 8), :]
            return tall[:, :LANES], tall[:, LANES:]

        def store(tile, values):
            flat_ref[slot, 8 * tile:8 * tile + 8, :] = values

        to_flat(load, store)
        here = slot // (SLOTS // 2) == core
        kept_slot = slot % (SLOTS // 2)
        content = jnp.where(here, density_ref[kept_slot], other_ref[kept_slot]) * (3.0 / math.pi)
        positive = jnp.where(content > 0, content, 1.0)
        root = jnp.exp(jnp.log(positive) * (1.0 / 3.0))
        root = root - (root - positive / (root * root)) * (1.0 / 3.0)
        root = jnp.where(content > 0, root, 0.0)
        inside = mesh_points(own_start + slot, circle_ref[...], length_cells) & (slot < thickness)
        flat_ref[slot] = jnp.where(inside, flat_ref[slot] - root, 0.0)

    @pl.loop(0, STRIDE)
    def _(step):
        tiles = [flat_ref[slot, tile_rows(step * 8), :] for slot in range(slots)]
        tiles += [jnp.zeros((8, LANES), jnp.float32)] * (SLOTS - slots)
        for part, values in enumerate(transposed(tiles)):
            lanes = pl.ds(pl.multiple_of((step * 8 + part) * LANES, LANES), LANES)
            out_ref[:, lanes] = values[:slots]


def from_behind(value, steps):
    count = lax.axis_size("domain")
    leading, last = (max(0, -steps), min(count, count - steps))
    return lax.ppermute(value, "domain", [(source, source + steps) for source in range(leading, last)])


def swapped(value, axis):
    return lax.ppermute(value, axis, [(0, 1), (1, 0)])


def shards(orbitals, occupation, potential, background, layer_start):
    domains = lax.axis_size("domain")
    rows = lax.axis_size("row")
    devices = domains * rows
    length_cells = SLAB * domains
    layer_cap, plane = potential.shape
    count = plane // (2 * devices)
    width = -(-(count + 1) // LANES) * LANES
    circle = jnp.asarray(circle_plane())
    flat_circle = jnp.asarray(circle_table().reshape(FLAT, LANES))
    table_z, into_y, out_of_y = (jnp.asarray(table) for table in tables_of_side())
    table_x = jnp.asarray(hartley_table(length_cells).astype(np.float32))
    params = pltpu.CompilerParams(vmem_limit_bytes=VMEM_BYTES)

    def f32(*shape):
        return jax.ShapeDtypeStruct(shape, jnp.float32)

    def scratch(*shape):
        return pltpu.VMEM(shape, jnp.float32)

    layers = orbitals.reshape(2, layer_cap, FLAT, LANES)
    v_rows, up, down, up_far, down_far = pl.pallas_call(
        pack_kernel,
        out_shape=tuple(f32(size, FLAT, LANES) for size in (HALO - 1, 2 * HALO, 2 * HALO, 2, 2)),
        in_specs=[SMEM_SPEC, VMEM_SPEC, ANY_SPEC],
        out_specs=(VMEM_SPEC,) * 5,
        scratch_shapes=[scratch(SLOTS, FLAT, LANES), pltpu.SemaphoreType.DMA((8,))],
        compiler_params=params,
        name="pack_halo",
    )(layer_start, potential, layers)
    v_rows = lax.ppermute(
        v_rows,
        ("core", "domain"),
        [(source, source + 1) for source in range(domains - 1)]
        + [(domains + source + 1, domains + source) for source in range(domains - 1)],
    )
    below = from_behind(up, 1)
    above = from_behind(down, -1)
    below_far = from_behind(up_far, 2)
    above_far = from_behind(down_far, -2)
    v_rows, below_far, above_far = lax.optimization_barrier((v_rows, below_far, above_far))
    v_others = swapped(v_rows, "core")

    ions = pl.pallas_call(
        functools.partial(ions_kernel, count, length_cells),
        out_shape=f32(domains, SLOTS, width),
        in_specs=[SMEM_SPEC] + [VMEM_SPEC] * 4,
        out_specs=VMEM_SPEC,
        scratch_shapes=[
            scratch(SLOTS, FLAT, LANES),
            scratch(layer_cap * SIDE, WIDTH),
            scratch(layer_cap * SIDE, WIDTH),
            scratch(SIDE, SLOTS, WIDTH),
        ],
        compiler_params=params,
        name="ion_waves",
    )(layer_start, background, circle, into_y, table_z)
    ions = lax.all_to_all(ions, "domain", split_axis=0, concat_axis=0, tiled=True)
    ions, below = lax.optimization_barrier((ions, below))

    span = layer_cap + 2 * HALO
    orbitals_next, density_kept, density_sent, kept, sent = pl.pallas_call(
        functools.partial(propagate_kernel, count, length_cells),
        out_shape=(
            f32(2, layer_cap, FLAT, LANES),
            f32(SLOTS // 2, FLAT, LANES),
            f32(SLOTS // 2, FLAT, LANES),
            f32(devices, SLOTS, width),
            f32(devices, SLOTS, width),
        ),
        in_specs=[SMEM_SPEC, SMEM_SPEC] + [VMEM_SPEC] * 11,
        out_specs=(VMEM_SPEC,) * 5,
        scratch_shapes=[
            scratch(2, span, TALL, WIDTH),
            scratch(2, span, TALL, WIDTH),
            scratch(2, span, TALL, WIDTH),
            scratch(2, span, TALL, WIDTH),
            scratch(2, SIDE, WIDTH),
            scratch(span, SIDE, WIDTH),
            scratch(span, SIDE, WIDTH),
            scratch(SLOTS, FLAT, LANES),
            scratch(SLOTS * SIDE, WIDTH),
            scratch(layer_cap * SIDE, WIDTH),
            scratch(SIDE, SLOTS, WIDTH),
        ],
        compiler_params=params,
        name="propagate",
    )(layer_start, occupation, layers, potential, below, above, below_far, above_far, v_rows,
      v_others, circle, into_y, table_z)
    waves = kept + swapped(sent, "core")
    density = density_kept + swapped(density_sent, "core")
    waves = lax.all_to_all(waves, ("row", "domain"), split_axis=0, concat_axis=0, tiled=True)
    other_density = swapped(density, "row")
    waves = pl.pallas_call(
        functools.partial(coulomb_kernel, count, length_cells),
        out_shape=f32(devices, SLOTS, width),
        in_specs=[SMEM_SPEC] + [VMEM_SPEC] * 3,
        out_specs=VMEM_SPEC,
        compiler_params=params,
        name="coulomb",
    )(layer_start, waves, ions, table_x)
    waves, other_density = lax.optimization_barrier((waves, other_density))
    density = density + other_density
    other_density = swapped(density, "core")
    waves = lax.all_to_all(waves, ("row", "domain"), split_axis=0, concat_axis=0, tiled=True)
    other_waves = swapped(waves, "core")
    potential_next = pl.pallas_call(
        functools.partial(field_kernel, count, length_cells),
        out_shape=f32(layer_cap, plane),
        in_specs=[SMEM_SPEC] + [VMEM_SPEC] * 7,
        out_specs=VMEM_SPEC,
        scratch_shapes=[
            scratch(SIDE, SLOTS, WIDTH),
            scratch(layer_cap * SIDE, WIDTH),
            scratch(layer_cap * SIDE, WIDTH),
            scratch(SLOTS, FLAT, LANES),
        ],
        compiler_params=params,
        name="field",
    )(layer_start, waves, other_waves, density, other_density, flat_circle, out_of_y, table_z)
    return orbitals_next.reshape(orbitals.shape), potential_next


def solution(mesh):
    domains = mesh.shape["domain"]
    split = Mesh(mesh.devices.reshape(-1, 2, domains), ("row", "core", "domain"))
    states = ("row", "core")
    return jax.shard_map(
        shards,
        mesh=split,
        in_specs=(
            P(None, states, "domain", None),
            P(states),
            P("domain", None),
            P("domain", None),
            P(),
        ),
        out_specs=(P(None, states, "domain", None), P("domain", None)),
        check_vma=False,
    )
```

```python
import functools
import math

import jax
import jax.numpy as jnp
import ml_dtypes
import numpy as np
from jax import lax
from jax.experimental import pallas as pl
from jax.experimental.pallas import tpu as pltpu
from jax.sharding import Mesh, PartitionSpec as P

SIDE = 160
SLAB = 5
TERMS = 4

HALO = TERMS
LANES = 128
SLOTS = 8
RUN = SIDE // 8
FLAT = SIDE * SIDE // LANES
STRIDE = FLAT // 8
WIDTH = 2 * LANES
BLOCK = 32
TALL = SIDE + 16

time_step = 0.3
four_pi = 4.0 * math.pi
two_pi = 2.0 * math.pi
highest = lax.Precision.HIGHEST
VMEM_BYTES = 56 * 1024 * 1024
SMEM_SPEC = pl.BlockSpec(memory_space=pltpu.SMEM)
VMEM_SPEC = pl.BlockSpec(memory_space=pltpu.VMEM)
ANY_SPEC = pl.BlockSpec(memory_space=pl.ANY)


def hartley_table(count_cells):
    index_run = np.arange(count_cells)
    angles = (index_run[:, None] * index_run[None, :] % count_cells) * (2.0 * np.pi / count_cells)
    return np.cos(angles) + np.sin(angles)


def plane_order():
    rows = np.arange(SIDE)
    return RUN * (rows % 8) + rows // 8


def two_parts(table):
    table = table.astype(np.float32)
    high = table.astype(ml_dtypes.bfloat16)
    low = (table - high.astype(np.float32)).astype(ml_dtypes.bfloat16)
    return high, low


def tables_of_side():
    table = hartley_table(SIDE)
    along_z = np.zeros((WIDTH, WIDTH))
    along_z[:SIDE, :SIDE] = table
    high, low = two_parts(along_z)
    along_z = np.concatenate([high, high, low], axis=0)
    high, low = two_parts(table[:, plane_order()])
    into_y = np.concatenate([high, high, low], axis=1)
    high, low = two_parts(table[plane_order(), :])
    out_of_y = np.concatenate([high, high, low], axis=1)
    return along_z, into_y, out_of_y


def circle_table():
    across = 2 * np.arange(SIDE, dtype=np.int64) - (SIDE - 1)
    return (across[:, None] ** 2 + across[None, :] ** 2).astype(np.int32)


def circle_plane():
    table = np.full((SIDE, WIDTH), 4 * SIDE * SIDE, np.int32)
    table[:, :SIDE] = circle_table()[plane_order()]
    return table


def mesh_points(x_row, circle, length_cells):
    room = ((length_cells - 2) ** 2 - (2 * x_row - (length_cells - 1)) ** 2) * (SIDE - 2) ** 2
    return (circle * (length_cells - 2) ** 2 <= room) & (circle < 4 * SIDE * SIDE)


def column_pieces(first, count):
    pieces = []
    column = first
    while column < first + count:
        row = column // SIDE
        stop = min((row + 1) * SIDE, first + count)
        pieces.append((row, column - row * SIDE, stop - row * SIDE))
        column = stop
    return pieces


def eight(values):
    missing = jnp.zeros((SLOTS - values.shape[0], values.shape[1]), values.dtype)
    return jnp.concatenate([values, missing], axis=0)


def to_plane(load, store):
    lane = lax.broadcasted_iota(jnp.int32, (8, LANES), 1)
    for step in range(RUN // 4):
        rows = [load(5 * step + part) for part in range(5)]
        store(4 * step, rows[0], rows[1])
        for part in range(1, 4):
            left = pltpu.roll(rows[part], LANES - 32 * part, 1)
            right = pltpu.roll(rows[part + 1], LANES - 32 * part, 1)
            store(4 * step + part, jnp.where(lane < LANES - 32 * part, left, right), right)


def to_flat(load, store):
    lane = lax.broadcasted_iota(jnp.int32, (8, LANES), 1)
    for step in range(RUN // 4):
        turned = []
        for part in range(4):
            low, high = load(4 * step + part)
            if part:
                low = pltpu.roll(low, 32 * part, 1)
                high = pltpu.roll(high, 32 * part, 1)
            turned.append((low, high))
        store(5 * step, turned[0][0])
        for part in range(1, 4):
            ended = 32 * (part - 1)
            values = jnp.where(lane < ended + 32, turned[part - 1][1], turned[part][0])
            if ended:
                values = jnp.where(lane < ended, turned[part - 1][0], values)
            store(5 * step + part, values)
        store(5 * step + 4, jnp.where(lane < 96, turned[3][0], turned[3][1]))


def chords():
    across = 2 * np.arange(SIDE, dtype=np.int64) - (SIDE - 1)
    room = (SIDE - 2) ** 2 - across**2
    return [max([w for w in range(1, SIDE // 2 + 1) if (2 * w - 1) ** 2 <= left], default=0) for left in room]


def chord_moves():
    moves = []
    packed = 0
    for row, half in enumerate(chords()):
        if half:
            moves.append((row * SIDE + SIDE // 2 - half, packed, 2 * half))
            packed += 2 * half
    return moves


def packed_tiles():
    _, start, length = chord_moves()[-1]
    return -(-(start + length) // LANES)


def move_lanes(moves, load, store):
    lane = lax.broadcasted_iota(jnp.int32, (8, LANES), 1)
    pieces = {}
    for source, target, length in moves:
        while length:
            size = min(length, LANES - source % LANES, LANES - target % LANES)
            pieces.setdefault(target // LANES, []).append((target % LANES, source // LANES, (target - source) % LANES))
            source, target, length = source + size, target + size, length - size
    loaded = {}
    turned = {}
    for tile in sorted(pieces):
        values = None
        for first, origin, shift in sorted(pieces[tile]):
            if origin not in loaded:
                loaded[origin] = load(origin)
            if (origin, shift) not in turned:
                turned[origin, shift] = pltpu.roll(loaded[origin], shift, 1) if shift else loaded[origin]
            piece = turned[origin, shift]
            values = piece if values is None else jnp.where(lane >= first, piece, values)
        store(tile, values)


def pack_chords(rows_ref, store):
    move_lanes(chord_moves(), lambda tile: rows_ref[pl.ds(tile, 8, stride=FLAT), :], store)


def unpack_chords(load, rows_ref):
    def store(tile, values):
        rows_ref[pl.ds(tile, 8, stride=FLAT), :] = values

    move_lanes([(target, source, length) for source, target, length in chord_moves()], load, store)


def parts_of(values):
    high = values.astype(jnp.bfloat16)
    low = (values - high.astype(jnp.float32)).astype(jnp.bfloat16)
    return high, low


def turn_z(values, table):
    high, low = parts_of(values)
    return jnp.dot(
        jnp.concatenate([high, low, high], axis=1), table, preferred_element_type=jnp.float32
    )


def turn_y(table, values):
    high, low = parts_of(values)
    return jnp.dot(
        table, jnp.concatenate([high, low, high], axis=0), preferred_element_type=jnp.float32
    )


def send_columns(planes_ref, slots, table_y, table_z, low_ref, high_ref):
    along_z = turn_z(planes_ref[:slots * SIDE, :], table_z)
    for slot in range(slots):
        rows = slice(slot * SIDE, (slot + 1) * SIDE)
        waves = turn_y(table_y, along_z[rows])
        low_ref[rows, :] = waves[:, :LANES]
        high_ref[rows, :] = waves[:, LANES:]
    low_ref[slots * SIDE:, :] = jnp.zeros(((SLOTS - slots) * SIDE, LANES), jnp.float32)
    high_ref[slots * SIDE:, :] = jnp.zeros(((SLOTS - slots) * SIDE, LANES), jnp.float32)


def chunk_of(low_ref, high_ref, first_row, pieces, extra):
    parts = []
    for row, start, stop in pieces:
        at = pl.ds(first_row + row, SLOTS, stride=SIDE)
        values = jnp.concatenate([low_ref[at, :], high_ref[at, :]], axis=1)
        parts.append(values[:, start:stop])
    return jnp.concatenate(parts + [extra], axis=1)


def layers_of(stored_ref, flat_ref):
    @pl.loop(0, FLAT // 8)
    def _(step):
        for part in range(8):
            lanes = pl.ds(pl.multiple_of((step * 8 + part) * LANES, LANES), LANES)
            flat_ref[pl.ds(step * 8 + part, SLOTS, stride=FLAT), :] = eight(stored_ref[:, lanes])


def place_of(start_ref):
    position = lax.axis_index("domain")
    return position, start_ref[position], start_ref[position + 1] - start_ref[position]


def pack_kernel(start_ref, potential_ref, orbitals_ref, v_ref, up_ref, down_ref, up_far_ref, down_far_ref,
                up_rows_ref, down_rows_ref, flat_ref, v_rows_ref, sems):
    _, _, thickness = place_of(start_ref)
    v_first = jnp.where(lax.axis_index("core") == 0, thickness - (HALO - 1), 0)
    first = jnp.maximum(thickness - HALO, 0)
    copies = []

    def copy(source, target):
        made = pltpu.make_async_copy(source, target, sems.at[len(copies)])
        made.start()
        copies.append(made)

    def layers(part, start, count):
        return orbitals_ref.at[part, pl.ds(pl.multiple_of(start * FLAT, 8), count * FLAT)]

    for part in range(2):
        rows = pl.ds(part * HALO * FLAT, HALO * FLAT)
        copy(layers(part, first, HALO), up_rows_ref.at[rows])
        copy(layers(part, 0, HALO), down_rows_ref.at[rows])
    for part in range(2):
        rows = pl.ds(part * FLAT, FLAT)
        copy(layers(part, thickness - 1, 1), up_far_ref.at[rows])
        copy(layers(part, 0, 1), down_far_ref.at[rows])
    layers_of(potential_ref, flat_ref)
    for layer in range(HALO - 1):
        v_rows_ref[layer * FLAT:(layer + 1) * FLAT, :] = flat_ref[
            pl.ds(pl.multiple_of((v_first + layer) * FLAT, 8), FLAT), :
        ]

    def store_v(tile, values):
        for layer in range(HALO - 1):
            v_ref[layer, tile:tile + 1, :] = values[layer:layer + 1]

    pack_chords(v_rows_ref, store_v)
    for made in copies[:4]:
        made.wait()
    for rows_ref, out_ref in ((up_rows_ref, up_ref), (down_rows_ref, down_ref)):

        def store(tile, values, out_ref=out_ref):
            out_ref[:, tile * LANES:(tile + 1) * LANES] = values

        pack_chords(rows_ref, store)
    for made in copies[4:]:
        made.wait()


def ions_kernel(count, length_cells, start_ref, background_ref, circle_ref, table_y_ref, table_z_ref,
                out_ref, flat_ref, planes_ref, low_ref, high_ref):
    _, own_start, thickness = place_of(start_ref)
    slots = background_ref.shape[0]
    groups, _, width = out_ref.shape
    layers_of(background_ref, flat_ref)

    def body(slot, total):
        def store(tile, low, high):
            rows = pl.ds(pl.multiple_of(slot * SIDE + tile * 8, 8), 8)
            planes_ref[rows, :LANES] = low
            planes_ref[rows, LANES:] = high

        to_plane(lambda k: flat_ref[pl.ds(slot * FLAT + k, 8, stride=STRIDE), :], store)
        rows = pl.ds(pl.multiple_of(slot * SIDE, 8), SIDE)
        inside = mesh_points(own_start + slot, circle_ref[...], length_cells) & (slot < thickness)
        values = jnp.where(inside, planes_ref[rows, :], 0.0)
        planes_ref[rows, :] = values
        return total + jnp.sum(values.reshape(RUN, 8, WIDTH), axis=0)

    total = lax.fori_loop(0, slots, body, jnp.zeros((8, WIDTH), jnp.float32))
    whole = jnp.broadcast_to(jnp.sum(total, keepdims=True), (SLOTS, LANES))[:, :width - count]
    send_columns(planes_ref, slots, table_y_ref[...], table_z_ref[...], low_ref, high_ref)
    core_rows = SIDE // lax.axis_size("core")
    first_row = lax.axis_index("core") * core_rows + lax.axis_index("row") * (core_rows // lax.axis_size("row"))
    for group in range(groups):
        out_ref[group] = chunk_of(low_ref, high_ref, first_row, column_pieces(group * count, count), whole)


def propagate_kernel(count, length_cells, start_ref, weight_ref, orbitals_ref, potential_ref, below_ref,
                     above_ref, below_far_ref, above_far_ref, v_ref, v_other_ref, circle_ref,
                     table_y_ref, table_z_ref, next_ref, density_kept_ref, density_sent_ref, kept_ref, sent_ref, first_ref, second_ref,
                     third_ref, fourth_ref, sum_ref, centre_ref, beside_ref, flat_ref, planes_ref, low_ref, high_ref,
                     below_rows_ref, above_rows_ref, v_rows_ref):
    position, own_start, thickness = place_of(start_ref)
    domains = lax.axis_size("domain")
    before = start_ref[jnp.maximum(position - 1, 0)]
    after = start_ref[jnp.minimum(position + 2, domains)]
    short_below = ((position > 0) & (own_start - before < HALO)).astype(jnp.int32)
    short_above = (position < domains - 1) & (after - own_start - thickness < HALO)
    weight = weight_ref[0]
    core = lax.axis_index("core")
    slots = orbitals_ref.shape[1]
    layers = slots + 2 * HALO
    devices, _, width = kept_ref.shape
    field_refs = (first_ref, second_ref, third_ref, fourth_ref)

    def field_layer(part, x_row):
        def store(tile, low, high):
            first_ref[part, x_row, 8 + 8 * tile:16 + 8 * tile, :LANES] = low
            first_ref[part, x_row, 8 + 8 * tile:16 + 8 * tile, LANES:] = high

        return store

    def potential_layer(x_row):
        def store(tile, low, high):
            centre_ref[x_row, 8 * tile:8 * tile + 8, :LANES] = low
            centre_ref[x_row, 8 * tile:8 * tile + 8, LANES:] = high

        return store

    def rows_from(ref, *at):
        return lambda k: ref[(*at, pl.ds(k, 8, stride=STRIDE), slice(None))]

    def layer_of(rows_ref, layer):
        return lambda k: rows_ref[pl.ds(layer * FLAT + k, 8, stride=STRIDE), :]

    for packed_ref, rows_ref in ((below_ref, below_rows_ref), (above_ref, above_rows_ref)):
        unpack_chords(
            lambda tile, packed_ref=packed_ref: packed_ref[:, tile * LANES:(tile + 1) * LANES], rows_ref
        )
    unpack_chords(
        lambda tile: eight(
            jnp.concatenate([ref[:, tile, :] for ref in (v_ref, v_other_ref)], axis=0)
        ),
        v_rows_ref,
    )

    layers_of(potential_ref, flat_ref)

    @pl.loop(0, slots)
    def _(slot):
        for part in range(2):
            to_plane(rows_from(orbitals_ref, part, slot), field_layer(part, HALO + slot))
        to_plane(layer_of(flat_ref, slot), potential_layer(HALO + slot))

    @pl.loop(0, HALO - 1)
    def _(layer):
        lower = 1 + layer
        upper = HALO + thickness + layer
        to_plane(layer_of(v_rows_ref, layer), potential_layer(jnp.where(core == 0, lower, upper)))
        to_plane(layer_of(v_rows_ref, HALO - 1 + layer), potential_layer(jnp.where(core == 0, upper, lower)))
        for part in range(2):
            to_plane(
                layer_of(below_rows_ref, part * HALO + 1 + layer - short_below), field_layer(part, 1 + layer)
            )
            to_plane(
                layer_of(above_rows_ref, part * HALO + layer), field_layer(part, HALO + thickness + layer)
            )

    @pl.loop(0, 2)
    def _(part):
        last = 2 * HALO - 1 + thickness

        @pl.when(short_below > 0)
        def _():
            to_plane(layer_of(below_far_ref, part), field_layer(part, 0))

        @pl.when(short_below == 0)
        def _():
            to_plane(layer_of(below_rows_ref, part * HALO), field_layer(part, 0))

        @pl.when(short_above)
        def _():
            to_plane(layer_of(above_far_ref, part), field_layer(part, last))

        @pl.when(jnp.logical_not(short_above))
        def _():
            to_plane(layer_of(above_rows_ref, part * HALO + HALO - 1), field_layer(part, last))

    def wrap(term, part, x_row):
        first = field_refs[term][part, x_row, 8:16, :]
        final = field_refs[term][part, x_row, SIDE:SIDE + 8, :]
        field_refs[term][part, x_row, :8, :] = pltpu.roll(final, 1, 0)
        field_refs[term][part, x_row, SIDE + 8:, :] = pltpu.roll(first, 7, 0)

    @pl.loop(0, layers)
    def _(x_row):
        known = x_row < thickness + 2 * HALO
        for block in range(SIDE // BLOCK):
            rows = slice(block * BLOCK, (block + 1) * BLOCK)
            inner = slice(8 + block * BLOCK, 8 + (block + 1) * BLOCK)
            inside = mesh_points(own_start - HALO + x_row, circle_ref[rows, :], length_cells) & known
            centre_ref[x_row, rows, :] = jnp.where(
                inside, (3.0 + centre_ref[x_row, rows, :]) * time_step, 0.0
            )
            beside_ref[x_row, rows, :] = jnp.where(inside, 0.5 * time_step, 0.0)
            for part in range(2):
                first_ref[part, x_row, inner, :] = jnp.where(
                    inside, first_ref[part, x_row, inner, :], 0.0
                )
        for part in range(2):
            wrap(0, part, x_row)

    def hamilton(term, part, x_row, block, centre, beside):
        field_ref = field_refs[term]
        tall = field_ref[part, x_row, block * BLOCK:block * BLOCK + BLOCK + 16, :]
        inner = slice(8 + block * BLOCK, 8 + (block + 1) * BLOCK)
        field = tall[8:8 + BLOCK]
        around = field_ref[part, x_row - 1, inner, :] + field_ref[part, x_row + 1, inner, :]
        around = around + (tall[:BLOCK] + tall[16:])
        around = around + (pltpu.roll(field, 1, 1) + pltpu.roll(field, WIDTH - 1, 1))
        return centre * field - beside * around

    for term in range(1, TERMS):

        @pl.loop(term, layers - term)
        def _(x_row, term=term):
            for block in range(SIDE // BLOCK):
                rows = slice(block * BLOCK, (block + 1) * BLOCK)
                inner = slice(8 + block * BLOCK, 8 + (block + 1) * BLOCK)
                centre = centre_ref[x_row, rows, :]
                beside = beside_ref[x_row, rows, :]
                for part in range(2):
                    field_refs[term][part, x_row, inner, :] = hamilton(
                        term - 1, part, x_row, block, centre, beside
                    )
            for part in range(2):
                wrap(term, part, x_row)

    def finish(slot, total):
        x_row = HALO + slot
        owned = slot < thickness
        for block in range(SIDE // BLOCK):
            rows = slice(block * BLOCK, (block + 1) * BLOCK)
            inner = slice(8 + block * BLOCK, 8 + (block + 1) * BLOCK)
            centre = centre_ref[x_row, rows, :]
            beside = beside_ref[x_row, rows, :]
            density = jnp.zeros((BLOCK, WIDTH), jnp.float32)
            for part, sign in ((0, 1.0), (1, -1.0)):
                summed = first_ref[part, x_row, inner, :]
                summed = summed + sign * second_ref[1 - part, x_row, inner, :]
                summed = summed - (1.0 / 2.0) * third_ref[part, x_row, inner, :]
                summed = summed - (sign / 6.0) * fourth_ref[1 - part, x_row, inner, :]
                summed = summed + (1.0 / 24.0) * hamilton(3, part, x_row, block, centre, beside)
                summed = jnp.where(owned, summed, 0.0)
                sum_ref[part, rows, :] = summed
                density = density + summed * summed
            density = weight * density
            planes_ref[pl.ds(pl.multiple_of(slot * SIDE + block * BLOCK, 8), BLOCK), :] = density
            total = total + jnp.sum(density.reshape(BLOCK // 8, 8, WIDTH), axis=0)

        for part in range(2):

            def load(tile, part=part):
                tall = sum_ref[part, 8 * tile:8 * tile + 8, :]
                return tall[:, :LANES], tall[:, LANES:]

            def store(k, values, part=part):
                next_ref[part, slot, pl.ds(k, 8, stride=STRIDE), :] = values

            to_flat(load, store)

        return total

    total = lax.fori_loop(0, slots, finish, jnp.zeros((8, WIDTH), jnp.float32))
    planes_ref[slots * SIDE:, :] = jnp.zeros(((SLOTS - slots) * SIDE, WIDTH), jnp.float32)

    @pl.loop(0, SLOTS // 2)
    def _(slot):
        for first, target_ref in ((core, density_kept_ref), (1 - core, density_sent_ref)):

            def load(tile, first=first):
                row = (first * (SLOTS // 2) + slot) * SIDE + tile * 8
                tall = planes_ref[pl.ds(pl.multiple_of(row, 8), 8), :]
                return tall[:, :LANES], tall[:, LANES:]

            def store(k, values, target_ref=target_ref):
                target_ref[slot, pl.ds(k, 8, stride=STRIDE), :] = values

            to_flat(load, store)

    whole = jnp.broadcast_to(jnp.sum(total, keepdims=True), (SLOTS, LANES))[:, :width - count]
    send_columns(planes_ref, slots, table_y_ref[...], table_z_ref[...], low_ref, high_ref)
    core_rows = SIDE // 2
    first_row = core * core_rows
    for device in range(devices):
        pieces = column_pieces(device * count, count)
        kept_ref[device] = chunk_of(low_ref, high_ref, first_row, pieces, whole)
        sent_ref[device] = chunk_of(low_ref, high_ref, core_rows - first_row, pieces, whole)


def wave_squared(index, count_cells):
    folded = jnp.where(2 * index <= count_cells, index, index - count_cells)
    wave_number = folded.astype(jnp.float32) * (two_pi / count_cells)
    return wave_number * wave_number


def coulomb_kernel(count, length_cells, start_ref, charge_ref, ions_ref, table_ref, out_ref):
    domains, _, width = ions_ref.shape
    states = charge_ref.shape[0] // domains
    device = (lax.axis_index("core") * states + lax.axis_index("row")) * domains + lax.axis_index("domain")
    charge = charge_ref[:domains]
    for state in range(1, states):
        charge = charge + charge_ref[state * domains:(state + 1) * domains]
    charge = charge.reshape(domains * SLOTS, width)
    ions = ions_ref[...].reshape(domains * SLOTS, width)
    first = lax.broadcasted_iota(jnp.int32, (domains * SLOTS, width), 0) % SLOTS == 0
    lane = lax.broadcasted_iota(jnp.int32, (domains * SLOTS, width), 1)
    chosen = first & (lane == count)
    electrons = jnp.sum(jnp.where(chosen, charge, 0.0), keepdims=True)
    ionic = jnp.sum(jnp.where(chosen, ions, 0.0), keepdims=True)
    charge = charge - (electrons / ionic) * ions
    layer = lax.broadcasted_iota(jnp.int32, (length_cells, domains * SLOTS), 0)
    place = lax.broadcasted_iota(jnp.int32, (length_cells, domains * SLOTS), 1)
    chosen_layer = jnp.full(layer.shape, -1, jnp.int32)
    for domain in range(domains):
        slot = place - domain * SLOTS
        here = (slot >= 0) & (slot < start_ref[domain + 1] - start_ref[domain])
        chosen_layer = jnp.where(here, start_ref[domain] + slot, chosen_layer)
    pick = (layer == chosen_layer).astype(jnp.float32)
    table = jnp.dot(table_ref[...], pick, precision=highest, preferred_element_type=jnp.float32)
    waves = jnp.dot(table, charge, precision=highest, preferred_element_type=jnp.float32)
    wave_x = lax.broadcasted_iota(jnp.int32, waves.shape, 0)
    column = device * count + lax.broadcasted_iota(jnp.int32, waves.shape, 1)
    wave_y = ((column.astype(jnp.float32) + 0.5) * (1.0 / SIDE)).astype(jnp.int32)
    wave_z = column - wave_y * SIDE
    squared = (
        wave_squared(wave_x, length_cells) + wave_squared(wave_y, SIDE) + wave_squared(wave_z, SIDE)
    )
    gain = jnp.where(squared > 0, four_pi / jnp.where(squared > 0, squared, 1.0), 0.0)
    waves = waves * (gain * (1.0 / (length_cells * SIDE * SIDE)))
    back = lax.dot_general(
        table, waves, (((0,), (0,)), ((), ())), precision=highest, preferred_element_type=jnp.float32
    )
    back = back.reshape(domains, SLOTS, width)
    for state in range(states):
        out_ref[state * domains:(state + 1) * domains] = back


def field_kernel(count, length_cells, start_ref, waves_ref, others_ref, density_ref, other_ref,
                 circle_ref, table_y_ref, table_z_ref, out_ref, low_ref, high_ref, planes_ref, flat_ref):
    _, own_start, thickness = place_of(start_ref)
    devices = waves_ref.shape[0]
    slots = out_ref.shape[0]
    core = lax.axis_index("core")
    core_rows = SIDE // 2
    first_row = core * core_rows
    for source_ref, first in ((waves_ref, first_row), (others_ref, core_rows - first_row)):
        pieces = []
        for device in range(devices):
            column = 0
            for row, start, stop in column_pieces(device * count, count):
                values = source_ref[device, :, column:column + stop - start]
                column += stop - start
                if start > 0:
                    pieces.append(values)
                    values = jnp.concatenate(pieces, axis=1)
                if stop < SIDE:
                    pieces = [values]
                    continue
                pieces = []
                at = pl.ds(first + row, SLOTS, stride=SIDE)
                low_ref[at, :] = values[:, :LANES]
                high_ref[at, :] = jnp.concatenate(
                    [values[:, LANES:], jnp.zeros((SLOTS, WIDTH - SIDE), jnp.float32)], axis=1
                )
    table_y = table_y_ref[...]
    table_z = table_z_ref[...]
    used = slice(0, slots * SIDE)
    along_z = turn_z(jnp.concatenate([low_ref[used, :], high_ref[used, :]], axis=1), table_z)
    for slot in range(slots):
        rows = slice(slot * SIDE, (slot + 1) * SIDE)
        planes_ref[rows, :] = turn_y(table_y, along_z[rows])

    @pl.loop(0, slots)
    def _(slot):
        def load(tile):
            tall = planes_ref[pl.ds(pl.multiple_of(slot * SIDE + tile * 8, 8), 8), :]
            return tall[:, :LANES], tall[:, LANES:]

        def store(k, values):
            flat_ref[pl.ds(slot * FLAT + k, 8, stride=STRIDE), :] = values

        to_flat(load, store)
        rows = pl.ds(pl.multiple_of(slot * FLAT, 8), FLAT)
        here = slot // (SLOTS // 2) == core
        kept_slot = slot % (SLOTS // 2)
        content = jnp.where(here, density_ref[kept_slot], other_ref[kept_slot]) * (3.0 / math.pi)
        positive = jnp.where(content > 0, content, 1.0)
        root = jnp.exp(jnp.log(positive) * (1.0 / 3.0))
        root = root - (root - positive / (root * root)) * (1.0 / 3.0)
        root = jnp.where(content > 0, root, 0.0)
        inside = mesh_points(own_start + slot, circle_ref[...], length_cells) & (slot < thickness)
        flat_ref[rows, :] = jnp.where(inside, flat_ref[rows, :] - root, 0.0)

    @pl.loop(0, FLAT // 8)
    def _(step):
        for part in range(8):
            lanes = pl.ds(pl.multiple_of((step * 8 + part) * LANES, LANES), LANES)
            out_ref[:, lanes] = flat_ref[pl.ds(step * 8 + part, SLOTS, stride=FLAT), :][:slots]


def from_behind(value, steps):
    count = lax.axis_size("domain")
    leading, last = (max(0, -steps), min(count, count - steps))
    return lax.ppermute(value, "domain", [(source, source + steps) for source in range(leading, last)])


def swapped(value, axis):
    return lax.ppermute(value, axis, [(0, 1), (1, 0)])


def shards(orbitals, occupation, potential, background, layer_start):
    domains = lax.axis_size("domain")
    rows = lax.axis_size("row")
    devices = domains * rows
    length_cells = SLAB * domains
    layer_cap, plane = potential.shape
    count = plane // (2 * devices)
    width = -(-(count + 1) // LANES) * LANES
    circle = jnp.asarray(circle_plane())
    flat_circle = jnp.asarray(circle_table().reshape(FLAT, LANES))
    table_z, into_y, out_of_y = (jnp.asarray(table) for table in tables_of_side())
    table_x = jnp.asarray(hartley_table(length_cells).astype(np.float32))
    params = pltpu.CompilerParams(vmem_limit_bytes=VMEM_BYTES)

    def f32(*shape):
        return jax.ShapeDtypeStruct(shape, jnp.float32)

    def scratch(*shape):
        return pltpu.VMEM(shape, jnp.float32)

    layers = orbitals.reshape(2, layer_cap, FLAT, LANES)
    packed = packed_tiles()
    v_rows, up, down, up_far, down_far = pl.pallas_call(
        pack_kernel,
        out_shape=(
            f32(HALO - 1, packed, LANES),
            f32(2 * HALO, packed * LANES),
            f32(2 * HALO, packed * LANES),
            f32(2 * FLAT, LANES),
            f32(2 * FLAT, LANES),
        ),
        in_specs=[SMEM_SPEC, VMEM_SPEC, ANY_SPEC],
        out_specs=(VMEM_SPEC,) * 5,
        scratch_shapes=[scratch(FLAT * 8, LANES)] * 4 + [pltpu.SemaphoreType.DMA((8,))],
        compiler_params=params,
        name="pack_halo",
    )(layer_start, potential, orbitals.reshape(2, layer_cap * FLAT, LANES))
    v_rows = lax.ppermute(
        v_rows,
        ("core", "domain"),
        [(source, source + 1) for source in range(domains - 1)]
        + [(domains + source + 1, domains + source) for source in range(domains - 1)],
    )
    below = from_behind(up, 1)
    above = from_behind(down, -1)
    below_far = from_behind(up_far, 2)
    above_far = from_behind(down_far, -2)
    v_rows, below_far, above_far = lax.optimization_barrier((v_rows, below_far, above_far))
    v_others = swapped(v_rows, "core")

    ions = pl.pallas_call(
        functools.partial(ions_kernel, count, length_cells),
        out_shape=f32(domains, SLOTS, width),
        in_specs=[SMEM_SPEC] + [VMEM_SPEC] * 4,
        out_specs=VMEM_SPEC,
        scratch_shapes=[
            scratch(SLOTS * FLAT, LANES),
            scratch(layer_cap * SIDE, WIDTH),
            scratch(SLOTS * SIDE, LANES),
            scratch(SLOTS * SIDE, LANES),
        ],
        compiler_params=params,
        name="ion_waves",
    )(layer_start, background, circle, into_y, table_z)
    ions = lax.all_to_all(ions, "domain", split_axis=0, concat_axis=0, tiled=True)
    ions, below = lax.optimization_barrier((ions, below))

    span = layer_cap + 2 * HALO
    orbitals_next, density_kept, density_sent, kept, sent = pl.pallas_call(
        functools.partial(propagate_kernel, count, length_cells),
        out_shape=(
            f32(2, layer_cap, FLAT, LANES),
            f32(SLOTS // 2, FLAT, LANES),
            f32(SLOTS // 2, FLAT, LANES),
            f32(devices, SLOTS, width),
            f32(devices, SLOTS, width),
        ),
        in_specs=[SMEM_SPEC, SMEM_SPEC] + [VMEM_SPEC] * 11,
        out_specs=(VMEM_SPEC,) * 5,
        scratch_shapes=[
            scratch(2, span, TALL, WIDTH),
            scratch(2, span, TALL, WIDTH),
            scratch(2, span, TALL, WIDTH),
            scratch(2, span, TALL, WIDTH),
            scratch(2, SIDE, WIDTH),
            scratch(span, SIDE, WIDTH),
            scratch(span, SIDE, WIDTH),
            scratch(SLOTS * FLAT, LANES),
            scratch(SLOTS * SIDE, WIDTH),
            scratch(SLOTS * SIDE, LANES),
            scratch(SLOTS * SIDE, LANES),
            scratch(SLOTS * FLAT, LANES),
            scratch(SLOTS * FLAT, LANES),
            scratch(SLOTS * FLAT, LANES),
        ],
        compiler_params=params,
        name="propagate",
    )(layer_start, occupation, layers, potential, below, above, below_far, above_far, v_rows,
      v_others, circle, into_y, table_z)
    waves = kept + swapped(sent, "core")
    density = density_kept + swapped(density_sent, "core")
    waves = lax.all_to_all(waves, ("row", "domain"), split_axis=0, concat_axis=0, tiled=True)
    other_density = swapped(density, "row")
    waves = pl.pallas_call(
        functools.partial(coulomb_kernel, count, length_cells),
        out_shape=f32(devices, SLOTS, width),
        in_specs=[SMEM_SPEC] + [VMEM_SPEC] * 3,
        out_specs=VMEM_SPEC,
        compiler_params=params,
        name="coulomb",
    )(layer_start, waves, ions, table_x)
    waves, other_density = lax.optimization_barrier((waves, other_density))
    density = density + other_density
    other_density = swapped(density, "core")
    waves = lax.all_to_all(waves, ("row", "domain"), split_axis=0, concat_axis=0, tiled=True)
    other_waves = swapped(waves, "core")
    potential_next = pl.pallas_call(
        functools.partial(field_kernel, count, length_cells),
        out_shape=f32(layer_cap, plane),
        in_specs=[SMEM_SPEC] + [VMEM_SPEC] * 7,
        out_specs=VMEM_SPEC,
        scratch_shapes=[
            scratch(SLOTS * SIDE, LANES),
            scratch(SLOTS * SIDE, LANES),
            scratch(layer_cap * SIDE, WIDTH),
            scratch(SLOTS * FLAT, LANES),
        ],
        compiler_params=params,
        name="field",
    )(layer_start, waves, other_waves, density, other_density, flat_circle, out_of_y, table_z)
    return orbitals_next.reshape(orbitals.shape), potential_next


def solution(mesh):
    domains = mesh.shape["domain"]
    split = Mesh(mesh.devices.reshape(-1, 2, domains), ("row", "core", "domain"))
    states = ("row", "core")
    return jax.shard_map(
        shards,
        mesh=split,
        in_specs=(
            P(None, states, "domain", None),
            P(states),
            P("domain", None),
            P("domain", None),
            P(),
        ),
        out_specs=(P(None, states, "domain", None), P("domain", None)),
        check_vma=False,
    )
```

```python
import functools
import math

import jax
import jax.numpy as jnp
import ml_dtypes
import numpy as np
from jax import lax
from jax.experimental import pallas as pl
from jax.experimental.pallas import tpu as pltpu
from jax.sharding import Mesh, PartitionSpec as P

SIDE = 160
SLAB = 5
TERMS = 4

HALO = TERMS
LANES = 128
SLOTS = 8
RUN = SIDE // 8
FLAT = SIDE * SIDE // LANES
STRIDE = FLAT // 8
WIDTH = 2 * LANES
BLOCK = 32
TALL = SIDE + 16

time_step = 0.3
four_pi = 4.0 * math.pi
two_pi = 2.0 * math.pi
highest = lax.Precision.HIGHEST
MEBI = 1024 * 1024
SMEM_SPEC = pl.BlockSpec(memory_space=pltpu.SMEM)
VMEM_SPEC = pl.BlockSpec(memory_space=pltpu.VMEM)
ANY_SPEC = pl.BlockSpec(memory_space=pl.ANY)


def hartley_table(count_cells):
    index_run = np.arange(count_cells)
    angles = (index_run[:, None] * index_run[None, :] % count_cells) * (2.0 * np.pi / count_cells)
    return np.cos(angles) + np.sin(angles)


def plane_order():
    rows = np.arange(SIDE)
    return RUN * (rows % 8) + rows // 8


def two_parts(table):
    table = table.astype(np.float32)
    high = table.astype(ml_dtypes.bfloat16)
    low = (table - high.astype(np.float32)).astype(ml_dtypes.bfloat16)
    return high, low


def tables_of_side():
    table = hartley_table(SIDE)
    along_z = np.zeros((WIDTH, WIDTH))
    along_z[:SIDE, :SIDE] = table
    high, low = two_parts(along_z)
    along_z = np.concatenate([high, high, low], axis=0)
    high, low = two_parts(table[:, plane_order()])
    into_y = np.concatenate([high, high, low], axis=1)
    high, low = two_parts(table[plane_order(), :])
    out_of_y = np.concatenate([high, high, low], axis=1)
    return along_z, into_y, out_of_y


def circle_table():
    across = 2 * np.arange(SIDE, dtype=np.int64) - (SIDE - 1)
    return (across[:, None] ** 2 + across[None, :] ** 2).astype(np.int32)


def circle_plane():
    table = np.full((SIDE, WIDTH), 4 * SIDE * SIDE, np.int32)
    table[:, :SIDE] = circle_table()[plane_order()]
    return table


def mesh_points(x_row, circle, length_cells):
    room = ((length_cells - 2) ** 2 - (2 * x_row - (length_cells - 1)) ** 2) * (SIDE - 2) ** 2
    return (circle * (length_cells - 2) ** 2 <= room) & (circle < 4 * SIDE * SIDE)


def column_pieces(first, count):
    pieces = []
    column = first
    while column < first + count:
        row = column // SIDE
        stop = min((row + 1) * SIDE, first + count)
        pieces.append((row, column - row * SIDE, stop - row * SIDE))
        column = stop
    return pieces


def eight(values):
    missing = jnp.zeros((SLOTS - values.shape[0], values.shape[1]), values.dtype)
    return jnp.concatenate([values, missing], axis=0)


def to_plane(load, store):
    lane = lax.broadcasted_iota(jnp.int32, (8, LANES), 1)
    for step in range(RUN // 4):
        rows = [load(5 * step + part) for part in range(5)]
        store(4 * step, rows[0], rows[1])
        for part in range(1, 4):
            left = pltpu.roll(rows[part], LANES - 32 * part, 1)
            right = pltpu.roll(rows[part + 1], LANES - 32 * part, 1)
            store(4 * step + part, jnp.where(lane < LANES - 32 * part, left, right), right)


def to_flat(load, store):
    lane = lax.broadcasted_iota(jnp.int32, (8, LANES), 1)
    for step in range(RUN // 4):
        turned = []
        for part in range(4):
            low, high = load(4 * step + part)
            if part:
                low = pltpu.roll(low, 32 * part, 1)
                high = pltpu.roll(high, 32 * part, 1)
            turned.append((low, high))
        store(5 * step, turned[0][0])
        for part in range(1, 4):
            ended = 32 * (part - 1)
            values = jnp.where(lane < ended + 32, turned[part - 1][1], turned[part][0])
            if ended:
                values = jnp.where(lane < ended, turned[part - 1][0], values)
            store(5 * step + part, values)
        store(5 * step + 4, jnp.where(lane < 96, turned[3][0], turned[3][1]))


def chords():
    across = 2 * np.arange(SIDE, dtype=np.int64) - (SIDE - 1)
    room = (SIDE - 2) ** 2 - across**2
    return [max([w for w in range(1, SIDE // 2 + 1) if (2 * w - 1) ** 2 <= left], default=0) for left in room]


def chord_moves():
    moves = []
    packed = 0
    for row, half in enumerate(chords()):
        if half:
            moves.append((row * SIDE + SIDE // 2 - half, packed, 2 * half))
            packed += 2 * half
    return moves


def packed_tiles():
    _, start, length = chord_moves()[-1]
    return -(-(start + length) // LANES)


def move_lanes(moves, load, store):
    lane = lax.broadcasted_iota(jnp.int32, (8, LANES), 1)
    pieces = {}
    for source, target, length in moves:
        while length:
            size = min(length, LANES - source % LANES, LANES - target % LANES)
            pieces.setdefault(target // LANES, []).append((target % LANES, source // LANES, (target - source) % LANES))
            source, target, length = source + size, target + size, length - size
    loaded = {}
    turned = {}
    for tile in sorted(pieces):
        values = None
        for first, origin, shift in sorted(pieces[tile]):
            if origin not in loaded:
                loaded[origin] = load(origin)
            if (origin, shift) not in turned:
                turned[origin, shift] = pltpu.roll(loaded[origin], shift, 1) if shift else loaded[origin]
            piece = turned[origin, shift]
            values = piece if values is None else jnp.where(lane >= first, piece, values)
        store(tile, values)


def pack_chords(rows_ref, store):
    move_lanes(chord_moves(), lambda tile: rows_ref[pl.ds(tile, 8, stride=FLAT), :], store)


def unpack_chords(load, rows_ref):
    def store(tile, values):
        rows_ref[pl.ds(tile, 8, stride=FLAT), :] = values

    move_lanes([(target, source, length) for source, target, length in chord_moves()], load, store)


def parts_of(values):
    high = values.astype(jnp.bfloat16)
    low = (values - high.astype(jnp.float32)).astype(jnp.bfloat16)
    return high, low


def turn_z(values, table):
    high, low = parts_of(values)
    return jnp.dot(
        jnp.concatenate([high, low, high], axis=1), table, preferred_element_type=jnp.float32
    )


def turn_y(table, values):
    high, low = parts_of(values)
    return jnp.dot(
        table, jnp.concatenate([high, low, high], axis=0), preferred_element_type=jnp.float32
    )


def send_columns(planes_ref, slots, table_y, table_z, low_ref, high_ref):
    along_z = turn_z(planes_ref[:slots * SIDE, :], table_z)
    for slot in range(slots):
        rows = slice(slot * SIDE, (slot + 1) * SIDE)
        waves = turn_y(table_y, along_z[rows])
        low_ref[rows, :] = waves[:, :LANES]
        high_ref[rows, :] = waves[:, LANES:]
    low_ref[slots * SIDE:, :] = jnp.zeros(((SLOTS - slots) * SIDE, LANES), jnp.float32)
    high_ref[slots * SIDE:, :] = jnp.zeros(((SLOTS - slots) * SIDE, LANES), jnp.float32)


def chunk_of(low_ref, high_ref, first_row, pieces, extra):
    parts = []
    for row, start, stop in pieces:
        at = pl.ds(first_row + row, SLOTS, stride=SIDE)
        values = jnp.concatenate([low_ref[at, :], high_ref[at, :]], axis=1)
        parts.append(values[:, start:stop])
    return jnp.concatenate(parts + [extra], axis=1)


def layers_of(stored_ref, flat_ref):
    @pl.loop(0, FLAT // 8)
    def _(step):
        for part in range(8):
            lanes = pl.ds(pl.multiple_of((step * 8 + part) * LANES, LANES), LANES)
            flat_ref[pl.ds(step * 8 + part, SLOTS, stride=FLAT), :] = eight(stored_ref[:, lanes])


def place_of(start_ref):
    position = lax.axis_index("domain")
    return position, start_ref[position], start_ref[position + 1] - start_ref[position]


def pack_kernel(start_ref, potential_ref, orbitals_ref, v_ref, up_ref, down_ref, up_far_ref, down_far_ref,
                up_rows_ref, down_rows_ref, flat_ref, v_rows_ref, sems):
    _, _, thickness = place_of(start_ref)
    v_first = jnp.where(lax.axis_index("core") == 0, thickness - (HALO - 1), 0)
    first = jnp.maximum(thickness - HALO, 0)
    copies = []

    def copy(source, target):
        made = pltpu.make_async_copy(source, target, sems.at[len(copies)])
        made.start()
        copies.append(made)

    def layers(part, start, count):
        return orbitals_ref.at[part, pl.ds(pl.multiple_of(start * FLAT, 8), count * FLAT)]

    for part in range(2):
        rows = pl.ds(part * HALO * FLAT, HALO * FLAT)
        copy(layers(part, first, HALO), up_rows_ref.at[rows])
        copy(layers(part, 0, HALO), down_rows_ref.at[rows])
    for part in range(2):
        rows = pl.ds(part * FLAT, FLAT)
        copy(layers(part, thickness - 1, 1), up_far_ref.at[rows])
        copy(layers(part, 0, 1), down_far_ref.at[rows])
    layers_of(potential_ref, flat_ref)
    for layer in range(HALO - 1):
        v_rows_ref[layer * FLAT:(layer + 1) * FLAT, :] = flat_ref[
            pl.ds(pl.multiple_of((v_first + layer) * FLAT, 8), FLAT), :
        ]

    def store_v(tile, values):
        for layer in range(HALO - 1):
            v_ref[layer, tile:tile + 1, :] = values[layer:layer + 1]

    pack_chords(v_rows_ref, store_v)
    for made in copies[:4]:
        made.wait()
    for rows_ref, out_ref in ((up_rows_ref, up_ref), (down_rows_ref, down_ref)):

        def store(tile, values, out_ref=out_ref):
            out_ref[:, tile * LANES:(tile + 1) * LANES] = values

        pack_chords(rows_ref, store)
    for made in copies[4:]:
        made.wait()


def ions_kernel(count, length_cells, start_ref, background_ref, circle_ref, table_y_ref, table_z_ref,
                out_ref, flat_ref, planes_ref, low_ref, high_ref):
    _, own_start, thickness = place_of(start_ref)
    slots = background_ref.shape[0]
    groups, _, width = out_ref.shape
    layers_of(background_ref, flat_ref)

    def body(slot, total):
        def store(tile, low, high):
            rows = pl.ds(pl.multiple_of(slot * SIDE + tile * 8, 8), 8)
            planes_ref[rows, :LANES] = low
            planes_ref[rows, LANES:] = high

        to_plane(lambda k: flat_ref[pl.ds(slot * FLAT + k, 8, stride=STRIDE), :], store)
        rows = pl.ds(pl.multiple_of(slot * SIDE, 8), SIDE)
        inside = mesh_points(own_start + slot, circle_ref[...], length_cells) & (slot < thickness)
        values = jnp.where(inside, planes_ref[rows, :], 0.0)
        planes_ref[rows, :] = values
        return total + jnp.sum(values.reshape(RUN, 8, WIDTH), axis=0)

    total = lax.fori_loop(0, slots, body, jnp.zeros((8, WIDTH), jnp.float32))
    whole = jnp.broadcast_to(jnp.sum(total, keepdims=True), (SLOTS, LANES))[:, :width - count]
    send_columns(planes_ref, slots, table_y_ref[...], table_z_ref[...], low_ref, high_ref)
    core_rows = SIDE // lax.axis_size("core")
    first_row = lax.axis_index("core") * core_rows + lax.axis_index("row") * (core_rows // lax.axis_size("row"))
    for group in range(groups):
        out_ref[group] = chunk_of(low_ref, high_ref, first_row, column_pieces(group * count, count), whole)


def propagate_kernel(count, length_cells, start_ref, weight_ref, orbitals_ref, potential_ref, below_ref,
                     above_ref, below_far_ref, above_far_ref, v_ref, v_other_ref, circle_ref,
                     table_y_ref, table_z_ref, next_ref, density_kept_ref, density_sent_ref, kept_ref, sent_ref, first_ref, second_ref,
                     third_ref, fourth_ref, sum_ref, centre_ref, beside_ref, flat_ref, planes_ref, low_ref, high_ref,
                     below_rows_ref, above_rows_ref, v_rows_ref):
    position, own_start, thickness = place_of(start_ref)
    domains = lax.axis_size("domain")
    before = start_ref[jnp.maximum(position - 1, 0)]
    after = start_ref[jnp.minimum(position + 2, domains)]
    short_below = ((position > 0) & (own_start - before < HALO)).astype(jnp.int32)
    short_above = (position < domains - 1) & (after - own_start - thickness < HALO)
    weight = weight_ref[0]
    core = lax.axis_index("core")
    slots = orbitals_ref.shape[1]
    layers = slots + 2 * HALO
    devices, _, width = kept_ref.shape
    field_refs = (first_ref, second_ref, third_ref, fourth_ref)

    def field_layer(part, x_row):
        def store(tile, low, high):
            first_ref[part, x_row, 8 + 8 * tile:16 + 8 * tile, :LANES] = low
            first_ref[part, x_row, 8 + 8 * tile:16 + 8 * tile, LANES:] = high

        return store

    def potential_layer(x_row):
        def store(tile, low, high):
            centre_ref[x_row, 8 * tile:8 * tile + 8, :LANES] = low
            centre_ref[x_row, 8 * tile:8 * tile + 8, LANES:] = high

        return store

    def rows_from(ref, *at):
        return lambda k: ref[(*at, pl.ds(k, 8, stride=STRIDE), slice(None))]

    def layer_of(rows_ref, layer):
        return lambda k: rows_ref[pl.ds(layer * FLAT + k, 8, stride=STRIDE), :]

    for packed_ref, rows_ref in ((below_ref, below_rows_ref), (above_ref, above_rows_ref)):
        unpack_chords(
            lambda tile, packed_ref=packed_ref: packed_ref[:, tile * LANES:(tile + 1) * LANES], rows_ref
        )
    unpack_chords(
        lambda tile: eight(
            jnp.concatenate([ref[:, tile, :] for ref in (v_ref, v_other_ref)], axis=0)
        ),
        v_rows_ref,
    )

    layers_of(potential_ref, flat_ref)

    @pl.loop(0, slots)
    def _(slot):
        for part in range(2):
            to_plane(rows_from(orbitals_ref, part, slot), field_layer(part, HALO + slot))
        to_plane(layer_of(flat_ref, slot), potential_layer(HALO + slot))

    @pl.loop(0, HALO - 1)
    def _(layer):
        lower = 1 + layer
        upper = HALO + thickness + layer
        to_plane(layer_of(v_rows_ref, layer), potential_layer(jnp.where(core == 0, lower, upper)))
        to_plane(layer_of(v_rows_ref, HALO - 1 + layer), potential_layer(jnp.where(core == 0, upper, lower)))
        for part in range(2):
            to_plane(
                layer_of(below_rows_ref, part * HALO + 1 + layer - short_below), field_layer(part, 1 + layer)
            )
            to_plane(
                layer_of(above_rows_ref, part * HALO + layer), field_layer(part, HALO + thickness + layer)
            )

    @pl.loop(0, 2)
    def _(part):
        last = 2 * HALO - 1 + thickness

        @pl.when(short_below > 0)
        def _():
            to_plane(layer_of(below_far_ref, part), field_layer(part, 0))

        @pl.when(short_below == 0)
        def _():
            to_plane(layer_of(below_rows_ref, part * HALO), field_layer(part, 0))

        @pl.when(short_above)
        def _():
            to_plane(layer_of(above_far_ref, part), field_layer(part, last))

        @pl.when(jnp.logical_not(short_above))
        def _():
            to_plane(layer_of(above_rows_ref, part * HALO + HALO - 1), field_layer(part, last))

    def wrap(term, part, x_row):
        first = field_refs[term][part, x_row, 8:16, :]
        final = field_refs[term][part, x_row, SIDE:SIDE + 8, :]
        field_refs[term][part, x_row, :8, :] = pltpu.roll(final, 1, 0)
        field_refs[term][part, x_row, SIDE + 8:, :] = pltpu.roll(first, 7, 0)

    @pl.loop(0, layers)
    def _(x_row):
        known = x_row < thickness + 2 * HALO
        for block in range(SIDE // BLOCK):
            rows = slice(block * BLOCK, (block + 1) * BLOCK)
            inner = slice(8 + block * BLOCK, 8 + (block + 1) * BLOCK)
            inside = mesh_points(own_start - HALO + x_row, circle_ref[rows, :], length_cells) & known
            centre_ref[x_row, rows, :] = jnp.where(
                inside, (3.0 + centre_ref[x_row, rows, :]) * time_step, 0.0
            )
            beside_ref[x_row, rows, :] = jnp.where(inside, 0.5 * time_step, 0.0)
            for part in range(2):
                first_ref[part, x_row, inner, :] = jnp.where(
                    inside, first_ref[part, x_row, inner, :], 0.0
                )
        for part in range(2):
            wrap(0, part, x_row)

    def hamilton(term, part, x_row, block, centre, beside):
        field_ref = field_refs[term]
        tall = field_ref[part, x_row, block * BLOCK:block * BLOCK + BLOCK + 16, :]
        inner = slice(8 + block * BLOCK, 8 + (block + 1) * BLOCK)
        field = tall[8:8 + BLOCK]
        around = field_ref[part, x_row - 1, inner, :] + field_ref[part, x_row + 1, inner, :]
        around = around + (tall[:BLOCK] + tall[16:])
        around = around + (pltpu.roll(field, 1, 1) + pltpu.roll(field, WIDTH - 1, 1))
        return centre * field - beside * around

    for term in range(1, TERMS):

        @pl.loop(term, layers - term)
        def _(x_row, term=term):
            for block in range(SIDE // BLOCK):
                rows = slice(block * BLOCK, (block + 1) * BLOCK)
                inner = slice(8 + block * BLOCK, 8 + (block + 1) * BLOCK)
                centre = centre_ref[x_row, rows, :]
                beside = beside_ref[x_row, rows, :]
                for part in range(2):
                    field_refs[term][part, x_row, inner, :] = hamilton(
                        term - 1, part, x_row, block, centre, beside
                    )
            for part in range(2):
                wrap(term, part, x_row)

    def finish(slot, total):
        x_row = HALO + slot
        owned = slot < thickness
        for block in range(SIDE // BLOCK):
            rows = slice(block * BLOCK, (block + 1) * BLOCK)
            inner = slice(8 + block * BLOCK, 8 + (block + 1) * BLOCK)
            centre = centre_ref[x_row, rows, :]
            beside = beside_ref[x_row, rows, :]
            density = jnp.zeros((BLOCK, WIDTH), jnp.float32)
            for part, sign in ((0, 1.0), (1, -1.0)):
                summed = first_ref[part, x_row, inner, :]
                summed = summed + sign * second_ref[1 - part, x_row, inner, :]
                summed = summed - (1.0 / 2.0) * third_ref[part, x_row, inner, :]
                summed = summed - (sign / 6.0) * fourth_ref[1 - part, x_row, inner, :]
                summed = summed + (1.0 / 24.0) * hamilton(3, part, x_row, block, centre, beside)
                summed = jnp.where(owned, summed, 0.0)
                sum_ref[part, rows, :] = summed
                density = density + summed * summed
            density = weight * density
            planes_ref[pl.ds(pl.multiple_of(slot * SIDE + block * BLOCK, 8), BLOCK), :] = density
            total = total + jnp.sum(density.reshape(BLOCK // 8, 8, WIDTH), axis=0)

        for part in range(2):

            def load(tile, part=part):
                tall = sum_ref[part, 8 * tile:8 * tile + 8, :]
                return tall[:, :LANES], tall[:, LANES:]

            def store(k, values, part=part):
                next_ref[part, slot, pl.ds(k, 8, stride=STRIDE), :] = values

            to_flat(load, store)

        return total

    total = lax.fori_loop(0, slots, finish, jnp.zeros((8, WIDTH), jnp.float32))
    planes_ref[slots * SIDE:, :] = jnp.zeros(((SLOTS - slots) * SIDE, WIDTH), jnp.float32)

    @pl.loop(0, SLOTS // 2)
    def _(slot):
        for first, target_ref in ((core, density_kept_ref), (1 - core, density_sent_ref)):

            def load(tile, first=first):
                row = (first * (SLOTS // 2) + slot) * SIDE + tile * 8
                tall = planes_ref[pl.ds(pl.multiple_of(row, 8), 8), :]
                return tall[:, :LANES], tall[:, LANES:]

            def store(k, values, target_ref=target_ref):
                target_ref[slot, pl.ds(k, 8, stride=STRIDE), :] = values

            to_flat(load, store)

    whole = jnp.broadcast_to(jnp.sum(total, keepdims=True), (SLOTS, LANES))[:, :width - count]
    send_columns(planes_ref, slots, table_y_ref[...], table_z_ref[...], low_ref, high_ref)
    core_rows = SIDE // 2
    first_row = core * core_rows
    for device in range(devices):
        pieces = column_pieces(device * count, count)
        kept_ref[device] = chunk_of(low_ref, high_ref, first_row, pieces, whole)
        sent_ref[device] = chunk_of(low_ref, high_ref, core_rows - first_row, pieces, whole)


def wave_squared(index, count_cells):
    folded = jnp.where(2 * index <= count_cells, index, index - count_cells)
    wave_number = folded.astype(jnp.float32) * (two_pi / count_cells)
    return wave_number * wave_number


def coulomb_kernel(count, length_cells, start_ref, charge_ref, ions_ref, table_ref, out_ref):
    domains, _, width = ions_ref.shape
    states = charge_ref.shape[0] // domains
    device = (lax.axis_index("core") * states + lax.axis_index("row")) * domains + lax.axis_index("domain")
    charge = charge_ref[:domains]
    for state in range(1, states):
        charge = charge + charge_ref[state * domains:(state + 1) * domains]
    charge = charge.reshape(domains * SLOTS, width)
    ions = ions_ref[...].reshape(domains * SLOTS, width)
    first = lax.broadcasted_iota(jnp.int32, (domains * SLOTS, width), 0) % SLOTS == 0
    lane = lax.broadcasted_iota(jnp.int32, (domains * SLOTS, width), 1)
    chosen = first & (lane == count)
    electrons = jnp.sum(jnp.where(chosen, charge, 0.0), keepdims=True)
    ionic = jnp.sum(jnp.where(chosen, ions, 0.0), keepdims=True)
    charge = charge - (electrons / ionic) * ions
    layer = lax.broadcasted_iota(jnp.int32, (length_cells, domains * SLOTS), 0)
    place = lax.broadcasted_iota(jnp.int32, (length_cells, domains * SLOTS), 1)
    chosen_layer = jnp.full(layer.shape, -1, jnp.int32)
    for domain in range(domains):
        slot = place - domain * SLOTS
        here = (slot >= 0) & (slot < start_ref[domain + 1] - start_ref[domain])
        chosen_layer = jnp.where(here, start_ref[domain] + slot, chosen_layer)
    pick = (layer == chosen_layer).astype(jnp.float32)
    table = jnp.dot(table_ref[...], pick, precision=highest, preferred_element_type=jnp.float32)
    waves = jnp.dot(table, charge, precision=highest, preferred_element_type=jnp.float32)
    wave_x = lax.broadcasted_iota(jnp.int32, waves.shape, 0)
    column = device * count + lax.broadcasted_iota(jnp.int32, waves.shape, 1)
    wave_y = ((column.astype(jnp.float32) + 0.5) * (1.0 / SIDE)).astype(jnp.int32)
    wave_z = column - wave_y * SIDE
    squared = (
        wave_squared(wave_x, length_cells) + wave_squared(wave_y, SIDE) + wave_squared(wave_z, SIDE)
    )
    gain = jnp.where(squared > 0, four_pi / jnp.where(squared > 0, squared, 1.0), 0.0)
    waves = waves * (gain * (1.0 / (length_cells * SIDE * SIDE)))
    back = lax.dot_general(
        table, waves, (((0,), (0,)), ((), ())), precision=highest, preferred_element_type=jnp.float32
    )
    back = back.reshape(domains, SLOTS, width)
    for state in range(states):
        out_ref[state * domains:(state + 1) * domains] = back


def field_kernel(count, length_cells, start_ref, waves_ref, others_ref, density_ref, other_ref,
                 circle_ref, table_y_ref, table_z_ref, out_ref, low_ref, high_ref, planes_ref, flat_ref):
    _, own_start, thickness = place_of(start_ref)
    devices = waves_ref.shape[0]
    slots = out_ref.shape[0]
    core = lax.axis_index("core")
    core_rows = SIDE // 2
    first_row = core * core_rows
    for source_ref, first in ((waves_ref, first_row), (others_ref, core_rows - first_row)):
        pieces = []
        for device in range(devices):
            column = 0
            for row, start, stop in column_pieces(device * count, count):
                values = source_ref[device, :, column:column + stop - start]
                column += stop - start
                if start > 0:
                    pieces.append(values)
                    values = jnp.concatenate(pieces, axis=1)
                if stop < SIDE:
                    pieces = [values]
                    continue
                pieces = []
                at = pl.ds(first + row, SLOTS, stride=SIDE)
                low_ref[at, :] = values[:, :LANES]
                high_ref[at, :] = jnp.concatenate(
                    [values[:, LANES:], jnp.zeros((SLOTS, WIDTH - SIDE), jnp.float32)], axis=1
                )
    table_y = table_y_ref[...]
    table_z = table_z_ref[...]
    used = slice(0, slots * SIDE)
    along_z = turn_z(jnp.concatenate([low_ref[used, :], high_ref[used, :]], axis=1), table_z)
    for slot in range(slots):
        rows = slice(slot * SIDE, (slot + 1) * SIDE)
        planes_ref[rows, :] = turn_y(table_y, along_z[rows])

    @pl.loop(0, slots)
    def _(slot):
        def load(tile):
            tall = planes_ref[pl.ds(pl.multiple_of(slot * SIDE + tile * 8, 8), 8), :]
            return tall[:, :LANES], tall[:, LANES:]

        def store(k, values):
            flat_ref[pl.ds(slot * FLAT + k, 8, stride=STRIDE), :] = values

        to_flat(load, store)
        rows = pl.ds(pl.multiple_of(slot * FLAT, 8), FLAT)
        here = slot // (SLOTS // 2) == core
        kept_slot = slot % (SLOTS // 2)
        content = jnp.where(here, density_ref[kept_slot], other_ref[kept_slot]) * (3.0 / math.pi)
        positive = jnp.where(content > 0, content, 1.0)
        root = jnp.exp(jnp.log(positive) * (1.0 / 3.0))
        root = root - (root - positive / (root * root)) * (1.0 / 3.0)
        root = jnp.where(content > 0, root, 0.0)
        inside = mesh_points(own_start + slot, circle_ref[...], length_cells) & (slot < thickness)
        flat_ref[rows, :] = jnp.where(inside, flat_ref[rows, :] - root, 0.0)

    @pl.loop(0, FLAT // 8)
    def _(step):
        for part in range(8):
            lanes = pl.ds(pl.multiple_of((step * 8 + part) * LANES, LANES), LANES)
            out_ref[:, lanes] = flat_ref[pl.ds(step * 8 + part, SLOTS, stride=FLAT), :][:slots]


def from_behind(value, steps):
    count = lax.axis_size("domain")
    leading, last = (max(0, -steps), min(count, count - steps))
    return lax.ppermute(value, "domain", [(source, source + steps) for source in range(leading, last)])


def swapped(value, axis):
    return lax.ppermute(value, axis, [(0, 1), (1, 0)])


def shards(orbitals, occupation, potential, background, layer_start):
    domains = lax.axis_size("domain")
    rows = lax.axis_size("row")
    devices = domains * rows
    length_cells = SLAB * domains
    layer_cap, plane = potential.shape
    count = plane // (2 * devices)
    width = -(-(count + 1) // LANES) * LANES
    circle = jnp.asarray(circle_plane())
    flat_circle = jnp.asarray(circle_table().reshape(FLAT, LANES))
    table_z, into_y, out_of_y = (jnp.asarray(table) for table in tables_of_side())
    table_x = jnp.asarray(hartley_table(length_cells).astype(np.float32))
    params = pltpu.CompilerParams(vmem_limit_bytes=16 * MEBI)
    large = pltpu.CompilerParams(vmem_limit_bytes=40 * MEBI)

    def f32(*shape):
        return jax.ShapeDtypeStruct(shape, jnp.float32)

    def scratch(*shape):
        return pltpu.VMEM(shape, jnp.float32)

    layers = orbitals.reshape(2, layer_cap, FLAT, LANES)
    packed = packed_tiles()
    v_rows, up, down, up_far, down_far = pl.pallas_call(
        pack_kernel,
        out_shape=(
            f32(HALO - 1, packed, LANES),
            f32(2 * HALO, packed * LANES),
            f32(2 * HALO, packed * LANES),
            f32(2 * FLAT, LANES),
            f32(2 * FLAT, LANES),
        ),
        in_specs=[SMEM_SPEC, VMEM_SPEC, ANY_SPEC],
        out_specs=(VMEM_SPEC,) * 5,
        scratch_shapes=[scratch(FLAT * 8, LANES)] * 4 + [pltpu.SemaphoreType.DMA((8,))],
        compiler_params=params,
        name="pack_halo",
    )(layer_start, potential, orbitals.reshape(2, layer_cap * FLAT, LANES))
    v_rows = lax.ppermute(
        v_rows,
        ("core", "domain"),
        [(source, source + 1) for source in range(domains - 1)]
        + [(domains + source + 1, domains + source) for source in range(domains - 1)],
    )
    below = from_behind(up, 1)
    above = from_behind(down, -1)
    below_far = from_behind(up_far, 2)
    above_far = from_behind(down_far, -2)
    v_rows, below_far, above_far = lax.optimization_barrier((v_rows, below_far, above_far))
    v_others = swapped(v_rows, "core")

    ions = pl.pallas_call(
        functools.partial(ions_kernel, count, length_cells),
        out_shape=f32(domains, SLOTS, width),
        in_specs=[SMEM_SPEC] + [VMEM_SPEC] * 4,
        out_specs=VMEM_SPEC,
        scratch_shapes=[
            scratch(SLOTS * FLAT, LANES),
            scratch(layer_cap * SIDE, WIDTH),
            scratch(SLOTS * SIDE, LANES),
            scratch(SLOTS * SIDE, LANES),
        ],
        compiler_params=params,
        name="ion_waves",
    )(layer_start, background, circle, into_y, table_z)
    ions = lax.all_to_all(ions, "domain", split_axis=0, concat_axis=0, tiled=True)
    ions, below = lax.optimization_barrier((ions, below))

    span = layer_cap + 2 * HALO
    orbitals_next, density_kept, density_sent, kept, sent = pl.pallas_call(
        functools.partial(propagate_kernel, count, length_cells),
        out_shape=(
            f32(2, layer_cap, FLAT, LANES),
            f32(SLOTS // 2, FLAT, LANES),
            f32(SLOTS // 2, FLAT, LANES),
            f32(devices, SLOTS, width),
            f32(devices, SLOTS, width),
        ),
        in_specs=[SMEM_SPEC, SMEM_SPEC] + [VMEM_SPEC] * 11,
        out_specs=(VMEM_SPEC,) * 5,
        scratch_shapes=[
            scratch(2, span, TALL, WIDTH),
            scratch(2, span, TALL, WIDTH),
            scratch(2, span, TALL, WIDTH),
            scratch(2, span, TALL, WIDTH),
            scratch(2, SIDE, WIDTH),
            scratch(span, SIDE, WIDTH),
            scratch(span, SIDE, WIDTH),
            scratch(SLOTS * FLAT, LANES),
            scratch(SLOTS * SIDE, WIDTH),
            scratch(SLOTS * SIDE, LANES),
            scratch(SLOTS * SIDE, LANES),
            scratch(SLOTS * FLAT, LANES),
            scratch(SLOTS * FLAT, LANES),
            scratch(SLOTS * FLAT, LANES),
        ],
        compiler_params=large,
        name="propagate",
    )(layer_start, occupation, layers, potential, below, above, below_far, above_far, v_rows,
      v_others, circle, into_y, table_z)
    waves = kept + swapped(sent, "core")
    density = density_kept + swapped(density_sent, "core")
    waves = lax.all_to_all(waves, ("row", "domain"), split_axis=0, concat_axis=0, tiled=True)
    other_density = swapped(density, "row")
    waves = pl.pallas_call(
        functools.partial(coulomb_kernel, count, length_cells),
        out_shape=f32(devices, SLOTS, width),
        in_specs=[SMEM_SPEC] + [VMEM_SPEC] * 3,
        out_specs=VMEM_SPEC,
        compiler_params=params,
        name="coulomb",
    )(layer_start, waves, ions, table_x)
    waves, other_density = lax.optimization_barrier((waves, other_density))
    density = density + other_density
    other_density = swapped(density, "core")
    waves = lax.all_to_all(waves, ("row", "domain"), split_axis=0, concat_axis=0, tiled=True)
    other_waves = swapped(waves, "core")
    potential_next = pl.pallas_call(
        functools.partial(field_kernel, count, length_cells),
        out_shape=f32(layer_cap, plane),
        in_specs=[SMEM_SPEC] + [VMEM_SPEC] * 7,
        out_specs=VMEM_SPEC,
        scratch_shapes=[
            scratch(SLOTS * SIDE, LANES),
            scratch(SLOTS * SIDE, LANES),
            scratch(layer_cap * SIDE, WIDTH),
            scratch(SLOTS * FLAT, LANES),
        ],
        compiler_params=params,
        name="field",
    )(layer_start, waves, other_waves, density, other_density, flat_circle, out_of_y, table_z)
    return orbitals_next.reshape(orbitals.shape), potential_next


def solution(mesh):
    domains = mesh.shape["domain"]
    split = Mesh(mesh.devices.reshape(-1, 2, domains), ("row", "core", "domain"))
    states = ("row", "core")
    return jax.shard_map(
        shards,
        mesh=split,
        in_specs=(
            P(None, states, "domain", None),
            P(states),
            P("domain", None),
            P("domain", None),
            P(),
        ),
        out_specs=(P(None, states, "domain", None), P("domain", None)),
        check_vma=False,
    )
```

```python
import functools
import math

import jax
import jax.numpy as jnp
import ml_dtypes
import numpy as np
from jax import lax
from jax.experimental import pallas as pl
from jax.experimental.pallas import tpu as pltpu
from jax.sharding import Mesh, PartitionSpec as P

SIDE = 160
SLAB = 5
TERMS = 4

HALO = TERMS
LANES = 128
SLOTS = 8
RUN = SIDE // 8
FLAT = SIDE * SIDE // LANES
STRIDE = FLAT // 8
WIDTH = 2 * LANES
BLOCK = 32
TALL = SIDE + 16

time_step = 0.3
four_pi = 4.0 * math.pi
two_pi = 2.0 * math.pi
highest = lax.Precision.HIGHEST
MEBI = 1024 * 1024
SMEM_SPEC = pl.BlockSpec(memory_space=pltpu.SMEM)
VMEM_SPEC = pl.BlockSpec(memory_space=pltpu.VMEM)
HBM_SPEC = pl.BlockSpec(memory_space=pltpu.HBM)


def hartley_table(count_cells):
    index_run = np.arange(count_cells)
    angles = (index_run[:, None] * index_run[None, :] % count_cells) * (2.0 * np.pi / count_cells)
    return np.cos(angles) + np.sin(angles)


def plane_order():
    rows = np.arange(SIDE)
    return RUN * (rows % 8) + rows // 8


def two_parts(table):
    table = table.astype(np.float32)
    high = table.astype(ml_dtypes.bfloat16)
    low = (table - high.astype(np.float32)).astype(ml_dtypes.bfloat16)
    return high, low


def tables_of_side():
    table = hartley_table(SIDE)
    along_z = np.zeros((WIDTH, WIDTH))
    along_z[:SIDE, :SIDE] = table
    high, low = two_parts(along_z)
    along_z = np.concatenate([high, high, low], axis=0)
    high, low = two_parts(table[:, plane_order()])
    into_y = np.concatenate([high, high, low], axis=1)
    high, low = two_parts(table[plane_order(), :])
    out_of_y = np.concatenate([high, high, low], axis=1)
    return along_z, into_y, out_of_y


def circle_table():
    across = 2 * np.arange(SIDE, dtype=np.int64) - (SIDE - 1)
    return (across[:, None] ** 2 + across[None, :] ** 2).astype(np.int32)


def circle_plane():
    table = np.full((SIDE, WIDTH), 4 * SIDE * SIDE, np.int32)
    table[:, :SIDE] = circle_table()[plane_order()]
    return table


def mesh_points(x_row, circle, length_cells):
    room = ((length_cells - 2) ** 2 - (2 * x_row - (length_cells - 1)) ** 2) * (SIDE - 2) ** 2
    return (circle * (length_cells - 2) ** 2 <= room) & (circle < 4 * SIDE * SIDE)


def column_pieces(first, count):
    pieces = []
    column = first
    while column < first + count:
        row = column // SIDE
        stop = min((row + 1) * SIDE, first + count)
        pieces.append((row, column - row * SIDE, stop - row * SIDE))
        column = stop
    return pieces


def eight(values):
    missing = jnp.zeros((SLOTS - values.shape[0], values.shape[1]), values.dtype)
    return jnp.concatenate([values, missing], axis=0)


def to_plane(load, store):
    lane = lax.broadcasted_iota(jnp.int32, (8, LANES), 1)
    for step in range(RUN // 4):
        rows = [load(5 * step + part) for part in range(5)]
        store(4 * step, rows[0], rows[1])
        for part in range(1, 4):
            left = pltpu.roll(rows[part], LANES - 32 * part, 1)
            right = pltpu.roll(rows[part + 1], LANES - 32 * part, 1)
            store(4 * step + part, jnp.where(lane < LANES - 32 * part, left, right), right)


def to_flat(load, store):
    lane = lax.broadcasted_iota(jnp.int32, (8, LANES), 1)
    for step in range(RUN // 4):
        turned = []
        for part in range(4):
            low, high = load(4 * step + part)
            if part:
                low = pltpu.roll(low, 32 * part, 1)
                high = pltpu.roll(high, 32 * part, 1)
            turned.append((low, high))
        store(5 * step, turned[0][0])
        for part in range(1, 4):
            ended = 32 * (part - 1)
            values = jnp.where(lane < ended + 32, turned[part - 1][1], turned[part][0])
            if ended:
                values = jnp.where(lane < ended, turned[part - 1][0], values)
            store(5 * step + part, values)
        store(5 * step + 4, jnp.where(lane < 96, turned[3][0], turned[3][1]))


def chords():
    across = 2 * np.arange(SIDE, dtype=np.int64) - (SIDE - 1)
    room = (SIDE - 2) ** 2 - across**2
    return [max([w for w in range(1, SIDE // 2 + 1) if (2 * w - 1) ** 2 <= left], default=0) for left in room]


def chord_moves():
    moves = []
    packed = 0
    for row, half in enumerate(chords()):
        if half:
            moves.append((row * SIDE + SIDE // 2 - half, packed, 2 * half))
            packed += 2 * half
    return moves


def packed_tiles():
    _, start, length = chord_moves()[-1]
    return -(-(start + length) // LANES)


def move_lanes(moves, load, store):
    lane = lax.broadcasted_iota(jnp.int32, (8, LANES), 1)
    pieces = {}
    for source, target, length in moves:
        while length:
            size = min(length, LANES - source % LANES, LANES - target % LANES)
            pieces.setdefault(target // LANES, []).append((target % LANES, source // LANES, (target - source) % LANES))
            source, target, length = source + size, target + size, length - size
    loaded = {}
    turned = {}
    for tile in sorted(pieces):
        values = None
        for first, origin, shift in sorted(pieces[tile]):
            if origin not in loaded:
                loaded[origin] = load(origin)
            if (origin, shift) not in turned:
                turned[origin, shift] = pltpu.roll(loaded[origin], shift, 1) if shift else loaded[origin]
            piece = turned[origin, shift]
            values = piece if values is None else jnp.where(lane >= first, piece, values)
        store(tile, values)


def pack_chords(rows_ref, store):
    move_lanes(chord_moves(), lambda tile: rows_ref[pl.ds(tile, 8, stride=FLAT), :], store)


def unpack_chords(load, rows_ref):
    def store(tile, values):
        rows_ref[pl.ds(tile, 8, stride=FLAT), :] = values

    move_lanes([(target, source, length) for source, target, length in chord_moves()], load, store)


def parts_of(values):
    high = values.astype(jnp.bfloat16)
    low = (values - high.astype(jnp.float32)).astype(jnp.bfloat16)
    return high, low


def turn_z(values, table):
    high, low = parts_of(values)
    return jnp.dot(
        jnp.concatenate([high, low, high], axis=1), table, preferred_element_type=jnp.float32
    )


def turn_y(table, values):
    high, low = parts_of(values)
    return jnp.dot(
        table, jnp.concatenate([high, low, high], axis=0), preferred_element_type=jnp.float32
    )


def send_columns(planes_ref, slots, table_y, table_z, low_ref, high_ref):
    along_z = turn_z(planes_ref[:slots * SIDE, :], table_z)
    for slot in range(slots):
        rows = slice(slot * SIDE, (slot + 1) * SIDE)
        waves = turn_y(table_y, along_z[rows])
        low_ref[rows, :] = waves[:, :LANES]
        high_ref[rows, :] = waves[:, LANES:]
    low_ref[slots * SIDE:, :] = jnp.zeros(((SLOTS - slots) * SIDE, LANES), jnp.float32)
    high_ref[slots * SIDE:, :] = jnp.zeros(((SLOTS - slots) * SIDE, LANES), jnp.float32)


def chunk_of(low_ref, high_ref, first_row, pieces, extra):
    parts = []
    for row, start, stop in pieces:
        at = pl.ds(first_row + row, SLOTS, stride=SIDE)
        values = jnp.concatenate([low_ref[at, :], high_ref[at, :]], axis=1)
        parts.append(values[:, start:stop])
    return jnp.concatenate(parts + [extra], axis=1)


def layers_of(stored_ref, flat_ref):
    @pl.loop(0, FLAT // 8)
    def _(step):
        for part in range(8):
            lanes = pl.ds(pl.multiple_of((step * 8 + part) * LANES, LANES), LANES)
            flat_ref[pl.ds(step * 8 + part, SLOTS, stride=FLAT), :] = eight(stored_ref[:, lanes])


def place_of(start_ref):
    position = lax.axis_index("domain")
    return position, start_ref[position], start_ref[position + 1] - start_ref[position]


def started(sems, pairs):
    copies = [pltpu.make_async_copy(*pair, sems.at[index]) for index, pair in enumerate(pairs)]
    for made in copies:
        made.start()
    return copies


def pack_kernel(start_ref, potential_ref, orbitals_ref, v_ref, up_ref, down_ref, up_far_ref, down_far_ref,
                up_rows_ref, down_rows_ref, flat_ref, v_rows_ref, stored_ref, v_buffer_ref, up_buffer_ref,
                down_buffer_ref, up_far_buffer_ref, down_far_buffer_ref, in_sems, out_sems):
    _, _, thickness = place_of(start_ref)
    v_first = jnp.where(lax.axis_index("core") == 0, thickness - (HALO - 1), 0)
    first = jnp.maximum(thickness - HALO, 0)

    def layers(part, start, count):
        return orbitals_ref.at[part, pl.ds(pl.multiple_of(start * FLAT, 8), count * FLAT)]

    def rows(part, count):
        return pl.ds(part * count * FLAT, count * FLAT)

    arrivals = started(
        in_sems,
        [(layers(part, first, HALO), up_rows_ref.at[rows(part, HALO)]) for part in range(2)]
        + [(layers(part, 0, HALO), down_rows_ref.at[rows(part, HALO)]) for part in range(2)]
        + [(layers(part, thickness - 1, 1), up_far_buffer_ref.at[rows(part, 1)]) for part in range(2)]
        + [(layers(part, 0, 1), down_far_buffer_ref.at[rows(part, 1)]) for part in range(2)]
        + [(potential_ref, stored_ref)],
    )
    departures = [
        pltpu.make_async_copy(source, target, out_sems.at[index])
        for index, (source, target) in enumerate(
            (
                (up_buffer_ref, up_ref),
                (down_buffer_ref, down_ref),
                (up_far_buffer_ref, up_far_ref),
                (down_far_buffer_ref, down_far_ref),
                (v_buffer_ref, v_ref),
            )
        )
    ]
    for index, (rows_ref, buffer_ref) in enumerate(
        ((up_rows_ref, up_buffer_ref), (down_rows_ref, down_buffer_ref))
    ):
        arrivals[2 * index].wait()
        arrivals[2 * index + 1].wait()

        def store(tile, values, buffer_ref=buffer_ref):
            buffer_ref[:, tile * LANES:(tile + 1) * LANES] = values

        pack_chords(rows_ref, store)
        departures[index].start()
    for made in arrivals[4:]:
        made.wait()
    departures[2].start()
    departures[3].start()
    layers_of(stored_ref, flat_ref)
    for layer in range(HALO - 1):
        v_rows_ref[layer * FLAT:(layer + 1) * FLAT, :] = flat_ref[
            pl.ds(pl.multiple_of((v_first + layer) * FLAT, 8), FLAT), :
        ]

    def store_v(tile, values):
        for layer in range(HALO - 1):
            v_buffer_ref[layer, tile:tile + 1, :] = values[layer:layer + 1]

    pack_chords(v_rows_ref, store_v)
    departures[4].start()
    for made in departures:
        made.wait()


def ions_kernel(count, length_cells, start_ref, background_ref, circle_ref, table_y_ref, table_z_ref,
                out_ref, flat_ref, planes_ref, low_ref, high_ref):
    _, own_start, thickness = place_of(start_ref)
    slots = background_ref.shape[0]
    groups, _, width = out_ref.shape
    layers_of(background_ref, flat_ref)

    def body(slot, total):
        def store(tile, low, high):
            rows = pl.ds(pl.multiple_of(slot * SIDE + tile * 8, 8), 8)
            planes_ref[rows, :LANES] = low
            planes_ref[rows, LANES:] = high

        to_plane(lambda k: flat_ref[pl.ds(slot * FLAT + k, 8, stride=STRIDE), :], store)
        rows = pl.ds(pl.multiple_of(slot * SIDE, 8), SIDE)
        inside = mesh_points(own_start + slot, circle_ref[...], length_cells) & (slot < thickness)
        values = jnp.where(inside, planes_ref[rows, :], 0.0)
        planes_ref[rows, :] = values
        return total + jnp.sum(values.reshape(RUN, 8, WIDTH), axis=0)

    total = lax.fori_loop(0, slots, body, jnp.zeros((8, WIDTH), jnp.float32))
    whole = jnp.broadcast_to(jnp.sum(total, keepdims=True), (SLOTS, LANES))[:, :width - count]
    send_columns(planes_ref, slots, table_y_ref[...], table_z_ref[...], low_ref, high_ref)
    core_rows = SIDE // lax.axis_size("core")
    first_row = lax.axis_index("core") * core_rows + lax.axis_index("row") * (core_rows // lax.axis_size("row"))
    for group in range(groups):
        out_ref[group] = chunk_of(low_ref, high_ref, first_row, column_pieces(group * count, count), whole)


def propagate_kernel(count, length_cells, start_ref, weight_ref, orbitals_ref, potential_ref, below_hbm_ref,
                     above_hbm_ref, below_far_hbm_ref, above_far_hbm_ref, v_hbm_ref, v_other_hbm_ref,
                     circle_ref, table_y_ref, table_z_ref, psi_ref, kept_ref, sent_ref, first_ref, second_ref,
                     third_ref, fourth_ref, sum_ref, centre_ref, beside_ref, flat_ref, planes_ref, low_ref,
                     high_ref, below_rows_ref, above_rows_ref, v_rows_ref, v_ref, v_other_ref, below_ref,
                     above_ref, below_far_ref, above_far_ref, in_sems, out_sem):
    arrivals = started(
        in_sems,
        [
            (v_hbm_ref, v_ref),
            (v_other_hbm_ref, v_other_ref),
            (below_hbm_ref, below_ref),
            (above_hbm_ref, above_ref),
            (below_far_hbm_ref, below_far_ref),
            (above_far_hbm_ref, above_far_ref),
        ],
    )
    position, own_start, thickness = place_of(start_ref)
    domains = lax.axis_size("domain")
    before = start_ref[jnp.maximum(position - 1, 0)]
    after = start_ref[jnp.minimum(position + 2, domains)]
    short_below = ((position > 0) & (own_start - before < HALO)).astype(jnp.int32)
    short_above = (position < domains - 1) & (after - own_start - thickness < HALO)
    weight = weight_ref[0]
    core = lax.axis_index("core")
    slots = orbitals_ref.shape[1]
    layers = slots + 2 * HALO
    devices, _, width = kept_ref.shape
    field_refs = (first_ref, second_ref, third_ref, fourth_ref)

    def field_layer(part, x_row):
        def store(tile, low, high):
            first_ref[part, x_row, 8 + 8 * tile:16 + 8 * tile, :LANES] = low
            first_ref[part, x_row, 8 + 8 * tile:16 + 8 * tile, LANES:] = high

        return store

    def potential_layer(x_row):
        def store(tile, low, high):
            centre_ref[x_row, 8 * tile:8 * tile + 8, :LANES] = low
            centre_ref[x_row, 8 * tile:8 * tile + 8, LANES:] = high

        return store

    def rows_from(ref, *at):
        return lambda k: ref[(*at, pl.ds(k, 8, stride=STRIDE), slice(None))]

    def layer_of(rows_ref, layer):
        return lambda k: rows_ref[pl.ds(layer * FLAT + k, 8, stride=STRIDE), :]

    layers_of(potential_ref, flat_ref)

    @pl.loop(0, slots)
    def _(slot):
        for part in range(2):
            to_plane(rows_from(orbitals_ref, part, slot), field_layer(part, HALO + slot))
        to_plane(layer_of(flat_ref, slot), potential_layer(HALO + slot))

    for made in arrivals:
        made.wait()
    for packed_ref, rows_ref in ((below_ref, below_rows_ref), (above_ref, above_rows_ref)):
        unpack_chords(
            lambda tile, packed_ref=packed_ref: packed_ref[:, tile * LANES:(tile + 1) * LANES], rows_ref
        )
    unpack_chords(
        lambda tile: eight(
            jnp.concatenate([ref[:, tile, :] for ref in (v_ref, v_other_ref)], axis=0)
        ),
        v_rows_ref,
    )

    @pl.loop(0, HALO - 1)
    def _(layer):
        lower = 1 + layer
        upper = HALO + thickness + layer
        to_plane(layer_of(v_rows_ref, layer), potential_layer(jnp.where(core == 0, lower, upper)))
        to_plane(layer_of(v_rows_ref, HALO - 1 + layer), potential_layer(jnp.where(core == 0, upper, lower)))
        for part in range(2):
            to_plane(
                layer_of(below_rows_ref, part * HALO + 1 + layer - short_below), field_layer(part, 1 + layer)
            )
            to_plane(
                layer_of(above_rows_ref, part * HALO + layer), field_layer(part, HALO + thickness + layer)
            )

    @pl.loop(0, 2)
    def _(part):
        last = 2 * HALO - 1 + thickness

        @pl.when(short_below > 0)
        def _():
            to_plane(layer_of(below_far_ref, part), field_layer(part, 0))

        @pl.when(short_below == 0)
        def _():
            to_plane(layer_of(below_rows_ref, part * HALO), field_layer(part, 0))

        @pl.when(short_above)
        def _():
            to_plane(layer_of(above_far_ref, part), field_layer(part, last))

        @pl.when(jnp.logical_not(short_above))
        def _():
            to_plane(layer_of(above_rows_ref, part * HALO + HALO - 1), field_layer(part, last))

    def wrap(term, part, x_row):
        first = field_refs[term][part, x_row, 8:16, :]
        final = field_refs[term][part, x_row, SIDE:SIDE + 8, :]
        field_refs[term][part, x_row, :8, :] = pltpu.roll(final, 1, 0)
        field_refs[term][part, x_row, SIDE + 8:, :] = pltpu.roll(first, 7, 0)

    @pl.loop(0, layers)
    def _(x_row):
        known = x_row < thickness + 2 * HALO
        for block in range(SIDE // BLOCK):
            rows = slice(block * BLOCK, (block + 1) * BLOCK)
            inner = slice(8 + block * BLOCK, 8 + (block + 1) * BLOCK)
            inside = mesh_points(own_start - HALO + x_row, circle_ref[rows, :], length_cells) & known
            centre_ref[x_row, rows, :] = jnp.where(
                inside, (3.0 + centre_ref[x_row, rows, :]) * time_step, 0.0
            )
            beside_ref[x_row, rows, :] = jnp.where(inside, 0.5 * time_step, 0.0)
            for part in range(2):
                first_ref[part, x_row, inner, :] = jnp.where(
                    inside, first_ref[part, x_row, inner, :], 0.0
                )
        for part in range(2):
            wrap(0, part, x_row)

    def hamilton(term, part, x_row, block, centre, beside):
        field_ref = field_refs[term]
        tall = field_ref[part, x_row, block * BLOCK:block * BLOCK + BLOCK + 16, :]
        inner = slice(8 + block * BLOCK, 8 + (block + 1) * BLOCK)
        field = tall[8:8 + BLOCK]
        around = field_ref[part, x_row - 1, inner, :] + field_ref[part, x_row + 1, inner, :]
        around = around + (tall[:BLOCK] + tall[16:])
        around = around + (pltpu.roll(field, 1, 1) + pltpu.roll(field, WIDTH - 1, 1))
        return centre * field - beside * around

    for term in range(1, TERMS):

        @pl.loop(term, layers - term)
        def _(x_row, term=term):
            for block in range(SIDE // BLOCK):
                rows = slice(block * BLOCK, (block + 1) * BLOCK)
                inner = slice(8 + block * BLOCK, 8 + (block + 1) * BLOCK)
                centre = centre_ref[x_row, rows, :]
                beside = beside_ref[x_row, rows, :]
                for part in range(2):
                    field_refs[term][part, x_row, inner, :] = hamilton(
                        term - 1, part, x_row, block, centre, beside
                    )
            for part in range(2):
                wrap(term, part, x_row)

    def finish(slot, total):
        x_row = HALO + slot
        owned = slot < thickness
        for block in range(SIDE // BLOCK):
            rows = slice(block * BLOCK, (block + 1) * BLOCK)
            inner = slice(8 + block * BLOCK, 8 + (block + 1) * BLOCK)
            centre = centre_ref[x_row, rows, :]
            beside = beside_ref[x_row, rows, :]
            density = jnp.zeros((BLOCK, WIDTH), jnp.float32)
            for part, sign in ((0, 1.0), (1, -1.0)):
                summed = first_ref[part, x_row, inner, :]
                summed = summed + sign * second_ref[1 - part, x_row, inner, :]
                summed = summed - (1.0 / 2.0) * third_ref[part, x_row, inner, :]
                summed = summed - (sign / 6.0) * fourth_ref[1 - part, x_row, inner, :]
                summed = summed + (1.0 / 24.0) * hamilton(3, part, x_row, block, centre, beside)
                summed = jnp.where(owned, summed, 0.0)
                sum_ref[part, slot, rows, :] = summed
                density = density + summed * summed
            density = weight * density
            planes_ref[pl.ds(pl.multiple_of(slot * SIDE + block * BLOCK, 8), BLOCK), :] = density
            total = total + jnp.sum(density.reshape(BLOCK // 8, 8, WIDTH), axis=0)

        return total

    total = lax.fori_loop(0, slots, finish, jnp.zeros((8, WIDTH), jnp.float32))
    departure = pltpu.make_async_copy(sum_ref, psi_ref, out_sem)
    departure.start()
    whole = jnp.broadcast_to(jnp.sum(total, keepdims=True), (SLOTS, LANES))[:, :width - count]
    send_columns(planes_ref, slots, table_y_ref[...], table_z_ref[...], low_ref, high_ref)
    core_rows = SIDE // 2
    first_row = core * core_rows
    for device in range(devices):
        pieces = column_pieces(device * count, count)
        kept_ref[device] = chunk_of(low_ref, high_ref, first_row, pieces, whole)
        sent_ref[device] = chunk_of(low_ref, high_ref, core_rows - first_row, pieces, whole)
    departure.wait()


def unpack_kernel(weight_ref, psi_ref, next_ref, density_kept_ref, density_sent_ref, density_ref):
    core = lax.axis_index("core")
    weight = weight_ref[0]
    slots = psi_ref.shape[1]

    @pl.loop(0, slots)
    def _(slot):
        for part in range(2):

            def load(tile, part=part):
                tall = psi_ref[part, slot, 8 * tile:8 * tile + 8, :]
                return tall[:, :LANES], tall[:, LANES:]

            def store(k, values, part=part):
                next_ref[part, slot, pl.ds(k, 8, stride=STRIDE), :] = values

            to_flat(load, store)
        real = next_ref[0, slot]
        imag = next_ref[1, slot]
        density_ref[slot] = weight * (real * real + imag * imag)

    for slot in range(slots, SLOTS):
        density_ref[slot] = jnp.zeros((FLAT, LANES), jnp.float32)

    @pl.loop(0, SLOTS // 2)
    def _(slot):
        density_kept_ref[slot] = density_ref[core * (SLOTS // 2) + slot]
        density_sent_ref[slot] = density_ref[(1 - core) * (SLOTS // 2) + slot]


def wave_squared(index, count_cells):
    folded = jnp.where(2 * index <= count_cells, index, index - count_cells)
    wave_number = folded.astype(jnp.float32) * (two_pi / count_cells)
    return wave_number * wave_number


def coulomb_kernel(count, length_cells, start_ref, charge_ref, ions_ref, table_ref, out_ref):
    domains, _, width = ions_ref.shape
    states = charge_ref.shape[0] // domains
    device = (lax.axis_index("core") * states + lax.axis_index("row")) * domains + lax.axis_index("domain")
    charge = charge_ref[:domains]
    for state in range(1, states):
        charge = charge + charge_ref[state * domains:(state + 1) * domains]
    charge = charge.reshape(domains * SLOTS, width)
    ions = ions_ref[...].reshape(domains * SLOTS, width)
    first = lax.broadcasted_iota(jnp.int32, (domains * SLOTS, width), 0) % SLOTS == 0
    lane = lax.broadcasted_iota(jnp.int32, (domains * SLOTS, width), 1)
    chosen = first & (lane == count)
    electrons = jnp.sum(jnp.where(chosen, charge, 0.0), keepdims=True)
    ionic = jnp.sum(jnp.where(chosen, ions, 0.0), keepdims=True)
    charge = charge - (electrons / ionic) * ions
    layer = lax.broadcasted_iota(jnp.int32, (length_cells, domains * SLOTS), 0)
    place = lax.broadcasted_iota(jnp.int32, (length_cells, domains * SLOTS), 1)
    chosen_layer = jnp.full(layer.shape, -1, jnp.int32)
    for domain in range(domains):
        slot = place - domain * SLOTS
        here = (slot >= 0) & (slot < start_ref[domain + 1] - start_ref[domain])
        chosen_layer = jnp.where(here, start_ref[domain] + slot, chosen_layer)
    pick = (layer == chosen_layer).astype(jnp.float32)
    table = jnp.dot(table_ref[...], pick, precision=highest, preferred_element_type=jnp.float32)
    waves = jnp.dot(table, charge, precision=highest, preferred_element_type=jnp.float32)
    wave_x = lax.broadcasted_iota(jnp.int32, waves.shape, 0)
    column = device * count + lax.broadcasted_iota(jnp.int32, waves.shape, 1)
    wave_y = ((column.astype(jnp.float32) + 0.5) * (1.0 / SIDE)).astype(jnp.int32)
    wave_z = column - wave_y * SIDE
    squared = (
        wave_squared(wave_x, length_cells) + wave_squared(wave_y, SIDE) + wave_squared(wave_z, SIDE)
    )
    gain = jnp.where(squared > 0, four_pi / jnp.where(squared > 0, squared, 1.0), 0.0)
    waves = waves * (gain * (1.0 / (length_cells * SIDE * SIDE)))
    back = lax.dot_general(
        table, waves, (((0,), (0,)), ((), ())), precision=highest, preferred_element_type=jnp.float32
    )
    back = back.reshape(domains, SLOTS, width)
    for state in range(states):
        out_ref[state * domains:(state + 1) * domains] = back


def field_kernel(count, length_cells, start_ref, waves_ref, others_ref, density_ref, other_ref,
                 circle_ref, table_y_ref, table_z_ref, out_ref, low_ref, high_ref, planes_ref, flat_ref):
    _, own_start, thickness = place_of(start_ref)
    devices = waves_ref.shape[0]
    slots = out_ref.shape[0]
    core = lax.axis_index("core")
    core_rows = SIDE // 2
    first_row = core * core_rows
    for source_ref, first in ((waves_ref, first_row), (others_ref, core_rows - first_row)):
        pieces = []
        for device in range(devices):
            column = 0
            for row, start, stop in column_pieces(device * count, count):
                values = source_ref[device, :, column:column + stop - start]
                column += stop - start
                if start > 0:
                    pieces.append(values)
                    values = jnp.concatenate(pieces, axis=1)
                if stop < SIDE:
                    pieces = [values]
                    continue
                pieces = []
                at = pl.ds(first + row, SLOTS, stride=SIDE)
                low_ref[at, :] = values[:, :LANES]
                high_ref[at, :] = jnp.concatenate(
                    [values[:, LANES:], jnp.zeros((SLOTS, WIDTH - SIDE), jnp.float32)], axis=1
                )
    table_y = table_y_ref[...]
    table_z = table_z_ref[...]
    used = slice(0, slots * SIDE)
    along_z = turn_z(jnp.concatenate([low_ref[used, :], high_ref[used, :]], axis=1), table_z)
    for slot in range(slots):
        rows = slice(slot * SIDE, (slot + 1) * SIDE)
        planes_ref[rows, :] = turn_y(table_y, along_z[rows])

    @pl.loop(0, slots)
    def _(slot):
        def load(tile):
            tall = planes_ref[pl.ds(pl.multiple_of(slot * SIDE + tile * 8, 8), 8), :]
            return tall[:, :LANES], tall[:, LANES:]

        def store(k, values):
            flat_ref[pl.ds(slot * FLAT + k, 8, stride=STRIDE), :] = values

        to_flat(load, store)
        rows = pl.ds(pl.multiple_of(slot * FLAT, 8), FLAT)
        here = slot // (SLOTS // 2) == core
        kept_slot = slot % (SLOTS // 2)
        content = jnp.where(here, density_ref[kept_slot], other_ref[kept_slot]) * (3.0 / math.pi)
        positive = jnp.where(content > 0, content, 1.0)
        root = jnp.exp(jnp.log(positive) * (1.0 / 3.0))
        root = root - (root - positive / (root * root)) * (1.0 / 3.0)
        root = jnp.where(content > 0, root, 0.0)
        inside = mesh_points(own_start + slot, circle_ref[...], length_cells) & (slot < thickness)
        flat_ref[rows, :] = jnp.where(inside, flat_ref[rows, :] - root, 0.0)

    @pl.loop(0, FLAT // 8)
    def _(step):
        for part in range(8):
            lanes = pl.ds(pl.multiple_of((step * 8 + part) * LANES, LANES), LANES)
            out_ref[:, lanes] = flat_ref[pl.ds(step * 8 + part, SLOTS, stride=FLAT), :][:slots]


def from_behind(value, steps):
    count = lax.axis_size("domain")
    leading, last = (max(0, -steps), min(count, count - steps))
    return lax.ppermute(value, "domain", [(source, source + steps) for source in range(leading, last)])


def swapped(value, axis):
    return lax.ppermute(value, axis, [(0, 1), (1, 0)])


def shards(orbitals, occupation, potential, background, layer_start):
    domains = lax.axis_size("domain")
    rows = lax.axis_size("row")
    devices = domains * rows
    length_cells = SLAB * domains
    layer_cap, plane = potential.shape
    count = plane // (2 * devices)
    width = -(-(count + 1) // LANES) * LANES
    circle = jnp.asarray(circle_plane())
    flat_circle = jnp.asarray(circle_table().reshape(FLAT, LANES))
    table_z, into_y, out_of_y = (jnp.asarray(table) for table in tables_of_side())
    table_x = jnp.asarray(hartley_table(length_cells).astype(np.float32))
    params = pltpu.CompilerParams(vmem_limit_bytes=16 * MEBI)
    large = pltpu.CompilerParams(vmem_limit_bytes=44 * MEBI)
    whole = pltpu.CompilerParams(vmem_limit_bytes=56 * MEBI)

    def f32(*shape):
        return jax.ShapeDtypeStruct(shape, jnp.float32)

    def scratch(*shape):
        return pltpu.VMEM(shape, jnp.float32)

    layers = orbitals.reshape(2, layer_cap, FLAT, LANES)
    packed = packed_tiles()
    v_rows, up, down, up_far, down_far = pl.pallas_call(
        pack_kernel,
        out_shape=(
            f32(HALO - 1, packed, LANES),
            f32(2 * HALO, packed * LANES),
            f32(2 * HALO, packed * LANES),
            f32(2 * FLAT, LANES),
            f32(2 * FLAT, LANES),
        ),
        in_specs=[SMEM_SPEC, HBM_SPEC, HBM_SPEC],
        out_specs=(HBM_SPEC,) * 5,
        scratch_shapes=[scratch(FLAT * 8, LANES)] * 4
        + [
            scratch(layer_cap, plane),
            scratch(HALO - 1, packed, LANES),
            scratch(2 * HALO, packed * LANES),
            scratch(2 * HALO, packed * LANES),
            scratch(2 * FLAT, LANES),
            scratch(2 * FLAT, LANES),
            pltpu.SemaphoreType.DMA((9,)),
            pltpu.SemaphoreType.DMA((5,)),
        ],
        compiler_params=whole,
        name="pack_halo",
    )(layer_start, potential, orbitals.reshape(2, layer_cap * FLAT, LANES))
    v_rows = lax.ppermute(
        v_rows,
        ("core", "domain"),
        [(source, source + 1) for source in range(domains - 1)]
        + [(domains + source + 1, domains + source) for source in range(domains - 1)],
    )
    below = from_behind(up, 1)
    above = from_behind(down, -1)
    below_far = from_behind(up_far, 2)
    above_far = from_behind(down_far, -2)
    v_rows, below_far, above_far = lax.optimization_barrier((v_rows, below_far, above_far))
    v_others = swapped(v_rows, "core")

    ions = pl.pallas_call(
        functools.partial(ions_kernel, count, length_cells),
        out_shape=f32(domains, SLOTS, width),
        in_specs=[SMEM_SPEC] + [VMEM_SPEC] * 4,
        out_specs=VMEM_SPEC,
        scratch_shapes=[
            scratch(SLOTS * FLAT, LANES),
            scratch(layer_cap * SIDE, WIDTH),
            scratch(SLOTS * SIDE, LANES),
            scratch(SLOTS * SIDE, LANES),
        ],
        compiler_params=params,
        name="ion_waves",
    )(layer_start, background, circle, into_y, table_z)
    ions = lax.all_to_all(ions, "domain", split_axis=0, concat_axis=0, tiled=True)
    ions, below = lax.optimization_barrier((ions, below))

    span = layer_cap + 2 * HALO
    fields = (2, span, TALL, WIDTH)
    psi, kept, sent = pl.pallas_call(
        functools.partial(propagate_kernel, count, length_cells),
        out_shape=(
            f32(2, layer_cap, SIDE, WIDTH),
            f32(devices, SLOTS, width),
            f32(devices, SLOTS, width),
        ),
        in_specs=[SMEM_SPEC, SMEM_SPEC, VMEM_SPEC, VMEM_SPEC] + [HBM_SPEC] * 6 + [VMEM_SPEC] * 3,
        out_specs=(HBM_SPEC, VMEM_SPEC, VMEM_SPEC),
        scratch_shapes=[scratch(*fields)] * TERMS
        + [
            scratch(2, layer_cap, SIDE, WIDTH),
            scratch(span, SIDE, WIDTH),
            scratch(span, SIDE, WIDTH),
            scratch(SLOTS * FLAT, LANES),
            scratch(layer_cap * SIDE, WIDTH),
            scratch(SLOTS * SIDE, LANES),
            scratch(SLOTS * SIDE, LANES),
            scratch(SLOTS * FLAT, LANES),
            scratch(SLOTS * FLAT, LANES),
            scratch(SLOTS * FLAT, LANES),
            scratch(HALO - 1, packed, LANES),
            scratch(HALO - 1, packed, LANES),
            scratch(2 * HALO, packed * LANES),
            scratch(2 * HALO, packed * LANES),
            scratch(2 * FLAT, LANES),
            scratch(2 * FLAT, LANES),
            pltpu.SemaphoreType.DMA((6,)),
            pltpu.SemaphoreType.DMA,
        ],
        compiler_params=large,
        name="propagate",
    )(layer_start, occupation, layers, potential, below, above, below_far, above_far, v_rows, v_others,
      circle, into_y, table_z)
    waves = kept + swapped(sent, "core")
    waves, psi = lax.optimization_barrier((waves, psi))
    waves = lax.all_to_all(waves, ("row", "domain"), split_axis=0, concat_axis=0, tiled=True)
    orbitals_next, density_kept, density_sent = pl.pallas_call(
        unpack_kernel,
        out_shape=(
            f32(2, layer_cap, FLAT, LANES),
            f32(SLOTS // 2, FLAT, LANES),
            f32(SLOTS // 2, FLAT, LANES),
        ),
        in_specs=[SMEM_SPEC, VMEM_SPEC],
        out_specs=(VMEM_SPEC,) * 3,
        scratch_shapes=[scratch(SLOTS, FLAT, LANES)],
        compiler_params=params,
        name="unpack",
    )(occupation, psi)
    density = density_kept + swapped(density_sent, "core")
    other_density = swapped(density, "row")
    waves = pl.pallas_call(
        functools.partial(coulomb_kernel, count, length_cells),
        out_shape=f32(devices, SLOTS, width),
        in_specs=[SMEM_SPEC] + [VMEM_SPEC] * 3,
        out_specs=VMEM_SPEC,
        compiler_params=params,
        name="coulomb",
    )(layer_start, waves, ions, table_x)
    waves, other_density = lax.optimization_barrier((waves, other_density))
    density = density + other_density
    other_density = swapped(density, "core")
    waves = lax.all_to_all(waves, ("row", "domain"), split_axis=0, concat_axis=0, tiled=True)
    other_waves = swapped(waves, "core")
    potential_next = pl.pallas_call(
        functools.partial(field_kernel, count, length_cells),
        out_shape=f32(layer_cap, plane),
        in_specs=[SMEM_SPEC] + [VMEM_SPEC] * 7,
        out_specs=VMEM_SPEC,
        scratch_shapes=[
            scratch(SLOTS * SIDE, LANES),
            scratch(SLOTS * SIDE, LANES),
            scratch(layer_cap * SIDE, WIDTH),
            scratch(SLOTS * FLAT, LANES),
        ],
        compiler_params=params,
        name="field",
    )(layer_start, waves, other_waves, density, other_density, flat_circle, out_of_y, table_z)
    return orbitals_next.reshape(orbitals.shape), potential_next


def solution(mesh):
    domains = mesh.shape["domain"]
    split = Mesh(mesh.devices.reshape(-1, 2, domains), ("row", "core", "domain"))
    states = ("row", "core")
    return jax.shard_map(
        shards,
        mesh=split,
        in_specs=(
            P(None, states, "domain", None),
            P(states),
            P("domain", None),
            P("domain", None),
            P(),
        ),
        out_specs=(P(None, states, "domain", None), P("domain", None)),
        check_vma=False,
    )
```

```python
import functools
import math

import jax
import jax.numpy as jnp
import ml_dtypes
import numpy as np
from jax import lax
from jax.experimental import pallas as pl
from jax.experimental.pallas import tpu as pltpu
from jax.sharding import Mesh, PartitionSpec as P

SIDE = 160
SLAB = 5
TERMS = 4

HALO = TERMS
LANES = 128
SLOTS = 8
RUN = SIDE // 8
FLAT = SIDE * SIDE // LANES
STRIDE = FLAT // 8
WIDTH = 2 * LANES
BLOCK = 32
TALL = SIDE + 16

time_step = 0.3
four_pi = 4.0 * math.pi
two_pi = 2.0 * math.pi
highest = lax.Precision.HIGHEST
MEBI = 1024 * 1024
SMEM_SPEC = pl.BlockSpec(memory_space=pltpu.SMEM)
VMEM_SPEC = pl.BlockSpec(memory_space=pltpu.VMEM)
HBM_SPEC = pl.BlockSpec(memory_space=pltpu.HBM)


def hartley_table(count_cells):
    index_run = np.arange(count_cells)
    angles = (index_run[:, None] * index_run[None, :] % count_cells) * (2.0 * np.pi / count_cells)
    return np.cos(angles) + np.sin(angles)


def plane_order():
    rows = np.arange(SIDE)
    return RUN * (rows % 8) + rows // 8


def two_parts(table):
    table = table.astype(np.float32)
    high = table.astype(ml_dtypes.bfloat16)
    low = (table - high.astype(np.float32)).astype(ml_dtypes.bfloat16)
    return high, low


def tables_of_side():
    table = hartley_table(SIDE)
    along_z = np.zeros((WIDTH, WIDTH))
    along_z[:SIDE, :SIDE] = table
    high, low = two_parts(along_z)
    along_z = np.concatenate([high, high, low], axis=0)
    high, low = two_parts(table[:, plane_order()])
    into_y = np.concatenate([high, high, low], axis=1)
    high, low = two_parts(table[plane_order(), :])
    out_of_y = np.concatenate([high, high, low], axis=1)
    return along_z, into_y, out_of_y


def circle_table():
    across = 2 * np.arange(SIDE, dtype=np.int64) - (SIDE - 1)
    return (across[:, None] ** 2 + across[None, :] ** 2).astype(np.int32)


def circle_plane():
    table = np.full((SIDE, WIDTH), 4 * SIDE * SIDE, np.int32)
    table[:, :SIDE] = circle_table()[plane_order()]
    return table


def mesh_points(x_row, circle, length_cells):
    room = ((length_cells - 2) ** 2 - (2 * x_row - (length_cells - 1)) ** 2) * (SIDE - 2) ** 2
    return (circle * (length_cells - 2) ** 2 <= room) & (circle < 4 * SIDE * SIDE)


def column_pieces(first, count):
    pieces = []
    column = first
    while column < first + count:
        row = column // SIDE
        stop = min((row + 1) * SIDE, first + count)
        pieces.append((row, column - row * SIDE, stop - row * SIDE))
        column = stop
    return pieces


def eight(values):
    missing = jnp.zeros((SLOTS - values.shape[0], values.shape[1]), values.dtype)
    return jnp.concatenate([values, missing], axis=0)


def to_plane(load, store):
    lane = lax.broadcasted_iota(jnp.int32, (8, LANES), 1)
    for step in range(RUN // 4):
        rows = [load(5 * step + part) for part in range(5)]
        store(4 * step, rows[0], rows[1])
        for part in range(1, 4):
            left = pltpu.roll(rows[part], LANES - 32 * part, 1)
            right = pltpu.roll(rows[part + 1], LANES - 32 * part, 1)
            store(4 * step + part, jnp.where(lane < LANES - 32 * part, left, right), right)


def to_flat(load, store):
    lane = lax.broadcasted_iota(jnp.int32, (8, LANES), 1)
    for step in range(RUN // 4):
        turned = []
        for part in range(4):
            low, high = load(4 * step + part)
            if part:
                low = pltpu.roll(low, 32 * part, 1)
                high = pltpu.roll(high, 32 * part, 1)
            turned.append((low, high))
        store(5 * step, turned[0][0])
        for part in range(1, 4):
            ended = 32 * (part - 1)
            values = jnp.where(lane < ended + 32, turned[part - 1][1], turned[part][0])
            if ended:
                values = jnp.where(lane < ended, turned[part - 1][0], values)
            store(5 * step + part, values)
        store(5 * step + 4, jnp.where(lane < 96, turned[3][0], turned[3][1]))


def chords():
    across = 2 * np.arange(SIDE, dtype=np.int64) - (SIDE - 1)
    room = (SIDE - 2) ** 2 - across**2
    return [max([w for w in range(1, SIDE // 2 + 1) if (2 * w - 1) ** 2 <= left], default=0) for left in room]


def chord_moves():
    moves = []
    packed = 0
    for row, half in enumerate(chords()):
        if half:
            moves.append((row * SIDE + SIDE // 2 - half, packed, 2 * half))
            packed += 2 * half
    return moves


def packed_tiles():
    _, start, length = chord_moves()[-1]
    return -(-(start + length) // LANES)


def move_lanes(moves, load, store):
    lane = lax.broadcasted_iota(jnp.int32, (8, LANES), 1)
    pieces = {}
    for source, target, length in moves:
        while length:
            size = min(length, LANES - source % LANES, LANES - target % LANES)
            pieces.setdefault(target // LANES, []).append((target % LANES, source // LANES, (target - source) % LANES))
            source, target, length = source + size, target + size, length - size
    loaded = {}
    turned = {}
    for tile in sorted(pieces):
        values = None
        for first, origin, shift in sorted(pieces[tile]):
            if origin not in loaded:
                loaded[origin] = load(origin)
            if (origin, shift) not in turned:
                turned[origin, shift] = pltpu.roll(loaded[origin], shift, 1) if shift else loaded[origin]
            piece = turned[origin, shift]
            values = piece if values is None else jnp.where(lane >= first, piece, values)
        store(tile, values)


def pack_chords(rows_ref, store):
    move_lanes(chord_moves(), lambda tile: rows_ref[pl.ds(tile, 8, stride=FLAT), :], store)


def unpack_chords(load, rows_ref):
    def store(tile, values):
        rows_ref[pl.ds(tile, 8, stride=FLAT), :] = values

    move_lanes([(target, source, length) for source, target, length in chord_moves()], load, store)


def parts_of(values):
    high = values.astype(jnp.bfloat16)
    low = (values - high.astype(jnp.float32)).astype(jnp.bfloat16)
    return high, low


def turn_z(values, table):
    high, low = parts_of(values)
    return jnp.dot(
        jnp.concatenate([high, low, high], axis=1), table, preferred_element_type=jnp.float32
    )


def turn_y(table, values):
    high, low = parts_of(values)
    return jnp.dot(
        table, jnp.concatenate([high, low, high], axis=0), preferred_element_type=jnp.float32
    )


def send_columns(planes_ref, slots, table_y, table_z, low_ref, high_ref):
    along_z = turn_z(planes_ref[:slots * SIDE, :], table_z)
    for slot in range(slots):
        rows = slice(slot * SIDE, (slot + 1) * SIDE)
        waves = turn_y(table_y, along_z[rows])
        low_ref[rows, :] = waves[:, :LANES]
        high_ref[rows, :] = waves[:, LANES:]
    low_ref[slots * SIDE:, :] = jnp.zeros(((SLOTS - slots) * SIDE, LANES), jnp.float32)
    high_ref[slots * SIDE:, :] = jnp.zeros(((SLOTS - slots) * SIDE, LANES), jnp.float32)


def chunk_of(low_ref, high_ref, first_row, pieces, extra):
    parts = []
    for row, start, stop in pieces:
        at = pl.ds(first_row + row, SLOTS, stride=SIDE)
        values = jnp.concatenate([low_ref[at, :], high_ref[at, :]], axis=1)
        parts.append(values[:, start:stop])
    return jnp.concatenate(parts + [extra], axis=1)


def layers_of(stored_ref, flat_ref):
    @pl.loop(0, FLAT // 8)
    def _(step):
        for part in range(8):
            lanes = pl.ds(pl.multiple_of((step * 8 + part) * LANES, LANES), LANES)
            flat_ref[pl.ds(step * 8 + part, SLOTS, stride=FLAT), :] = eight(stored_ref[:, lanes])


def place_of(start_ref):
    position = lax.axis_index("domain")
    return position, start_ref[position], start_ref[position + 1] - start_ref[position]


def started(sems, pairs):
    copies = [pltpu.make_async_copy(*pair, sems.at[index]) for index, pair in enumerate(pairs)]
    for made in copies:
        made.start()
    return copies


def layers_at(orbitals_ref, part, start, count):
    return orbitals_ref.at[part, pl.ds(pl.multiple_of(start * FLAT, 8), count * FLAT)]


def rows_at(ref, part, count):
    return ref.at[pl.ds(part * count * FLAT, count * FLAT)]


def pack_kernel(start_ref, orbitals_ref, up_ref, down_ref, up_rows_ref, down_rows_ref, up_buffer_ref,
                down_buffer_ref, in_sems, out_sems):
    _, _, thickness = place_of(start_ref)
    first = jnp.maximum(thickness - HALO, 0)
    arrivals = started(
        in_sems,
        [
            (layers_at(orbitals_ref, part, start, HALO), rows_at(rows_ref, part, HALO))
            for start, rows_ref in ((first, up_rows_ref), (0, down_rows_ref))
            for part in range(2)
        ],
    )
    departures = []
    for index, (rows_ref, buffer_ref, out_ref) in enumerate(
        ((up_rows_ref, up_buffer_ref, up_ref), (down_rows_ref, down_buffer_ref, down_ref))
    ):
        arrivals[2 * index].wait()
        arrivals[2 * index + 1].wait()

        def store(tile, values, buffer_ref=buffer_ref):
            buffer_ref[:, tile * LANES:(tile + 1) * LANES] = values

        pack_chords(rows_ref, store)
        departures.append(pltpu.make_async_copy(buffer_ref, out_ref, out_sems.at[index]))
        departures[-1].start()
    for made in departures:
        made.wait()


def pack_rest_kernel(start_ref, potential_ref, orbitals_ref, v_ref, up_far_ref, down_far_ref, flat_ref,
                     v_rows_ref, stored_ref, in_sems):
    _, _, thickness = place_of(start_ref)
    v_first = jnp.where(lax.axis_index("core") == 0, thickness - (HALO - 1), 0)
    arrivals = started(
        in_sems,
        [(potential_ref, stored_ref)]
        + [
            (layers_at(orbitals_ref, part, start, 1), rows_at(far_ref, part, 1))
            for start, far_ref in ((thickness - 1, up_far_ref), (0, down_far_ref))
            for part in range(2)
        ],
    )
    arrivals[0].wait()
    layers_of(stored_ref, flat_ref)
    for layer in range(HALO - 1):
        v_rows_ref[layer * FLAT:(layer + 1) * FLAT, :] = flat_ref[
            pl.ds(pl.multiple_of((v_first + layer) * FLAT, 8), FLAT), :
        ]

    def store_v(tile, values):
        for layer in range(HALO - 1):
            v_ref[layer, tile:tile + 1, :] = values[layer:layer + 1]

    pack_chords(v_rows_ref, store_v)
    for made in arrivals[1:]:
        made.wait()


def ions_kernel(count, length_cells, start_ref, background_ref, circle_ref, table_y_ref, table_z_ref,
                out_ref, flat_ref, planes_ref, low_ref, high_ref):
    _, own_start, thickness = place_of(start_ref)
    slots = background_ref.shape[0]
    groups, _, width = out_ref.shape
    layers_of(background_ref, flat_ref)

    def body(slot, total):
        def store(tile, low, high):
            rows = pl.ds(pl.multiple_of(slot * SIDE + tile * 8, 8), 8)
            planes_ref[rows, :LANES] = low
            planes_ref[rows, LANES:] = high

        to_plane(lambda k: flat_ref[pl.ds(slot * FLAT + k, 8, stride=STRIDE), :], store)
        rows = pl.ds(pl.multiple_of(slot * SIDE, 8), SIDE)
        inside = mesh_points(own_start + slot, circle_ref[...], length_cells) & (slot < thickness)
        values = jnp.where(inside, planes_ref[rows, :], 0.0)
        planes_ref[rows, :] = values
        return total + jnp.sum(values.reshape(RUN, 8, WIDTH), axis=0)

    total = lax.fori_loop(0, slots, body, jnp.zeros((8, WIDTH), jnp.float32))
    whole = jnp.broadcast_to(jnp.sum(total, keepdims=True), (SLOTS, LANES))[:, :width - count]
    send_columns(planes_ref, slots, table_y_ref[...], table_z_ref[...], low_ref, high_ref)
    core_rows = SIDE // lax.axis_size("core")
    first_row = lax.axis_index("core") * core_rows + lax.axis_index("row") * (core_rows // lax.axis_size("row"))
    for group in range(groups):
        out_ref[group] = chunk_of(low_ref, high_ref, first_row, column_pieces(group * count, count), whole)


def propagate_kernel(count, length_cells, start_ref, weight_ref, orbitals_ref, potential_ref, below_hbm_ref,
                     above_hbm_ref, below_far_hbm_ref, above_far_hbm_ref, v_hbm_ref, v_other_hbm_ref,
                     circle_ref, table_y_ref, table_z_ref, psi_ref, kept_ref, sent_ref, first_ref, second_ref,
                     third_ref, fourth_ref, sum_ref, centre_ref, beside_ref, flat_ref, planes_ref, low_ref,
                     high_ref, below_rows_ref, above_rows_ref, v_rows_ref, v_ref, v_other_ref, below_ref,
                     above_ref, below_far_ref, above_far_ref, in_sems, out_sem):
    arrivals = started(
        in_sems,
        [
            (v_hbm_ref, v_ref),
            (v_other_hbm_ref, v_other_ref),
            (below_hbm_ref, below_ref),
            (above_hbm_ref, above_ref),
            (below_far_hbm_ref, below_far_ref),
            (above_far_hbm_ref, above_far_ref),
        ],
    )
    position, own_start, thickness = place_of(start_ref)
    domains = lax.axis_size("domain")
    before = start_ref[jnp.maximum(position - 1, 0)]
    after = start_ref[jnp.minimum(position + 2, domains)]
    short_below = ((position > 0) & (own_start - before < HALO)).astype(jnp.int32)
    short_above = (position < domains - 1) & (after - own_start - thickness < HALO)
    weight = weight_ref[0]
    core = lax.axis_index("core")
    slots = orbitals_ref.shape[1]
    layers = slots + 2 * HALO
    devices, _, width = kept_ref.shape
    field_refs = (first_ref, second_ref, third_ref, fourth_ref)

    def field_layer(part, x_row):
        def store(tile, low, high):
            first_ref[part, x_row, 8 + 8 * tile:16 + 8 * tile, :LANES] = low
            first_ref[part, x_row, 8 + 8 * tile:16 + 8 * tile, LANES:] = high

        return store

    def potential_layer(x_row):
        def store(tile, low, high):
            centre_ref[x_row, 8 * tile:8 * tile + 8, :LANES] = low
            centre_ref[x_row, 8 * tile:8 * tile + 8, LANES:] = high

        return store

    def rows_from(ref, *at):
        return lambda k: ref[(*at, pl.ds(k, 8, stride=STRIDE), slice(None))]

    def layer_of(rows_ref, layer):
        return lambda k: rows_ref[pl.ds(layer * FLAT + k, 8, stride=STRIDE), :]

    layers_of(potential_ref, flat_ref)

    @pl.loop(0, slots)
    def _(slot):
        for part in range(2):
            to_plane(rows_from(orbitals_ref, part, slot), field_layer(part, HALO + slot))
        to_plane(layer_of(flat_ref, slot), potential_layer(HALO + slot))

    for made in arrivals:
        made.wait()
    for packed_ref, rows_ref in ((below_ref, below_rows_ref), (above_ref, above_rows_ref)):
        unpack_chords(
            lambda tile, packed_ref=packed_ref: packed_ref[:, tile * LANES:(tile + 1) * LANES], rows_ref
        )
    unpack_chords(
        lambda tile: eight(
            jnp.concatenate([ref[:, tile, :] for ref in (v_ref, v_other_ref)], axis=0)
        ),
        v_rows_ref,
    )

    @pl.loop(0, HALO - 1)
    def _(layer):
        lower = 1 + layer
        upper = HALO + thickness + layer
        to_plane(layer_of(v_rows_ref, layer), potential_layer(jnp.where(core == 0, lower, upper)))
        to_plane(layer_of(v_rows_ref, HALO - 1 + layer), potential_layer(jnp.where(core == 0, upper, lower)))
        for part in range(2):
            to_plane(
                layer_of(below_rows_ref, part * HALO + 1 + layer - short_below), field_layer(part, 1 + layer)
            )
            to_plane(
                layer_of(above_rows_ref, part * HALO + layer), field_layer(part, HALO + thickness + layer)
            )

    @pl.loop(0, 2)
    def _(part):
        last = 2 * HALO - 1 + thickness

        @pl.when(short_below > 0)
        def _():
            to_plane(layer_of(below_far_ref, part), field_layer(part, 0))

        @pl.when(short_below == 0)
        def _():
            to_plane(layer_of(below_rows_ref, part * HALO), field_layer(part, 0))

        @pl.when(short_above)
        def _():
            to_plane(layer_of(above_far_ref, part), field_layer(part, last))

        @pl.when(jnp.logical_not(short_above))
        def _():
            to_plane(layer_of(above_rows_ref, part * HALO + HALO - 1), field_layer(part, last))

    def wrap(term, part, x_row):
        first = field_refs[term][part, x_row, 8:16, :]
        final = field_refs[term][part, x_row, SIDE:SIDE + 8, :]
        field_refs[term][part, x_row, :8, :] = pltpu.roll(final, 1, 0)
        field_refs[term][part, x_row, SIDE + 8:, :] = pltpu.roll(first, 7, 0)

    @pl.loop(0, layers)
    def _(x_row):
        known = x_row < thickness + 2 * HALO
        for block in range(SIDE // BLOCK):
            rows = slice(block * BLOCK, (block + 1) * BLOCK)
            inner = slice(8 + block * BLOCK, 8 + (block + 1) * BLOCK)
            inside = mesh_points(own_start - HALO + x_row, circle_ref[rows, :], length_cells) & known
            centre_ref[x_row, rows, :] = jnp.where(
                inside, (3.0 + centre_ref[x_row, rows, :]) * time_step, 0.0
            )
            beside_ref[x_row, rows, :] = jnp.where(inside, 0.5 * time_step, 0.0)
            for part in range(2):
                first_ref[part, x_row, inner, :] = jnp.where(
                    inside, first_ref[part, x_row, inner, :], 0.0
                )
        for part in range(2):
            wrap(0, part, x_row)

    def hamilton(term, part, x_row, block, centre, beside):
        field_ref = field_refs[term]
        tall = field_ref[part, x_row, block * BLOCK:block * BLOCK + BLOCK + 16, :]
        inner = slice(8 + block * BLOCK, 8 + (block + 1) * BLOCK)
        field = tall[8:8 + BLOCK]
        around = field_ref[part, x_row - 1, inner, :] + field_ref[part, x_row + 1, inner, :]
        around = around + (tall[:BLOCK] + tall[16:])
        around = around + (pltpu.roll(field, 1, 1) + pltpu.roll(field, WIDTH - 1, 1))
        return centre * field - beside * around

    for term in range(1, TERMS):

        @pl.loop(term, layers - term)
        def _(x_row, term=term):
            for block in range(SIDE // BLOCK):
                rows = slice(block * BLOCK, (block + 1) * BLOCK)
                inner = slice(8 + block * BLOCK, 8 + (block + 1) * BLOCK)
                centre = centre_ref[x_row, rows, :]
                beside = beside_ref[x_row, rows, :]
                for part in range(2):
                    field_refs[term][part, x_row, inner, :] = hamilton(
                        term - 1, part, x_row, block, centre, beside
                    )
            for part in range(2):
                wrap(term, part, x_row)

    def finish(slot, total):
        x_row = HALO + slot
        owned = slot < thickness
        for block in range(SIDE // BLOCK):
            rows = slice(block * BLOCK, (block + 1) * BLOCK)
            inner = slice(8 + block * BLOCK, 8 + (block + 1) * BLOCK)
            centre = centre_ref[x_row, rows, :]
            beside = beside_ref[x_row, rows, :]
            density = jnp.zeros((BLOCK, WIDTH), jnp.float32)
            for part, sign in ((0, 1.0), (1, -1.0)):
                summed = first_ref[part, x_row, inner, :]
                summed = summed + sign * second_ref[1 - part, x_row, inner, :]
                summed = summed - (1.0 / 2.0) * third_ref[part, x_row, inner, :]
                summed = summed - (sign / 6.0) * fourth_ref[1 - part, x_row, inner, :]
                summed = summed + (1.0 / 24.0) * hamilton(3, part, x_row, block, centre, beside)
                summed = jnp.where(owned, summed, 0.0)
                sum_ref[part, slot, rows, :] = summed
                density = density + summed * summed
            density = weight * density
            planes_ref[pl.ds(pl.multiple_of(slot * SIDE + block * BLOCK, 8), BLOCK), :] = density
            total = total + jnp.sum(density.reshape(BLOCK // 8, 8, WIDTH), axis=0)

        return total

    total = lax.fori_loop(0, slots, finish, jnp.zeros((8, WIDTH), jnp.float32))
    departure = pltpu.make_async_copy(sum_ref, psi_ref, out_sem)
    departure.start()
    whole = jnp.broadcast_to(jnp.sum(total, keepdims=True), (SLOTS, LANES))[:, :width - count]
    send_columns(planes_ref, slots, table_y_ref[...], table_z_ref[...], low_ref, high_ref)
    core_rows = SIDE // 2
    first_row = core * core_rows
    for device in range(devices):
        pieces = column_pieces(device * count, count)
        kept_ref[device] = chunk_of(low_ref, high_ref, first_row, pieces, whole)
        sent_ref[device] = chunk_of(low_ref, high_ref, core_rows - first_row, pieces, whole)
    departure.wait()


def unpack_kernel(weight_ref, psi_ref, next_ref, density_kept_ref, density_sent_ref, density_ref):
    core = lax.axis_index("core")
    weight = weight_ref[0]
    slots = psi_ref.shape[1]

    @pl.loop(0, slots)
    def _(slot):
        for part in range(2):

            def load(tile, part=part):
                tall = psi_ref[part, slot, 8 * tile:8 * tile + 8, :]
                return tall[:, :LANES], tall[:, LANES:]

            def store(k, values, part=part):
                next_ref[part, slot, pl.ds(k, 8, stride=STRIDE), :] = values

            to_flat(load, store)
        real = next_ref[0, slot]
        imag = next_ref[1, slot]
        density_ref[slot] = weight * (real * real + imag * imag)

    for slot in range(slots, SLOTS):
        density_ref[slot] = jnp.zeros((FLAT, LANES), jnp.float32)

    @pl.loop(0, SLOTS // 2)
    def _(slot):
        density_kept_ref[slot] = density_ref[core * (SLOTS // 2) + slot]
        density_sent_ref[slot] = density_ref[(1 - core) * (SLOTS // 2) + slot]


def wave_squared(index, count_cells):
    folded = jnp.where(2 * index <= count_cells, index, index - count_cells)
    wave_number = folded.astype(jnp.float32) * (two_pi / count_cells)
    return wave_number * wave_number


def coulomb_kernel(count, length_cells, start_ref, charge_ref, ions_ref, table_ref, out_ref):
    domains, _, width = ions_ref.shape
    states = charge_ref.shape[0] // domains
    device = (lax.axis_index("core") * states + lax.axis_index("row")) * domains + lax.axis_index("domain")
    charge = charge_ref[:domains]
    for state in range(1, states):
        charge = charge + charge_ref[state * domains:(state + 1) * domains]
    charge = charge.reshape(domains * SLOTS, width)
    ions = ions_ref[...].reshape(domains * SLOTS, width)
    first = lax.broadcasted_iota(jnp.int32, (domains * SLOTS, width), 0) % SLOTS == 0
    lane = lax.broadcasted_iota(jnp.int32, (domains * SLOTS, width), 1)
    chosen = first & (lane == count)
    electrons = jnp.sum(jnp.where(chosen, charge, 0.0), keepdims=True)
    ionic = jnp.sum(jnp.where(chosen, ions, 0.0), keepdims=True)
    charge = charge - (electrons / ionic) * ions
    layer = lax.broadcasted_iota(jnp.int32, (length_cells, domains * SLOTS), 0)
    place = lax.broadcasted_iota(jnp.int32, (length_cells, domains * SLOTS), 1)
    chosen_layer = jnp.full(layer.shape, -1, jnp.int32)
    for domain in range(domains):
        slot = place - domain * SLOTS
        here = (slot >= 0) & (slot < start_ref[domain + 1] - start_ref[domain])
        chosen_layer = jnp.where(here, start_ref[domain] + slot, chosen_layer)
    pick = (layer == chosen_layer).astype(jnp.float32)
    table = jnp.dot(table_ref[...], pick, precision=highest, preferred_element_type=jnp.float32)
    waves = jnp.dot(table, charge, precision=highest, preferred_element_type=jnp.float32)
    wave_x = lax.broadcasted_iota(jnp.int32, waves.shape, 0)
    column = device * count + lax.broadcasted_iota(jnp.int32, waves.shape, 1)
    wave_y = ((column.astype(jnp.float32) + 0.5) * (1.0 / SIDE)).astype(jnp.int32)
    wave_z = column - wave_y * SIDE
    squared = (
        wave_squared(wave_x, length_cells) + wave_squared(wave_y, SIDE) + wave_squared(wave_z, SIDE)
    )
    gain = jnp.where(squared > 0, four_pi / jnp.where(squared > 0, squared, 1.0), 0.0)
    waves = waves * (gain * (1.0 / (length_cells * SIDE * SIDE)))
    back = lax.dot_general(
        table, waves, (((0,), (0,)), ((), ())), precision=highest, preferred_element_type=jnp.float32
    )
    back = back.reshape(domains, SLOTS, width)
    for state in range(states):
        out_ref[state * domains:(state + 1) * domains] = back


def field_kernel(count, length_cells, start_ref, waves_ref, others_ref, density_ref, other_ref,
                 circle_ref, table_y_ref, table_z_ref, out_ref, low_ref, high_ref, planes_ref, flat_ref):
    _, own_start, thickness = place_of(start_ref)
    devices = waves_ref.shape[0]
    slots = out_ref.shape[0]
    core = lax.axis_index("core")
    core_rows = SIDE // 2
    first_row = core * core_rows
    for source_ref, first in ((waves_ref, first_row), (others_ref, core_rows - first_row)):
        pieces = []
        for device in range(devices):
            column = 0
            for row, start, stop in column_pieces(device * count, count):
                values = source_ref[device, :, column:column + stop - start]
                column += stop - start
                if start > 0:
                    pieces.append(values)
                    values = jnp.concatenate(pieces, axis=1)
                if stop < SIDE:
                    pieces = [values]
                    continue
                pieces = []
                at = pl.ds(first + row, SLOTS, stride=SIDE)
                low_ref[at, :] = values[:, :LANES]
                high_ref[at, :] = jnp.concatenate(
                    [values[:, LANES:], jnp.zeros((SLOTS, WIDTH - SIDE), jnp.float32)], axis=1
                )
    table_y = table_y_ref[...]
    table_z = table_z_ref[...]
    used = slice(0, slots * SIDE)
    along_z = turn_z(jnp.concatenate([low_ref[used, :], high_ref[used, :]], axis=1), table_z)
    for slot in range(slots):
        rows = slice(slot * SIDE, (slot + 1) * SIDE)
        planes_ref[rows, :] = turn_y(table_y, along_z[rows])

    @pl.loop(0, slots)
    def _(slot):
        def load(tile):
            tall = planes_ref[pl.ds(pl.multiple_of(slot * SIDE + tile * 8, 8), 8), :]
            return tall[:, :LANES], tall[:, LANES:]

        def store(k, values):
            flat_ref[pl.ds(slot * FLAT + k, 8, stride=STRIDE), :] = values

        to_flat(load, store)
        rows = pl.ds(pl.multiple_of(slot * FLAT, 8), FLAT)
        here = slot // (SLOTS // 2) == core
        kept_slot = slot % (SLOTS // 2)
        content = jnp.where(here, density_ref[kept_slot], other_ref[kept_slot]) * (3.0 / math.pi)
        positive = jnp.where(content > 0, content, 1.0)
        root = jnp.exp(jnp.log(positive) * (1.0 / 3.0))
        root = root - (root - positive / (root * root)) * (1.0 / 3.0)
        root = jnp.where(content > 0, root, 0.0)
        inside = mesh_points(own_start + slot, circle_ref[...], length_cells) & (slot < thickness)
        flat_ref[rows, :] = jnp.where(inside, flat_ref[rows, :] - root, 0.0)

    @pl.loop(0, FLAT // 8)
    def _(step):
        for part in range(8):
            lanes = pl.ds(pl.multiple_of((step * 8 + part) * LANES, LANES), LANES)
            out_ref[:, lanes] = flat_ref[pl.ds(step * 8 + part, SLOTS, stride=FLAT), :][:slots]


def from_behind(value, steps):
    count = lax.axis_size("domain")
    leading, last = (max(0, -steps), min(count, count - steps))
    return lax.ppermute(value, "domain", [(source, source + steps) for source in range(leading, last)])


def swapped(value, axis):
    return lax.ppermute(value, axis, [(0, 1), (1, 0)])


def shards(orbitals, occupation, potential, background, layer_start):
    domains = lax.axis_size("domain")
    rows = lax.axis_size("row")
    devices = domains * rows
    length_cells = SLAB * domains
    layer_cap, plane = potential.shape
    count = plane // (2 * devices)
    width = -(-(count + 1) // LANES) * LANES
    circle = jnp.asarray(circle_plane())
    flat_circle = jnp.asarray(circle_table().reshape(FLAT, LANES))
    table_z, into_y, out_of_y = (jnp.asarray(table) for table in tables_of_side())
    table_x = jnp.asarray(hartley_table(length_cells).astype(np.float32))
    params = pltpu.CompilerParams(vmem_limit_bytes=16 * MEBI)
    large = pltpu.CompilerParams(vmem_limit_bytes=44 * MEBI)
    whole = pltpu.CompilerParams(vmem_limit_bytes=56 * MEBI)

    def f32(*shape):
        return jax.ShapeDtypeStruct(shape, jnp.float32)

    def scratch(*shape):
        return pltpu.VMEM(shape, jnp.float32)

    layers = orbitals.reshape(2, layer_cap, FLAT, LANES)
    packed = packed_tiles()
    outer = orbitals.reshape(2, layer_cap * FLAT, LANES)
    up, down = pl.pallas_call(
        pack_kernel,
        out_shape=(f32(2 * HALO, packed * LANES), f32(2 * HALO, packed * LANES)),
        in_specs=[SMEM_SPEC, HBM_SPEC],
        out_specs=(HBM_SPEC, HBM_SPEC),
        scratch_shapes=[
            scratch(2 * HALO * FLAT, LANES),
            scratch(2 * HALO * FLAT, LANES),
            scratch(2 * HALO, packed * LANES),
            scratch(2 * HALO, packed * LANES),
            pltpu.SemaphoreType.DMA((4,)),
            pltpu.SemaphoreType.DMA((2,)),
        ],
        compiler_params=whole,
        name="pack_halo",
    )(layer_start, outer)
    up, down, potential_rest, outer = lax.optimization_barrier((up, down, potential, outer))
    v_rows, up_far, down_far = pl.pallas_call(
        pack_rest_kernel,
        out_shape=(f32(HALO - 1, packed, LANES), f32(2 * FLAT, LANES), f32(2 * FLAT, LANES)),
        in_specs=[SMEM_SPEC, HBM_SPEC, HBM_SPEC],
        out_specs=(VMEM_SPEC,) * 3,
        scratch_shapes=[
            scratch(SLOTS * FLAT, LANES),
            scratch(SLOTS * FLAT, LANES),
            scratch(layer_cap, plane),
            pltpu.SemaphoreType.DMA((5,)),
        ],
        compiler_params=whole,
        cost_estimate=pl.CostEstimate(flops=0, transcendentals=0, bytes_accessed=30_000_000),
        name="pack_rest",
    )(layer_start, potential_rest, outer)
    v_rows = lax.ppermute(
        v_rows,
        ("core", "domain"),
        [(source, source + 1) for source in range(domains - 1)]
        + [(domains + source + 1, domains + source) for source in range(domains - 1)],
    )
    below = from_behind(up, 1)
    above = from_behind(down, -1)
    below_far = from_behind(up_far, 2)
    above_far = from_behind(down_far, -2)
    v_rows, below_far, above_far = lax.optimization_barrier((v_rows, below_far, above_far))
    v_others = swapped(v_rows, "core")

    ions = pl.pallas_call(
        functools.partial(ions_kernel, count, length_cells),
        out_shape=f32(domains, SLOTS, width),
        in_specs=[SMEM_SPEC] + [VMEM_SPEC] * 4,
        out_specs=VMEM_SPEC,
        scratch_shapes=[
            scratch(SLOTS * FLAT, LANES),
            scratch(layer_cap * SIDE, WIDTH),
            scratch(SLOTS * SIDE, LANES),
            scratch(SLOTS * SIDE, LANES),
        ],
        compiler_params=params,
        name="ion_waves",
    )(layer_start, background, circle, into_y, table_z)
    ions = lax.all_to_all(ions, "domain", split_axis=0, concat_axis=0, tiled=True)
    ions, below = lax.optimization_barrier((ions, below))

    span = layer_cap + 2 * HALO
    fields = (2, span, TALL, WIDTH)
    psi, kept, sent = pl.pallas_call(
        functools.partial(propagate_kernel, count, length_cells),
        out_shape=(
            pltpu.HBM((2, layer_cap, SIDE, WIDTH), jnp.float32),
            f32(devices, SLOTS, width),
            f32(devices, SLOTS, width),
        ),
        in_specs=[SMEM_SPEC, SMEM_SPEC, VMEM_SPEC, VMEM_SPEC] + [HBM_SPEC] * 6 + [VMEM_SPEC] * 3,
        out_specs=(HBM_SPEC, VMEM_SPEC, VMEM_SPEC),
        scratch_shapes=[scratch(*fields)] * TERMS
        + [
            scratch(2, layer_cap, SIDE, WIDTH),
            scratch(span, SIDE, WIDTH),
            scratch(span, SIDE, WIDTH),
            scratch(SLOTS * FLAT, LANES),
            scratch(layer_cap * SIDE, WIDTH),
            scratch(SLOTS * SIDE, LANES),
            scratch(SLOTS * SIDE, LANES),
            scratch(SLOTS * FLAT, LANES),
            scratch(SLOTS * FLAT, LANES),
            scratch(SLOTS * FLAT, LANES),
            scratch(HALO - 1, packed, LANES),
            scratch(HALO - 1, packed, LANES),
            scratch(2 * HALO, packed * LANES),
            scratch(2 * HALO, packed * LANES),
            scratch(2 * FLAT, LANES),
            scratch(2 * FLAT, LANES),
            pltpu.SemaphoreType.DMA((6,)),
            pltpu.SemaphoreType.DMA,
        ],
        compiler_params=large,
        name="propagate",
    )(layer_start, occupation, layers, potential, below, above, below_far, above_far, v_rows, v_others,
      circle, into_y, table_z)
    waves = kept + swapped(sent, "core")
    waves, psi = lax.optimization_barrier((waves, psi))
    waves = lax.all_to_all(waves, ("row", "domain"), split_axis=0, concat_axis=0, tiled=True)
    orbitals_next, density_kept, density_sent = pl.pallas_call(
        unpack_kernel,
        out_shape=(
            f32(2, layer_cap, FLAT, LANES),
            f32(SLOTS // 2, FLAT, LANES),
            f32(SLOTS // 2, FLAT, LANES),
        ),
        in_specs=[SMEM_SPEC, VMEM_SPEC],
        out_specs=(VMEM_SPEC,) * 3,
        scratch_shapes=[scratch(SLOTS, FLAT, LANES)],
        compiler_params=params,
        name="unpack",
    )(occupation, psi)
    density = density_kept + swapped(density_sent, "core")
    other_density = swapped(density, "row")
    waves = pl.pallas_call(
        functools.partial(coulomb_kernel, count, length_cells),
        out_shape=f32(devices, SLOTS, width),
        in_specs=[SMEM_SPEC] + [VMEM_SPEC] * 3,
        out_specs=VMEM_SPEC,
        compiler_params=params,
        name="coulomb",
    )(layer_start, waves, ions, table_x)
    waves = lax.all_to_all(waves, ("row", "domain"), split_axis=0, concat_axis=0, tiled=True)
    waves, other_density = lax.optimization_barrier((waves, other_density))
    density = density + other_density
    other_density = swapped(density, "core")
    other_waves = swapped(waves, "core")
    potential_next = pl.pallas_call(
        functools.partial(field_kernel, count, length_cells),
        out_shape=f32(layer_cap, plane),
        in_specs=[SMEM_SPEC] + [VMEM_SPEC] * 7,
        out_specs=VMEM_SPEC,
        scratch_shapes=[
            scratch(SLOTS * SIDE, LANES),
            scratch(SLOTS * SIDE, LANES),
            scratch(layer_cap * SIDE, WIDTH),
            scratch(SLOTS * FLAT, LANES),
        ],
        compiler_params=params,
        name="field",
    )(layer_start, waves, other_waves, density, other_density, flat_circle, out_of_y, table_z)
    return orbitals_next.reshape(orbitals.shape), potential_next


def solution(mesh):
    domains = mesh.shape["domain"]
    split = Mesh(mesh.devices.reshape(-1, 2, domains), ("row", "core", "domain"))
    states = ("row", "core")
    return jax.shard_map(
        shards,
        mesh=split,
        in_specs=(
            P(None, states, "domain", None),
            P(states),
            P("domain", None),
            P("domain", None),
            P(),
        ),
        out_specs=(P(None, states, "domain", None), P("domain", None)),
        check_vma=False,
    )
```

```python
import functools
import math

import jax
import jax.numpy as jnp
import ml_dtypes
import numpy as np
from jax import lax
from jax.experimental import pallas as pl
from jax.experimental.pallas import tpu as pltpu
from jax.sharding import Mesh, PartitionSpec as P

SIDE = 160
SLAB = 5
TERMS = 4

HALO = TERMS
LANES = 128
SLOTS = 8
RUN = SIDE // 8
FLAT = SIDE * SIDE // LANES
STRIDE = FLAT // 8
WIDTH = 2 * LANES
BLOCK = 32
TALL = SIDE + 16

time_step = 0.3
four_pi = 4.0 * math.pi
two_pi = 2.0 * math.pi
highest = lax.Precision.HIGHEST
MEBI = 1024 * 1024
SMEM_SPEC = pl.BlockSpec(memory_space=pltpu.SMEM)
VMEM_SPEC = pl.BlockSpec(memory_space=pltpu.VMEM)
HBM_SPEC = pl.BlockSpec(memory_space=pltpu.HBM)


def hartley_table(count_cells):
    index_run = np.arange(count_cells)
    angles = (index_run[:, None] * index_run[None, :] % count_cells) * (2.0 * np.pi / count_cells)
    return np.cos(angles) + np.sin(angles)


def plane_order():
    rows = np.arange(SIDE)
    return RUN * (rows % 8) + rows // 8


def two_parts(table):
    table = table.astype(np.float32)
    high = table.astype(ml_dtypes.bfloat16)
    low = (table - high.astype(np.float32)).astype(ml_dtypes.bfloat16)
    return high, low


def tables_of_side():
    table = hartley_table(SIDE)
    along_z = np.zeros((WIDTH, WIDTH))
    along_z[:SIDE, :SIDE] = table
    high, low = two_parts(along_z)
    along_z = np.concatenate([high, high, low], axis=0)
    high, low = two_parts(table[:, plane_order()])
    into_y = np.concatenate([high, high, low], axis=1)
    high, low = two_parts(table[plane_order(), :])
    out_of_y = np.concatenate([high, high, low], axis=1)
    return along_z, into_y, out_of_y


def circle_table():
    across = 2 * np.arange(SIDE, dtype=np.int64) - (SIDE - 1)
    return (across[:, None] ** 2 + across[None, :] ** 2).astype(np.int32)


def circle_plane():
    table = np.full((SIDE, WIDTH), 4 * SIDE * SIDE, np.int32)
    table[:, :SIDE] = circle_table()[plane_order()]
    return table


def mesh_points(x_row, circle, length_cells):
    room = ((length_cells - 2) ** 2 - (2 * x_row - (length_cells - 1)) ** 2) * (SIDE - 2) ** 2
    return (circle * (length_cells - 2) ** 2 <= room) & (circle < 4 * SIDE * SIDE)


def column_pieces(first, count):
    pieces = []
    column = first
    while column < first + count:
        row = column // SIDE
        stop = min((row + 1) * SIDE, first + count)
        pieces.append((row, column - row * SIDE, stop - row * SIDE))
        column = stop
    return pieces


def eight(values):
    missing = jnp.zeros((SLOTS - values.shape[0], values.shape[1]), values.dtype)
    return jnp.concatenate([values, missing], axis=0)


def to_plane(load, store):
    lane = lax.broadcasted_iota(jnp.int32, (8, LANES), 1)
    for step in range(RUN // 4):
        rows = [load(5 * step + part) for part in range(5)]
        store(4 * step, rows[0], rows[1])
        for part in range(1, 4):
            left = pltpu.roll(rows[part], LANES - 32 * part, 1)
            right = pltpu.roll(rows[part + 1], LANES - 32 * part, 1)
            store(4 * step + part, jnp.where(lane < LANES - 32 * part, left, right), right)


def to_flat(load, store):
    lane = lax.broadcasted_iota(jnp.int32, (8, LANES), 1)
    for step in range(RUN // 4):
        turned = []
        for part in range(4):
            low, high = load(4 * step + part)
            if part:
                low = pltpu.roll(low, 32 * part, 1)
                high = pltpu.roll(high, 32 * part, 1)
            turned.append((low, high))
        store(5 * step, turned[0][0])
        for part in range(1, 4):
            ended = 32 * (part - 1)
            values = jnp.where(lane < ended + 32, turned[part - 1][1], turned[part][0])
            if ended:
                values = jnp.where(lane < ended, turned[part - 1][0], values)
            store(5 * step + part, values)
        store(5 * step + 4, jnp.where(lane < 96, turned[3][0], turned[3][1]))


def chords():
    across = 2 * np.arange(SIDE, dtype=np.int64) - (SIDE - 1)
    room = (SIDE - 2) ** 2 - across**2
    return [max([w for w in range(1, SIDE // 2 + 1) if (2 * w - 1) ** 2 <= left], default=0) for left in room]


def chord_moves():
    moves = []
    packed = 0
    for row, half in enumerate(chords()):
        if half:
            moves.append((row * SIDE + SIDE // 2 - half, packed, 2 * half))
            packed += 2 * half
    return moves


def packed_tiles():
    _, start, length = chord_moves()[-1]
    return -(-(start + length) // LANES)


def move_lanes(moves, load, store):
    lane = lax.broadcasted_iota(jnp.int32, (8, LANES), 1)
    pieces = {}
    for source, target, length in moves:
        while length:
            size = min(length, LANES - source % LANES, LANES - target % LANES)
            pieces.setdefault(target // LANES, []).append((target % LANES, source // LANES, (target - source) % LANES))
            source, target, length = source + size, target + size, length - size
    loaded = {}
    turned = {}
    for tile in sorted(pieces):
        values = None
        for first, origin, shift in sorted(pieces[tile]):
            if origin not in loaded:
                loaded[origin] = load(origin)
            if (origin, shift) not in turned:
                turned[origin, shift] = pltpu.roll(loaded[origin], shift, 1) if shift else loaded[origin]
            piece = turned[origin, shift]
            values = piece if values is None else jnp.where(lane >= first, piece, values)
        store(tile, values)


def pack_chords(rows_ref, store):
    move_lanes(chord_moves(), lambda tile: rows_ref[pl.ds(tile, 8, stride=FLAT), :], store)


def unpack_chords(load, rows_ref):
    def store(tile, values):
        rows_ref[pl.ds(tile, 8, stride=FLAT), :] = values

    move_lanes([(target, source, length) for source, target, length in chord_moves()], load, store)


def parts_of(values):
    high = values.astype(jnp.bfloat16)
    low = (values - high.astype(jnp.float32)).astype(jnp.bfloat16)
    return high, low


def turn_z(values, table):
    high, low = parts_of(values)
    return jnp.dot(
        jnp.concatenate([high, low, high], axis=1), table, preferred_element_type=jnp.float32
    )


def turn_y(table, values):
    high, low = parts_of(values)
    return jnp.dot(
        table, jnp.concatenate([high, low, high], axis=0), preferred_element_type=jnp.float32
    )


def send_columns(planes_ref, slots, table_y, table_z, low_ref, high_ref):
    along_z = turn_z(planes_ref[:slots * SIDE, :], table_z)
    for slot in range(slots):
        rows = slice(slot * SIDE, (slot + 1) * SIDE)
        waves = turn_y(table_y, along_z[rows])
        low_ref[rows, :] = waves[:, :LANES]
        high_ref[rows, :] = waves[:, LANES:]
    low_ref[slots * SIDE:, :] = jnp.zeros(((SLOTS - slots) * SIDE, LANES), jnp.float32)
    high_ref[slots * SIDE:, :] = jnp.zeros(((SLOTS - slots) * SIDE, LANES), jnp.float32)


def chunk_of(low_ref, high_ref, first_row, pieces, extra):
    parts = []
    for row, start, stop in pieces:
        at = pl.ds(first_row + row, SLOTS, stride=SIDE)
        values = jnp.concatenate([low_ref[at, :], high_ref[at, :]], axis=1)
        parts.append(values[:, start:stop])
    return jnp.concatenate(parts + [extra], axis=1)


def layers_of(stored_ref, flat_ref):
    @pl.loop(0, FLAT // 8)
    def _(step):
        for part in range(8):
            lanes = pl.ds(pl.multiple_of((step * 8 + part) * LANES, LANES), LANES)
            flat_ref[pl.ds(step * 8 + part, SLOTS, stride=FLAT), :] = eight(stored_ref[:, lanes])


def place_of(start_ref):
    position = lax.axis_index("domain")
    return position, start_ref[position], start_ref[position + 1] - start_ref[position]


def started(sems, pairs):
    copies = [pltpu.make_async_copy(*pair, sems.at[index]) for index, pair in enumerate(pairs)]
    for made in copies:
        made.start()
    return copies


def layers_at(orbitals_ref, part, start, count):
    return orbitals_ref.at[part, pl.ds(pl.multiple_of(start * FLAT, 8), count * FLAT)]


def rows_at(ref, part, count):
    return ref.at[pl.ds(part * count * FLAT, count * FLAT)]


def pack_kernel(start_ref, orbitals_ref, up_ref, down_ref, up_far_ref, down_far_ref, up_rows_ref,
                down_rows_ref, up_buffer_ref, down_buffer_ref, in_sems, out_sems):
    _, _, thickness = place_of(start_ref)
    first = jnp.maximum(thickness - HALO, 0)
    arrivals = started(
        in_sems,
        [
            (layers_at(orbitals_ref, part, start, count), rows_at(rows_ref, part, count))
            for start, rows_ref, count in (
                (first, up_rows_ref, HALO),
                (0, down_rows_ref, HALO),
                (thickness - 1, up_far_ref, 1),
                (0, down_far_ref, 1),
            )
            for part in range(2)
        ],
    )
    departures = []
    for index, (rows_ref, buffer_ref, out_ref) in enumerate(
        ((up_rows_ref, up_buffer_ref, up_ref), (down_rows_ref, down_buffer_ref, down_ref))
    ):
        arrivals[2 * index].wait()
        arrivals[2 * index + 1].wait()

        def store(tile, values, buffer_ref=buffer_ref):
            buffer_ref[:, tile * LANES:(tile + 1) * LANES] = values

        pack_chords(rows_ref, store)
        departures.append(pltpu.make_async_copy(buffer_ref, out_ref, out_sems.at[index]))
        departures[-1].start()
    for made in arrivals[4:] + departures:
        made.wait()


def pack_potential_kernel(start_ref, potential_ref, v_ref, flat_ref, v_rows_ref):
    _, _, thickness = place_of(start_ref)
    v_first = jnp.where(lax.axis_index("core") == 0, thickness - (HALO - 1), 0)
    layers_of(potential_ref, flat_ref)
    for layer in range(HALO - 1):
        v_rows_ref[layer * FLAT:(layer + 1) * FLAT, :] = flat_ref[
            pl.ds(pl.multiple_of((v_first + layer) * FLAT, 8), FLAT), :
        ]

    def store_v(tile, values):
        for layer in range(HALO - 1):
            v_ref[layer, tile:tile + 1, :] = values[layer:layer + 1]

    pack_chords(v_rows_ref, store_v)


def ions_kernel(count, length_cells, start_ref, background_ref, circle_ref, table_y_ref, table_z_ref,
                out_ref, flat_ref, planes_ref, low_ref, high_ref):
    _, own_start, thickness = place_of(start_ref)
    slots = background_ref.shape[0]
    groups, _, width = out_ref.shape
    layers_of(background_ref, flat_ref)

    def body(slot, total):
        def store(tile, low, high):
            rows = pl.ds(pl.multiple_of(slot * SIDE + tile * 8, 8), 8)
            planes_ref[rows, :LANES] = low
            planes_ref[rows, LANES:] = high

        to_plane(lambda k: flat_ref[pl.ds(slot * FLAT + k, 8, stride=STRIDE), :], store)
        rows = pl.ds(pl.multiple_of(slot * SIDE, 8), SIDE)
        inside = mesh_points(own_start + slot, circle_ref[...], length_cells) & (slot < thickness)
        values = jnp.where(inside, planes_ref[rows, :], 0.0)
        planes_ref[rows, :] = values
        return total + jnp.sum(values.reshape(RUN, 8, WIDTH), axis=0)

    total = lax.fori_loop(0, slots, body, jnp.zeros((8, WIDTH), jnp.float32))
    whole = jnp.broadcast_to(jnp.sum(total, keepdims=True), (SLOTS, LANES))[:, :width - count]
    send_columns(planes_ref, slots, table_y_ref[...], table_z_ref[...], low_ref, high_ref)
    core_rows = SIDE // lax.axis_size("core")
    first_row = lax.axis_index("core") * core_rows + lax.axis_index("row") * (core_rows // lax.axis_size("row"))
    for group in range(groups):
        out_ref[group] = chunk_of(low_ref, high_ref, first_row, column_pieces(group * count, count), whole)


def propagate_kernel(count, length_cells, start_ref, weight_ref, orbitals_ref, potential_ref, below_hbm_ref,
                     above_hbm_ref, below_far_hbm_ref, above_far_hbm_ref, v_hbm_ref, v_other_hbm_ref,
                     circle_ref, table_y_ref, table_z_ref, psi_ref, kept_ref, sent_ref, first_ref, second_ref,
                     third_ref, fourth_ref, sum_ref, centre_ref, beside_ref, flat_ref, planes_ref, low_ref,
                     high_ref, below_rows_ref, above_rows_ref, v_rows_ref, v_ref, v_other_ref, below_ref,
                     above_ref, below_far_ref, above_far_ref, in_sems, out_sem):
    arrivals = started(
        in_sems,
        [
            (v_hbm_ref, v_ref),
            (v_other_hbm_ref, v_other_ref),
            (below_hbm_ref, below_ref),
            (above_hbm_ref, above_ref),
            (below_far_hbm_ref, below_far_ref),
            (above_far_hbm_ref, above_far_ref),
        ],
    )
    position, own_start, thickness = place_of(start_ref)
    domains = lax.axis_size("domain")
    before = start_ref[jnp.maximum(position - 1, 0)]
    after = start_ref[jnp.minimum(position + 2, domains)]
    short_below = ((position > 0) & (own_start - before < HALO)).astype(jnp.int32)
    short_above = (position < domains - 1) & (after - own_start - thickness < HALO)
    weight = weight_ref[0]
    core = lax.axis_index("core")
    slots = orbitals_ref.shape[1]
    layers = slots + 2 * HALO
    devices, _, width = kept_ref.shape
    field_refs = (first_ref, second_ref, third_ref, fourth_ref)

    def field_layer(part, x_row):
        def store(tile, low, high):
            first_ref[part, x_row, 8 + 8 * tile:16 + 8 * tile, :LANES] = low
            first_ref[part, x_row, 8 + 8 * tile:16 + 8 * tile, LANES:] = high

        return store

    def potential_layer(x_row):
        def store(tile, low, high):
            centre_ref[x_row, 8 * tile:8 * tile + 8, :LANES] = low
            centre_ref[x_row, 8 * tile:8 * tile + 8, LANES:] = high

        return store

    def rows_from(ref, *at):
        return lambda k: ref[(*at, pl.ds(k, 8, stride=STRIDE), slice(None))]

    def layer_of(rows_ref, layer):
        return lambda k: rows_ref[pl.ds(layer * FLAT + k, 8, stride=STRIDE), :]

    layers_of(potential_ref, flat_ref)

    @pl.loop(0, slots)
    def _(slot):
        for part in range(2):
            to_plane(rows_from(orbitals_ref, part, slot), field_layer(part, HALO + slot))
        to_plane(layer_of(flat_ref, slot), potential_layer(HALO + slot))

    for made in arrivals:
        made.wait()
    for packed_ref, rows_ref in ((below_ref, below_rows_ref), (above_ref, above_rows_ref)):
        unpack_chords(
            lambda tile, packed_ref=packed_ref: packed_ref[:, tile * LANES:(tile + 1) * LANES], rows_ref
        )
    unpack_chords(
        lambda tile: eight(
            jnp.concatenate([ref[:, tile, :] for ref in (v_ref, v_other_ref)], axis=0)
        ),
        v_rows_ref,
    )

    @pl.loop(0, HALO - 1)
    def _(layer):
        lower = 1 + layer
        upper = HALO + thickness + layer
        to_plane(layer_of(v_rows_ref, layer), potential_layer(jnp.where(core == 0, lower, upper)))
        to_plane(layer_of(v_rows_ref, HALO - 1 + layer), potential_layer(jnp.where(core == 0, upper, lower)))
        for part in range(2):
            to_plane(
                layer_of(below_rows_ref, part * HALO + 1 + layer - short_below), field_layer(part, 1 + layer)
            )
            to_plane(
                layer_of(above_rows_ref, part * HALO + layer), field_layer(part, HALO + thickness + layer)
            )

    @pl.loop(0, 2)
    def _(part):
        last = 2 * HALO - 1 + thickness

        @pl.when(short_below > 0)
        def _():
            to_plane(layer_of(below_far_ref, part), field_layer(part, 0))

        @pl.when(short_below == 0)
        def _():
            to_plane(layer_of(below_rows_ref, part * HALO), field_layer(part, 0))

        @pl.when(short_above)
        def _():
            to_plane(layer_of(above_far_ref, part), field_layer(part, last))

        @pl.when(jnp.logical_not(short_above))
        def _():
            to_plane(layer_of(above_rows_ref, part * HALO + HALO - 1), field_layer(part, last))

    def wrap(term, part, x_row):
        first = field_refs[term][part, x_row, 8:16, :]
        final = field_refs[term][part, x_row, SIDE:SIDE + 8, :]
        field_refs[term][part, x_row, :8, :] = pltpu.roll(final, 1, 0)
        field_refs[term][part, x_row, SIDE + 8:, :] = pltpu.roll(first, 7, 0)

    @pl.loop(0, layers)
    def _(x_row):
        known = x_row < thickness + 2 * HALO
        for block in range(SIDE // BLOCK):
            rows = slice(block * BLOCK, (block + 1) * BLOCK)
            inner = slice(8 + block * BLOCK, 8 + (block + 1) * BLOCK)
            inside = mesh_points(own_start - HALO + x_row, circle_ref[rows, :], length_cells) & known
            centre_ref[x_row, rows, :] = jnp.where(
                inside, (3.0 + centre_ref[x_row, rows, :]) * time_step, 0.0
            )
            beside_ref[x_row, rows, :] = jnp.where(inside, 0.5 * time_step, 0.0)
            for part in range(2):
                first_ref[part, x_row, inner, :] = jnp.where(
                    inside, first_ref[part, x_row, inner, :], 0.0
                )
        for part in range(2):
            wrap(0, part, x_row)

    def hamilton(term, part, x_row, block, centre, beside):
        field_ref = field_refs[term]
        tall = field_ref[part, x_row, block * BLOCK:block * BLOCK + BLOCK + 16, :]
        inner = slice(8 + block * BLOCK, 8 + (block + 1) * BLOCK)
        field = tall[8:8 + BLOCK]
        around = field_ref[part, x_row - 1, inner, :] + field_ref[part, x_row + 1, inner, :]
        around = around + (tall[:BLOCK] + tall[16:])
        around = around + (pltpu.roll(field, 1, 1) + pltpu.roll(field, WIDTH - 1, 1))
        return centre * field - beside * around

    for term in range(1, TERMS):

        @pl.loop(term, layers - term)
        def _(x_row, term=term):
            for block in range(SIDE // BLOCK):
                rows = slice(block * BLOCK, (block + 1) * BLOCK)
                inner = slice(8 + block * BLOCK, 8 + (block + 1) * BLOCK)
                centre = centre_ref[x_row, rows, :]
                beside = beside_ref[x_row, rows, :]
                for part in range(2):
                    field_refs[term][part, x_row, inner, :] = hamilton(
                        term - 1, part, x_row, block, centre, beside
                    )
            for part in range(2):
                wrap(term, part, x_row)

    def finish(slot, total):
        x_row = HALO + slot
        owned = slot < thickness
        for block in range(SIDE // BLOCK):
            rows = slice(block * BLOCK, (block + 1) * BLOCK)
            inner = slice(8 + block * BLOCK, 8 + (block + 1) * BLOCK)
            centre = centre_ref[x_row, rows, :]
            beside = beside_ref[x_row, rows, :]
            density = jnp.zeros((BLOCK, WIDTH), jnp.float32)
            for part, sign in ((0, 1.0), (1, -1.0)):
                summed = first_ref[part, x_row, inner, :]
                summed = summed + sign * second_ref[1 - part, x_row, inner, :]
                summed = summed - (1.0 / 2.0) * third_ref[part, x_row, inner, :]
                summed = summed - (sign / 6.0) * fourth_ref[1 - part, x_row, inner, :]
                summed = summed + (1.0 / 24.0) * hamilton(3, part, x_row, block, centre, beside)
                summed = jnp.where(owned, summed, 0.0)
                sum_ref[part, slot, rows, :] = summed
                density = density + summed * summed
            density = weight * density
            planes_ref[pl.ds(pl.multiple_of(slot * SIDE + block * BLOCK, 8), BLOCK), :] = density
            total = total + jnp.sum(density.reshape(BLOCK // 8, 8, WIDTH), axis=0)

        return total

    total = lax.fori_loop(0, slots, finish, jnp.zeros((8, WIDTH), jnp.float32))
    departure = pltpu.make_async_copy(sum_ref, psi_ref, out_sem)
    departure.start()
    whole = jnp.broadcast_to(jnp.sum(total, keepdims=True), (SLOTS, LANES))[:, :width - count]
    send_columns(planes_ref, slots, table_y_ref[...], table_z_ref[...], low_ref, high_ref)
    core_rows = SIDE // 2
    first_row = core * core_rows
    for device in range(devices):
        pieces = column_pieces(device * count, count)
        kept_ref[device] = chunk_of(low_ref, high_ref, first_row, pieces, whole)
        sent_ref[device] = chunk_of(low_ref, high_ref, core_rows - first_row, pieces, whole)
    departure.wait()


def unpack_kernel(weight_ref, psi_ref, next_ref, density_kept_ref, density_sent_ref, density_ref):
    core = lax.axis_index("core")
    weight = weight_ref[0]
    slots = psi_ref.shape[1]

    @pl.loop(0, slots)
    def _(slot):
        for part in range(2):

            def load(tile, part=part):
                tall = psi_ref[part, slot, 8 * tile:8 * tile + 8, :]
                return tall[:, :LANES], tall[:, LANES:]

            def store(k, values, part=part):
                next_ref[part, slot, pl.ds(k, 8, stride=STRIDE), :] = values

            to_flat(load, store)
        real = next_ref[0, slot]
        imag = next_ref[1, slot]
        density_ref[slot] = weight * (real * real + imag * imag)

    for slot in range(slots, SLOTS):
        density_ref[slot] = jnp.zeros((FLAT, LANES), jnp.float32)

    @pl.loop(0, SLOTS // 2)
    def _(slot):
        density_kept_ref[slot] = density_ref[core * (SLOTS // 2) + slot]
        density_sent_ref[slot] = density_ref[(1 - core) * (SLOTS // 2) + slot]


def wave_squared(index, count_cells):
    folded = jnp.where(2 * index <= count_cells, index, index - count_cells)
    wave_number = folded.astype(jnp.float32) * (two_pi / count_cells)
    return wave_number * wave_number


def coulomb_kernel(count, length_cells, start_ref, charge_ref, ions_ref, table_ref, out_ref):
    domains, _, width = ions_ref.shape
    states = charge_ref.shape[0] // domains
    device = (lax.axis_index("core") * states + lax.axis_index("row")) * domains + lax.axis_index("domain")
    charge = charge_ref[:domains]
    for state in range(1, states):
        charge = charge + charge_ref[state * domains:(state + 1) * domains]
    charge = charge.reshape(domains * SLOTS, width)
    ions = ions_ref[...].reshape(domains * SLOTS, width)
    first = lax.broadcasted_iota(jnp.int32, (domains * SLOTS, width), 0) % SLOTS == 0
    lane = lax.broadcasted_iota(jnp.int32, (domains * SLOTS, width), 1)
    chosen = first & (lane == count)
    electrons = jnp.sum(jnp.where(chosen, charge, 0.0), keepdims=True)
    ionic = jnp.sum(jnp.where(chosen, ions, 0.0), keepdims=True)
    charge = charge - (electrons / ionic) * ions
    layer = lax.broadcasted_iota(jnp.int32, (length_cells, domains * SLOTS), 0)
    place = lax.broadcasted_iota(jnp.int32, (length_cells, domains * SLOTS), 1)
    chosen_layer = jnp.full(layer.shape, -1, jnp.int32)
    for domain in range(domains):
        slot = place - domain * SLOTS
        here = (slot >= 0) & (slot < start_ref[domain + 1] - start_ref[domain])
        chosen_layer = jnp.where(here, start_ref[domain] + slot, chosen_layer)
    pick = (layer == chosen_layer).astype(jnp.float32)
    table = jnp.dot(table_ref[...], pick, precision=highest, preferred_element_type=jnp.float32)
    waves = jnp.dot(table, charge, precision=highest, preferred_element_type=jnp.float32)
    wave_x = lax.broadcasted_iota(jnp.int32, waves.shape, 0)
    column = device * count + lax.broadcasted_iota(jnp.int32, waves.shape, 1)
    wave_y = ((column.astype(jnp.float32) + 0.5) * (1.0 / SIDE)).astype(jnp.int32)
    wave_z = column - wave_y * SIDE
    squared = (
        wave_squared(wave_x, length_cells) + wave_squared(wave_y, SIDE) + wave_squared(wave_z, SIDE)
    )
    gain = jnp.where(squared > 0, four_pi / jnp.where(squared > 0, squared, 1.0), 0.0)
    waves = waves * (gain * (1.0 / (length_cells * SIDE * SIDE)))
    back = lax.dot_general(
        table, waves, (((0,), (0,)), ((), ())), precision=highest, preferred_element_type=jnp.float32
    )
    back = back.reshape(domains, SLOTS, width)
    for state in range(states):
        out_ref[state * domains:(state + 1) * domains] = back


def field_kernel(count, length_cells, start_ref, waves_ref, others_ref, density_ref, other_ref,
                 circle_ref, table_y_ref, table_z_ref, out_ref, low_ref, high_ref, planes_ref, flat_ref):
    _, own_start, thickness = place_of(start_ref)
    devices = waves_ref.shape[0]
    slots = out_ref.shape[0]
    core = lax.axis_index("core")
    core_rows = SIDE // 2
    first_row = core * core_rows
    for source_ref, first in ((waves_ref, first_row), (others_ref, core_rows - first_row)):
        pieces = []
        for device in range(devices):
            column = 0
            for row, start, stop in column_pieces(device * count, count):
                values = source_ref[device, :, column:column + stop - start]
                column += stop - start
                if start > 0:
                    pieces.append(values)
                    values = jnp.concatenate(pieces, axis=1)
                if stop < SIDE:
                    pieces = [values]
                    continue
                pieces = []
                at = pl.ds(first + row, SLOTS, stride=SIDE)
                low_ref[at, :] = values[:, :LANES]
                high_ref[at, :] = jnp.concatenate(
                    [values[:, LANES:], jnp.zeros((SLOTS, WIDTH - SIDE), jnp.float32)], axis=1
                )
    table_y = table_y_ref[...]
    table_z = table_z_ref[...]
    used = slice(0, slots * SIDE)
    along_z = turn_z(jnp.concatenate([low_ref[used, :], high_ref[used, :]], axis=1), table_z)
    for slot in range(slots):
        rows = slice(slot * SIDE, (slot + 1) * SIDE)
        planes_ref[rows, :] = turn_y(table_y, along_z[rows])

    @pl.loop(0, slots)
    def _(slot):
        def load(tile):
            tall = planes_ref[pl.ds(pl.multiple_of(slot * SIDE + tile * 8, 8), 8), :]
            return tall[:, :LANES], tall[:, LANES:]

        def store(k, values):
            flat_ref[pl.ds(slot * FLAT + k, 8, stride=STRIDE), :] = values

        to_flat(load, store)
        rows = pl.ds(pl.multiple_of(slot * FLAT, 8), FLAT)
        here = slot // (SLOTS // 2) == core
        kept_slot = slot % (SLOTS // 2)
        content = jnp.where(here, density_ref[kept_slot], other_ref[kept_slot]) * (3.0 / math.pi)
        positive = jnp.where(content > 0, content, 1.0)
        root = jnp.exp(jnp.log(positive) * (1.0 / 3.0))
        root = root - (root - positive / (root * root)) * (1.0 / 3.0)
        root = jnp.where(content > 0, root, 0.0)
        inside = mesh_points(own_start + slot, circle_ref[...], length_cells) & (slot < thickness)
        flat_ref[rows, :] = jnp.where(inside, flat_ref[rows, :] - root, 0.0)

    @pl.loop(0, FLAT // 8)
    def _(step):
        for part in range(8):
            lanes = pl.ds(pl.multiple_of((step * 8 + part) * LANES, LANES), LANES)
            out_ref[:, lanes] = flat_ref[pl.ds(step * 8 + part, SLOTS, stride=FLAT), :][:slots]


def from_behind(value, steps):
    count = lax.axis_size("domain")
    leading, last = (max(0, -steps), min(count, count - steps))
    return lax.ppermute(value, "domain", [(source, source + steps) for source in range(leading, last)])


def swapped(value, axis):
    return lax.ppermute(value, axis, [(0, 1), (1, 0)])


def shards(orbitals, occupation, potential, background, layer_start):
    domains = lax.axis_size("domain")
    rows = lax.axis_size("row")
    devices = domains * rows
    length_cells = SLAB * domains
    layer_cap, plane = potential.shape
    count = plane // (2 * devices)
    width = -(-(count + 1) // LANES) * LANES
    circle = jnp.asarray(circle_plane())
    flat_circle = jnp.asarray(circle_table().reshape(FLAT, LANES))
    table_z, into_y, out_of_y = (jnp.asarray(table) for table in tables_of_side())
    table_x = jnp.asarray(hartley_table(length_cells).astype(np.float32))
    params = pltpu.CompilerParams(vmem_limit_bytes=16 * MEBI)
    large = pltpu.CompilerParams(vmem_limit_bytes=44 * MEBI)
    whole = pltpu.CompilerParams(vmem_limit_bytes=56 * MEBI)

    def f32(*shape):
        return jax.ShapeDtypeStruct(shape, jnp.float32)

    def scratch(*shape):
        return pltpu.VMEM(shape, jnp.float32)

    layers = orbitals.reshape(2, layer_cap, FLAT, LANES)
    packed = packed_tiles()
    v_rows = pl.pallas_call(
        pack_potential_kernel,
        out_shape=f32(HALO - 1, packed, LANES),
        in_specs=[SMEM_SPEC, VMEM_SPEC],
        out_specs=VMEM_SPEC,
        scratch_shapes=[scratch(SLOTS * FLAT, LANES), scratch(SLOTS * FLAT, LANES)],
        compiler_params=whole,
        name="pack_potential",
    )(layer_start, potential)
    v_rows, outer = lax.optimization_barrier((v_rows, orbitals))
    up, down, up_far, down_far = pl.pallas_call(
        pack_kernel,
        out_shape=(
            f32(2 * HALO, packed * LANES),
            f32(2 * HALO, packed * LANES),
            f32(2 * FLAT, LANES),
            f32(2 * FLAT, LANES),
        ),
        in_specs=[SMEM_SPEC, HBM_SPEC],
        out_specs=(HBM_SPEC, HBM_SPEC, VMEM_SPEC, VMEM_SPEC),
        scratch_shapes=[
            scratch(2 * HALO * FLAT, LANES),
            scratch(2 * HALO * FLAT, LANES),
            scratch(2 * HALO, packed * LANES),
            scratch(2 * HALO, packed * LANES),
            pltpu.SemaphoreType.DMA((8,)),
            pltpu.SemaphoreType.DMA((2,)),
        ],
        compiler_params=whole,
        cost_estimate=pl.CostEstimate(flops=0, transcendentals=0, bytes_accessed=30_000_000),
        name="pack_halo",
    )(layer_start, outer.reshape(2, layer_cap * FLAT, LANES))
    v_rows = lax.ppermute(
        v_rows,
        ("core", "domain"),
        [(source, source + 1) for source in range(domains - 1)]
        + [(domains + source + 1, domains + source) for source in range(domains - 1)],
    )
    below = from_behind(up, 1)
    above = from_behind(down, -1)
    below_far = from_behind(up_far, 2)
    above_far = from_behind(down_far, -2)
    v_rows, below_far, above_far = lax.optimization_barrier((v_rows, below_far, above_far))
    v_others = swapped(v_rows, "core")

    ions = pl.pallas_call(
        functools.partial(ions_kernel, count, length_cells),
        out_shape=f32(domains, SLOTS, width),
        in_specs=[SMEM_SPEC] + [VMEM_SPEC] * 4,
        out_specs=VMEM_SPEC,
        scratch_shapes=[
            scratch(SLOTS * FLAT, LANES),
            scratch(layer_cap * SIDE, WIDTH),
            scratch(SLOTS * SIDE, LANES),
            scratch(SLOTS * SIDE, LANES),
        ],
        compiler_params=params,
        name="ion_waves",
    )(layer_start, background, circle, into_y, table_z)
    ions = lax.all_to_all(ions, "domain", split_axis=0, concat_axis=0, tiled=True)
    ions, below = lax.optimization_barrier((ions, below))

    span = layer_cap + 2 * HALO
    fields = (2, span, TALL, WIDTH)
    psi, kept, sent = pl.pallas_call(
        functools.partial(propagate_kernel, count, length_cells),
        out_shape=(
            pltpu.HBM((2, layer_cap, SIDE, WIDTH), jnp.float32),
            f32(devices, SLOTS, width),
            f32(devices, SLOTS, width),
        ),
        in_specs=[SMEM_SPEC, SMEM_SPEC, VMEM_SPEC, VMEM_SPEC] + [HBM_SPEC] * 6 + [VMEM_SPEC] * 3,
        out_specs=(HBM_SPEC, VMEM_SPEC, VMEM_SPEC),
        scratch_shapes=[scratch(*fields)] * TERMS
        + [
            scratch(2, layer_cap, SIDE, WIDTH),
            scratch(span, SIDE, WIDTH),
            scratch(span, SIDE, WIDTH),
            scratch(SLOTS * FLAT, LANES),
            scratch(layer_cap * SIDE, WIDTH),
            scratch(SLOTS * SIDE, LANES),
            scratch(SLOTS * SIDE, LANES),
            scratch(SLOTS * FLAT, LANES),
            scratch(SLOTS * FLAT, LANES),
            scratch(SLOTS * FLAT, LANES),
            scratch(HALO - 1, packed, LANES),
            scratch(HALO - 1, packed, LANES),
            scratch(2 * HALO, packed * LANES),
            scratch(2 * HALO, packed * LANES),
            scratch(2 * FLAT, LANES),
            scratch(2 * FLAT, LANES),
            pltpu.SemaphoreType.DMA((6,)),
            pltpu.SemaphoreType.DMA,
        ],
        compiler_params=large,
        name="propagate",
    )(layer_start, occupation, layers, potential, below, above, below_far, above_far, v_rows, v_others,
      circle, into_y, table_z)
    waves = kept + swapped(sent, "core")
    waves, psi = lax.optimization_barrier((waves, psi))
    waves = lax.all_to_all(waves, ("row", "domain"), split_axis=0, concat_axis=0, tiled=True)
    orbitals_next, density_kept, density_sent = pl.pallas_call(
        unpack_kernel,
        out_shape=(
            f32(2, layer_cap, FLAT, LANES),
            f32(SLOTS // 2, FLAT, LANES),
            f32(SLOTS // 2, FLAT, LANES),
        ),
        in_specs=[SMEM_SPEC, VMEM_SPEC],
        out_specs=(VMEM_SPEC,) * 3,
        scratch_shapes=[scratch(SLOTS, FLAT, LANES)],
        compiler_params=params,
        name="unpack",
    )(occupation, psi)
    density = density_kept + swapped(density_sent, "core")
    waves, density = lax.optimization_barrier((waves, density))
    other_density = swapped(density, "row")
    waves = pl.pallas_call(
        functools.partial(coulomb_kernel, count, length_cells),
        out_shape=f32(devices, SLOTS, width),
        in_specs=[SMEM_SPEC] + [VMEM_SPEC] * 3,
        out_specs=VMEM_SPEC,
        compiler_params=params,
        name="coulomb",
    )(layer_start, waves, ions, table_x)
    waves = lax.all_to_all(waves, ("row", "domain"), split_axis=0, concat_axis=0, tiled=True)
    waves, other_density = lax.optimization_barrier((waves, other_density))
    density = density + other_density
    other_density = swapped(density, "core")
    other_waves = swapped(waves, "core")
    potential_next = pl.pallas_call(
        functools.partial(field_kernel, count, length_cells),
        out_shape=f32(layer_cap, plane),
        in_specs=[SMEM_SPEC] + [VMEM_SPEC] * 7,
        out_specs=VMEM_SPEC,
        scratch_shapes=[
            scratch(SLOTS * SIDE, LANES),
            scratch(SLOTS * SIDE, LANES),
            scratch(layer_cap * SIDE, WIDTH),
            scratch(SLOTS * FLAT, LANES),
        ],
        compiler_params=params,
        name="field",
    )(layer_start, waves, other_waves, density, other_density, flat_circle, out_of_y, table_z)
    return orbitals_next.reshape(orbitals.shape), potential_next


def solution(mesh):
    domains = mesh.shape["domain"]
    split = Mesh(mesh.devices.reshape(-1, 2, domains), ("row", "core", "domain"))
    states = ("row", "core")
    return jax.shard_map(
        shards,
        mesh=split,
        in_specs=(
            P(None, states, "domain", None),
            P(states),
            P("domain", None),
            P("domain", None),
            P(),
        ),
        out_specs=(P(None, states, "domain", None), P("domain", None)),
        check_vma=False,
    )
```

```python
import functools
import math

import jax
import jax.numpy as jnp
import ml_dtypes
import numpy as np
from jax import lax
from jax.experimental import pallas as pl
from jax.experimental.pallas import tpu as pltpu
from jax.sharding import Mesh, PartitionSpec as P

SIDE = 160
SLAB = 5
TERMS = 4

HALO = TERMS
LANES = 128
SLOTS = 8
RUN = SIDE // 8
FLAT = SIDE * SIDE // LANES
STRIDE = FLAT // 8
WIDTH = 2 * LANES
BLOCK = 32
TALL = SIDE + 16

time_step = 0.3
four_pi = 4.0 * math.pi
two_pi = 2.0 * math.pi
highest = lax.Precision.HIGHEST
MEBI = 1024 * 1024
SMEM_SPEC = pl.BlockSpec(memory_space=pltpu.SMEM)
VMEM_SPEC = pl.BlockSpec(memory_space=pltpu.VMEM)
HBM_SPEC = pl.BlockSpec(memory_space=pltpu.HBM)


def hartley_table(count_cells):
    index_run = np.arange(count_cells)
    angles = (index_run[:, None] * index_run[None, :] % count_cells) * (2.0 * np.pi / count_cells)
    return np.cos(angles) + np.sin(angles)


def plane_order():
    rows = np.arange(SIDE)
    return RUN * (rows % 8) + rows // 8


def two_parts(table):
    table = table.astype(np.float32)
    high = table.astype(ml_dtypes.bfloat16)
    low = (table - high.astype(np.float32)).astype(ml_dtypes.bfloat16)
    return high, low


def tables_of_side():
    table = hartley_table(SIDE)
    along_z = np.zeros((WIDTH, WIDTH))
    along_z[:SIDE, :SIDE] = table
    high, low = two_parts(along_z)
    along_z = np.concatenate([high, high, low], axis=0)
    high, low = two_parts(table[:, plane_order()])
    into_y = np.concatenate([high, high, low], axis=1)
    high, low = two_parts(table[plane_order(), :])
    out_of_y = np.concatenate([high, high, low], axis=1)
    return along_z, into_y, out_of_y


def circle_table():
    across = 2 * np.arange(SIDE, dtype=np.int64) - (SIDE - 1)
    return (across[:, None] ** 2 + across[None, :] ** 2).astype(np.int32)


def circle_plane():
    table = np.full((SIDE, WIDTH), 4 * SIDE * SIDE, np.int32)
    table[:, :SIDE] = circle_table()[plane_order()]
    return table


def circle_pair():
    table = circle_plane()
    table[:, LANES + 64:LANES + 96] = table[:, LANES:LANES + 32]
    return table


def mesh_points(x_row, circle, length_cells):
    room = ((length_cells - 2) ** 2 - (2 * x_row - (length_cells - 1)) ** 2) * (SIDE - 2) ** 2
    return (circle * (length_cells - 2) ** 2 <= room) & (circle < 4 * SIDE * SIDE)


def column_pieces(first, count):
    pieces = []
    column = first
    while column < first + count:
        row = column // SIDE
        stop = min((row + 1) * SIDE, first + count)
        pieces.append((row, column - row * SIDE, stop - row * SIDE))
        column = stop
    return pieces


def eight(values):
    missing = jnp.zeros((SLOTS - values.shape[0], values.shape[1]), values.dtype)
    return jnp.concatenate([values, missing], axis=0)


def plane_tiles(load, step):
    lane = lax.broadcasted_iota(jnp.int32, (8, LANES), 1)
    rows = [load(5 * step + part) for part in range(5)]
    tiles = [(rows[0], rows[1])]
    for part in range(1, 4):
        left = pltpu.roll(rows[part], LANES - 32 * part, 1)
        right = pltpu.roll(rows[part + 1], LANES - 32 * part, 1)
        tiles.append((jnp.where(lane < LANES - 32 * part, left, right), right))
    return tiles


def to_plane(load, store):
    for step in range(RUN // 4):
        for part, (low, high) in enumerate(plane_tiles(load, step)):
            store(4 * step + part, low, high)


def joined_tail(real, imag):
    lane = lax.broadcasted_iota(jnp.int32, real.shape, 1)
    return jnp.where(lane < 64, real, pltpu.roll(imag, 64, 1))


def to_plane_pair(load_real, load_imag, store):
    for step in range(RUN // 4):
        pairs = zip(plane_tiles(load_real, step), plane_tiles(load_imag, step))
        for part, ((real, real_tail), (imag, imag_tail)) in enumerate(pairs):
            store(4 * step + part, real, imag, joined_tail(real_tail, imag_tail))


def to_flat(load, store):
    lane = lax.broadcasted_iota(jnp.int32, (8, LANES), 1)
    for step in range(RUN // 4):
        turned = []
        for part in range(4):
            low, high = load(4 * step + part)
            if part:
                low = pltpu.roll(low, 32 * part, 1)
                high = pltpu.roll(high, 32 * part, 1)
            turned.append((low, high))
        store(5 * step, turned[0][0])
        for part in range(1, 4):
            ended = 32 * (part - 1)
            values = jnp.where(lane < ended + 32, turned[part - 1][1], turned[part][0])
            if ended:
                values = jnp.where(lane < ended, turned[part - 1][0], values)
            store(5 * step + part, values)
        store(5 * step + 4, jnp.where(lane < 96, turned[3][0], turned[3][1]))


def chords():
    across = 2 * np.arange(SIDE, dtype=np.int64) - (SIDE - 1)
    room = (SIDE - 2) ** 2 - across**2
    return [max([w for w in range(1, SIDE // 2 + 1) if (2 * w - 1) ** 2 <= left], default=0) for left in room]


def chord_moves():
    moves = []
    packed = 0
    for row, half in enumerate(chords()):
        if half:
            moves.append((row * SIDE + SIDE // 2 - half, packed, 2 * half))
            packed += 2 * half
    return moves


def packed_tiles():
    _, start, length = chord_moves()[-1]
    return -(-(start + length) // LANES)


def move_lanes(moves, load, store):
    lane = lax.broadcasted_iota(jnp.int32, (8, LANES), 1)
    pieces = {}
    for source, target, length in moves:
        while length:
            size = min(length, LANES - source % LANES, LANES - target % LANES)
            pieces.setdefault(target // LANES, []).append((target % LANES, source // LANES, (target - source) % LANES))
            source, target, length = source + size, target + size, length - size
    loaded = {}
    turned = {}
    for tile in sorted(pieces):
        values = None
        for first, origin, shift in sorted(pieces[tile]):
            if origin not in loaded:
                loaded[origin] = load(origin)
            if (origin, shift) not in turned:
                turned[origin, shift] = pltpu.roll(loaded[origin], shift, 1) if shift else loaded[origin]
            piece = turned[origin, shift]
            values = piece if values is None else jnp.where(lane >= first, piece, values)
        store(tile, values)


def pack_chords(rows_ref, store):
    move_lanes(chord_moves(), lambda tile: rows_ref[pl.ds(tile, 8, stride=FLAT), :], store)


def unpack_chords(load, rows_ref):
    def store(tile, values):
        rows_ref[pl.ds(tile, 8, stride=FLAT), :] = values

    move_lanes([(target, source, length) for source, target, length in chord_moves()], load, store)


def parts_of(values):
    high = values.astype(jnp.bfloat16)
    low = (values - high.astype(jnp.float32)).astype(jnp.bfloat16)
    return high, low


def turn_z(values, table):
    high, low = parts_of(values)
    return jnp.dot(
        jnp.concatenate([high, low, high], axis=1), table, preferred_element_type=jnp.float32
    )


def turn_y(table, values):
    high, low = parts_of(values)
    return jnp.dot(
        table, jnp.concatenate([high, low, high], axis=0), preferred_element_type=jnp.float32
    )


def send_columns(planes_ref, slots, table_y, table_z, low_ref, high_ref):
    along_z = turn_z(planes_ref[:slots * SIDE, :], table_z)
    for slot in range(slots):
        rows = slice(slot * SIDE, (slot + 1) * SIDE)
        waves = turn_y(table_y, along_z[rows])
        low_ref[rows, :] = waves[:, :LANES]
        high_ref[rows, :] = waves[:, LANES:]
    low_ref[slots * SIDE:, :] = jnp.zeros(((SLOTS - slots) * SIDE, LANES), jnp.float32)
    high_ref[slots * SIDE:, :] = jnp.zeros(((SLOTS - slots) * SIDE, LANES), jnp.float32)


def chunk_of(low_ref, high_ref, first_row, pieces, extra):
    parts = []
    for row, start, stop in pieces:
        at = pl.ds(first_row + row, SLOTS, stride=SIDE)
        values = jnp.concatenate([low_ref[at, :], high_ref[at, :]], axis=1)
        parts.append(values[:, start:stop])
    return jnp.concatenate(parts + [extra], axis=1)


def layers_of(stored_ref, flat_ref):
    @pl.loop(0, FLAT // 8)
    def _(step):
        for part in range(8):
            lanes = pl.ds(pl.multiple_of((step * 8 + part) * LANES, LANES), LANES)
            flat_ref[pl.ds(step * 8 + part, SLOTS, stride=FLAT), :] = eight(stored_ref[:, lanes])


def place_of(start_ref):
    position = lax.axis_index("domain")
    return position, start_ref[position], start_ref[position + 1] - start_ref[position]


def started(sems, pairs):
    copies = [pltpu.make_async_copy(*pair, sems.at[index]) for index, pair in enumerate(pairs)]
    for made in copies:
        made.start()
    return copies


def layers_at(orbitals_ref, part, start, count):
    return orbitals_ref.at[part, pl.ds(pl.multiple_of(start * FLAT, 8), count * FLAT)]


def rows_at(ref, part, count):
    return ref.at[pl.ds(part * count * FLAT, count * FLAT)]


def pack_kernel(start_ref, orbitals_ref, up_ref, down_ref, up_rows_ref, down_rows_ref, up_buffer_ref,
                down_buffer_ref, in_sems, out_sems):
    _, _, thickness = place_of(start_ref)
    first = jnp.maximum(thickness - HALO, 0)
    arrivals = started(
        in_sems,
        [
            (layers_at(orbitals_ref, part, start, HALO), rows_at(rows_ref, part, HALO))
            for start, rows_ref in ((first, up_rows_ref), (0, down_rows_ref))
            for part in range(2)
        ],
    )
    departures = []
    for index, (rows_ref, buffer_ref, out_ref) in enumerate(
        ((up_rows_ref, up_buffer_ref, up_ref), (down_rows_ref, down_buffer_ref, down_ref))
    ):
        arrivals[2 * index].wait()
        arrivals[2 * index + 1].wait()

        def store(tile, values, buffer_ref=buffer_ref):
            buffer_ref[:, tile * LANES:(tile + 1) * LANES] = values

        pack_chords(rows_ref, store)
        departures.append(pltpu.make_async_copy(buffer_ref, out_ref, out_sems.at[index]))
        departures[-1].start()
    for made in departures:
        made.wait()


def pack_rest_kernel(start_ref, potential_ref, orbitals_ref, v_ref, up_far_ref, down_far_ref, flat_ref,
                     v_rows_ref, stored_ref, in_sems):
    _, _, thickness = place_of(start_ref)
    v_first = jnp.where(lax.axis_index("core") == 0, thickness - (HALO - 1), 0)
    arrivals = started(
        in_sems,
        [(potential_ref, stored_ref)]
        + [
            (layers_at(orbitals_ref, part, start, 1), rows_at(far_ref, part, 1))
            for start, far_ref in ((thickness - 1, up_far_ref), (0, down_far_ref))
            for part in range(2)
        ],
    )
    arrivals[0].wait()
    layers_of(stored_ref, flat_ref)
    for layer in range(HALO - 1):
        v_rows_ref[layer * FLAT:(layer + 1) * FLAT, :] = flat_ref[
            pl.ds(pl.multiple_of((v_first + layer) * FLAT, 8), FLAT), :
        ]

    def store_v(tile, values):
        for layer in range(HALO - 1):
            v_ref[layer, tile:tile + 1, :] = values[layer:layer + 1]

    pack_chords(v_rows_ref, store_v)
    for made in arrivals[1:]:
        made.wait()


def ions_kernel(count, length_cells, start_ref, background_ref, circle_ref, table_y_ref, table_z_ref,
                out_ref, flat_ref, planes_ref, low_ref, high_ref):
    _, own_start, thickness = place_of(start_ref)
    slots = background_ref.shape[0]
    groups, _, width = out_ref.shape
    layers_of(background_ref, flat_ref)

    def body(slot, total):
        def store(tile, low, high):
            rows = pl.ds(pl.multiple_of(slot * SIDE + tile * 8, 8), 8)
            planes_ref[rows, :LANES] = low
            planes_ref[rows, LANES:] = high

        to_plane(lambda k: flat_ref[pl.ds(slot * FLAT + k, 8, stride=STRIDE), :], store)
        rows = pl.ds(pl.multiple_of(slot * SIDE, 8), SIDE)
        inside = mesh_points(own_start + slot, circle_ref[...], length_cells) & (slot < thickness)
        values = jnp.where(inside, planes_ref[rows, :], 0.0)
        planes_ref[rows, :] = values
        return total + jnp.sum(values.reshape(RUN, 8, WIDTH), axis=0)

    total = lax.fori_loop(0, slots, body, jnp.zeros((8, WIDTH), jnp.float32))
    whole = jnp.broadcast_to(jnp.sum(total, keepdims=True), (SLOTS, LANES))[:, :width - count]
    send_columns(planes_ref, slots, table_y_ref[...], table_z_ref[...], low_ref, high_ref)
    core_rows = SIDE // lax.axis_size("core")
    first_row = lax.axis_index("core") * core_rows + lax.axis_index("row") * (core_rows // lax.axis_size("row"))
    for group in range(groups):
        out_ref[group] = chunk_of(low_ref, high_ref, first_row, column_pieces(group * count, count), whole)


def propagate_kernel(count, length_cells, start_ref, weight_ref, orbitals_ref, potential_ref, below_hbm_ref,
                     above_hbm_ref, below_far_hbm_ref, above_far_hbm_ref, v_hbm_ref, v_other_hbm_ref,
                     circle_ref, table_y_ref, table_z_ref, psi_ref, kept_ref, sent_ref, first_ref, second_ref,
                     third_ref, fourth_ref, sum_ref, centre_ref, beside_ref, flat_ref, planes_ref, low_ref,
                     high_ref, below_rows_ref, above_rows_ref, v_rows_ref, v_ref, v_other_ref, below_ref,
                     above_ref, below_far_ref, above_far_ref, in_sems, out_sem):
    arrivals = started(
        in_sems,
        [
            (v_hbm_ref, v_ref),
            (v_other_hbm_ref, v_other_ref),
            (below_hbm_ref, below_ref),
            (above_hbm_ref, above_ref),
            (below_far_hbm_ref, below_far_ref),
            (above_far_hbm_ref, above_far_ref),
        ],
    )
    position, own_start, thickness = place_of(start_ref)
    domains = lax.axis_size("domain")
    before = start_ref[jnp.maximum(position - 1, 0)]
    after = start_ref[jnp.minimum(position + 2, domains)]
    short_below = ((position > 0) & (own_start - before < HALO)).astype(jnp.int32)
    short_above = (position < domains - 1) & (after - own_start - thickness < HALO)
    weight = weight_ref[0]
    core = lax.axis_index("core")
    slots = orbitals_ref.shape[1]
    layers = slots + 2 * HALO
    devices, _, width = kept_ref.shape
    field_refs = (first_ref, second_ref, third_ref, fourth_ref)
    spans = (slice(0, LANES), slice(LANES, 2 * LANES), slice(2 * LANES, 3 * LANES))
    lane = lax.broadcasted_iota(jnp.int32, (BLOCK, LANES), 1)

    def field_layer(x_row):
        def store(tile, *pieces):
            for span, piece in zip(spans, pieces):
                first_ref[x_row, 8 + 8 * tile:16 + 8 * tile, span] = piece

        return store

    def potential_layer(x_row):
        def store(tile, low, high):
            centre_ref[x_row, 8 * tile:8 * tile + 8, :LANES] = low
            centre_ref[x_row, 8 * tile:8 * tile + 8, LANES:] = joined_tail(high, high)

        return store

    def rows_from(ref, *at):
        return lambda k: ref[(*at, pl.ds(k, 8, stride=STRIDE), slice(None))]

    def layer_of(rows_ref, layer):
        return lambda k: rows_ref[pl.ds(layer * FLAT + k, 8, stride=STRIDE), :]

    layers_of(potential_ref, flat_ref)

    @pl.loop(0, slots)
    def _(slot):
        to_plane_pair(
            rows_from(orbitals_ref, 0, slot), rows_from(orbitals_ref, 1, slot), field_layer(HALO + slot)
        )
        to_plane(layer_of(flat_ref, slot), potential_layer(HALO + slot))

    for made in arrivals:
        made.wait()
    for packed_ref, rows_ref in ((below_ref, below_rows_ref), (above_ref, above_rows_ref)):
        unpack_chords(
            lambda tile, packed_ref=packed_ref: packed_ref[:, tile * LANES:(tile + 1) * LANES], rows_ref
        )
    unpack_chords(
        lambda tile: eight(
            jnp.concatenate([ref[:, tile, :] for ref in (v_ref, v_other_ref)], axis=0)
        ),
        v_rows_ref,
    )

    def halo_layer(rows_ref, layer, x_row):
        to_plane_pair(layer_of(rows_ref, layer), layer_of(rows_ref, HALO + layer), field_layer(x_row))

    @pl.loop(0, HALO - 1)
    def _(layer):
        lower = 1 + layer
        upper = HALO + thickness + layer
        to_plane(layer_of(v_rows_ref, layer), potential_layer(jnp.where(core == 0, lower, upper)))
        to_plane(layer_of(v_rows_ref, HALO - 1 + layer), potential_layer(jnp.where(core == 0, upper, lower)))
        halo_layer(below_rows_ref, 1 + layer - short_below, lower)
        halo_layer(above_rows_ref, layer, upper)

    last = 2 * HALO - 1 + thickness

    @pl.when(short_below > 0)
    def _():
        to_plane_pair(layer_of(below_far_ref, 0), layer_of(below_far_ref, 1), field_layer(0))

    @pl.when(short_below == 0)
    def _():
        halo_layer(below_rows_ref, 0, 0)

    @pl.when(short_above)
    def _():
        to_plane_pair(layer_of(above_far_ref, 0), layer_of(above_far_ref, 1), field_layer(last))

    @pl.when(jnp.logical_not(short_above))
    def _():
        halo_layer(above_rows_ref, HALO - 1, last)

    def wrap(term, x_row):
        first = field_refs[term][x_row, 8:16, :]
        final = field_refs[term][x_row, SIDE:SIDE + 8, :]
        field_refs[term][x_row, :8, :] = pltpu.roll(final, 1, 0)
        field_refs[term][x_row, SIDE + 8:, :] = pltpu.roll(first, 7, 0)

    @pl.loop(0, layers)
    def _(x_row):
        known = x_row < thickness + 2 * HALO
        for block in range(SIDE // BLOCK):
            rows = slice(block * BLOCK, (block + 1) * BLOCK)
            inner = slice(8 + block * BLOCK, 8 + (block + 1) * BLOCK)
            inside = mesh_points(own_start - HALO + x_row, circle_ref[rows, :], length_cells) & known
            centre_ref[x_row, rows, :] = jnp.where(
                inside, (3.0 + centre_ref[x_row, rows, :]) * time_step, 0.0
            )
            beside_ref[x_row, rows, :] = jnp.where(inside, 0.5 * time_step, 0.0)
            for span, part in zip(spans, (inside[:, :LANES], inside[:, :LANES], inside[:, LANES:])):
                first_ref[x_row, inner, span] = jnp.where(part, first_ref[x_row, inner, span], 0.0)
        wrap(0, x_row)

    def hamilton(term, x_row, block):
        field_ref = field_refs[term]
        rows = slice(block * BLOCK, (block + 1) * BLOCK)
        inner = slice(8 + block * BLOCK, 8 + (block + 1) * BLOCK)
        tall = field_ref[x_row, block * BLOCK:block * BLOCK + BLOCK + 16, :]
        around = field_ref[x_row - 1, inner, :] + field_ref[x_row + 1, inner, :]
        around = around + (tall[:BLOCK] + tall[16:])
        field = tall[8:8 + BLOCK]
        real, imag, tail = (field[:, span] for span in spans)
        real_left = pltpu.roll(real, 1, 1)
        tail_right = pltpu.roll(tail, LANES - 1, 1)
        along_z = (
            real_left + jnp.where(lane == LANES - 1, tail_right, pltpu.roll(real, LANES - 1, 1)),
            pltpu.roll(imag, 1, 1)
            + jnp.where(lane == LANES - 1, pltpu.roll(tail, 63, 1), pltpu.roll(imag, LANES - 1, 1)),
            tail_right
            + jnp.where(
                lane == 0,
                real_left,
                jnp.where(lane == 64, pltpu.roll(imag, 65, 1), pltpu.roll(tail, 1, 1)),
            ),
        )
        centre = centre_ref[x_row, rows, :]
        beside = beside_ref[x_row, rows, :]
        factors = [(centre[:, :LANES], beside[:, :LANES])] * 2 + [(centre[:, LANES:], beside[:, LANES:])]
        return [
            own * values - near * (around[:, span] + sides)
            for (own, near), values, span, sides in zip(factors, (real, imag, tail), spans, along_z)
        ]

    for term in range(1, TERMS):

        @pl.loop(term, layers - term)
        def _(x_row, term=term):
            for block in range(SIDE // BLOCK):
                inner = slice(8 + block * BLOCK, 8 + (block + 1) * BLOCK)
                for span, piece in zip(spans, hamilton(term - 1, x_row, block)):
                    field_refs[term][x_row, inner, span] = piece
            wrap(term, x_row)

    def finish(slot, total):
        x_row = HALO + slot
        owned = slot < thickness
        for block in range(SIDE // BLOCK):
            rows = slice(block * BLOCK, (block + 1) * BLOCK)
            inner = slice(8 + block * BLOCK, 8 + (block + 1) * BLOCK)
            even = []
            odd = []
            for span, last_term in zip(spans, hamilton(TERMS - 1, x_row, block)):
                terms = [ref[x_row, inner, span] for ref in field_refs]
                even.append(terms[0] - (1.0 / 2.0) * terms[2] + (1.0 / 24.0) * last_term)
                odd.append(terms[1] - (1.0 / 6.0) * terms[3])
            crossed = pltpu.roll(odd[2], 64, 1)
            pieces = [
                even[0] + odd[1],
                even[1] - odd[0],
                even[2] + jnp.where(lane < 64, crossed, -crossed),
            ]
            pieces = [jnp.where(owned, piece, 0.0) for piece in pieces]
            for span, piece in zip(spans, pieces):
                sum_ref[slot, rows, span] = piece
            real, imag, tail = (piece * piece for piece in pieces)
            density = weight * (real + imag)
            density_tail = weight * jnp.where(lane < 32, tail + pltpu.roll(tail, 64, 1), 0.0)
            at = pl.ds(pl.multiple_of(slot * SIDE + block * BLOCK, 8), BLOCK)
            planes_ref[at, :LANES] = density
            planes_ref[at, LANES:] = density_tail
            total = total + jnp.sum((density + density_tail).reshape(BLOCK // 8, 8, LANES), axis=0)
        return total

    total = lax.fori_loop(0, slots, finish, jnp.zeros((8, LANES), jnp.float32))
    departure = pltpu.make_async_copy(sum_ref, psi_ref, out_sem)
    departure.start()
    whole = jnp.broadcast_to(jnp.sum(total, keepdims=True), (SLOTS, LANES))[:, :width - count]
    send_columns(planes_ref, slots, table_y_ref[...], table_z_ref[...], low_ref, high_ref)
    core_rows = SIDE // 2
    first_row = core * core_rows
    for device in range(devices):
        pieces = column_pieces(device * count, count)
        kept_ref[device] = chunk_of(low_ref, high_ref, first_row, pieces, whole)
        sent_ref[device] = chunk_of(low_ref, high_ref, core_rows - first_row, pieces, whole)
    departure.wait()


def unpack_kernel(weight_ref, psi_ref, next_ref, density_kept_ref, density_sent_ref, density_ref):
    core = lax.axis_index("core")
    weight = weight_ref[0]
    slots = psi_ref.shape[0]

    @pl.loop(0, slots)
    def _(slot):
        for part in range(2):

            def load(tile, part=part):
                rows = psi_ref[slot, 8 * tile:8 * tile + 8, :]
                tail = rows[:, 2 * LANES:]
                return rows[:, part * LANES:(part + 1) * LANES], pltpu.roll(tail, 64, 1) if part else tail

            def store(k, values, part=part):
                next_ref[part, slot, pl.ds(k, 8, stride=STRIDE), :] = values

            to_flat(load, store)
        real = next_ref[0, slot]
        imag = next_ref[1, slot]
        density_ref[slot] = weight * (real * real + imag * imag)

    for slot in range(slots, SLOTS):
        density_ref[slot] = jnp.zeros((FLAT, LANES), jnp.float32)

    @pl.loop(0, SLOTS // 2)
    def _(slot):
        density_kept_ref[slot] = density_ref[core * (SLOTS // 2) + slot]
        density_sent_ref[slot] = density_ref[(1 - core) * (SLOTS // 2) + slot]


def wave_squared(index, count_cells):
    folded = jnp.where(2 * index <= count_cells, index, index - count_cells)
    wave_number = folded.astype(jnp.float32) * (two_pi / count_cells)
    return wave_number * wave_number


def coulomb_kernel(count, length_cells, start_ref, charge_ref, ions_ref, table_ref, out_ref):
    domains, _, width = ions_ref.shape
    states = charge_ref.shape[0] // domains
    device = (lax.axis_index("core") * states + lax.axis_index("row")) * domains + lax.axis_index("domain")
    charge = charge_ref[:domains]
    for state in range(1, states):
        charge = charge + charge_ref[state * domains:(state + 1) * domains]
    charge = charge.reshape(domains * SLOTS, width)
    ions = ions_ref[...].reshape(domains * SLOTS, width)
    first = lax.broadcasted_iota(jnp.int32, (domains * SLOTS, width), 0) % SLOTS == 0
    lane = lax.broadcasted_iota(jnp.int32, (domains * SLOTS, width), 1)
    chosen = first & (lane == count)
    electrons = jnp.sum(jnp.where(chosen, charge, 0.0), keepdims=True)
    ionic = jnp.sum(jnp.where(chosen, ions, 0.0), keepdims=True)
    charge = charge - (electrons / ionic) * ions
    layer = lax.broadcasted_iota(jnp.int32, (length_cells, domains * SLOTS), 0)
    place = lax.broadcasted_iota(jnp.int32, (length_cells, domains * SLOTS), 1)
    chosen_layer = jnp.full(layer.shape, -1, jnp.int32)
    for domain in range(domains):
        slot = place - domain * SLOTS
        here = (slot >= 0) & (slot < start_ref[domain + 1] - start_ref[domain])
        chosen_layer = jnp.where(here, start_ref[domain] + slot, chosen_layer)
    pick = (layer == chosen_layer).astype(jnp.float32)
    table = jnp.dot(table_ref[...], pick, precision=highest, preferred_element_type=jnp.float32)
    waves = jnp.dot(table, charge, precision=highest, preferred_element_type=jnp.float32)
    wave_x = lax.broadcasted_iota(jnp.int32, waves.shape, 0)
    column = device * count + lax.broadcasted_iota(jnp.int32, waves.shape, 1)
    wave_y = ((column.astype(jnp.float32) + 0.5) * (1.0 / SIDE)).astype(jnp.int32)
    wave_z = column - wave_y * SIDE
    squared = (
        wave_squared(wave_x, length_cells) + wave_squared(wave_y, SIDE) + wave_squared(wave_z, SIDE)
    )
    gain = jnp.where(squared > 0, four_pi / jnp.where(squared > 0, squared, 1.0), 0.0)
    waves = waves * (gain * (1.0 / (length_cells * SIDE * SIDE)))
    back = lax.dot_general(
        table, waves, (((0,), (0,)), ((), ())), precision=highest, preferred_element_type=jnp.float32
    )
    back = back.reshape(domains, SLOTS, width)
    for state in range(states):
        out_ref[state * domains:(state + 1) * domains] = back


def field_kernel(count, length_cells, start_ref, waves_ref, others_ref, density_ref, other_ref,
                 circle_ref, table_y_ref, table_z_ref, out_ref, low_ref, high_ref, planes_ref, flat_ref):
    _, own_start, thickness = place_of(start_ref)
    devices = waves_ref.shape[0]
    slots = out_ref.shape[0]
    core = lax.axis_index("core")
    core_rows = SIDE // 2
    first_row = core * core_rows
    for source_ref, first in ((waves_ref, first_row), (others_ref, core_rows - first_row)):
        pieces = []
        for device in range(devices):
            column = 0
            for row, start, stop in column_pieces(device * count, count):
                values = source_ref[device, :, column:column + stop - start]
                column += stop - start
                if start > 0:
                    pieces.append(values)
                    values = jnp.concatenate(pieces, axis=1)
                if stop < SIDE:
                    pieces = [values]
                    continue
                pieces = []
                at = pl.ds(first + row, SLOTS, stride=SIDE)
                low_ref[at, :] = values[:, :LANES]
                high_ref[at, :] = jnp.concatenate(
                    [values[:, LANES:], jnp.zeros((SLOTS, WIDTH - SIDE), jnp.float32)], axis=1
                )
    table_y = table_y_ref[...]
    table_z = table_z_ref[...]
    used = slice(0, slots * SIDE)
    along_z = turn_z(jnp.concatenate([low_ref[used, :], high_ref[used, :]], axis=1), table_z)
    for slot in range(slots):
        rows = slice(slot * SIDE, (slot + 1) * SIDE)
        planes_ref[rows, :] = turn_y(table_y, along_z[rows])

    @pl.loop(0, slots)
    def _(slot):
        def load(tile):
            tall = planes_ref[pl.ds(pl.multiple_of(slot * SIDE + tile * 8, 8), 8), :]
            return tall[:, :LANES], tall[:, LANES:]

        def store(k, values):
            flat_ref[pl.ds(slot * FLAT + k, 8, stride=STRIDE), :] = values

        to_flat(load, store)
        rows = pl.ds(pl.multiple_of(slot * FLAT, 8), FLAT)
        here = slot // (SLOTS // 2) == core
        kept_slot = slot % (SLOTS // 2)
        content = jnp.where(here, density_ref[kept_slot], other_ref[kept_slot]) * (3.0 / math.pi)
        positive = jnp.where(content > 0, content, 1.0)
        root = jnp.exp(jnp.log(positive) * (1.0 / 3.0))
        root = root - (root - positive / (root * root)) * (1.0 / 3.0)
        root = jnp.where(content > 0, root, 0.0)
        inside = mesh_points(own_start + slot, circle_ref[...], length_cells) & (slot < thickness)
        flat_ref[rows, :] = jnp.where(inside, flat_ref[rows, :] - root, 0.0)

    @pl.loop(0, FLAT // 8)
    def _(step):
        for part in range(8):
            lanes = pl.ds(pl.multiple_of((step * 8 + part) * LANES, LANES), LANES)
            out_ref[:, lanes] = flat_ref[pl.ds(step * 8 + part, SLOTS, stride=FLAT), :][:slots]


def from_behind(value, steps):
    count = lax.axis_size("domain")
    leading, last = (max(0, -steps), min(count, count - steps))
    return lax.ppermute(value, "domain", [(source, source + steps) for source in range(leading, last)])


def swapped(value, axis):
    return lax.ppermute(value, axis, [(0, 1), (1, 0)])


def shards(orbitals, occupation, potential, background, layer_start):
    domains = lax.axis_size("domain")
    rows = lax.axis_size("row")
    devices = domains * rows
    length_cells = SLAB * domains
    layer_cap, plane = potential.shape
    count = plane // (2 * devices)
    width = -(-(count + 1) // LANES) * LANES
    circle = jnp.asarray(circle_plane())
    flat_circle = jnp.asarray(circle_table().reshape(FLAT, LANES))
    table_z, into_y, out_of_y = (jnp.asarray(table) for table in tables_of_side())
    table_x = jnp.asarray(hartley_table(length_cells).astype(np.float32))
    params = pltpu.CompilerParams(vmem_limit_bytes=16 * MEBI)
    large = pltpu.CompilerParams(vmem_limit_bytes=44 * MEBI)
    whole = pltpu.CompilerParams(vmem_limit_bytes=56 * MEBI)

    def f32(*shape):
        return jax.ShapeDtypeStruct(shape, jnp.float32)

    def scratch(*shape):
        return pltpu.VMEM(shape, jnp.float32)

    layers = orbitals.reshape(2, layer_cap, FLAT, LANES)
    packed = packed_tiles()
    outer = orbitals.reshape(2, layer_cap * FLAT, LANES)
    up, down = pl.pallas_call(
        pack_kernel,
        out_shape=(f32(2 * HALO, packed * LANES), f32(2 * HALO, packed * LANES)),
        in_specs=[SMEM_SPEC, HBM_SPEC],
        out_specs=(HBM_SPEC, HBM_SPEC),
        scratch_shapes=[
            scratch(2 * HALO * FLAT, LANES),
            scratch(2 * HALO * FLAT, LANES),
            scratch(2 * HALO, packed * LANES),
            scratch(2 * HALO, packed * LANES),
            pltpu.SemaphoreType.DMA((4,)),
            pltpu.SemaphoreType.DMA((2,)),
        ],
        compiler_params=whole,
        name="pack_halo",
    )(layer_start, outer)
    up, down, potential_rest, outer = lax.optimization_barrier((up, down, potential, outer))
    v_rows, up_far, down_far = pl.pallas_call(
        pack_rest_kernel,
        out_shape=(f32(HALO - 1, packed, LANES), f32(2 * FLAT, LANES), f32(2 * FLAT, LANES)),
        in_specs=[SMEM_SPEC, HBM_SPEC, HBM_SPEC],
        out_specs=(VMEM_SPEC,) * 3,
        scratch_shapes=[
            scratch(SLOTS * FLAT, LANES),
            scratch(SLOTS * FLAT, LANES),
            scratch(layer_cap, plane),
            pltpu.SemaphoreType.DMA((5,)),
        ],
        compiler_params=whole,
        cost_estimate=pl.CostEstimate(flops=0, transcendentals=0, bytes_accessed=30_000_000),
        name="pack_rest",
    )(layer_start, potential_rest, outer)
    v_rows = lax.ppermute(
        v_rows,
        ("core", "domain"),
        [(source, source + 1) for source in range(domains - 1)]
        + [(domains + source + 1, domains + source) for source in range(domains - 1)],
    )
    below = from_behind(up, 1)
    above = from_behind(down, -1)
    below_far = from_behind(up_far, 2)
    above_far = from_behind(down_far, -2)
    v_rows, below_far, above_far = lax.optimization_barrier((v_rows, below_far, above_far))
    v_others = swapped(v_rows, "core")

    ions = pl.pallas_call(
        functools.partial(ions_kernel, count, length_cells),
        out_shape=f32(domains, SLOTS, width),
        in_specs=[SMEM_SPEC] + [VMEM_SPEC] * 4,
        out_specs=VMEM_SPEC,
        scratch_shapes=[
            scratch(SLOTS * FLAT, LANES),
            scratch(layer_cap * SIDE, WIDTH),
            scratch(SLOTS * SIDE, LANES),
            scratch(SLOTS * SIDE, LANES),
        ],
        compiler_params=params,
        name="ion_waves",
    )(layer_start, background, circle, into_y, table_z)
    ions = lax.all_to_all(ions, "domain", split_axis=0, concat_axis=0, tiled=True)
    ions, below = lax.optimization_barrier((ions, below))

    span = layer_cap + 2 * HALO
    fields = (span, TALL, 3 * LANES)
    psi, kept, sent = pl.pallas_call(
        functools.partial(propagate_kernel, count, length_cells),
        out_shape=(
            pltpu.HBM((layer_cap, SIDE, 3 * LANES), jnp.float32),
            f32(devices, SLOTS, width),
            f32(devices, SLOTS, width),
        ),
        in_specs=[SMEM_SPEC, SMEM_SPEC, VMEM_SPEC, VMEM_SPEC] + [HBM_SPEC] * 6 + [VMEM_SPEC] * 3,
        out_specs=(HBM_SPEC, VMEM_SPEC, VMEM_SPEC),
        scratch_shapes=[scratch(*fields)] * TERMS
        + [
            scratch(layer_cap, SIDE, 3 * LANES),
            scratch(span, SIDE, WIDTH),
            scratch(span, SIDE, WIDTH),
            scratch(SLOTS * FLAT, LANES),
            scratch(layer_cap * SIDE, WIDTH),
            scratch(SLOTS * SIDE, LANES),
            scratch(SLOTS * SIDE, LANES),
            scratch(SLOTS * FLAT, LANES),
            scratch(SLOTS * FLAT, LANES),
            scratch(SLOTS * FLAT, LANES),
            scratch(HALO - 1, packed, LANES),
            scratch(HALO - 1, packed, LANES),
            scratch(2 * HALO, packed * LANES),
            scratch(2 * HALO, packed * LANES),
            scratch(2 * FLAT, LANES),
            scratch(2 * FLAT, LANES),
            pltpu.SemaphoreType.DMA((6,)),
            pltpu.SemaphoreType.DMA,
        ],
        compiler_params=large,
        name="propagate",
    )(layer_start, occupation, layers, potential, below, above, below_far, above_far, v_rows, v_others,
      jnp.asarray(circle_pair()), into_y, table_z)
    waves = kept + swapped(sent, "core")
    waves, psi = lax.optimization_barrier((waves, psi))
    waves = lax.all_to_all(waves, ("row", "domain"), split_axis=0, concat_axis=0, tiled=True)
    orbitals_next, density_kept, density_sent = pl.pallas_call(
        unpack_kernel,
        out_shape=(
            f32(2, layer_cap, FLAT, LANES),
            f32(SLOTS // 2, FLAT, LANES),
            f32(SLOTS // 2, FLAT, LANES),
        ),
        in_specs=[SMEM_SPEC, VMEM_SPEC],
        out_specs=(VMEM_SPEC,) * 3,
        scratch_shapes=[scratch(SLOTS, FLAT, LANES)],
        compiler_params=params,
        name="unpack",
    )(occupation, psi)
    density = density_kept + swapped(density_sent, "core")
    waves, density = lax.optimization_barrier((waves, density))
    other_density = swapped(density, "row")
    waves = pl.pallas_call(
        functools.partial(coulomb_kernel, count, length_cells),
        out_shape=f32(devices, SLOTS, width),
        in_specs=[SMEM_SPEC] + [VMEM_SPEC] * 3,
        out_specs=VMEM_SPEC,
        compiler_params=params,
        name="coulomb",
    )(layer_start, waves, ions, table_x)
    waves = lax.all_to_all(waves, ("row", "domain"), split_axis=0, concat_axis=0, tiled=True)
    waves, other_density = lax.optimization_barrier((waves, other_density))
    density = density + other_density
    other_density = swapped(density, "core")
    other_waves = swapped(waves, "core")
    potential_next = pl.pallas_call(
        functools.partial(field_kernel, count, length_cells),
        out_shape=f32(layer_cap, plane),
        in_specs=[SMEM_SPEC] + [VMEM_SPEC] * 7,
        out_specs=VMEM_SPEC,
        scratch_shapes=[
            scratch(SLOTS * SIDE, LANES),
            scratch(SLOTS * SIDE, LANES),
            scratch(layer_cap * SIDE, WIDTH),
            scratch(SLOTS * FLAT, LANES),
        ],
        compiler_params=params,
        name="field",
    )(layer_start, waves, other_waves, density, other_density, flat_circle, out_of_y, table_z)
    return orbitals_next.reshape(orbitals.shape), potential_next


def solution(mesh):
    domains = mesh.shape["domain"]
    split = Mesh(mesh.devices.reshape(-1, 2, domains), ("row", "core", "domain"))
    states = ("row", "core")
    return jax.shard_map(
        shards,
        mesh=split,
        in_specs=(
            P(None, states, "domain", None),
            P(states),
            P("domain", None),
            P("domain", None),
            P(),
        ),
        out_specs=(P(None, states, "domain", None), P("domain", None)),
        check_vma=False,
    )
```

```python
import functools
import math

import jax
import jax.numpy as jnp
import ml_dtypes
import numpy as np
from jax import lax
from jax.experimental import pallas as pl
from jax.experimental.pallas import tpu as pltpu
from jax.sharding import Mesh, PartitionSpec as P

SIDE = 160
SLAB = 5
TERMS = 4

HALO = TERMS
LANES = 128
SLOTS = 8
RUN = SIDE // 8
FLAT = SIDE * SIDE // LANES
STRIDE = FLAT // 8
WIDTH = 2 * LANES
BLOCK = 32
TALL = SIDE + 16

time_step = 0.3
four_pi = 4.0 * math.pi
two_pi = 2.0 * math.pi
highest = lax.Precision.HIGHEST
MEBI = 1024 * 1024
SMEM_SPEC = pl.BlockSpec(memory_space=pltpu.SMEM)
VMEM_SPEC = pl.BlockSpec(memory_space=pltpu.VMEM)
HBM_SPEC = pl.BlockSpec(memory_space=pltpu.HBM)


def hartley_table(count_cells):
    index_run = np.arange(count_cells)
    angles = (index_run[:, None] * index_run[None, :] % count_cells) * (2.0 * np.pi / count_cells)
    return np.cos(angles) + np.sin(angles)


def plane_order():
    rows = np.arange(SIDE)
    return RUN * (rows % 8) + rows // 8


def two_parts(table):
    table = table.astype(np.float32)
    high = table.astype(ml_dtypes.bfloat16)
    low = (table - high.astype(np.float32)).astype(ml_dtypes.bfloat16)
    return high, low


def tables_of_side():
    table = hartley_table(SIDE)
    along_z = np.zeros((WIDTH, WIDTH))
    along_z[:SIDE, :SIDE] = table
    high, low = two_parts(along_z)
    along_z = np.concatenate([high, high, low], axis=0)
    high, low = two_parts(table[:, plane_order()])
    into_y = np.concatenate([high, high, low], axis=1)
    high, low = two_parts(table[plane_order(), :])
    out_of_y = np.concatenate([high, high, low], axis=1)
    return along_z, into_y, out_of_y


def circle_table():
    across = 2 * np.arange(SIDE, dtype=np.int64) - (SIDE - 1)
    return (across[:, None] ** 2 + across[None, :] ** 2).astype(np.int32)


def circle_plane():
    table = np.full((SIDE, WIDTH), 4 * SIDE * SIDE, np.int32)
    table[:, :SIDE] = circle_table()[plane_order()]
    return table


def mesh_points(x_row, circle, length_cells):
    room = ((length_cells - 2) ** 2 - (2 * x_row - (length_cells - 1)) ** 2) * (SIDE - 2) ** 2
    return (circle * (length_cells - 2) ** 2 <= room) & (circle < 4 * SIDE * SIDE)


def column_pieces(first, count):
    pieces = []
    column = first
    while column < first + count:
        row = column // SIDE
        stop = min((row + 1) * SIDE, first + count)
        pieces.append((row, column - row * SIDE, stop - row * SIDE))
        column = stop
    return pieces


def eight(values):
    missing = jnp.zeros((SLOTS - values.shape[0], values.shape[1]), values.dtype)
    return jnp.concatenate([values, missing], axis=0)


def to_plane(load, store):
    lane = lax.broadcasted_iota(jnp.int32, (8, LANES), 1)
    for step in range(RUN // 4):
        rows = [load(5 * step + part) for part in range(5)]
        store(4 * step, rows[0], rows[1])
        for part in range(1, 4):
            left = pltpu.roll(rows[part], LANES - 32 * part, 1)
            right = pltpu.roll(rows[part + 1], LANES - 32 * part, 1)
            store(4 * step + part, jnp.where(lane < LANES - 32 * part, left, right), right)


def to_flat(load, store):
    lane = lax.broadcasted_iota(jnp.int32, (8, LANES), 1)
    for step in range(RUN // 4):
        turned = []
        for part in range(4):
            low, high = load(4 * step + part)
            if part:
                low = pltpu.roll(low, 32 * part, 1)
                high = pltpu.roll(high, 32 * part, 1)
            turned.append((low, high))
        store(5 * step, turned[0][0])
        for part in range(1, 4):
            ended = 32 * (part - 1)
            values = jnp.where(lane < ended + 32, turned[part - 1][1], turned[part][0])
            if ended:
                values = jnp.where(lane < ended, turned[part - 1][0], values)
            store(5 * step + part, values)
        store(5 * step + 4, jnp.where(lane < 96, turned[3][0], turned[3][1]))


def chords():
    across = 2 * np.arange(SIDE, dtype=np.int64) - (SIDE - 1)
    room = (SIDE - 2) ** 2 - across**2
    return [max([w for w in range(1, SIDE // 2 + 1) if (2 * w - 1) ** 2 <= left], default=0) for left in room]


def chord_moves():
    moves = []
    packed = 0
    for row, half in enumerate(chords()):
        if half:
            moves.append((row * SIDE + SIDE // 2 - half, packed, 2 * half))
            packed += 2 * half
    return moves


def packed_tiles():
    _, start, length = chord_moves()[-1]
    return -(-(start + length) // LANES)


def move_lanes(moves, load, store):
    lane = lax.broadcasted_iota(jnp.int32, (8, LANES), 1)
    pieces = {}
    for source, target, length in moves:
        while length:
            size = min(length, LANES - source % LANES, LANES - target % LANES)
            pieces.setdefault(target // LANES, []).append((target % LANES, source // LANES, (target - source) % LANES))
            source, target, length = source + size, target + size, length - size
    loaded = {}
    turned = {}
    for tile in sorted(pieces):
        values = None
        for first, origin, shift in sorted(pieces[tile]):
            if origin not in loaded:
                loaded[origin] = load(origin)
            if (origin, shift) not in turned:
                turned[origin, shift] = pltpu.roll(loaded[origin], shift, 1) if shift else loaded[origin]
            piece = turned[origin, shift]
            values = piece if values is None else jnp.where(lane >= first, piece, values)
        store(tile, values)


def pack_chords(rows_ref, store):
    move_lanes(chord_moves(), lambda tile: rows_ref[pl.ds(tile, 8, stride=FLAT), :], store)


def unpack_chords(load, rows_ref):
    def store(tile, values):
        rows_ref[pl.ds(tile, 8, stride=FLAT), :] = values

    move_lanes([(target, source, length) for source, target, length in chord_moves()], load, store)


def parts_of(values):
    high = values.astype(jnp.bfloat16)
    low = (values - high.astype(jnp.float32)).astype(jnp.bfloat16)
    return high, low


def turn_z(values, table):
    high, low = parts_of(values)
    return jnp.dot(
        jnp.concatenate([high, low, high], axis=1), table, preferred_element_type=jnp.float32
    )


def turn_y(table, values):
    high, low = parts_of(values)
    return jnp.dot(
        table, jnp.concatenate([high, low, high], axis=0), preferred_element_type=jnp.float32
    )


def send_columns(planes_ref, slots, table_y, table_z, low_ref, high_ref):
    along_z = turn_z(planes_ref[:slots * SIDE, :], table_z)
    for slot in range(slots):
        rows = slice(slot * SIDE, (slot + 1) * SIDE)
        waves = turn_y(table_y, along_z[rows])
        low_ref[rows, :] = waves[:, :LANES]
        high_ref[rows, :] = waves[:, LANES:]
    low_ref[slots * SIDE:, :] = jnp.zeros(((SLOTS - slots) * SIDE, LANES), jnp.float32)
    high_ref[slots * SIDE:, :] = jnp.zeros(((SLOTS - slots) * SIDE, LANES), jnp.float32)


def chunk_of(low_ref, high_ref, first_row, pieces, extra):
    parts = []
    for row, start, stop in pieces:
        at = pl.ds(first_row + row, SLOTS, stride=SIDE)
        values = jnp.concatenate([low_ref[at, :], high_ref[at, :]], axis=1)
        parts.append(values[:, start:stop])
    return jnp.concatenate(parts + [extra], axis=1)


def layers_of(stored_ref, flat_ref):
    @pl.loop(0, FLAT // 8)
    def _(step):
        for part in range(8):
            lanes = pl.ds(pl.multiple_of((step * 8 + part) * LANES, LANES), LANES)
            flat_ref[pl.ds(step * 8 + part, SLOTS, stride=FLAT), :] = eight(stored_ref[:, lanes])


def place_of(start_ref):
    position = lax.axis_index("domain")
    return position, start_ref[position], start_ref[position + 1] - start_ref[position]


def started(sems, pairs):
    copies = [pltpu.make_async_copy(*pair, sems.at[index]) for index, pair in enumerate(pairs)]
    for made in copies:
        made.start()
    return copies


def layers_at(orbitals_ref, part, start, count):
    return orbitals_ref.at[part, pl.ds(pl.multiple_of(start * FLAT, 8), count * FLAT)]


def rows_at(ref, part, count):
    return ref.at[pl.ds(part * count * FLAT, count * FLAT)]


def pack_kernel(start_ref, orbitals_ref, up_ref, down_ref, up_rows_ref, down_rows_ref, up_buffer_ref,
                down_buffer_ref, in_sems, out_sems):
    _, _, thickness = place_of(start_ref)
    first = jnp.maximum(thickness - HALO, 0)
    arrivals = started(
        in_sems,
        [
            (layers_at(orbitals_ref, part, start, HALO), rows_at(rows_ref, part, HALO))
            for start, rows_ref in ((first, up_rows_ref), (0, down_rows_ref))
            for part in range(2)
        ],
    )
    departures = []
    for index, (rows_ref, buffer_ref, out_ref) in enumerate(
        ((up_rows_ref, up_buffer_ref, up_ref), (down_rows_ref, down_buffer_ref, down_ref))
    ):
        arrivals[2 * index].wait()
        arrivals[2 * index + 1].wait()

        def store(tile, values, buffer_ref=buffer_ref):
            buffer_ref[:, tile * LANES:(tile + 1) * LANES] = values

        pack_chords(rows_ref, store)
        departures.append(pltpu.make_async_copy(buffer_ref, out_ref, out_sems.at[index]))
        departures[-1].start()
    for made in departures:
        made.wait()


def pack_rest_kernel(start_ref, potential_ref, orbitals_ref, v_ref, up_far_ref, down_far_ref, flat_ref,
                     v_rows_ref, stored_ref, in_sems):
    _, _, thickness = place_of(start_ref)
    v_first = jnp.where(lax.axis_index("core") == 0, thickness - (HALO - 1), 0)
    arrivals = started(
        in_sems,
        [(potential_ref, stored_ref)]
        + [
            (layers_at(orbitals_ref, part, start, 1), rows_at(far_ref, part, 1))
            for start, far_ref in ((thickness - 1, up_far_ref), (0, down_far_ref))
            for part in range(2)
        ],
    )
    arrivals[0].wait()
    layers_of(stored_ref, flat_ref)
    for layer in range(HALO - 1):
        v_rows_ref[layer * FLAT:(layer + 1) * FLAT, :] = flat_ref[
            pl.ds(pl.multiple_of((v_first + layer) * FLAT, 8), FLAT), :
        ]

    def store_v(tile, values):
        for layer in range(HALO - 1):
            v_ref[layer, tile:tile + 1, :] = values[layer:layer + 1]

    pack_chords(v_rows_ref, store_v)
    for made in arrivals[1:]:
        made.wait()


def ions_kernel(count, length_cells, start_ref, background_ref, circle_ref, table_y_ref, table_z_ref,
                out_ref, flat_ref, planes_ref, low_ref, high_ref):
    _, own_start, thickness = place_of(start_ref)
    slots = background_ref.shape[0]
    groups, _, width = out_ref.shape
    layers_of(background_ref, flat_ref)

    def body(slot, total):
        def store(tile, low, high):
            rows = pl.ds(pl.multiple_of(slot * SIDE + tile * 8, 8), 8)
            planes_ref[rows, :LANES] = low
            planes_ref[rows, LANES:] = high

        to_plane(lambda k: flat_ref[pl.ds(slot * FLAT + k, 8, stride=STRIDE), :], store)
        rows = pl.ds(pl.multiple_of(slot * SIDE, 8), SIDE)
        inside = mesh_points(own_start + slot, circle_ref[...], length_cells) & (slot < thickness)
        values = jnp.where(inside, planes_ref[rows, :], 0.0)
        planes_ref[rows, :] = values
        return total + jnp.sum(values.reshape(RUN, 8, WIDTH), axis=0)

    total = lax.fori_loop(0, slots, body, jnp.zeros((8, WIDTH), jnp.float32))
    whole = jnp.broadcast_to(jnp.sum(total, keepdims=True), (SLOTS, LANES))[:, :width - count]
    send_columns(planes_ref, slots, table_y_ref[...], table_z_ref[...], low_ref, high_ref)
    core_rows = SIDE // lax.axis_size("core")
    first_row = lax.axis_index("core") * core_rows + lax.axis_index("row") * (core_rows // lax.axis_size("row"))
    for group in range(groups):
        out_ref[group] = chunk_of(low_ref, high_ref, first_row, column_pieces(group * count, count), whole)


def propagate_kernel(count, length_cells, start_ref, weight_ref, orbitals_ref, potential_ref, below_hbm_ref,
                     above_hbm_ref, below_far_hbm_ref, above_far_hbm_ref, v_hbm_ref, v_other_hbm_ref,
                     circle_ref, table_y_ref, table_z_ref, psi_ref, kept_ref, sent_ref, first_ref, second_ref,
                     third_ref, fourth_ref, sum_ref, centre_ref, beside_ref, flat_ref, planes_ref, low_ref,
                     high_ref, below_rows_ref, above_rows_ref, v_rows_ref, v_ref, v_other_ref, below_ref,
                     above_ref, below_far_ref, above_far_ref, in_sems, out_sem):
    arrivals = started(
        in_sems,
        [
            (v_hbm_ref, v_ref),
            (v_other_hbm_ref, v_other_ref),
            (below_hbm_ref, below_ref),
            (above_hbm_ref, above_ref),
            (below_far_hbm_ref, below_far_ref),
            (above_far_hbm_ref, above_far_ref),
        ],
    )
    position, own_start, thickness = place_of(start_ref)
    domains = lax.axis_size("domain")
    before = start_ref[jnp.maximum(position - 1, 0)]
    after = start_ref[jnp.minimum(position + 2, domains)]
    short_below = ((position > 0) & (own_start - before < HALO)).astype(jnp.int32)
    short_above = (position < domains - 1) & (after - own_start - thickness < HALO)
    weight = weight_ref[0]
    core = lax.axis_index("core")
    slots = orbitals_ref.shape[1]
    layers = slots + 2 * HALO
    devices, _, width = kept_ref.shape
    field_refs = (first_ref, second_ref, third_ref, fourth_ref)

    def field_layer(part, x_row):
        def store(tile, low, high):
            first_ref[part, x_row, 8 + 8 * tile:16 + 8 * tile, :LANES] = low
            first_ref[part, x_row, 8 + 8 * tile:16 + 8 * tile, LANES:] = high

        return store

    def potential_layer(x_row):
        def store(tile, low, high):
            centre_ref[x_row, 8 * tile:8 * tile + 8, :LANES] = low
            centre_ref[x_row, 8 * tile:8 * tile + 8, LANES:] = high

        return store

    def rows_from(ref, *at):
        return lambda k: ref[(*at, pl.ds(k, 8, stride=STRIDE), slice(None))]

    def layer_of(rows_ref, layer):
        return lambda k: rows_ref[pl.ds(layer * FLAT + k, 8, stride=STRIDE), :]

    layers_of(potential_ref, flat_ref)

    @pl.loop(0, slots)
    def _(slot):
        for part in range(2):
            to_plane(rows_from(orbitals_ref, part, slot), field_layer(part, HALO + slot))
        to_plane(layer_of(flat_ref, slot), potential_layer(HALO + slot))

    for made in arrivals:
        made.wait()
    for packed_ref, rows_ref in ((below_ref, below_rows_ref), (above_ref, above_rows_ref)):
        unpack_chords(
            lambda tile, packed_ref=packed_ref: packed_ref[:, tile * LANES:(tile + 1) * LANES], rows_ref
        )
    unpack_chords(
        lambda tile: eight(
            jnp.concatenate([ref[:, tile, :] for ref in (v_ref, v_other_ref)], axis=0)
        ),
        v_rows_ref,
    )

    @pl.loop(0, HALO - 1)
    def _(layer):
        lower = 1 + layer
        upper = HALO + thickness + layer
        to_plane(layer_of(v_rows_ref, layer), potential_layer(jnp.where(core == 0, lower, upper)))
        to_plane(layer_of(v_rows_ref, HALO - 1 + layer), potential_layer(jnp.where(core == 0, upper, lower)))
        for part in range(2):
            to_plane(
                layer_of(below_rows_ref, part * HALO + 1 + layer - short_below), field_layer(part, 1 + layer)
            )
            to_plane(
                layer_of(above_rows_ref, part * HALO + layer), field_layer(part, HALO + thickness + layer)
            )

    @pl.loop(0, 2)
    def _(part):
        last = 2 * HALO - 1 + thickness

        @pl.when(short_below > 0)
        def _():
            to_plane(layer_of(below_far_ref, part), field_layer(part, 0))

        @pl.when(short_below == 0)
        def _():
            to_plane(layer_of(below_rows_ref, part * HALO), field_layer(part, 0))

        @pl.when(short_above)
        def _():
            to_plane(layer_of(above_far_ref, part), field_layer(part, last))

        @pl.when(jnp.logical_not(short_above))
        def _():
            to_plane(layer_of(above_rows_ref, part * HALO + HALO - 1), field_layer(part, last))

    def wrap(term, part, x_row):
        first = field_refs[term][part, x_row, 8:16, :]
        final = field_refs[term][part, x_row, SIDE:SIDE + 8, :]
        field_refs[term][part, x_row, :8, :] = pltpu.roll(final, 1, 0)
        field_refs[term][part, x_row, SIDE + 8:, :] = pltpu.roll(first, 7, 0)

    @pl.loop(0, layers)
    def _(x_row):
        known = x_row < thickness + 2 * HALO
        for block in range(SIDE // BLOCK):
            rows = slice(block * BLOCK, (block + 1) * BLOCK)
            inner = slice(8 + block * BLOCK, 8 + (block + 1) * BLOCK)
            inside = mesh_points(own_start - HALO + x_row, circle_ref[rows, :], length_cells) & known
            centre_ref[x_row, rows, :] = jnp.where(
                inside, (3.0 + centre_ref[x_row, rows, :]) * time_step, 0.0
            )
            beside_ref[x_row, rows, :] = jnp.where(inside, 0.5 * time_step, 0.0)
            for part in range(2):
                first_ref[part, x_row, inner, :] = jnp.where(
                    inside, first_ref[part, x_row, inner, :], 0.0
                )
        for part in range(2):
            wrap(0, part, x_row)

    def hamilton(term, part, x_row, block, centre, beside):
        field_ref = field_refs[term]
        tall = field_ref[part, x_row, block * BLOCK:block * BLOCK + BLOCK + 16, :]
        inner = slice(8 + block * BLOCK, 8 + (block + 1) * BLOCK)
        field = tall[8:8 + BLOCK]
        around = field_ref[part, x_row - 1, inner, :] + field_ref[part, x_row + 1, inner, :]
        around = around + (tall[:BLOCK] + tall[16:])
        around = around + (pltpu.roll(field, 1, 1) + pltpu.roll(field, WIDTH - 1, 1))
        return centre * field - beside * around

    for term in range(1, TERMS):

        @pl.loop(term, layers - term)
        def _(x_row, term=term):
            for block in range(SIDE // BLOCK):
                rows = slice(block * BLOCK, (block + 1) * BLOCK)
                inner = slice(8 + block * BLOCK, 8 + (block + 1) * BLOCK)
                centre = centre_ref[x_row, rows, :]
                beside = beside_ref[x_row, rows, :]
                for part in range(2):
                    field_refs[term][part, x_row, inner, :] = hamilton(
                        term - 1, part, x_row, block, centre, beside
                    )
            for part in range(2):
                wrap(term, part, x_row)

    def finish(slot, total):
        x_row = HALO + slot
        owned = slot < thickness
        for block in range(SIDE // BLOCK):
            rows = slice(block * BLOCK, (block + 1) * BLOCK)
            inner = slice(8 + block * BLOCK, 8 + (block + 1) * BLOCK)
            centre = centre_ref[x_row, rows, :]
            beside = beside_ref[x_row, rows, :]
            density = jnp.zeros((BLOCK, WIDTH), jnp.float32)
            for part, sign in ((0, 1.0), (1, -1.0)):
                summed = first_ref[part, x_row, inner, :]
                summed = summed + sign * second_ref[1 - part, x_row, inner, :]
                summed = summed - (1.0 / 2.0) * third_ref[part, x_row, inner, :]
                summed = summed - (sign / 6.0) * fourth_ref[1 - part, x_row, inner, :]
                summed = summed + (1.0 / 24.0) * hamilton(3, part, x_row, block, centre, beside)
                summed = jnp.where(owned, summed, 0.0)
                sum_ref[part, slot, rows, :] = summed
                density = density + summed * summed
            density = weight * density
            planes_ref[pl.ds(pl.multiple_of(slot * SIDE + block * BLOCK, 8), BLOCK), :] = density
            total = total + jnp.sum(density.reshape(BLOCK // 8, 8, WIDTH), axis=0)

        return total

    total = lax.fori_loop(0, slots, finish, jnp.zeros((8, WIDTH), jnp.float32))
    departure = pltpu.make_async_copy(sum_ref, psi_ref, out_sem)
    departure.start()
    whole = jnp.broadcast_to(jnp.sum(total, keepdims=True), (SLOTS, LANES))[:, :width - count]
    send_columns(planes_ref, slots, table_y_ref[...], table_z_ref[...], low_ref, high_ref)
    core_rows = SIDE // 2
    first_row = core * core_rows
    for device in range(devices):
        pieces = column_pieces(device * count, count)
        kept_ref[device] = chunk_of(low_ref, high_ref, first_row, pieces, whole)
        sent_ref[device] = chunk_of(low_ref, high_ref, core_rows - first_row, pieces, whole)
    departure.wait()


def unpack_kernel(weight_ref, psi_ref, next_ref, density_kept_ref, density_sent_ref, density_ref):
    core = lax.axis_index("core")
    weight = weight_ref[0]
    slots = psi_ref.shape[1]

    @pl.loop(0, slots)
    def _(slot):
        for part in range(2):

            def load(tile, part=part):
                tall = psi_ref[part, slot, 8 * tile:8 * tile + 8, :]
                return tall[:, :LANES], tall[:, LANES:]

            def store(k, values, part=part):
                next_ref[part, slot, pl.ds(k, 8, stride=STRIDE), :] = values

            to_flat(load, store)
        real = next_ref[0, slot]
        imag = next_ref[1, slot]
        density_ref[slot] = weight * (real * real + imag * imag)

    for slot in range(slots, SLOTS):
        density_ref[slot] = jnp.zeros((FLAT, LANES), jnp.float32)

    @pl.loop(0, SLOTS // 2)
    def _(slot):
        density_kept_ref[slot] = density_ref[core * (SLOTS // 2) + slot]
        density_sent_ref[slot] = density_ref[(1 - core) * (SLOTS // 2) + slot]


def wave_squared(index, count_cells):
    folded = jnp.where(2 * index <= count_cells, index, index - count_cells)
    wave_number = folded.astype(jnp.float32) * (two_pi / count_cells)
    return wave_number * wave_number


def coulomb_kernel(count, length_cells, start_ref, charge_ref, ions_ref, table_ref, out_ref):
    domains, _, width = ions_ref.shape
    states = charge_ref.shape[0] // domains
    device = (lax.axis_index("core") * states + lax.axis_index("row")) * domains + lax.axis_index("domain")
    charge = charge_ref[:domains]
    for state in range(1, states):
        charge = charge + charge_ref[state * domains:(state + 1) * domains]
    charge = charge.reshape(domains * SLOTS, width)
    ions = ions_ref[...].reshape(domains * SLOTS, width)
    first = lax.broadcasted_iota(jnp.int32, (domains * SLOTS, width), 0) % SLOTS == 0
    lane = lax.broadcasted_iota(jnp.int32, (domains * SLOTS, width), 1)
    chosen = first & (lane == count)
    electrons = jnp.sum(jnp.where(chosen, charge, 0.0), keepdims=True)
    ionic = jnp.sum(jnp.where(chosen, ions, 0.0), keepdims=True)
    charge = charge - (electrons / ionic) * ions
    layer = lax.broadcasted_iota(jnp.int32, (length_cells, domains * SLOTS), 0)
    place = lax.broadcasted_iota(jnp.int32, (length_cells, domains * SLOTS), 1)
    chosen_layer = jnp.full(layer.shape, -1, jnp.int32)
    for domain in range(domains):
        slot = place - domain * SLOTS
        here = (slot >= 0) & (slot < start_ref[domain + 1] - start_ref[domain])
        chosen_layer = jnp.where(here, start_ref[domain] + slot, chosen_layer)
    pick = (layer == chosen_layer).astype(jnp.float32)
    table = jnp.dot(table_ref[...], pick, precision=highest, preferred_element_type=jnp.float32)
    waves = jnp.dot(table, charge, precision=highest, preferred_element_type=jnp.float32)
    wave_x = lax.broadcasted_iota(jnp.int32, waves.shape, 0)
    column = device * count + lax.broadcasted_iota(jnp.int32, waves.shape, 1)
    wave_y = ((column.astype(jnp.float32) + 0.5) * (1.0 / SIDE)).astype(jnp.int32)
    wave_z = column - wave_y * SIDE
    squared = (
        wave_squared(wave_x, length_cells) + wave_squared(wave_y, SIDE) + wave_squared(wave_z, SIDE)
    )
    gain = jnp.where(squared > 0, four_pi / jnp.where(squared > 0, squared, 1.0), 0.0)
    waves = waves * (gain * (1.0 / (length_cells * SIDE * SIDE)))
    back = lax.dot_general(
        table, waves, (((0,), (0,)), ((), ())), precision=highest, preferred_element_type=jnp.float32
    )
    back = back.reshape(domains, SLOTS, width)
    for state in range(states):
        out_ref[state * domains:(state + 1) * domains] = back


def field_kernel(count, length_cells, start_ref, waves_ref, others_ref, density_ref, other_ref,
                 circle_ref, table_y_ref, table_z_ref, out_ref, low_ref, high_ref, planes_ref, flat_ref):
    _, own_start, thickness = place_of(start_ref)
    devices = waves_ref.shape[0]
    slots = out_ref.shape[0]
    core = lax.axis_index("core")
    core_rows = SIDE // 2
    first_row = core * core_rows
    for source_ref, first in ((waves_ref, first_row), (others_ref, core_rows - first_row)):
        pieces = []
        for device in range(devices):
            column = 0
            for row, start, stop in column_pieces(device * count, count):
                values = source_ref[device, :, column:column + stop - start]
                column += stop - start
                if start > 0:
                    pieces.append(values)
                    values = jnp.concatenate(pieces, axis=1)
                if stop < SIDE:
                    pieces = [values]
                    continue
                pieces = []
                at = pl.ds(first + row, SLOTS, stride=SIDE)
                low_ref[at, :] = values[:, :LANES]
                high_ref[at, :] = jnp.concatenate(
                    [values[:, LANES:], jnp.zeros((SLOTS, WIDTH - SIDE), jnp.float32)], axis=1
                )
    table_y = table_y_ref[...]
    table_z = table_z_ref[...]
    used = slice(0, slots * SIDE)
    along_z = turn_z(jnp.concatenate([low_ref[used, :], high_ref[used, :]], axis=1), table_z)
    for slot in range(slots):
        rows = slice(slot * SIDE, (slot + 1) * SIDE)
        planes_ref[rows, :] = turn_y(table_y, along_z[rows])

    @pl.loop(0, slots)
    def _(slot):
        def load(tile):
            tall = planes_ref[pl.ds(pl.multiple_of(slot * SIDE + tile * 8, 8), 8), :]
            return tall[:, :LANES], tall[:, LANES:]

        def store(k, values):
            flat_ref[pl.ds(slot * FLAT + k, 8, stride=STRIDE), :] = values

        to_flat(load, store)
        rows = pl.ds(pl.multiple_of(slot * FLAT, 8), FLAT)
        here = slot // (SLOTS // 2) == core
        kept_slot = slot % (SLOTS // 2)
        content = jnp.where(here, density_ref[kept_slot], other_ref[kept_slot]) * (3.0 / math.pi)
        positive = jnp.where(content > 0, content, 1.0)
        root = jnp.exp(jnp.log(positive) * (1.0 / 3.0))
        root = root - (root - positive / (root * root)) * (1.0 / 3.0)
        root = jnp.where(content > 0, root, 0.0)
        inside = mesh_points(own_start + slot, circle_ref[...], length_cells) & (slot < thickness)
        flat_ref[rows, :] = jnp.where(inside, flat_ref[rows, :] - root, 0.0)

    @pl.loop(0, FLAT // 8)
    def _(step):
        for part in range(8):
            lanes = pl.ds(pl.multiple_of((step * 8 + part) * LANES, LANES), LANES)
            out_ref[:, lanes] = flat_ref[pl.ds(step * 8 + part, SLOTS, stride=FLAT), :][:slots]


def from_behind(value, steps):
    count = lax.axis_size("domain")
    leading, last = (max(0, -steps), min(count, count - steps))
    return lax.ppermute(value, "domain", [(source, source + steps) for source in range(leading, last)])


def swapped(value, axis):
    return lax.ppermute(value, axis, [(0, 1), (1, 0)])


def shards(orbitals, occupation, potential, background, layer_start):
    domains = lax.axis_size("domain")
    rows = lax.axis_size("row")
    devices = domains * rows
    length_cells = SLAB * domains
    layer_cap, plane = potential.shape
    count = plane // (2 * devices)
    width = -(-(count + 1) // LANES) * LANES
    circle = jnp.asarray(circle_plane())
    flat_circle = jnp.asarray(circle_table().reshape(FLAT, LANES))
    table_z, into_y, out_of_y = (jnp.asarray(table) for table in tables_of_side())
    table_x = jnp.asarray(hartley_table(length_cells).astype(np.float32))
    params = pltpu.CompilerParams(vmem_limit_bytes=16 * MEBI)
    large = pltpu.CompilerParams(vmem_limit_bytes=44 * MEBI)
    whole = pltpu.CompilerParams(vmem_limit_bytes=56 * MEBI)

    def f32(*shape):
        return jax.ShapeDtypeStruct(shape, jnp.float32)

    def scratch(*shape):
        return pltpu.VMEM(shape, jnp.float32)

    layers = orbitals.reshape(2, layer_cap, FLAT, LANES)
    packed = packed_tiles()
    outer = orbitals.reshape(2, layer_cap * FLAT, LANES)
    up, down = pl.pallas_call(
        pack_kernel,
        out_shape=(f32(2 * HALO, packed * LANES), f32(2 * HALO, packed * LANES)),
        in_specs=[SMEM_SPEC, HBM_SPEC],
        out_specs=(HBM_SPEC, HBM_SPEC),
        scratch_shapes=[
            scratch(2 * HALO * FLAT, LANES),
            scratch(2 * HALO * FLAT, LANES),
            scratch(2 * HALO, packed * LANES),
            scratch(2 * HALO, packed * LANES),
            pltpu.SemaphoreType.DMA((4,)),
            pltpu.SemaphoreType.DMA((2,)),
        ],
        compiler_params=whole,
        name="pack_halo",
    )(layer_start, outer)
    up, down, potential_rest, outer = lax.optimization_barrier((up, down, potential, outer))
    v_rows, up_far, down_far = pl.pallas_call(
        pack_rest_kernel,
        out_shape=(f32(HALO - 1, packed, LANES), f32(2 * FLAT, LANES), f32(2 * FLAT, LANES)),
        in_specs=[SMEM_SPEC, HBM_SPEC, HBM_SPEC],
        out_specs=(VMEM_SPEC,) * 3,
        scratch_shapes=[
            scratch(SLOTS * FLAT, LANES),
            scratch(SLOTS * FLAT, LANES),
            scratch(layer_cap, plane),
            pltpu.SemaphoreType.DMA((5,)),
        ],
        compiler_params=whole,
        cost_estimate=pl.CostEstimate(flops=0, transcendentals=0, bytes_accessed=30_000_000),
        name="pack_rest",
    )(layer_start, potential_rest, outer)
    v_rows = lax.ppermute(
        v_rows,
        ("core", "domain"),
        [(source, source + 1) for source in range(domains - 1)]
        + [(domains + source + 1, domains + source) for source in range(domains - 1)],
    )
    below = from_behind(up, 1)
    above = from_behind(down, -1)
    below_far = from_behind(up_far, 2)
    above_far = from_behind(down_far, -2)
    v_rows, below_far, above_far = lax.optimization_barrier((v_rows, below_far, above_far))
    v_others = swapped(v_rows, "core")

    ions = pl.pallas_call(
        functools.partial(ions_kernel, count, length_cells),
        out_shape=f32(domains, SLOTS, width),
        in_specs=[SMEM_SPEC] + [VMEM_SPEC] * 4,
        out_specs=VMEM_SPEC,
        scratch_shapes=[
            scratch(SLOTS * FLAT, LANES),
            scratch(layer_cap * SIDE, WIDTH),
            scratch(SLOTS * SIDE, LANES),
            scratch(SLOTS * SIDE, LANES),
        ],
        compiler_params=params,
        name="ion_waves",
    )(layer_start, background, circle, into_y, table_z)
    ions = lax.all_to_all(ions, "domain", split_axis=0, concat_axis=0, tiled=True)
    ions, below = lax.optimization_barrier((ions, below))

    span = layer_cap + 2 * HALO
    fields = (2, span, TALL, WIDTH)
    psi, kept, sent = pl.pallas_call(
        functools.partial(propagate_kernel, count, length_cells),
        out_shape=(
            pltpu.HBM((2, layer_cap, SIDE, WIDTH), jnp.float32),
            f32(devices, SLOTS, width),
            f32(devices, SLOTS, width),
        ),
        in_specs=[SMEM_SPEC, SMEM_SPEC, VMEM_SPEC, VMEM_SPEC] + [HBM_SPEC] * 6 + [VMEM_SPEC] * 3,
        out_specs=(HBM_SPEC, VMEM_SPEC, VMEM_SPEC),
        scratch_shapes=[scratch(*fields)] * TERMS
        + [
            scratch(2, layer_cap, SIDE, WIDTH),
            scratch(span, SIDE, WIDTH),
            scratch(span, SIDE, WIDTH),
            scratch(SLOTS * FLAT, LANES),
            scratch(layer_cap * SIDE, WIDTH),
            scratch(SLOTS * SIDE, LANES),
            scratch(SLOTS * SIDE, LANES),
            scratch(SLOTS * FLAT, LANES),
            scratch(SLOTS * FLAT, LANES),
            scratch(SLOTS * FLAT, LANES),
            scratch(HALO - 1, packed, LANES),
            scratch(HALO - 1, packed, LANES),
            scratch(2 * HALO, packed * LANES),
            scratch(2 * HALO, packed * LANES),
            scratch(2 * FLAT, LANES),
            scratch(2 * FLAT, LANES),
            pltpu.SemaphoreType.DMA((6,)),
            pltpu.SemaphoreType.DMA,
        ],
        compiler_params=large,
        name="propagate",
    )(layer_start, occupation, layers, potential, below, above, below_far, above_far, v_rows, v_others,
      circle, into_y, table_z)
    waves = kept + swapped(sent, "core")
    waves, psi = lax.optimization_barrier((waves, psi))
    waves = lax.all_to_all(waves, ("row", "domain"), split_axis=0, concat_axis=0, tiled=True)
    orbitals_next, density_kept, density_sent = pl.pallas_call(
        unpack_kernel,
        out_shape=(
            f32(2, layer_cap, FLAT, LANES),
            f32(SLOTS // 2, FLAT, LANES),
            f32(SLOTS // 2, FLAT, LANES),
        ),
        in_specs=[SMEM_SPEC, VMEM_SPEC],
        out_specs=(VMEM_SPEC,) * 3,
        scratch_shapes=[scratch(SLOTS, FLAT, LANES)],
        compiler_params=params,
        name="unpack",
    )(occupation, psi)
    density = density_kept + swapped(density_sent, "core")
    waves, density = lax.optimization_barrier((waves, density))
    other_density = swapped(density, "row")
    waves = pl.pallas_call(
        functools.partial(coulomb_kernel, count, length_cells),
        out_shape=f32(devices, SLOTS, width),
        in_specs=[SMEM_SPEC] + [VMEM_SPEC] * 3,
        out_specs=VMEM_SPEC,
        compiler_params=params,
        name="coulomb",
    )(layer_start, waves, ions, table_x)
    waves = lax.all_to_all(waves, ("row", "domain"), split_axis=0, concat_axis=0, tiled=True)
    waves, other_density = lax.optimization_barrier((waves, other_density))
    density = density + other_density
    other_density = swapped(density, "core")
    other_waves = swapped(waves, "core")
    potential_next = pl.pallas_call(
        functools.partial(field_kernel, count, length_cells),
        out_shape=f32(layer_cap, plane),
        in_specs=[SMEM_SPEC] + [VMEM_SPEC] * 7,
        out_specs=VMEM_SPEC,
        scratch_shapes=[
            scratch(SLOTS * SIDE, LANES),
            scratch(SLOTS * SIDE, LANES),
            scratch(layer_cap * SIDE, WIDTH),
            scratch(SLOTS * FLAT, LANES),
        ],
        compiler_params=params,
        name="field",
    )(layer_start, waves, other_waves, density, other_density, flat_circle, out_of_y, table_z)
    return orbitals_next.reshape(orbitals.shape), potential_next


def solution(mesh):
    domains = mesh.shape["domain"]
    split = Mesh(mesh.devices.reshape(-1, 2, domains), ("row", "core", "domain"))
    states = ("row", "core")
    return jax.shard_map(
        shards,
        mesh=split,
        in_specs=(
            P(None, states, "domain", None),
            P(states),
            P("domain", None),
            P("domain", None),
            P(),
        ),
        out_specs=(P(None, states, "domain", None), P("domain", None)),
        check_vma=False,
    )
```

```python
import functools
import math

import jax
import jax.numpy as jnp
import ml_dtypes
import numpy as np
from jax import lax
from jax.experimental import pallas as pl
from jax.experimental.pallas import tpu as pltpu
from jax.sharding import Mesh, PartitionSpec as P

SIDE = 160
SLAB = 5
TERMS = 4

HALO = TERMS
LANES = 128
SLOTS = 8
RUN = SIDE // 8
FLAT = SIDE * SIDE // LANES
STRIDE = FLAT // 8
WIDTH = 2 * LANES
BLOCK = 32
TALL = SIDE + 16

time_step = 0.3
four_pi = 4.0 * math.pi
two_pi = 2.0 * math.pi
highest = lax.Precision.HIGHEST
MEBI = 1024 * 1024
SMEM_SPEC = pl.BlockSpec(memory_space=pltpu.SMEM)
VMEM_SPEC = pl.BlockSpec(memory_space=pltpu.VMEM)
HBM_SPEC = pl.BlockSpec(memory_space=pltpu.HBM)


def hartley_table(count_cells):
    index_run = np.arange(count_cells)
    angles = (index_run[:, None] * index_run[None, :] % count_cells) * (2.0 * np.pi / count_cells)
    return np.cos(angles) + np.sin(angles)


def plane_order():
    rows = np.arange(SIDE)
    return RUN * (rows % 8) + rows // 8


def two_parts(table):
    table = table.astype(np.float32)
    high = table.astype(ml_dtypes.bfloat16)
    low = (table - high.astype(np.float32)).astype(ml_dtypes.bfloat16)
    return high, low


def tables_of_side():
    table = hartley_table(SIDE)
    along_z = np.zeros((WIDTH, WIDTH))
    along_z[:SIDE, :SIDE] = table
    high, low = two_parts(along_z)
    along_z = np.concatenate([high, high, low], axis=0)
    high, low = two_parts(table[:, plane_order()])
    into_y = np.concatenate([high, high, low], axis=1)
    high, low = two_parts(table[plane_order(), :])
    out_of_y = np.concatenate([high, high, low], axis=1)
    return along_z, into_y, out_of_y


def circle_table():
    across = 2 * np.arange(SIDE, dtype=np.int64) - (SIDE - 1)
    return (across[:, None] ** 2 + across[None, :] ** 2).astype(np.int32)


def circle_plane():
    table = np.full((SIDE, WIDTH), 4 * SIDE * SIDE, np.int32)
    table[:, :SIDE] = circle_table()[plane_order()]
    return table


def mesh_points(x_row, circle, length_cells):
    room = ((length_cells - 2) ** 2 - (2 * x_row - (length_cells - 1)) ** 2) * (SIDE - 2) ** 2
    return (circle * (length_cells - 2) ** 2 <= room) & (circle < 4 * SIDE * SIDE)


def column_pieces(first, count):
    pieces = []
    column = first
    while column < first + count:
        row = column // SIDE
        stop = min((row + 1) * SIDE, first + count)
        pieces.append((row, column - row * SIDE, stop - row * SIDE))
        column = stop
    return pieces


def eight(values):
    missing = jnp.zeros((SLOTS - values.shape[0], values.shape[1]), values.dtype)
    return jnp.concatenate([values, missing], axis=0)


def two_by_two(first, last, body):
    pairs = (last - first) // 2

    @pl.loop(0, pairs)
    def _(pair):
        body(first + 2 * pair)
        body(first + 2 * pair + 1)

    if (last - first) % 2:
        body(last - 1)


def to_plane(load, store):
    lane = lax.broadcasted_iota(jnp.int32, (8, LANES), 1)
    for step in range(RUN // 4):
        rows = [load(5 * step + part) for part in range(5)]
        store(4 * step, rows[0], rows[1])
        for part in range(1, 4):
            left = pltpu.roll(rows[part], LANES - 32 * part, 1)
            right = pltpu.roll(rows[part + 1], LANES - 32 * part, 1)
            store(4 * step + part, jnp.where(lane < LANES - 32 * part, left, right), right)


def to_flat(load, store):
    lane = lax.broadcasted_iota(jnp.int32, (8, LANES), 1)
    for step in range(RUN // 4):
        turned = []
        for part in range(4):
            low, high = load(4 * step + part)
            if part:
                low = pltpu.roll(low, 32 * part, 1)
                high = pltpu.roll(high, 32 * part, 1)
            turned.append((low, high))
        store(5 * step, turned[0][0])
        for part in range(1, 4):
            ended = 32 * (part - 1)
            values = jnp.where(lane < ended + 32, turned[part - 1][1], turned[part][0])
            if ended:
                values = jnp.where(lane < ended, turned[part - 1][0], values)
            store(5 * step + part, values)
        store(5 * step + 4, jnp.where(lane < 96, turned[3][0], turned[3][1]))


def chords():
    across = 2 * np.arange(SIDE, dtype=np.int64) - (SIDE - 1)
    room = (SIDE - 2) ** 2 - across**2
    return [max([w for w in range(1, SIDE // 2 + 1) if (2 * w - 1) ** 2 <= left], default=0) for left in room]


def chord_moves():
    moves = []
    packed = 0
    for row, half in enumerate(chords()):
        if half:
            moves.append((row * SIDE + SIDE // 2 - half, packed, 2 * half))
            packed += 2 * half
    return moves


def packed_tiles():
    _, start, length = chord_moves()[-1]
    return -(-(start + length) // LANES)


def move_lanes(moves, load, store):
    lane = lax.broadcasted_iota(jnp.int32, (8, LANES), 1)
    pieces = {}
    for source, target, length in moves:
        while length:
            size = min(length, LANES - source % LANES, LANES - target % LANES)
            pieces.setdefault(target // LANES, []).append((target % LANES, source // LANES, (target - source) % LANES))
            source, target, length = source + size, target + size, length - size
    loaded = {}
    turned = {}
    for tile in sorted(pieces):
        values = None
        for first, origin, shift in sorted(pieces[tile]):
            if origin not in loaded:
                loaded[origin] = load(origin)
            if (origin, shift) not in turned:
                turned[origin, shift] = pltpu.roll(loaded[origin], shift, 1) if shift else loaded[origin]
            piece = turned[origin, shift]
            values = piece if values is None else jnp.where(lane >= first, piece, values)
        store(tile, values)


def pack_chords(rows_ref, store):
    move_lanes(chord_moves(), lambda tile: rows_ref[pl.ds(tile, 8, stride=FLAT), :], store)


def unpack_chords(load, rows_ref):
    def store(tile, values):
        rows_ref[pl.ds(tile, 8, stride=FLAT), :] = values

    move_lanes([(target, source, length) for source, target, length in chord_moves()], load, store)


def parts_of(values):
    high = values.astype(jnp.bfloat16)
    low = (values - high.astype(jnp.float32)).astype(jnp.bfloat16)
    return high, low


def turn_z(values, table):
    high, low = parts_of(values)
    return jnp.dot(
        jnp.concatenate([high, low, high], axis=1), table, preferred_element_type=jnp.float32
    )


def turn_y(table, values):
    high, low = parts_of(values)
    return jnp.dot(
        table, jnp.concatenate([high, low, high], axis=0), preferred_element_type=jnp.float32
    )


def send_columns(planes_ref, slots, table_y, table_z, low_ref, high_ref):
    along_z = turn_z(planes_ref[:slots * SIDE, :], table_z)
    for slot in range(slots):
        rows = slice(slot * SIDE, (slot + 1) * SIDE)
        waves = turn_y(table_y, along_z[rows])
        low_ref[rows, :] = waves[:, :LANES]
        high_ref[rows, :] = waves[:, LANES:]
    low_ref[slots * SIDE:, :] = jnp.zeros(((SLOTS - slots) * SIDE, LANES), jnp.float32)
    high_ref[slots * SIDE:, :] = jnp.zeros(((SLOTS - slots) * SIDE, LANES), jnp.float32)


def chunk_of(low_ref, high_ref, first_row, pieces, extra):
    parts = []
    for row, start, stop in pieces:
        at = pl.ds(first_row + row, SLOTS, stride=SIDE)
        values = jnp.concatenate([low_ref[at, :], high_ref[at, :]], axis=1)
        parts.append(values[:, start:stop])
    return jnp.concatenate(parts + [extra], axis=1)


def layers_of(stored_ref, flat_ref):
    @pl.loop(0, FLAT // 8)
    def _(step):
        for part in range(8):
            lanes = pl.ds(pl.multiple_of((step * 8 + part) * LANES, LANES), LANES)
            flat_ref[pl.ds(step * 8 + part, SLOTS, stride=FLAT), :] = eight(stored_ref[:, lanes])


def place_of(start_ref):
    position = lax.axis_index("domain")
    return position, start_ref[position], start_ref[position + 1] - start_ref[position]


def started(sems, pairs):
    copies = [pltpu.make_async_copy(*pair, sems.at[index]) for index, pair in enumerate(pairs)]
    for made in copies:
        made.start()
    return copies


def layers_at(orbitals_ref, part, start, count):
    return orbitals_ref.at[part, pl.ds(pl.multiple_of(start * FLAT, 8), count * FLAT)]


def rows_at(ref, part, count):
    return ref.at[pl.ds(part * count * FLAT, count * FLAT)]


def pack_kernel(start_ref, orbitals_ref, up_ref, down_ref, up_rows_ref, down_rows_ref, up_buffer_ref,
                down_buffer_ref, in_sems, out_sems):
    _, _, thickness = place_of(start_ref)
    first = jnp.maximum(thickness - HALO, 0)
    arrivals = started(
        in_sems,
        [
            (layers_at(orbitals_ref, part, start, HALO), rows_at(rows_ref, part, HALO))
            for start, rows_ref in ((first, up_rows_ref), (0, down_rows_ref))
            for part in range(2)
        ],
    )
    departures = []
    for index, (rows_ref, buffer_ref, out_ref) in enumerate(
        ((up_rows_ref, up_buffer_ref, up_ref), (down_rows_ref, down_buffer_ref, down_ref))
    ):
        arrivals[2 * index].wait()
        arrivals[2 * index + 1].wait()

        def store(tile, values, buffer_ref=buffer_ref):
            buffer_ref[:, tile * LANES:(tile + 1) * LANES] = values

        pack_chords(rows_ref, store)
        departures.append(pltpu.make_async_copy(buffer_ref, out_ref, out_sems.at[index]))
        departures[-1].start()
    for made in departures:
        made.wait()


def pack_rest_kernel(start_ref, potential_ref, orbitals_ref, v_ref, up_far_ref, down_far_ref, flat_ref,
                     v_rows_ref, stored_ref, in_sems):
    _, _, thickness = place_of(start_ref)
    v_first = jnp.where(lax.axis_index("core") == 0, thickness - (HALO - 1), 0)
    arrivals = started(
        in_sems,
        [(potential_ref, stored_ref)]
        + [
            (layers_at(orbitals_ref, part, start, 1), rows_at(far_ref, part, 1))
            for start, far_ref in ((thickness - 1, up_far_ref), (0, down_far_ref))
            for part in range(2)
        ],
    )
    arrivals[0].wait()
    layers_of(stored_ref, flat_ref)
    for layer in range(HALO - 1):
        v_rows_ref[layer * FLAT:(layer + 1) * FLAT, :] = flat_ref[
            pl.ds(pl.multiple_of((v_first + layer) * FLAT, 8), FLAT), :
        ]

    def store_v(tile, values):
        for layer in range(HALO - 1):
            v_ref[layer, tile:tile + 1, :] = values[layer:layer + 1]

    pack_chords(v_rows_ref, store_v)
    for made in arrivals[1:]:
        made.wait()


def ions_kernel(count, length_cells, start_ref, background_ref, circle_ref, table_y_ref, table_z_ref,
                out_ref, flat_ref, planes_ref, low_ref, high_ref):
    _, own_start, thickness = place_of(start_ref)
    slots = background_ref.shape[0]
    groups, _, width = out_ref.shape
    layers_of(background_ref, flat_ref)

    def body(slot, total):
        def store(tile, low, high):
            rows = pl.ds(pl.multiple_of(slot * SIDE + tile * 8, 8), 8)
            planes_ref[rows, :LANES] = low
            planes_ref[rows, LANES:] = high

        to_plane(lambda k: flat_ref[pl.ds(slot * FLAT + k, 8, stride=STRIDE), :], store)
        rows = pl.ds(pl.multiple_of(slot * SIDE, 8), SIDE)
        inside = mesh_points(own_start + slot, circle_ref[...], length_cells) & (slot < thickness)
        values = jnp.where(inside, planes_ref[rows, :], 0.0)
        planes_ref[rows, :] = values
        return total + jnp.sum(values.reshape(RUN, 8, WIDTH), axis=0)

    total = lax.fori_loop(0, slots, body, jnp.zeros((8, WIDTH), jnp.float32))
    whole = jnp.broadcast_to(jnp.sum(total, keepdims=True), (SLOTS, LANES))[:, :width - count]
    send_columns(planes_ref, slots, table_y_ref[...], table_z_ref[...], low_ref, high_ref)
    core_rows = SIDE // lax.axis_size("core")
    first_row = lax.axis_index("core") * core_rows + lax.axis_index("row") * (core_rows // lax.axis_size("row"))
    for group in range(groups):
        out_ref[group] = chunk_of(low_ref, high_ref, first_row, column_pieces(group * count, count), whole)


def propagate_kernel(count, length_cells, start_ref, weight_ref, orbitals_ref, potential_ref, below_hbm_ref,
                     above_hbm_ref, below_far_hbm_ref, above_far_hbm_ref, v_hbm_ref, v_other_hbm_ref,
                     circle_ref, table_y_ref, table_z_ref, psi_ref, kept_ref, sent_ref, first_ref, second_ref,
                     third_ref, fourth_ref, sum_ref, centre_ref, beside_ref, flat_ref, planes_ref, low_ref,
                     high_ref, below_rows_ref, above_rows_ref, v_rows_ref, v_ref, v_other_ref, below_ref,
                     above_ref, below_far_ref, above_far_ref, in_sems, out_sem):
    arrivals = started(
        in_sems,
        [
            (v_hbm_ref, v_ref),
            (v_other_hbm_ref, v_other_ref),
            (below_hbm_ref, below_ref),
            (above_hbm_ref, above_ref),
            (below_far_hbm_ref, below_far_ref),
            (above_far_hbm_ref, above_far_ref),
        ],
    )
    position, own_start, thickness = place_of(start_ref)
    domains = lax.axis_size("domain")
    before = start_ref[jnp.maximum(position - 1, 0)]
    after = start_ref[jnp.minimum(position + 2, domains)]
    short_below = ((position > 0) & (own_start - before < HALO)).astype(jnp.int32)
    short_above = (position < domains - 1) & (after - own_start - thickness < HALO)
    weight = weight_ref[0]
    core = lax.axis_index("core")
    slots = orbitals_ref.shape[1]
    layers = slots + 2 * HALO
    devices, _, width = kept_ref.shape
    field_refs = (first_ref, second_ref, third_ref, fourth_ref)

    def field_layer(part, x_row):
        def store(tile, low, high):
            first_ref[part, x_row, 8 + 8 * tile:16 + 8 * tile, :LANES] = low
            first_ref[part, x_row, 8 + 8 * tile:16 + 8 * tile, LANES:] = high

        return store

    def potential_layer(x_row):
        def store(tile, low, high):
            centre_ref[x_row, 8 * tile:8 * tile + 8, :LANES] = low
            centre_ref[x_row, 8 * tile:8 * tile + 8, LANES:] = high

        return store

    def rows_from(ref, *at):
        return lambda k: ref[(*at, pl.ds(k, 8, stride=STRIDE), slice(None))]

    def layer_of(rows_ref, layer):
        return lambda k: rows_ref[pl.ds(layer * FLAT + k, 8, stride=STRIDE), :]

    layers_of(potential_ref, flat_ref)

    @pl.loop(0, slots)
    def _(slot):
        for part in range(2):
            to_plane(rows_from(orbitals_ref, part, slot), field_layer(part, HALO + slot))
        to_plane(layer_of(flat_ref, slot), potential_layer(HALO + slot))

    for made in arrivals:
        made.wait()
    for packed_ref, rows_ref in ((below_ref, below_rows_ref), (above_ref, above_rows_ref)):
        unpack_chords(
            lambda tile, packed_ref=packed_ref: packed_ref[:, tile * LANES:(tile + 1) * LANES], rows_ref
        )
    unpack_chords(
        lambda tile: eight(
            jnp.concatenate([ref[:, tile, :] for ref in (v_ref, v_other_ref)], axis=0)
        ),
        v_rows_ref,
    )

    @pl.loop(0, HALO - 1)
    def _(layer):
        lower = 1 + layer
        upper = HALO + thickness + layer
        to_plane(layer_of(v_rows_ref, layer), potential_layer(jnp.where(core == 0, lower, upper)))
        to_plane(layer_of(v_rows_ref, HALO - 1 + layer), potential_layer(jnp.where(core == 0, upper, lower)))
        for part in range(2):
            to_plane(
                layer_of(below_rows_ref, part * HALO + 1 + layer - short_below), field_layer(part, 1 + layer)
            )
            to_plane(
                layer_of(above_rows_ref, part * HALO + layer), field_layer(part, HALO + thickness + layer)
            )

    @pl.loop(0, 2)
    def _(part):
        last = 2 * HALO - 1 + thickness

        @pl.when(short_below > 0)
        def _():
            to_plane(layer_of(below_far_ref, part), field_layer(part, 0))

        @pl.when(short_below == 0)
        def _():
            to_plane(layer_of(below_rows_ref, part * HALO), field_layer(part, 0))

        @pl.when(short_above)
        def _():
            to_plane(layer_of(above_far_ref, part), field_layer(part, last))

        @pl.when(jnp.logical_not(short_above))
        def _():
            to_plane(layer_of(above_rows_ref, part * HALO + HALO - 1), field_layer(part, last))

    def wrap(field_ref, part, x_row, first, final):
        field_ref[part, x_row, :8, :] = pltpu.roll(final, 1, 0)
        field_ref[part, x_row, SIDE + 8:, :] = pltpu.roll(first, 7, 0)

    blocks = SIDE // BLOCK

    def confine(x_row):
        known = x_row < thickness + 2 * HALO
        ends = {}
        for block in range(blocks):
            rows = slice(block * BLOCK, (block + 1) * BLOCK)
            inner = slice(8 + block * BLOCK, 8 + (block + 1) * BLOCK)
            inside = mesh_points(own_start - HALO + x_row, circle_ref[rows, :], length_cells) & known
            centre_ref[x_row, rows, :] = jnp.where(
                inside, (3.0 + centre_ref[x_row, rows, :]) * time_step, 0.0
            )
            beside_ref[x_row, rows, :] = jnp.where(inside, 0.5 * time_step, 0.0)
            for part in range(2):
                field = jnp.where(inside, first_ref[part, x_row, inner, :], 0.0)
                first_ref[part, x_row, inner, :] = field
                ends[part, block] = field
        for part in range(2):
            wrap(first_ref, part, x_row, ends[part, 0][:8], ends[part, blocks - 1][BLOCK - 8:])

    two_by_two(0, layers, confine)

    def hamilton(term, part, x_row, block, centre, beside):
        field_ref = field_refs[term]
        tall = field_ref[part, x_row, block * BLOCK:block * BLOCK + BLOCK + 16, :]
        inner = slice(8 + block * BLOCK, 8 + (block + 1) * BLOCK)
        field = tall[8:8 + BLOCK]
        around = field_ref[part, x_row - 1, inner, :] + field_ref[part, x_row + 1, inner, :]
        around = around + (tall[:BLOCK] + tall[16:])
        around = around + (pltpu.roll(field, 1, 1) + pltpu.roll(field, WIDTH - 1, 1))
        return centre * field - beside * around

    for term in range(1, TERMS):

        def step(x_row, term=term):
            ends = {}
            for block in range(blocks):
                rows = slice(block * BLOCK, (block + 1) * BLOCK)
                inner = slice(8 + block * BLOCK, 8 + (block + 1) * BLOCK)
                centre = centre_ref[x_row, rows, :]
                beside = beside_ref[x_row, rows, :]
                for part in range(2):
                    field = hamilton(term - 1, part, x_row, block, centre, beside)
                    field_refs[term][part, x_row, inner, :] = field
                    ends[part, block] = field
            for part in range(2):
                wrap(field_refs[term], part, x_row, ends[part, 0][:8], ends[part, blocks - 1][BLOCK - 8:])

        two_by_two(term, layers - term, step)

    def finish(slot, total):
        x_row = HALO + slot
        owned = slot < thickness
        for block in range(SIDE // BLOCK):
            rows = slice(block * BLOCK, (block + 1) * BLOCK)
            inner = slice(8 + block * BLOCK, 8 + (block + 1) * BLOCK)
            centre = centre_ref[x_row, rows, :]
            beside = beside_ref[x_row, rows, :]
            density = jnp.zeros((BLOCK, WIDTH), jnp.float32)
            for part, sign in ((0, 1.0), (1, -1.0)):
                summed = first_ref[part, x_row, inner, :]
                summed = summed + sign * second_ref[1 - part, x_row, inner, :]
                summed = summed - (1.0 / 2.0) * third_ref[part, x_row, inner, :]
                summed = summed - (sign / 6.0) * fourth_ref[1 - part, x_row, inner, :]
                summed = summed + (1.0 / 24.0) * hamilton(3, part, x_row, block, centre, beside)
                summed = jnp.where(owned, summed, 0.0)
                sum_ref[part, slot, rows, :] = summed
                density = density + summed * summed
            density = weight * density
            planes_ref[pl.ds(pl.multiple_of(slot * SIDE + block * BLOCK, 8), BLOCK), :] = density
            total = total + jnp.sum(density.reshape(BLOCK // 8, 8, WIDTH), axis=0)

        return total

    total = lax.fori_loop(0, slots, finish, jnp.zeros((8, WIDTH), jnp.float32))
    departure = pltpu.make_async_copy(sum_ref, psi_ref, out_sem)
    departure.start()
    whole = jnp.broadcast_to(jnp.sum(total, keepdims=True), (SLOTS, LANES))[:, :width - count]
    send_columns(planes_ref, slots, table_y_ref[...], table_z_ref[...], low_ref, high_ref)
    core_rows = SIDE // 2
    first_row = core * core_rows
    for device in range(devices):
        pieces = column_pieces(device * count, count)
        kept_ref[device] = chunk_of(low_ref, high_ref, first_row, pieces, whole)
        sent_ref[device] = chunk_of(low_ref, high_ref, core_rows - first_row, pieces, whole)
    departure.wait()


def unpack_kernel(weight_ref, psi_ref, next_ref, density_kept_ref, density_sent_ref, density_ref):
    core = lax.axis_index("core")
    weight = weight_ref[0]
    slots = psi_ref.shape[1]

    @pl.loop(0, slots)
    def _(slot):
        for part in range(2):

            def load(tile, part=part):
                tall = psi_ref[part, slot, 8 * tile:8 * tile + 8, :]
                return tall[:, :LANES], tall[:, LANES:]

            def store(k, values, part=part):
                next_ref[part, slot, pl.ds(k, 8, stride=STRIDE), :] = values

            to_flat(load, store)
        real = next_ref[0, slot]
        imag = next_ref[1, slot]
        density_ref[slot] = weight * (real * real + imag * imag)

    for slot in range(slots, SLOTS):
        density_ref[slot] = jnp.zeros((FLAT, LANES), jnp.float32)

    @pl.loop(0, SLOTS // 2)
    def _(slot):
        density_kept_ref[slot] = density_ref[core * (SLOTS // 2) + slot]
        density_sent_ref[slot] = density_ref[(1 - core) * (SLOTS // 2) + slot]


def wave_squared(index, count_cells):
    folded = jnp.where(2 * index <= count_cells, index, index - count_cells)
    wave_number = folded.astype(jnp.float32) * (two_pi / count_cells)
    return wave_number * wave_number


def coulomb_kernel(count, length_cells, start_ref, charge_ref, ions_ref, table_ref, out_ref):
    domains, _, width = ions_ref.shape
    states = charge_ref.shape[0] // domains
    device = (lax.axis_index("core") * states + lax.axis_index("row")) * domains + lax.axis_index("domain")
    charge = charge_ref[:domains]
    for state in range(1, states):
        charge = charge + charge_ref[state * domains:(state + 1) * domains]
    charge = charge.reshape(domains * SLOTS, width)
    ions = ions_ref[...].reshape(domains * SLOTS, width)
    first = lax.broadcasted_iota(jnp.int32, (domains * SLOTS, width), 0) % SLOTS == 0
    lane = lax.broadcasted_iota(jnp.int32, (domains * SLOTS, width), 1)
    chosen = first & (lane == count)
    electrons = jnp.sum(jnp.where(chosen, charge, 0.0), keepdims=True)
    ionic = jnp.sum(jnp.where(chosen, ions, 0.0), keepdims=True)
    charge = charge - (electrons / ionic) * ions
    layer = lax.broadcasted_iota(jnp.int32, (length_cells, domains * SLOTS), 0)
    place = lax.broadcasted_iota(jnp.int32, (length_cells, domains * SLOTS), 1)
    chosen_layer = jnp.full(layer.shape, -1, jnp.int32)
    for domain in range(domains):
        slot = place - domain * SLOTS
        here = (slot >= 0) & (slot < start_ref[domain + 1] - start_ref[domain])
        chosen_layer = jnp.where(here, start_ref[domain] + slot, chosen_layer)
    pick = (layer == chosen_layer).astype(jnp.float32)
    table = jnp.dot(table_ref[...], pick, precision=highest, preferred_element_type=jnp.float32)
    waves = jnp.dot(table, charge, precision=highest, preferred_element_type=jnp.float32)
    wave_x = lax.broadcasted_iota(jnp.int32, waves.shape, 0)
    column = device * count + lax.broadcasted_iota(jnp.int32, waves.shape, 1)
    wave_y = ((column.astype(jnp.float32) + 0.5) * (1.0 / SIDE)).astype(jnp.int32)
    wave_z = column - wave_y * SIDE
    squared = (
        wave_squared(wave_x, length_cells) + wave_squared(wave_y, SIDE) + wave_squared(wave_z, SIDE)
    )
    gain = jnp.where(squared > 0, four_pi / jnp.where(squared > 0, squared, 1.0), 0.0)
    waves = waves * (gain * (1.0 / (length_cells * SIDE * SIDE)))
    back = lax.dot_general(
        table, waves, (((0,), (0,)), ((), ())), precision=highest, preferred_element_type=jnp.float32
    )
    back = back.reshape(domains, SLOTS, width)
    for state in range(states):
        out_ref[state * domains:(state + 1) * domains] = back


def field_kernel(count, length_cells, start_ref, waves_ref, others_ref, density_ref, other_ref,
                 circle_ref, table_y_ref, table_z_ref, out_ref, low_ref, high_ref, planes_ref, flat_ref):
    _, own_start, thickness = place_of(start_ref)
    devices = waves_ref.shape[0]
    slots = out_ref.shape[0]
    core = lax.axis_index("core")
    core_rows = SIDE // 2
    first_row = core * core_rows
    for source_ref, first in ((waves_ref, first_row), (others_ref, core_rows - first_row)):
        pieces = []
        for device in range(devices):
            column = 0
            for row, start, stop in column_pieces(device * count, count):
                values = source_ref[device, :, column:column + stop - start]
                column += stop - start
                if start > 0:
                    pieces.append(values)
                    values = jnp.concatenate(pieces, axis=1)
                if stop < SIDE:
                    pieces = [values]
                    continue
                pieces = []
                at = pl.ds(first + row, SLOTS, stride=SIDE)
                low_ref[at, :] = values[:, :LANES]
                high_ref[at, :] = jnp.concatenate(
                    [values[:, LANES:], jnp.zeros((SLOTS, WIDTH - SIDE), jnp.float32)], axis=1
                )
    table_y = table_y_ref[...]
    table_z = table_z_ref[...]
    used = slice(0, slots * SIDE)
    along_z = turn_z(jnp.concatenate([low_ref[used, :], high_ref[used, :]], axis=1), table_z)
    for slot in range(slots):
        rows = slice(slot * SIDE, (slot + 1) * SIDE)
        planes_ref[rows, :] = turn_y(table_y, along_z[rows])

    @pl.loop(0, slots)
    def _(slot):
        def load(tile):
            tall = planes_ref[pl.ds(pl.multiple_of(slot * SIDE + tile * 8, 8), 8), :]
            return tall[:, :LANES], tall[:, LANES:]

        def store(k, values):
            flat_ref[pl.ds(slot * FLAT + k, 8, stride=STRIDE), :] = values

        to_flat(load, store)
        rows = pl.ds(pl.multiple_of(slot * FLAT, 8), FLAT)
        here = slot // (SLOTS // 2) == core
        kept_slot = slot % (SLOTS // 2)
        content = jnp.where(here, density_ref[kept_slot], other_ref[kept_slot]) * (3.0 / math.pi)
        positive = jnp.where(content > 0, content, 1.0)
        root = jnp.exp(jnp.log(positive) * (1.0 / 3.0))
        root = root - (root - positive / (root * root)) * (1.0 / 3.0)
        root = jnp.where(content > 0, root, 0.0)
        inside = mesh_points(own_start + slot, circle_ref[...], length_cells) & (slot < thickness)
        flat_ref[rows, :] = jnp.where(inside, flat_ref[rows, :] - root, 0.0)

    @pl.loop(0, FLAT // 8)
    def _(step):
        for part in range(8):
            lanes = pl.ds(pl.multiple_of((step * 8 + part) * LANES, LANES), LANES)
            out_ref[:, lanes] = flat_ref[pl.ds(step * 8 + part, SLOTS, stride=FLAT), :][:slots]


def from_behind(value, steps):
    count = lax.axis_size("domain")
    leading, last = (max(0, -steps), min(count, count - steps))
    return lax.ppermute(value, "domain", [(source, source + steps) for source in range(leading, last)])


def swapped(value, axis):
    return lax.ppermute(value, axis, [(0, 1), (1, 0)])


def shards(orbitals, occupation, potential, background, layer_start):
    domains = lax.axis_size("domain")
    rows = lax.axis_size("row")
    devices = domains * rows
    length_cells = SLAB * domains
    layer_cap, plane = potential.shape
    count = plane // (2 * devices)
    width = -(-(count + 1) // LANES) * LANES
    circle = jnp.asarray(circle_plane())
    flat_circle = jnp.asarray(circle_table().reshape(FLAT, LANES))
    table_z, into_y, out_of_y = (jnp.asarray(table) for table in tables_of_side())
    table_x = jnp.asarray(hartley_table(length_cells).astype(np.float32))
    params = pltpu.CompilerParams(vmem_limit_bytes=16 * MEBI)
    large = pltpu.CompilerParams(vmem_limit_bytes=44 * MEBI)
    whole = pltpu.CompilerParams(vmem_limit_bytes=56 * MEBI)

    def f32(*shape):
        return jax.ShapeDtypeStruct(shape, jnp.float32)

    def scratch(*shape):
        return pltpu.VMEM(shape, jnp.float32)

    layers = orbitals.reshape(2, layer_cap, FLAT, LANES)
    packed = packed_tiles()
    outer = orbitals.reshape(2, layer_cap * FLAT, LANES)
    up, down = pl.pallas_call(
        pack_kernel,
        out_shape=(f32(2 * HALO, packed * LANES), f32(2 * HALO, packed * LANES)),
        in_specs=[SMEM_SPEC, HBM_SPEC],
        out_specs=(HBM_SPEC, HBM_SPEC),
        scratch_shapes=[
            scratch(2 * HALO * FLAT, LANES),
            scratch(2 * HALO * FLAT, LANES),
            scratch(2 * HALO, packed * LANES),
            scratch(2 * HALO, packed * LANES),
            pltpu.SemaphoreType.DMA((4,)),
            pltpu.SemaphoreType.DMA((2,)),
        ],
        compiler_params=whole,
        name="pack_halo",
    )(layer_start, outer)
    up, down, potential_rest, outer = lax.optimization_barrier((up, down, potential, outer))
    v_rows, up_far, down_far = pl.pallas_call(
        pack_rest_kernel,
        out_shape=(f32(HALO - 1, packed, LANES), f32(2 * FLAT, LANES), f32(2 * FLAT, LANES)),
        in_specs=[SMEM_SPEC, HBM_SPEC, HBM_SPEC],
        out_specs=(VMEM_SPEC,) * 3,
        scratch_shapes=[
            scratch(SLOTS * FLAT, LANES),
            scratch(SLOTS * FLAT, LANES),
            scratch(layer_cap, plane),
            pltpu.SemaphoreType.DMA((5,)),
        ],
        compiler_params=whole,
        cost_estimate=pl.CostEstimate(flops=0, transcendentals=0, bytes_accessed=30_000_000),
        name="pack_rest",
    )(layer_start, potential_rest, outer)
    v_rows = lax.ppermute(
        v_rows,
        ("core", "domain"),
        [(source, source + 1) for source in range(domains - 1)]
        + [(domains + source + 1, domains + source) for source in range(domains - 1)],
    )
    below = from_behind(up, 1)
    above = from_behind(down, -1)
    below_far = from_behind(up_far, 2)
    above_far = from_behind(down_far, -2)
    v_rows, below_far, above_far = lax.optimization_barrier((v_rows, below_far, above_far))
    v_others = swapped(v_rows, "core")

    ions = pl.pallas_call(
        functools.partial(ions_kernel, count, length_cells),
        out_shape=f32(domains, SLOTS, width),
        in_specs=[SMEM_SPEC] + [VMEM_SPEC] * 4,
        out_specs=VMEM_SPEC,
        scratch_shapes=[
            scratch(SLOTS * FLAT, LANES),
            scratch(layer_cap * SIDE, WIDTH),
            scratch(SLOTS * SIDE, LANES),
            scratch(SLOTS * SIDE, LANES),
        ],
        compiler_params=params,
        name="ion_waves",
    )(layer_start, background, circle, into_y, table_z)
    ions = lax.all_to_all(ions, "domain", split_axis=0, concat_axis=0, tiled=True)
    ions, below = lax.optimization_barrier((ions, below))

    span = layer_cap + 2 * HALO
    fields = (2, span, TALL, WIDTH)
    psi, kept, sent = pl.pallas_call(
        functools.partial(propagate_kernel, count, length_cells),
        out_shape=(
            pltpu.HBM((2, layer_cap, SIDE, WIDTH), jnp.float32),
            f32(devices, SLOTS, width),
            f32(devices, SLOTS, width),
        ),
        in_specs=[SMEM_SPEC, SMEM_SPEC, VMEM_SPEC, VMEM_SPEC] + [HBM_SPEC] * 6 + [VMEM_SPEC] * 3,
        out_specs=(HBM_SPEC, VMEM_SPEC, VMEM_SPEC),
        scratch_shapes=[scratch(*fields)] * TERMS
        + [
            scratch(2, layer_cap, SIDE, WIDTH),
            scratch(span, SIDE, WIDTH),
            scratch(span, SIDE, WIDTH),
            scratch(SLOTS * FLAT, LANES),
            scratch(layer_cap * SIDE, WIDTH),
            scratch(SLOTS * SIDE, LANES),
            scratch(SLOTS * SIDE, LANES),
            scratch(SLOTS * FLAT, LANES),
            scratch(SLOTS * FLAT, LANES),
            scratch(SLOTS * FLAT, LANES),
            scratch(HALO - 1, packed, LANES),
            scratch(HALO - 1, packed, LANES),
            scratch(2 * HALO, packed * LANES),
            scratch(2 * HALO, packed * LANES),
            scratch(2 * FLAT, LANES),
            scratch(2 * FLAT, LANES),
            pltpu.SemaphoreType.DMA((6,)),
            pltpu.SemaphoreType.DMA,
        ],
        compiler_params=large,
        name="propagate",
    )(layer_start, occupation, layers, potential, below, above, below_far, above_far, v_rows, v_others,
      circle, into_y, table_z)
    waves = kept + swapped(sent, "core")
    waves, psi = lax.optimization_barrier((waves, psi))
    waves = lax.all_to_all(waves, ("row", "domain"), split_axis=0, concat_axis=0, tiled=True)
    orbitals_next, density_kept, density_sent = pl.pallas_call(
        unpack_kernel,
        out_shape=(
            f32(2, layer_cap, FLAT, LANES),
            f32(SLOTS // 2, FLAT, LANES),
            f32(SLOTS // 2, FLAT, LANES),
        ),
        in_specs=[SMEM_SPEC, VMEM_SPEC],
        out_specs=(VMEM_SPEC,) * 3,
        scratch_shapes=[scratch(SLOTS, FLAT, LANES)],
        compiler_params=params,
        name="unpack",
    )(occupation, psi)
    density = density_kept + swapped(density_sent, "core")
    waves, density = lax.optimization_barrier((waves, density))
    other_density = swapped(density, "row")
    waves = pl.pallas_call(
        functools.partial(coulomb_kernel, count, length_cells),
        out_shape=f32(devices, SLOTS, width),
        in_specs=[SMEM_SPEC] + [VMEM_SPEC] * 3,
        out_specs=VMEM_SPEC,
        compiler_params=params,
        name="coulomb",
    )(layer_start, waves, ions, table_x)
    waves = lax.all_to_all(waves, ("row", "domain"), split_axis=0, concat_axis=0, tiled=True)
    waves, other_density = lax.optimization_barrier((waves, other_density))
    density = density + other_density
    other_density = swapped(density, "core")
    other_waves = swapped(waves, "core")
    potential_next = pl.pallas_call(
        functools.partial(field_kernel, count, length_cells),
        out_shape=f32(layer_cap, plane),
        in_specs=[SMEM_SPEC] + [VMEM_SPEC] * 7,
        out_specs=VMEM_SPEC,
        scratch_shapes=[
            scratch(SLOTS * SIDE, LANES),
            scratch(SLOTS * SIDE, LANES),
            scratch(layer_cap * SIDE, WIDTH),
            scratch(SLOTS * FLAT, LANES),
        ],
        compiler_params=params,
        name="field",
    )(layer_start, waves, other_waves, density, other_density, flat_circle, out_of_y, table_z)
    return orbitals_next.reshape(orbitals.shape), potential_next


def solution(mesh):
    domains = mesh.shape["domain"]
    split = Mesh(mesh.devices.reshape(-1, 2, domains), ("row", "core", "domain"))
    states = ("row", "core")
    return jax.shard_map(
        shards,
        mesh=split,
        in_specs=(
            P(None, states, "domain", None),
            P(states),
            P("domain", None),
            P("domain", None),
            P(),
        ),
        out_specs=(P(None, states, "domain", None), P("domain", None)),
        check_vma=False,
    )
```

```python
import functools
import math

import jax
import jax.numpy as jnp
import ml_dtypes
import numpy as np
from jax import lax
from jax.experimental import pallas as pl
from jax.experimental.pallas import tpu as pltpu
from jax.sharding import Mesh, PartitionSpec as P

SIDE = 160
SLAB = 5
TERMS = 4

HALO = TERMS
LANES = 128
SLOTS = 8
RUN = SIDE // 8
FLAT = SIDE * SIDE // LANES
STRIDE = FLAT // 8
WIDTH = 2 * LANES
BLOCK = 32
TALL = SIDE + 16

time_step = 0.3
four_pi = 4.0 * math.pi
two_pi = 2.0 * math.pi
highest = lax.Precision.HIGHEST
MEBI = 1024 * 1024
SMEM_SPEC = pl.BlockSpec(memory_space=pltpu.SMEM)
VMEM_SPEC = pl.BlockSpec(memory_space=pltpu.VMEM)
HBM_SPEC = pl.BlockSpec(memory_space=pltpu.HBM)


def hartley_table(count_cells):
    index_run = np.arange(count_cells)
    angles = (index_run[:, None] * index_run[None, :] % count_cells) * (2.0 * np.pi / count_cells)
    return np.cos(angles) + np.sin(angles)


def plane_order():
    rows = np.arange(SIDE)
    return RUN * (rows % 8) + rows // 8


def two_parts(table):
    table = table.astype(np.float32)
    high = table.astype(ml_dtypes.bfloat16)
    low = (table - high.astype(np.float32)).astype(ml_dtypes.bfloat16)
    return high, low


def tables_of_side():
    table = hartley_table(SIDE)
    along_z = np.zeros((WIDTH, WIDTH))
    along_z[:SIDE, :SIDE] = table
    high, low = two_parts(along_z)
    along_z = np.concatenate([high, high, low], axis=0)
    high, low = two_parts(table[:, plane_order()])
    into_y = np.concatenate([high, high, low], axis=1)
    high, low = two_parts(table[plane_order(), :])
    out_of_y = np.concatenate([high, high, low], axis=1)
    return along_z, into_y, out_of_y


def circle_table():
    across = 2 * np.arange(SIDE, dtype=np.int64) - (SIDE - 1)
    return (across[:, None] ** 2 + across[None, :] ** 2).astype(np.int32)


def circle_plane():
    table = np.full((SIDE, WIDTH), 4 * SIDE * SIDE, np.int32)
    table[:, :SIDE] = circle_table()[plane_order()]
    return table


def mesh_points(x_row, circle, length_cells):
    room = ((length_cells - 2) ** 2 - (2 * x_row - (length_cells - 1)) ** 2) * (SIDE - 2) ** 2
    return (circle * (length_cells - 2) ** 2 <= room) & (circle < 4 * SIDE * SIDE)


def column_pieces(first, count):
    pieces = []
    column = first
    while column < first + count:
        row = column // SIDE
        stop = min((row + 1) * SIDE, first + count)
        pieces.append((row, column - row * SIDE, stop - row * SIDE))
        column = stop
    return pieces


def tile_rows(first, count):
    return pl.ds(first if isinstance(first, int) else pl.multiple_of(first, 8), count)


def eight(values):
    missing = jnp.zeros((SLOTS - values.shape[0], values.shape[1]), values.dtype)
    return jnp.concatenate([values, missing], axis=0)


def in_turns(first, last, size, body):
    turns = (last - first) // size
    if turns > 1:

        @pl.loop(0, turns)
        def _(turn):
            for index in range(size):
                body(first + turn * size + index)

        first += turns * size
    for index in range(first, last):
        body(index)


def to_plane(load, store):
    lane = lax.broadcasted_iota(jnp.int32, (8, LANES), 1)
    for step in range(RUN // 4):
        rows = [load(5 * step + part) for part in range(5)]
        store(4 * step, rows[0], rows[1])
        for part in range(1, 4):
            left = pltpu.roll(rows[part], LANES - 32 * part, 1)
            right = pltpu.roll(rows[part + 1], LANES - 32 * part, 1)
            store(4 * step + part, jnp.where(lane < LANES - 32 * part, left, right), right)


def to_flat(load, store):
    lane = lax.broadcasted_iota(jnp.int32, (8, LANES), 1)
    for step in range(RUN // 4):
        turned = []
        for part in range(4):
            low, high = load(4 * step + part)
            if part:
                low = pltpu.roll(low, 32 * part, 1)
                high = pltpu.roll(high, 32 * part, 1)
            turned.append((low, high))
        store(5 * step, turned[0][0])
        for part in range(1, 4):
            ended = 32 * (part - 1)
            values = jnp.where(lane < ended + 32, turned[part - 1][1], turned[part][0])
            if ended:
                values = jnp.where(lane < ended, turned[part - 1][0], values)
            store(5 * step + part, values)
        store(5 * step + 4, jnp.where(lane < 96, turned[3][0], turned[3][1]))


def chords():
    across = 2 * np.arange(SIDE, dtype=np.int64) - (SIDE - 1)
    room = (SIDE - 2) ** 2 - across**2
    return [max([w for w in range(1, SIDE // 2 + 1) if (2 * w - 1) ** 2 <= left], default=0) for left in room]


def chord_moves():
    moves = []
    packed = 0
    for row, half in enumerate(chords()):
        if half:
            moves.append((row * SIDE + SIDE // 2 - half, packed, 2 * half))
            packed += 2 * half
    return moves


def packed_tiles():
    _, start, length = chord_moves()[-1]
    return -(-(start + length) // LANES)


def move_lanes(moves, load, store):
    lane = lax.broadcasted_iota(jnp.int32, (8, LANES), 1)
    pieces = {}
    for source, target, length in moves:
        while length:
            size = min(length, LANES - source % LANES, LANES - target % LANES)
            pieces.setdefault(target // LANES, []).append((target % LANES, source // LANES, (target - source) % LANES))
            source, target, length = source + size, target + size, length - size
    loaded = {}
    turned = {}
    for tile in sorted(pieces):
        values = None
        for first, origin, shift in sorted(pieces[tile]):
            if origin not in loaded:
                loaded[origin] = load(origin)
            if (origin, shift) not in turned:
                turned[origin, shift] = pltpu.roll(loaded[origin], shift, 1) if shift else loaded[origin]
            piece = turned[origin, shift]
            values = piece if values is None else jnp.where(lane >= first, piece, values)
        store(tile, values)


def pack_chords(rows_ref, store):
    move_lanes(chord_moves(), lambda tile: rows_ref[pl.ds(tile, 8, stride=FLAT), :], store)


def unpack_chords(load, rows_ref):
    def store(tile, values):
        rows_ref[pl.ds(tile, 8, stride=FLAT), :] = values

    move_lanes([(target, source, length) for source, target, length in chord_moves()], load, store)


def parts_of(values):
    high = values.astype(jnp.bfloat16)
    low = (values - high.astype(jnp.float32)).astype(jnp.bfloat16)
    return high, low


def turn_z(values, table):
    high, low = parts_of(values)
    return jnp.dot(
        jnp.concatenate([high, low, high], axis=1), table, preferred_element_type=jnp.float32
    )


def turn_y(table, values):
    high, low = parts_of(values)
    return jnp.dot(
        table, jnp.concatenate([high, low, high], axis=0), preferred_element_type=jnp.float32
    )


def send_columns(planes_ref, slots, table_y, table_z, low_ref, high_ref):
    along_z = turn_z(planes_ref[:slots * SIDE, :], table_z)
    for slot in range(slots):
        rows = slice(slot * SIDE, (slot + 1) * SIDE)
        waves = turn_y(table_y, along_z[rows])
        low_ref[rows, :] = waves[:, :LANES]
        high_ref[rows, :] = waves[:, LANES:]
    low_ref[slots * SIDE:, :] = jnp.zeros(((SLOTS - slots) * SIDE, LANES), jnp.float32)
    high_ref[slots * SIDE:, :] = jnp.zeros(((SLOTS - slots) * SIDE, LANES), jnp.float32)


def chunk_of(low_ref, high_ref, first_row, pieces, extra):
    parts = []
    for row, start, stop in pieces:
        at = pl.ds(first_row + row, SLOTS, stride=SIDE)
        values = jnp.concatenate([low_ref[at, :], high_ref[at, :]], axis=1)
        parts.append(values[:, start:stop])
    return jnp.concatenate(parts + [extra], axis=1)


def layers_of(stored_ref, flat_ref):
    @pl.loop(0, FLAT // 8)
    def _(step):
        for part in range(8):
            lanes = pl.ds(pl.multiple_of((step * 8 + part) * LANES, LANES), LANES)
            flat_ref[pl.ds(step * 8 + part, SLOTS, stride=FLAT), :] = eight(stored_ref[:, lanes])


def place_of(start_ref):
    position = lax.axis_index("domain")
    return position, start_ref[position], start_ref[position + 1] - start_ref[position]


def started(sems, pairs):
    copies = [pltpu.make_async_copy(*pair, sems.at[index]) for index, pair in enumerate(pairs)]
    for made in copies:
        made.start()
    return copies


def layers_at(orbitals_ref, part, start, count):
    return orbitals_ref.at[part, pl.ds(pl.multiple_of(start * FLAT, 8), count * FLAT)]


def rows_at(ref, part, count):
    return ref.at[pl.ds(part * count * FLAT, count * FLAT)]


def pack_kernel(start_ref, orbitals_ref, up_ref, down_ref, up_rows_ref, down_rows_ref, up_buffer_ref,
                down_buffer_ref, in_sems, out_sems):
    _, _, thickness = place_of(start_ref)
    first = jnp.maximum(thickness - HALO, 0)
    arrivals = started(
        in_sems,
        [
            (layers_at(orbitals_ref, part, start, HALO), rows_at(rows_ref, part, HALO))
            for start, rows_ref in ((first, up_rows_ref), (0, down_rows_ref))
            for part in range(2)
        ],
    )
    departures = []
    for index, (rows_ref, buffer_ref, out_ref) in enumerate(
        ((up_rows_ref, up_buffer_ref, up_ref), (down_rows_ref, down_buffer_ref, down_ref))
    ):
        arrivals[2 * index].wait()
        arrivals[2 * index + 1].wait()

        def store(tile, values, buffer_ref=buffer_ref):
            buffer_ref[:, tile * LANES:(tile + 1) * LANES] = values

        pack_chords(rows_ref, store)
        departures.append(pltpu.make_async_copy(buffer_ref, out_ref, out_sems.at[index]))
        departures[-1].start()
    for made in departures:
        made.wait()


def pack_rest_kernel(start_ref, potential_ref, orbitals_ref, v_ref, up_far_ref, down_far_ref, flat_ref,
                     v_rows_ref, stored_ref, in_sems):
    _, _, thickness = place_of(start_ref)
    v_first = jnp.where(lax.axis_index("core") == 0, thickness - (HALO - 1), 0)
    arrivals = started(
        in_sems,
        [(potential_ref, stored_ref)]
        + [
            (layers_at(orbitals_ref, part, start, 1), rows_at(far_ref, part, 1))
            for start, far_ref in ((thickness - 1, up_far_ref), (0, down_far_ref))
            for part in range(2)
        ],
    )
    arrivals[0].wait()
    layers_of(stored_ref, flat_ref)
    for layer in range(HALO - 1):
        v_rows_ref[layer * FLAT:(layer + 1) * FLAT, :] = flat_ref[
            pl.ds(pl.multiple_of((v_first + layer) * FLAT, 8), FLAT), :
        ]

    def store_v(tile, values):
        for layer in range(HALO - 1):
            v_ref[layer, tile:tile + 1, :] = values[layer:layer + 1]

    pack_chords(v_rows_ref, store_v)
    for made in arrivals[1:]:
        made.wait()


def ions_kernel(count, length_cells, start_ref, background_ref, circle_ref, table_y_ref, table_z_ref,
                out_ref, flat_ref, planes_ref, low_ref, high_ref):
    _, own_start, thickness = place_of(start_ref)
    slots = background_ref.shape[0]
    groups, _, width = out_ref.shape
    layers_of(background_ref, flat_ref)

    def body(slot, total):
        def store(tile, low, high):
            rows = pl.ds(pl.multiple_of(slot * SIDE + tile * 8, 8), 8)
            planes_ref[rows, :LANES] = low
            planes_ref[rows, LANES:] = high

        to_plane(lambda k: flat_ref[pl.ds(slot * FLAT + k, 8, stride=STRIDE), :], store)
        rows = pl.ds(pl.multiple_of(slot * SIDE, 8), SIDE)
        inside = mesh_points(own_start + slot, circle_ref[...], length_cells) & (slot < thickness)
        values = jnp.where(inside, planes_ref[rows, :], 0.0)
        planes_ref[rows, :] = values
        return total + jnp.sum(values.reshape(RUN, 8, WIDTH), axis=0)

    total = lax.fori_loop(0, slots, body, jnp.zeros((8, WIDTH), jnp.float32))
    whole = jnp.broadcast_to(jnp.sum(total, keepdims=True), (SLOTS, LANES))[:, :width - count]
    send_columns(planes_ref, slots, table_y_ref[...], table_z_ref[...], low_ref, high_ref)
    core_rows = SIDE // lax.axis_size("core")
    first_row = lax.axis_index("core") * core_rows + lax.axis_index("row") * (core_rows // lax.axis_size("row"))
    for group in range(groups):
        out_ref[group] = chunk_of(low_ref, high_ref, first_row, column_pieces(group * count, count), whole)


def propagate_kernel(count, length_cells, start_ref, weight_ref, orbitals_ref, potential_ref, below_hbm_ref,
                     above_hbm_ref, below_far_hbm_ref, above_far_hbm_ref, v_hbm_ref, v_other_hbm_ref,
                     circle_ref, table_y_ref, table_z_ref, psi_ref, kept_ref, sent_ref, first_ref, second_ref,
                     third_ref, fourth_ref, sum_ref, centre_ref, beside_ref, flat_ref, planes_ref, low_ref,
                     high_ref, below_rows_ref, above_rows_ref, v_rows_ref, v_ref, v_other_ref, below_ref,
                     above_ref, below_far_ref, above_far_ref, in_sems, out_sem):
    arrivals = started(
        in_sems,
        [
            (v_hbm_ref, v_ref),
            (v_other_hbm_ref, v_other_ref),
            (below_hbm_ref, below_ref),
            (above_hbm_ref, above_ref),
            (below_far_hbm_ref, below_far_ref),
            (above_far_hbm_ref, above_far_ref),
        ],
    )
    position, own_start, thickness = place_of(start_ref)
    domains = lax.axis_size("domain")
    before = start_ref[jnp.maximum(position - 1, 0)]
    after = start_ref[jnp.minimum(position + 2, domains)]
    short_below = ((position > 0) & (own_start - before < HALO)).astype(jnp.int32)
    short_above = (position < domains - 1) & (after - own_start - thickness < HALO)
    weight = weight_ref[0]
    core = lax.axis_index("core")
    slots = orbitals_ref.shape[1]
    layers = slots + 2 * HALO
    devices, _, width = kept_ref.shape
    field_refs = (first_ref, second_ref, third_ref, fourth_ref)

    def field_layer(part, x_row):
        def store(tile, low, high):
            first_ref[part, x_row, 8 + 8 * tile:16 + 8 * tile, :LANES] = low
            first_ref[part, x_row, 8 + 8 * tile:16 + 8 * tile, LANES:] = high

        return store

    def potential_layer(x_row):
        def store(tile, low, high):
            centre_ref[x_row, 8 * tile:8 * tile + 8, :LANES] = low
            centre_ref[x_row, 8 * tile:8 * tile + 8, LANES:] = high

        return store

    def rows_from(ref, *at):
        return lambda k: ref[(*at, pl.ds(k, 8, stride=STRIDE), slice(None))]

    def layer_of(rows_ref, layer):
        return lambda k: rows_ref[pl.ds(layer * FLAT + k, 8, stride=STRIDE), :]

    layers_of(potential_ref, flat_ref)

    for slot in range(slots):
        for part in range(2):
            to_plane(rows_from(orbitals_ref, part, slot), field_layer(part, HALO + slot))
        to_plane(layer_of(flat_ref, slot), potential_layer(HALO + slot))

    for made in arrivals:
        made.wait()
    for packed_ref, rows_ref in ((below_ref, below_rows_ref), (above_ref, above_rows_ref)):
        unpack_chords(
            lambda tile, packed_ref=packed_ref: packed_ref[:, tile * LANES:(tile + 1) * LANES], rows_ref
        )
    unpack_chords(
        lambda tile: eight(
            jnp.concatenate([ref[:, tile, :] for ref in (v_ref, v_other_ref)], axis=0)
        ),
        v_rows_ref,
    )

    for layer in range(HALO - 1):
        lower = 1 + layer
        upper = HALO + thickness + layer
        to_plane(layer_of(v_rows_ref, layer), potential_layer(jnp.where(core == 0, lower, upper)))
        to_plane(layer_of(v_rows_ref, HALO - 1 + layer), potential_layer(jnp.where(core == 0, upper, lower)))
        for part in range(2):
            to_plane(
                layer_of(below_rows_ref, part * HALO + 1 + layer - short_below), field_layer(part, 1 + layer)
            )
            to_plane(
                layer_of(above_rows_ref, part * HALO + layer), field_layer(part, HALO + thickness + layer)
            )

    @pl.loop(0, 2)
    def _(part):
        last = 2 * HALO - 1 + thickness

        @pl.when(short_below > 0)
        def _():
            to_plane(layer_of(below_far_ref, part), field_layer(part, 0))

        @pl.when(short_below == 0)
        def _():
            to_plane(layer_of(below_rows_ref, part * HALO), field_layer(part, 0))

        @pl.when(short_above)
        def _():
            to_plane(layer_of(above_far_ref, part), field_layer(part, last))

        @pl.when(jnp.logical_not(short_above))
        def _():
            to_plane(layer_of(above_rows_ref, part * HALO + HALO - 1), field_layer(part, last))

    def wrap(field_ref, part, x_row, first, final):
        field_ref[part, x_row, :8, :] = pltpu.roll(final, 1, 0)
        field_ref[part, x_row, SIDE + 8:, :] = pltpu.roll(first, 7, 0)

    blocks = SIDE // BLOCK

    def confine(x_row):
        known = x_row < thickness + 2 * HALO
        ends = {}
        for block in range(blocks):
            rows = slice(block * BLOCK, (block + 1) * BLOCK)
            inner = slice(8 + block * BLOCK, 8 + (block + 1) * BLOCK)
            inside = mesh_points(own_start - HALO + x_row, circle_ref[rows, :], length_cells) & known
            centre_ref[x_row, rows, :] = jnp.where(
                inside, (3.0 + centre_ref[x_row, rows, :]) * time_step, 0.0
            )
            beside_ref[x_row, rows, :] = jnp.where(inside, 0.5 * time_step, 0.0)
            for part in range(2):
                field = jnp.where(inside, first_ref[part, x_row, inner, :], 0.0)
                first_ref[part, x_row, inner, :] = field
                ends[part, block] = field
        for part in range(2):
            wrap(first_ref, part, x_row, ends[part, 0][:8], ends[part, blocks - 1][BLOCK - 8:])

    in_turns(0, layers, 5, confine)

    def hamilton(term, part, x_row, block, centre, beside):
        field_ref = field_refs[term]
        tall = field_ref[part, x_row, block * BLOCK:block * BLOCK + BLOCK + 16, :]
        inner = slice(8 + block * BLOCK, 8 + (block + 1) * BLOCK)
        field = tall[8:8 + BLOCK]
        around = field_ref[part, x_row - 1, inner, :] + field_ref[part, x_row + 1, inner, :]
        around = around + (tall[:BLOCK] + tall[16:])
        around = around + (pltpu.roll(field, 1, 1) + pltpu.roll(field, WIDTH - 1, 1))
        return centre * field - beside * around

    for term in range(1, TERMS):

        def step(x_row, term=term):
            ends = {}
            for block in range(blocks):
                rows = slice(block * BLOCK, (block + 1) * BLOCK)
                inner = slice(8 + block * BLOCK, 8 + (block + 1) * BLOCK)
                centre = centre_ref[x_row, rows, :]
                beside = beside_ref[x_row, rows, :]
                for part in range(2):
                    field = hamilton(term - 1, part, x_row, block, centre, beside)
                    field_refs[term][part, x_row, inner, :] = field
                    ends[part, block] = field
            for part in range(2):
                wrap(field_refs[term], part, x_row, ends[part, 0][:8], ends[part, blocks - 1][BLOCK - 8:])

        in_turns(term, layers - term, 4, step)

    def finish(slot, total):
        x_row = HALO + slot
        owned = slot < thickness
        for block in range(SIDE // BLOCK):
            rows = slice(block * BLOCK, (block + 1) * BLOCK)
            inner = slice(8 + block * BLOCK, 8 + (block + 1) * BLOCK)
            centre = centre_ref[x_row, rows, :]
            beside = beside_ref[x_row, rows, :]
            density = jnp.zeros((BLOCK, WIDTH), jnp.float32)
            for part, sign in ((0, 1.0), (1, -1.0)):
                summed = first_ref[part, x_row, inner, :]
                summed = summed + sign * second_ref[1 - part, x_row, inner, :]
                summed = summed - (1.0 / 2.0) * third_ref[part, x_row, inner, :]
                summed = summed - (sign / 6.0) * fourth_ref[1 - part, x_row, inner, :]
                summed = summed + (1.0 / 24.0) * hamilton(3, part, x_row, block, centre, beside)
                summed = jnp.where(owned, summed, 0.0)
                sum_ref[part, slot, rows, :] = summed
                density = density + summed * summed
            density = weight * density
            planes_ref[tile_rows(slot * SIDE + block * BLOCK, BLOCK), :] = density
            total = total + jnp.sum(density.reshape(BLOCK // 8, 8, WIDTH), axis=0)

        return total

    total = lax.fori_loop(
        0, slots // 2, lambda pair, total: finish(2 * pair + 1, finish(2 * pair, total)), jnp.zeros((8, WIDTH), jnp.float32)
    )
    for slot in range(slots // 2 * 2, slots):
        total = finish(slot, total)
    departure = pltpu.make_async_copy(sum_ref, psi_ref, out_sem)
    departure.start()
    whole = jnp.broadcast_to(jnp.sum(total, keepdims=True), (SLOTS, LANES))[:, :width - count]
    send_columns(planes_ref, slots, table_y_ref[...], table_z_ref[...], low_ref, high_ref)
    core_rows = SIDE // 2
    first_row = core * core_rows
    for device in range(devices):
        pieces = column_pieces(device * count, count)
        kept_ref[device] = chunk_of(low_ref, high_ref, first_row, pieces, whole)
        sent_ref[device] = chunk_of(low_ref, high_ref, core_rows - first_row, pieces, whole)
    departure.wait()


def unpack_kernel(weight_ref, psi_ref, next_ref, density_kept_ref, density_sent_ref, density_ref):
    core = lax.axis_index("core")
    weight = weight_ref[0]
    slots = psi_ref.shape[1]

    def unpack(slot):
        for part in range(2):

            def load(tile, part=part):
                tall = psi_ref[part, slot, 8 * tile:8 * tile + 8, :]
                return tall[:, :LANES], tall[:, LANES:]

            def store(k, values, part=part):
                next_ref[part, slot, pl.ds(k, 8, stride=STRIDE), :] = values

            to_flat(load, store)
        real = next_ref[0, slot]
        imag = next_ref[1, slot]
        density_ref[slot] = weight * (real * real + imag * imag)

    in_turns(0, slots, 2, unpack)
    for slot in range(slots, SLOTS):
        density_ref[slot] = jnp.zeros((FLAT, LANES), jnp.float32)

    @pl.loop(0, SLOTS // 2)
    def _(slot):
        density_kept_ref[slot] = density_ref[core * (SLOTS // 2) + slot]
        density_sent_ref[slot] = density_ref[(1 - core) * (SLOTS // 2) + slot]


def wave_squared(index, count_cells):
    folded = jnp.where(2 * index <= count_cells, index, index - count_cells)
    wave_number = folded.astype(jnp.float32) * (two_pi / count_cells)
    return wave_number * wave_number


def coulomb_kernel(count, length_cells, start_ref, charge_ref, ions_ref, table_ref, out_ref):
    domains, _, width = ions_ref.shape
    states = charge_ref.shape[0] // domains
    device = (lax.axis_index("core") * states + lax.axis_index("row")) * domains + lax.axis_index("domain")
    charge = charge_ref[:domains]
    for state in range(1, states):
        charge = charge + charge_ref[state * domains:(state + 1) * domains]
    charge = charge.reshape(domains * SLOTS, width)
    ions = ions_ref[...].reshape(domains * SLOTS, width)
    first = lax.broadcasted_iota(jnp.int32, (domains * SLOTS, width), 0) % SLOTS == 0
    lane = lax.broadcasted_iota(jnp.int32, (domains * SLOTS, width), 1)
    chosen = first & (lane == count)
    electrons = jnp.sum(jnp.where(chosen, charge, 0.0), keepdims=True)
    ionic = jnp.sum(jnp.where(chosen, ions, 0.0), keepdims=True)
    charge = charge - (electrons / ionic) * ions
    layer = lax.broadcasted_iota(jnp.int32, (length_cells, domains * SLOTS), 0)
    place = lax.broadcasted_iota(jnp.int32, (length_cells, domains * SLOTS), 1)
    chosen_layer = jnp.full(layer.shape, -1, jnp.int32)
    for domain in range(domains):
        slot = place - domain * SLOTS
        here = (slot >= 0) & (slot < start_ref[domain + 1] - start_ref[domain])
        chosen_layer = jnp.where(here, start_ref[domain] + slot, chosen_layer)
    pick = (layer == chosen_layer).astype(jnp.float32)
    table = jnp.dot(table_ref[...], pick, precision=highest, preferred_element_type=jnp.float32)
    waves = jnp.dot(table, charge, precision=highest, preferred_element_type=jnp.float32)
    wave_x = lax.broadcasted_iota(jnp.int32, waves.shape, 0)
    column = device * count + lax.broadcasted_iota(jnp.int32, waves.shape, 1)
    wave_y = ((column.astype(jnp.float32) + 0.5) * (1.0 / SIDE)).astype(jnp.int32)
    wave_z = column - wave_y * SIDE
    squared = (
        wave_squared(wave_x, length_cells) + wave_squared(wave_y, SIDE) + wave_squared(wave_z, SIDE)
    )
    gain = jnp.where(squared > 0, four_pi / jnp.where(squared > 0, squared, 1.0), 0.0)
    waves = waves * (gain * (1.0 / (length_cells * SIDE * SIDE)))
    back = lax.dot_general(
        table, waves, (((0,), (0,)), ((), ())), precision=highest, preferred_element_type=jnp.float32
    )
    back = back.reshape(domains, SLOTS, width)
    for state in range(states):
        out_ref[state * domains:(state + 1) * domains] = back


def field_kernel(count, length_cells, start_ref, waves_ref, others_ref, density_ref, other_ref,
                 circle_ref, table_y_ref, table_z_ref, out_ref, low_ref, high_ref, planes_ref, flat_ref):
    _, own_start, thickness = place_of(start_ref)
    devices = waves_ref.shape[0]
    slots = out_ref.shape[0]
    core = lax.axis_index("core")
    core_rows = SIDE // 2
    first_row = core * core_rows
    for source_ref, first in ((waves_ref, first_row), (others_ref, core_rows - first_row)):
        pieces = []
        for device in range(devices):
            column = 0
            for row, start, stop in column_pieces(device * count, count):
                values = source_ref[device, :, column:column + stop - start]
                column += stop - start
                if start > 0:
                    pieces.append(values)
                    values = jnp.concatenate(pieces, axis=1)
                if stop < SIDE:
                    pieces = [values]
                    continue
                pieces = []
                at = pl.ds(first + row, SLOTS, stride=SIDE)
                low_ref[at, :] = values[:, :LANES]
                high_ref[at, :] = jnp.concatenate(
                    [values[:, LANES:], jnp.zeros((SLOTS, WIDTH - SIDE), jnp.float32)], axis=1
                )
    table_y = table_y_ref[...]
    table_z = table_z_ref[...]
    used = slice(0, slots * SIDE)
    along_z = turn_z(jnp.concatenate([low_ref[used, :], high_ref[used, :]], axis=1), table_z)
    for slot in range(slots):
        rows = slice(slot * SIDE, (slot + 1) * SIDE)
        planes_ref[rows, :] = turn_y(table_y, along_z[rows])

    def field(slot):
        def load(tile):
            tall = planes_ref[tile_rows(slot * SIDE + tile * 8, 8), :]
            return tall[:, :LANES], tall[:, LANES:]

        def store(k, values):
            flat_ref[pl.ds(slot * FLAT + k, 8, stride=STRIDE), :] = values

        to_flat(load, store)
        rows = tile_rows(slot * FLAT, FLAT)
        here = slot // (SLOTS // 2) == core
        kept_slot = slot % (SLOTS // 2)
        content = jnp.where(here, density_ref[kept_slot], other_ref[kept_slot]) * (3.0 / math.pi)
        positive = jnp.where(content > 0, content, 1.0)
        root = jnp.exp(jnp.log(positive) * (1.0 / 3.0))
        root = root - (root - positive / (root * root)) * (1.0 / 3.0)
        root = jnp.where(content > 0, root, 0.0)
        inside = mesh_points(own_start + slot, circle_ref[...], length_cells) & (slot < thickness)
        flat_ref[rows, :] = jnp.where(inside, flat_ref[rows, :] - root, 0.0)

    in_turns(0, slots, 2, field)

    @pl.loop(0, FLAT // 8)
    def _(step):
        for part in range(8):
            lanes = pl.ds(pl.multiple_of((step * 8 + part) * LANES, LANES), LANES)
            out_ref[:, lanes] = flat_ref[pl.ds(step * 8 + part, SLOTS, stride=FLAT), :][:slots]


def from_behind(value, steps):
    count = lax.axis_size("domain")
    leading, last = (max(0, -steps), min(count, count - steps))
    return lax.ppermute(value, "domain", [(source, source + steps) for source in range(leading, last)])


def swapped(value, axis):
    return lax.ppermute(value, axis, [(0, 1), (1, 0)])


def shards(orbitals, occupation, potential, background, layer_start):
    domains = lax.axis_size("domain")
    rows = lax.axis_size("row")
    devices = domains * rows
    length_cells = SLAB * domains
    layer_cap, plane = potential.shape
    count = plane // (2 * devices)
    width = -(-(count + 1) // LANES) * LANES
    circle = jnp.asarray(circle_plane())
    flat_circle = jnp.asarray(circle_table().reshape(FLAT, LANES))
    table_z, into_y, out_of_y = (jnp.asarray(table) for table in tables_of_side())
    table_x = jnp.asarray(hartley_table(length_cells).astype(np.float32))
    params = pltpu.CompilerParams(vmem_limit_bytes=16 * MEBI)
    large = pltpu.CompilerParams(vmem_limit_bytes=44 * MEBI)
    whole = pltpu.CompilerParams(vmem_limit_bytes=56 * MEBI)

    def f32(*shape):
        return jax.ShapeDtypeStruct(shape, jnp.float32)

    def scratch(*shape):
        return pltpu.VMEM(shape, jnp.float32)

    layers = orbitals.reshape(2, layer_cap, FLAT, LANES)
    packed = packed_tiles()
    outer = orbitals.reshape(2, layer_cap * FLAT, LANES)
    up, down = pl.pallas_call(
        pack_kernel,
        out_shape=(f32(2 * HALO, packed * LANES), f32(2 * HALO, packed * LANES)),
        in_specs=[SMEM_SPEC, HBM_SPEC],
        out_specs=(HBM_SPEC, HBM_SPEC),
        scratch_shapes=[
            scratch(2 * HALO * FLAT, LANES),
            scratch(2 * HALO * FLAT, LANES),
            scratch(2 * HALO, packed * LANES),
            scratch(2 * HALO, packed * LANES),
            pltpu.SemaphoreType.DMA((4,)),
            pltpu.SemaphoreType.DMA((2,)),
        ],
        compiler_params=whole,
        name="pack_halo",
    )(layer_start, outer)
    up, down, potential_rest, outer = lax.optimization_barrier((up, down, potential, outer))
    v_rows, up_far, down_far = pl.pallas_call(
        pack_rest_kernel,
        out_shape=(f32(HALO - 1, packed, LANES), f32(2 * FLAT, LANES), f32(2 * FLAT, LANES)),
        in_specs=[SMEM_SPEC, HBM_SPEC, HBM_SPEC],
        out_specs=(VMEM_SPEC,) * 3,
        scratch_shapes=[
            scratch(SLOTS * FLAT, LANES),
            scratch(SLOTS * FLAT, LANES),
            scratch(layer_cap, plane),
            pltpu.SemaphoreType.DMA((5,)),
        ],
        compiler_params=whole,
        cost_estimate=pl.CostEstimate(flops=0, transcendentals=0, bytes_accessed=30_000_000),
        name="pack_rest",
    )(layer_start, potential_rest, outer)
    v_rows = lax.ppermute(
        v_rows,
        ("core", "domain"),
        [(source, source + 1) for source in range(domains - 1)]
        + [(domains + source + 1, domains + source) for source in range(domains - 1)],
    )
    below = from_behind(up, 1)
    above = from_behind(down, -1)
    below_far = from_behind(up_far, 2)
    above_far = from_behind(down_far, -2)
    v_rows, below_far, above_far = lax.optimization_barrier((v_rows, below_far, above_far))
    v_others = swapped(v_rows, "core")

    ions = pl.pallas_call(
        functools.partial(ions_kernel, count, length_cells),
        out_shape=f32(domains, SLOTS, width),
        in_specs=[SMEM_SPEC] + [VMEM_SPEC] * 4,
        out_specs=VMEM_SPEC,
        scratch_shapes=[
            scratch(SLOTS * FLAT, LANES),
            scratch(layer_cap * SIDE, WIDTH),
            scratch(SLOTS * SIDE, LANES),
            scratch(SLOTS * SIDE, LANES),
        ],
        compiler_params=params,
        name="ion_waves",
    )(layer_start, background, circle, into_y, table_z)
    ions = lax.all_to_all(ions, "domain", split_axis=0, concat_axis=0, tiled=True)
    ions, below = lax.optimization_barrier((ions, below))

    span = layer_cap + 2 * HALO
    fields = (2, span, TALL, WIDTH)
    psi, kept, sent = pl.pallas_call(
        functools.partial(propagate_kernel, count, length_cells),
        out_shape=(
            pltpu.HBM((2, layer_cap, SIDE, WIDTH), jnp.float32),
            f32(devices, SLOTS, width),
            f32(devices, SLOTS, width),
        ),
        in_specs=[SMEM_SPEC, SMEM_SPEC, VMEM_SPEC, VMEM_SPEC] + [HBM_SPEC] * 6 + [VMEM_SPEC] * 3,
        out_specs=(HBM_SPEC, VMEM_SPEC, VMEM_SPEC),
        scratch_shapes=[scratch(*fields)] * TERMS
        + [
            scratch(2, layer_cap, SIDE, WIDTH),
            scratch(span, SIDE, WIDTH),
            scratch(span, SIDE, WIDTH),
            scratch(SLOTS * FLAT, LANES),
            scratch(layer_cap * SIDE, WIDTH),
            scratch(SLOTS * SIDE, LANES),
            scratch(SLOTS * SIDE, LANES),
            scratch(SLOTS * FLAT, LANES),
            scratch(SLOTS * FLAT, LANES),
            scratch(SLOTS * FLAT, LANES),
            scratch(HALO - 1, packed, LANES),
            scratch(HALO - 1, packed, LANES),
            scratch(2 * HALO, packed * LANES),
            scratch(2 * HALO, packed * LANES),
            scratch(2 * FLAT, LANES),
            scratch(2 * FLAT, LANES),
            pltpu.SemaphoreType.DMA((6,)),
            pltpu.SemaphoreType.DMA,
        ],
        compiler_params=large,
        name="propagate",
    )(layer_start, occupation, layers, potential, below, above, below_far, above_far, v_rows, v_others,
      circle, into_y, table_z)
    waves = kept + swapped(sent, "core")
    waves, psi = lax.optimization_barrier((waves, psi))
    waves = lax.all_to_all(waves, ("row", "domain"), split_axis=0, concat_axis=0, tiled=True)
    orbitals_next, density_kept, density_sent = pl.pallas_call(
        unpack_kernel,
        out_shape=(
            f32(2, layer_cap, FLAT, LANES),
            f32(SLOTS // 2, FLAT, LANES),
            f32(SLOTS // 2, FLAT, LANES),
        ),
        in_specs=[SMEM_SPEC, VMEM_SPEC],
        out_specs=(VMEM_SPEC,) * 3,
        scratch_shapes=[scratch(SLOTS, FLAT, LANES)],
        compiler_params=params,
        name="unpack",
    )(occupation, psi)
    density = density_kept + swapped(density_sent, "core")
    waves, density = lax.optimization_barrier((waves, density))
    other_density = swapped(density, "row")
    waves = pl.pallas_call(
        functools.partial(coulomb_kernel, count, length_cells),
        out_shape=f32(devices, SLOTS, width),
        in_specs=[SMEM_SPEC] + [VMEM_SPEC] * 3,
        out_specs=VMEM_SPEC,
        compiler_params=params,
        name="coulomb",
    )(layer_start, waves, ions, table_x)
    waves = lax.all_to_all(waves, ("row", "domain"), split_axis=0, concat_axis=0, tiled=True)
    waves, other_density = lax.optimization_barrier((waves, other_density))
    density = density + other_density
    other_density = swapped(density, "core")
    other_waves = swapped(waves, "core")
    potential_next = pl.pallas_call(
        functools.partial(field_kernel, count, length_cells),
        out_shape=f32(layer_cap, plane),
        in_specs=[SMEM_SPEC] + [VMEM_SPEC] * 7,
        out_specs=VMEM_SPEC,
        scratch_shapes=[
            scratch(SLOTS * SIDE, LANES),
            scratch(SLOTS * SIDE, LANES),
            scratch(layer_cap * SIDE, WIDTH),
            scratch(SLOTS * FLAT, LANES),
        ],
        compiler_params=params,
        name="field",
    )(layer_start, waves, other_waves, density, other_density, flat_circle, out_of_y, table_z)
    return orbitals_next.reshape(orbitals.shape), potential_next


def solution(mesh):
    domains = mesh.shape["domain"]
    split = Mesh(mesh.devices.reshape(-1, 2, domains), ("row", "core", "domain"))
    states = ("row", "core")
    return jax.shard_map(
        shards,
        mesh=split,
        in_specs=(
            P(None, states, "domain", None),
            P(states),
            P("domain", None),
            P("domain", None),
            P(),
        ),
        out_specs=(P(None, states, "domain", None), P("domain", None)),
        check_vma=False,
    )
```

```python
import functools
import math

import jax
import jax.numpy as jnp
import ml_dtypes
import numpy as np
from jax import lax
from jax.experimental import pallas as pl
from jax.experimental.pallas import tpu as pltpu
from jax.sharding import Mesh, PartitionSpec as P

SIDE = 160
SLAB = 5
TERMS = 4

HALO = TERMS
LANES = 128
SLOTS = 8
RUN = SIDE // 8
FLAT = SIDE * SIDE // LANES
STRIDE = FLAT // 8
WIDTH = 2 * LANES
BLOCK = 32
TALL = SIDE + 16

time_step = 0.3
four_pi = 4.0 * math.pi
two_pi = 2.0 * math.pi
highest = lax.Precision.HIGHEST
MEBI = 1024 * 1024
SMEM_SPEC = pl.BlockSpec(memory_space=pltpu.SMEM)
VMEM_SPEC = pl.BlockSpec(memory_space=pltpu.VMEM)
HBM_SPEC = pl.BlockSpec(memory_space=pltpu.HBM)


def hartley_table(count_cells):
    index_run = np.arange(count_cells)
    angles = (index_run[:, None] * index_run[None, :] % count_cells) * (2.0 * np.pi / count_cells)
    return np.cos(angles) + np.sin(angles)


def plane_order():
    rows = np.arange(SIDE)
    return RUN * (rows % 8) + rows // 8


def two_parts(table):
    table = table.astype(np.float32)
    high = table.astype(ml_dtypes.bfloat16)
    low = (table - high.astype(np.float32)).astype(ml_dtypes.bfloat16)
    return high, low


def tables_of_side():
    table = hartley_table(SIDE)
    along_z = np.zeros((WIDTH, WIDTH))
    along_z[:SIDE, :SIDE] = table
    high, low = two_parts(along_z)
    along_z = np.concatenate([high, high, low], axis=0)
    high, low = two_parts(table[:, plane_order()])
    into_y = np.concatenate([high, high, low], axis=1)
    high, low = two_parts(table[plane_order(), :])
    half = SIDE // 2
    halves = [slice(0, half), slice(half, SIDE)]
    out_of_y = np.stack([np.concatenate([high[:, at], high[:, at], low[:, at]], axis=1) for at in halves])
    return along_z, into_y, out_of_y


def circle_table():
    across = 2 * np.arange(SIDE, dtype=np.int64) - (SIDE - 1)
    return (across[:, None] ** 2 + across[None, :] ** 2).astype(np.int32)


def circle_plane():
    table = np.full((SIDE, WIDTH), 4 * SIDE * SIDE, np.int32)
    table[:, :SIDE] = circle_table()[plane_order()]
    return table


def mesh_points(x_row, circle, length_cells):
    room = ((length_cells - 2) ** 2 - (2 * x_row - (length_cells - 1)) ** 2) * (SIDE - 2) ** 2
    return (circle * (length_cells - 2) ** 2 <= room) & (circle < 4 * SIDE * SIDE)


def column_pieces(first, count):
    pieces = []
    column = first
    while column < first + count:
        row = column // SIDE
        stop = min((row + 1) * SIDE, first + count)
        pieces.append((row, column - row * SIDE, stop - row * SIDE))
        column = stop
    return pieces


def tile_rows(first, count):
    return pl.ds(first if isinstance(first, int) else pl.multiple_of(first, 8), count)


def eight(values):
    missing = jnp.zeros((SLOTS - values.shape[0], values.shape[1]), values.dtype)
    return jnp.concatenate([values, missing], axis=0)


def in_turns(first, last, size, body):
    turns = (last - first) // size
    if turns > 1:

        @pl.loop(0, turns)
        def _(turn):
            for index in range(size):
                body(first + turn * size + index)

        first += turns * size
    for index in range(first, last):
        body(index)


def to_plane(load, store):
    lane = lax.broadcasted_iota(jnp.int32, (8, LANES), 1)
    for step in range(RUN // 4):
        rows = [load(5 * step + part) for part in range(5)]
        store(4 * step, rows[0], rows[1])
        for part in range(1, 4):
            left = pltpu.roll(rows[part], LANES - 32 * part, 1)
            right = pltpu.roll(rows[part + 1], LANES - 32 * part, 1)
            store(4 * step + part, jnp.where(lane < LANES - 32 * part, left, right), right)


def to_flat(load, store):
    lane = lax.broadcasted_iota(jnp.int32, (8, LANES), 1)
    for step in range(RUN // 4):
        turned = []
        for part in range(4):
            low, high = load(4 * step + part)
            if part:
                low = pltpu.roll(low, 32 * part, 1)
                high = pltpu.roll(high, 32 * part, 1)
            turned.append((low, high))
        store(5 * step, turned[0][0])
        for part in range(1, 4):
            ended = 32 * (part - 1)
            values = jnp.where(lane < ended + 32, turned[part - 1][1], turned[part][0])
            if ended:
                values = jnp.where(lane < ended, turned[part - 1][0], values)
            store(5 * step + part, values)
        store(5 * step + 4, jnp.where(lane < 96, turned[3][0], turned[3][1]))


def chords():
    across = 2 * np.arange(SIDE, dtype=np.int64) - (SIDE - 1)
    room = (SIDE - 2) ** 2 - across**2
    return [max([w for w in range(1, SIDE // 2 + 1) if (2 * w - 1) ** 2 <= left], default=0) for left in room]


def chord_moves():
    moves = []
    packed = 0
    for row, half in enumerate(chords()):
        if half:
            moves.append((row * SIDE + SIDE // 2 - half, packed, 2 * half))
            packed += 2 * half
    return moves


def packed_tiles():
    _, start, length = chord_moves()[-1]
    return -(-(start + length) // LANES)


def move_lanes(moves, load, store):
    lane = lax.broadcasted_iota(jnp.int32, (8, LANES), 1)
    pieces = {}
    for source, target, length in moves:
        while length:
            size = min(length, LANES - source % LANES, LANES - target % LANES)
            pieces.setdefault(target // LANES, []).append((target % LANES, source // LANES, (target - source) % LANES))
            source, target, length = source + size, target + size, length - size
    loaded = {}
    turned = {}
    for tile in sorted(pieces):
        values = None
        for first, origin, shift in sorted(pieces[tile]):
            if origin not in loaded:
                loaded[origin] = load(origin)
            if (origin, shift) not in turned:
                turned[origin, shift] = pltpu.roll(loaded[origin], shift, 1) if shift else loaded[origin]
            piece = turned[origin, shift]
            values = piece if values is None else jnp.where(lane >= first, piece, values)
        store(tile, values)


def pack_chords(rows_ref, store):
    move_lanes(chord_moves(), lambda tile: rows_ref[pl.ds(tile, 8, stride=FLAT), :], store)


def unpack_chords(load, rows_ref):
    def store(tile, values):
        rows_ref[pl.ds(tile, 8, stride=FLAT), :] = values

    move_lanes([(target, source, length) for source, target, length in chord_moves()], load, store)


def parts_of(values):
    high = values.astype(jnp.bfloat16)
    low = (values - high.astype(jnp.float32)).astype(jnp.bfloat16)
    return high, low


def turn_z(values, table):
    high, low = parts_of(values)
    return jnp.dot(
        jnp.concatenate([high, low, high], axis=1), table, preferred_element_type=jnp.float32
    )


def turn_y(table, values):
    high, low = parts_of(values)
    return jnp.dot(
        table, jnp.concatenate([high, low, high], axis=0), preferred_element_type=jnp.float32
    )


def send_columns(planes_ref, slots, table_y, table_z, low_ref, high_ref):
    along_z = turn_z(planes_ref[:slots * SIDE, :], table_z)
    for slot in range(slots):
        rows = slice(slot * SIDE, (slot + 1) * SIDE)
        waves = turn_y(table_y, along_z[rows])
        low_ref[rows, :] = waves[:, :LANES]
        high_ref[rows, :] = waves[:, LANES:]
    low_ref[slots * SIDE:, :] = jnp.zeros(((SLOTS - slots) * SIDE, LANES), jnp.float32)
    high_ref[slots * SIDE:, :] = jnp.zeros(((SLOTS - slots) * SIDE, LANES), jnp.float32)


def chunk_of(low_ref, high_ref, first_row, pieces, extra):
    parts = []
    for row, start, stop in pieces:
        at = pl.ds(first_row + row, SLOTS, stride=SIDE)
        values = jnp.concatenate([low_ref[at, :], high_ref[at, :]], axis=1)
        parts.append(values[:, start:stop])
    return jnp.concatenate(parts + [extra], axis=1)


def layers_of(stored_ref, flat_ref):
    @pl.loop(0, FLAT // 8)
    def _(step):
        for part in range(8):
            lanes = pl.ds(pl.multiple_of((step * 8 + part) * LANES, LANES), LANES)
            flat_ref[pl.ds(step * 8 + part, SLOTS, stride=FLAT), :] = eight(stored_ref[:, lanes])


def place_of(start_ref):
    position = lax.axis_index("domain")
    return position, start_ref[position], start_ref[position + 1] - start_ref[position]


def started(sems, pairs):
    copies = [pltpu.make_async_copy(*pair, sems.at[index]) for index, pair in enumerate(pairs)]
    for made in copies:
        made.start()
    return copies


def layers_at(orbitals_ref, part, start, count):
    return orbitals_ref.at[part, pl.ds(pl.multiple_of(start * FLAT, 8), count * FLAT)]


def rows_at(ref, part, count):
    return ref.at[pl.ds(part * count * FLAT, count * FLAT)]


def pack_kernel(start_ref, orbitals_ref, up_ref, down_ref, up_rows_ref, down_rows_ref, up_buffer_ref,
                down_buffer_ref, in_sems, out_sems):
    _, _, thickness = place_of(start_ref)
    first = jnp.maximum(thickness - HALO, 0)
    arrivals = started(
        in_sems,
        [
            (layers_at(orbitals_ref, part, start, HALO), rows_at(rows_ref, part, HALO))
            for start, rows_ref in ((first, up_rows_ref), (0, down_rows_ref))
            for part in range(2)
        ],
    )
    departures = []
    for index, (rows_ref, buffer_ref, out_ref) in enumerate(
        ((up_rows_ref, up_buffer_ref, up_ref), (down_rows_ref, down_buffer_ref, down_ref))
    ):
        arrivals[2 * index].wait()
        arrivals[2 * index + 1].wait()

        def store(tile, values, buffer_ref=buffer_ref):
            buffer_ref[:, tile * LANES:(tile + 1) * LANES] = values

        pack_chords(rows_ref, store)
        departures.append(pltpu.make_async_copy(buffer_ref, out_ref, out_sems.at[index]))
        departures[-1].start()
    for made in departures:
        made.wait()


def pack_rest_kernel(start_ref, potential_ref, orbitals_ref, v_ref, up_far_ref, down_far_ref, flat_ref,
                     v_rows_ref, stored_ref, in_sems):
    _, _, thickness = place_of(start_ref)
    v_first = jnp.where(lax.axis_index("core") == 0, thickness - (HALO - 1), 0)
    arrivals = started(
        in_sems,
        [(potential_ref, stored_ref)]
        + [
            (layers_at(orbitals_ref, part, start, 1), rows_at(far_ref, part, 1))
            for start, far_ref in ((thickness - 1, up_far_ref), (0, down_far_ref))
            for part in range(2)
        ],
    )
    arrivals[0].wait()
    layers_of(stored_ref, flat_ref)
    for layer in range(HALO - 1):
        v_rows_ref[layer * FLAT:(layer + 1) * FLAT, :] = flat_ref[
            pl.ds(pl.multiple_of((v_first + layer) * FLAT, 8), FLAT), :
        ]

    def store_v(tile, values):
        for layer in range(HALO - 1):
            v_ref[layer, tile:tile + 1, :] = values[layer:layer + 1]

    pack_chords(v_rows_ref, store_v)
    for made in arrivals[1:]:
        made.wait()


def ions_kernel(count, length_cells, start_ref, background_ref, circle_ref, table_y_ref, table_z_ref,
                out_ref, flat_ref, planes_ref, low_ref, high_ref):
    _, own_start, thickness = place_of(start_ref)
    slots = background_ref.shape[0]
    groups, _, width = out_ref.shape
    layers_of(background_ref, flat_ref)

    def body(slot, total):
        def store(tile, low, high):
            rows = pl.ds(pl.multiple_of(slot * SIDE + tile * 8, 8), 8)
            planes_ref[rows, :LANES] = low
            planes_ref[rows, LANES:] = high

        to_plane(lambda k: flat_ref[pl.ds(slot * FLAT + k, 8, stride=STRIDE), :], store)
        rows = pl.ds(pl.multiple_of(slot * SIDE, 8), SIDE)
        inside = mesh_points(own_start + slot, circle_ref[...], length_cells) & (slot < thickness)
        values = jnp.where(inside, planes_ref[rows, :], 0.0)
        planes_ref[rows, :] = values
        return total + jnp.sum(values.reshape(RUN, 8, WIDTH), axis=0)

    total = lax.fori_loop(0, slots, body, jnp.zeros((8, WIDTH), jnp.float32))
    whole = jnp.broadcast_to(jnp.sum(total, keepdims=True), (SLOTS, LANES))[:, :width - count]
    send_columns(planes_ref, slots, table_y_ref[...], table_z_ref[...], low_ref, high_ref)
    core_rows = SIDE // lax.axis_size("core")
    first_row = lax.axis_index("core") * core_rows + lax.axis_index("row") * (core_rows // lax.axis_size("row"))
    for group in range(groups):
        out_ref[group] = chunk_of(low_ref, high_ref, first_row, column_pieces(group * count, count), whole)


def propagate_kernel(count, length_cells, start_ref, weight_ref, orbitals_ref, potential_ref, below_hbm_ref,
                     above_hbm_ref, below_far_hbm_ref, above_far_hbm_ref, v_hbm_ref, v_other_hbm_ref,
                     circle_ref, table_y_ref, table_z_ref, psi_ref, kept_ref, sent_ref, first_ref, second_ref,
                     third_ref, fourth_ref, sum_ref, centre_ref, beside_ref, flat_ref, planes_ref, low_ref,
                     high_ref, below_rows_ref, above_rows_ref, v_rows_ref, v_ref, v_other_ref, below_ref,
                     above_ref, below_far_ref, above_far_ref, in_sems, out_sem):
    arrivals = started(
        in_sems,
        [
            (v_hbm_ref, v_ref),
            (v_other_hbm_ref, v_other_ref),
            (below_hbm_ref, below_ref),
            (above_hbm_ref, above_ref),
            (below_far_hbm_ref, below_far_ref),
            (above_far_hbm_ref, above_far_ref),
        ],
    )
    position, own_start, thickness = place_of(start_ref)
    domains = lax.axis_size("domain")
    before = start_ref[jnp.maximum(position - 1, 0)]
    after = start_ref[jnp.minimum(position + 2, domains)]
    short_below = ((position > 0) & (own_start - before < HALO)).astype(jnp.int32)
    short_above = (position < domains - 1) & (after - own_start - thickness < HALO)
    weight = weight_ref[0]
    core = lax.axis_index("core")
    slots = orbitals_ref.shape[1]
    layers = slots + 2 * HALO
    devices, _, width = kept_ref.shape
    field_refs = (first_ref, second_ref, third_ref, fourth_ref)

    def field_layer(part, x_row):
        def store(tile, low, high):
            first_ref[part, x_row, 8 + 8 * tile:16 + 8 * tile, :LANES] = low
            first_ref[part, x_row, 8 + 8 * tile:16 + 8 * tile, LANES:] = high

        return store

    def potential_layer(x_row):
        def store(tile, low, high):
            centre_ref[x_row, 8 * tile:8 * tile + 8, :LANES] = low
            centre_ref[x_row, 8 * tile:8 * tile + 8, LANES:] = high

        return store

    def rows_from(ref, *at):
        return lambda k: ref[(*at, pl.ds(k, 8, stride=STRIDE), slice(None))]

    def layer_of(rows_ref, layer):
        return lambda k: rows_ref[pl.ds(layer * FLAT + k, 8, stride=STRIDE), :]

    layers_of(potential_ref, flat_ref)

    for slot in range(slots):
        for part in range(2):
            to_plane(rows_from(orbitals_ref, part, slot), field_layer(part, HALO + slot))
        to_plane(layer_of(flat_ref, slot), potential_layer(HALO + slot))

    for made in arrivals:
        made.wait()
    for packed_ref, rows_ref in ((below_ref, below_rows_ref), (above_ref, above_rows_ref)):
        unpack_chords(
            lambda tile, packed_ref=packed_ref: packed_ref[:, tile * LANES:(tile + 1) * LANES], rows_ref
        )
    unpack_chords(
        lambda tile: eight(
            jnp.concatenate([ref[:, tile, :] for ref in (v_ref, v_other_ref)], axis=0)
        ),
        v_rows_ref,
    )

    for layer in range(HALO - 1):
        lower = 1 + layer
        upper = HALO + thickness + layer
        to_plane(layer_of(v_rows_ref, layer), potential_layer(jnp.where(core == 0, lower, upper)))
        to_plane(layer_of(v_rows_ref, HALO - 1 + layer), potential_layer(jnp.where(core == 0, upper, lower)))
        for part in range(2):
            to_plane(
                layer_of(below_rows_ref, part * HALO + 1 + layer - short_below), field_layer(part, 1 + layer)
            )
            to_plane(
                layer_of(above_rows_ref, part * HALO + layer), field_layer(part, HALO + thickness + layer)
            )

    @pl.loop(0, 2)
    def _(part):
        last = 2 * HALO - 1 + thickness

        @pl.when(short_below > 0)
        def _():
            to_plane(layer_of(below_far_ref, part), field_layer(part, 0))

        @pl.when(short_below == 0)
        def _():
            to_plane(layer_of(below_rows_ref, part * HALO), field_layer(part, 0))

        @pl.when(short_above)
        def _():
            to_plane(layer_of(above_far_ref, part), field_layer(part, last))

        @pl.when(jnp.logical_not(short_above))
        def _():
            to_plane(layer_of(above_rows_ref, part * HALO + HALO - 1), field_layer(part, last))

    def wrap(field_ref, part, x_row, first, final):
        field_ref[part, x_row, :8, :] = pltpu.roll(final, 1, 0)
        field_ref[part, x_row, SIDE + 8:, :] = pltpu.roll(first, 7, 0)

    blocks = SIDE // BLOCK

    def confine(x_row):
        known = x_row < thickness + 2 * HALO
        ends = {}
        for block in range(blocks):
            rows = slice(block * BLOCK, (block + 1) * BLOCK)
            inner = slice(8 + block * BLOCK, 8 + (block + 1) * BLOCK)
            inside = mesh_points(own_start - HALO + x_row, circle_ref[rows, :], length_cells) & known
            centre_ref[x_row, rows, :] = jnp.where(
                inside, (3.0 + centre_ref[x_row, rows, :]) * time_step, 0.0
            )
            beside_ref[x_row, rows, :] = jnp.where(inside, 0.5 * time_step, 0.0)
            for part in range(2):
                field = jnp.where(inside, first_ref[part, x_row, inner, :], 0.0)
                first_ref[part, x_row, inner, :] = field
                ends[part, block] = field
        for part in range(2):
            wrap(first_ref, part, x_row, ends[part, 0][:8], ends[part, blocks - 1][BLOCK - 8:])

    in_turns(0, layers, 5, confine)

    def hamilton(term, part, x_row, block, centre, beside):
        field_ref = field_refs[term]
        tall = field_ref[part, x_row, block * BLOCK:block * BLOCK + BLOCK + 16, :]
        inner = slice(8 + block * BLOCK, 8 + (block + 1) * BLOCK)
        field = tall[8:8 + BLOCK]
        around = field_ref[part, x_row - 1, inner, :] + field_ref[part, x_row + 1, inner, :]
        around = around + (tall[:BLOCK] + tall[16:])
        around = around + (pltpu.roll(field, 1, 1) + pltpu.roll(field, WIDTH - 1, 1))
        return centre * field - beside * around

    for term in range(1, TERMS):

        def step(x_row, term=term):
            ends = {}
            for block in range(blocks):
                rows = slice(block * BLOCK, (block + 1) * BLOCK)
                inner = slice(8 + block * BLOCK, 8 + (block + 1) * BLOCK)
                centre = centre_ref[x_row, rows, :]
                beside = beside_ref[x_row, rows, :]
                for part in range(2):
                    field = hamilton(term - 1, part, x_row, block, centre, beside)
                    field_refs[term][part, x_row, inner, :] = field
                    ends[part, block] = field
            for part in range(2):
                wrap(field_refs[term], part, x_row, ends[part, 0][:8], ends[part, blocks - 1][BLOCK - 8:])

        in_turns(term, layers - term, 4, step)

    def finish(slot, total):
        x_row = HALO + slot
        owned = slot < thickness
        for block in range(SIDE // BLOCK):
            rows = slice(block * BLOCK, (block + 1) * BLOCK)
            inner = slice(8 + block * BLOCK, 8 + (block + 1) * BLOCK)
            centre = centre_ref[x_row, rows, :]
            beside = beside_ref[x_row, rows, :]
            density = jnp.zeros((BLOCK, WIDTH), jnp.float32)
            for part, sign in ((0, 1.0), (1, -1.0)):
                summed = first_ref[part, x_row, inner, :]
                summed = summed + sign * second_ref[1 - part, x_row, inner, :]
                summed = summed - (1.0 / 2.0) * third_ref[part, x_row, inner, :]
                summed = summed - (sign / 6.0) * fourth_ref[1 - part, x_row, inner, :]
                summed = summed + (1.0 / 24.0) * hamilton(3, part, x_row, block, centre, beside)
                summed = jnp.where(owned, summed, 0.0)
                sum_ref[part, slot, rows, :] = summed
                density = density + summed * summed
            density = weight * density
            planes_ref[tile_rows(slot * SIDE + block * BLOCK, BLOCK), :] = density
            total = total + jnp.sum(density.reshape(BLOCK // 8, 8, WIDTH), axis=0)

        return total

    total = lax.fori_loop(
        0, slots // 2, lambda pair, total: finish(2 * pair + 1, finish(2 * pair, total)), jnp.zeros((8, WIDTH), jnp.float32)
    )
    for slot in range(slots // 2 * 2, slots):
        total = finish(slot, total)
    departure = pltpu.make_async_copy(sum_ref, psi_ref, out_sem)
    departure.start()
    whole = jnp.broadcast_to(jnp.sum(total, keepdims=True), (SLOTS, LANES))[:, :width - count]
    send_columns(planes_ref, slots, table_y_ref[...], table_z_ref[...], low_ref, high_ref)
    core_rows = SIDE // 2
    first_row = core * core_rows
    for device in range(devices):
        pieces = column_pieces(device * count, count)
        kept_ref[device] = chunk_of(low_ref, high_ref, first_row, pieces, whole)
        sent_ref[device] = chunk_of(low_ref, high_ref, core_rows - first_row, pieces, whole)
    departure.wait()


def unpack_kernel(weight_ref, psi_ref, next_ref, density_kept_ref, density_sent_ref, density_ref):
    core = lax.axis_index("core")
    weight = weight_ref[0]
    slots = psi_ref.shape[1]

    def unpack(slot):
        for part in range(2):

            def load(tile, part=part):
                tall = psi_ref[part, slot, 8 * tile:8 * tile + 8, :]
                return tall[:, :LANES], tall[:, LANES:]

            def store(k, values, part=part):
                next_ref[part, slot, pl.ds(k, 8, stride=STRIDE), :] = values

            to_flat(load, store)
        real = next_ref[0, slot]
        imag = next_ref[1, slot]
        density_ref[slot] = weight * (real * real + imag * imag)

    in_turns(0, slots, 2, unpack)
    for slot in range(slots, SLOTS):
        density_ref[slot] = jnp.zeros((FLAT, LANES), jnp.float32)

    @pl.loop(0, SLOTS // 2)
    def _(slot):
        density_kept_ref[slot] = density_ref[core * (SLOTS // 2) + slot]
        density_sent_ref[slot] = density_ref[(1 - core) * (SLOTS // 2) + slot]


def wave_squared(index, count_cells):
    folded = jnp.where(2 * index <= count_cells, index, index - count_cells)
    wave_number = folded.astype(jnp.float32) * (two_pi / count_cells)
    return wave_number * wave_number


def coulomb_kernel(count, length_cells, start_ref, charge_ref, ions_ref, table_ref, out_ref):
    domains, _, width = ions_ref.shape
    states = charge_ref.shape[0] // domains
    device = (lax.axis_index("core") * states + lax.axis_index("row")) * domains + lax.axis_index("domain")
    charge = charge_ref[:domains]
    for state in range(1, states):
        charge = charge + charge_ref[state * domains:(state + 1) * domains]
    charge = charge.reshape(domains * SLOTS, width)
    ions = ions_ref[...].reshape(domains * SLOTS, width)
    first = lax.broadcasted_iota(jnp.int32, (domains * SLOTS, width), 0) % SLOTS == 0
    lane = lax.broadcasted_iota(jnp.int32, (domains * SLOTS, width), 1)
    chosen = first & (lane == count)
    electrons = jnp.sum(jnp.where(chosen, charge, 0.0), keepdims=True)
    ionic = jnp.sum(jnp.where(chosen, ions, 0.0), keepdims=True)
    charge = charge - (electrons / ionic) * ions
    layer = lax.broadcasted_iota(jnp.int32, (length_cells, domains * SLOTS), 0)
    place = lax.broadcasted_iota(jnp.int32, (length_cells, domains * SLOTS), 1)
    chosen_layer = jnp.full(layer.shape, -1, jnp.int32)
    for domain in range(domains):
        slot = place - domain * SLOTS
        here = (slot >= 0) & (slot < start_ref[domain + 1] - start_ref[domain])
        chosen_layer = jnp.where(here, start_ref[domain] + slot, chosen_layer)
    pick = (layer == chosen_layer).astype(jnp.float32)
    table = jnp.dot(table_ref[...], pick, precision=highest, preferred_element_type=jnp.float32)
    waves = jnp.dot(table, charge, precision=highest, preferred_element_type=jnp.float32)
    wave_x = lax.broadcasted_iota(jnp.int32, waves.shape, 0)
    column = device * count + lax.broadcasted_iota(jnp.int32, waves.shape, 1)
    wave_y = ((column.astype(jnp.float32) + 0.5) * (1.0 / SIDE)).astype(jnp.int32)
    wave_z = column - wave_y * SIDE
    squared = (
        wave_squared(wave_x, length_cells) + wave_squared(wave_y, SIDE) + wave_squared(wave_z, SIDE)
    )
    gain = jnp.where(squared > 0, four_pi / jnp.where(squared > 0, squared, 1.0), 0.0)
    waves = waves * (gain * (1.0 / (length_cells * SIDE * SIDE)))
    back = lax.dot_general(
        table, waves, (((0,), (0,)), ((), ())), precision=highest, preferred_element_type=jnp.float32
    )
    back = back.reshape(domains, SLOTS, width)
    for state in range(states):
        out_ref[state * domains:(state + 1) * domains] = back


def half_planes(count, source_ref, table_y, table_z, low_ref, high_ref, slots):
    half = SIDE // 2
    pieces = []
    for device in range(source_ref.shape[0]):
        column = 0
        for row, start, stop in column_pieces(device * count, count):
            values = source_ref[device, :, column:column + stop - start]
            column += stop - start
            if start > 0:
                pieces.append(values)
                values = jnp.concatenate(pieces, axis=1)
            if stop < SIDE:
                pieces = [values]
                continue
            pieces = []
            at = pl.ds(row, SLOTS, stride=half)
            low_ref[at, :] = values[:, :LANES]
            high_ref[at, :] = jnp.concatenate(
                [values[:, LANES:], jnp.zeros((SLOTS, WIDTH - SIDE), jnp.float32)], axis=1
            )
    used = slice(0, slots * half)
    along_z = turn_z(jnp.concatenate([low_ref[used, :], high_ref[used, :]], axis=1), table_z)
    return [turn_y(table_y, along_z[slot * half:(slot + 1) * half]) for slot in range(slots)]


def half_kernel(count, waves_ref, table_y_ref, table_z_ref, out_ref, low_ref, high_ref):
    table_y = table_y_ref[lax.axis_index("core")]
    slots = out_ref.shape[0] // SIDE
    planes = half_planes(count, waves_ref, table_y, table_z_ref[...], low_ref, high_ref, slots)
    for slot, plane in enumerate(planes):
        out_ref[slot * SIDE:(slot + 1) * SIDE, :] = plane


def field_kernel(count, length_cells, start_ref, others_ref, half_ref, density_ref, other_ref, circle_ref,
                 table_y_ref, table_z_ref, out_ref, low_ref, high_ref, planes_ref, flat_ref):
    _, own_start, thickness = place_of(start_ref)
    slots = out_ref.shape[0]
    core = lax.axis_index("core")
    planes = half_planes(count, others_ref, table_y_ref[1 - core], table_z_ref[...], low_ref, high_ref, slots)
    for slot, plane in enumerate(planes):
        rows = slice(slot * SIDE, (slot + 1) * SIDE)
        planes_ref[rows, :] = half_ref[rows, :] + plane

    def field(slot):
        def load(tile):
            tall = planes_ref[tile_rows(slot * SIDE + tile * 8, 8), :]
            return tall[:, :LANES], tall[:, LANES:]

        def store(k, values):
            flat_ref[pl.ds(slot * FLAT + k, 8, stride=STRIDE), :] = values

        to_flat(load, store)
        rows = tile_rows(slot * FLAT, FLAT)
        here = slot // (SLOTS // 2) == core
        kept_slot = slot % (SLOTS // 2)
        content = jnp.where(here, density_ref[kept_slot], other_ref[kept_slot]) * (3.0 / math.pi)
        positive = jnp.where(content > 0, content, 1.0)
        root = jnp.exp(jnp.log(positive) * (1.0 / 3.0))
        root = root - (root - positive / (root * root)) * (1.0 / 3.0)
        root = jnp.where(content > 0, root, 0.0)
        inside = mesh_points(own_start + slot, circle_ref[...], length_cells) & (slot < thickness)
        flat_ref[rows, :] = jnp.where(inside, flat_ref[rows, :] - root, 0.0)

    in_turns(0, slots, 4, field)

    @pl.loop(0, FLAT // 8)
    def _(step):
        for part in range(8):
            lanes = pl.ds(pl.multiple_of((step * 8 + part) * LANES, LANES), LANES)
            out_ref[:, lanes] = flat_ref[pl.ds(step * 8 + part, SLOTS, stride=FLAT), :][:slots]


def from_behind(value, steps):
    count = lax.axis_size("domain")
    leading, last = (max(0, -steps), min(count, count - steps))
    return lax.ppermute(value, "domain", [(source, source + steps) for source in range(leading, last)])


def swapped(value, axis):
    return lax.ppermute(value, axis, [(0, 1), (1, 0)])


def shards(orbitals, occupation, potential, background, layer_start):
    domains = lax.axis_size("domain")
    rows = lax.axis_size("row")
    devices = domains * rows
    length_cells = SLAB * domains
    layer_cap, plane = potential.shape
    count = plane // (2 * devices)
    width = -(-(count + 1) // LANES) * LANES
    circle = jnp.asarray(circle_plane())
    flat_circle = jnp.asarray(circle_table().reshape(FLAT, LANES))
    table_z, into_y, out_of_y = (jnp.asarray(table) for table in tables_of_side())
    table_x = jnp.asarray(hartley_table(length_cells).astype(np.float32))
    params = pltpu.CompilerParams(vmem_limit_bytes=16 * MEBI)
    large = pltpu.CompilerParams(vmem_limit_bytes=44 * MEBI)
    whole = pltpu.CompilerParams(vmem_limit_bytes=56 * MEBI)

    def f32(*shape):
        return jax.ShapeDtypeStruct(shape, jnp.float32)

    def scratch(*shape):
        return pltpu.VMEM(shape, jnp.float32)

    layers = orbitals.reshape(2, layer_cap, FLAT, LANES)
    packed = packed_tiles()
    outer = orbitals.reshape(2, layer_cap * FLAT, LANES)
    up, down = pl.pallas_call(
        pack_kernel,
        out_shape=(f32(2 * HALO, packed * LANES), f32(2 * HALO, packed * LANES)),
        in_specs=[SMEM_SPEC, HBM_SPEC],
        out_specs=(HBM_SPEC, HBM_SPEC),
        scratch_shapes=[
            scratch(2 * HALO * FLAT, LANES),
            scratch(2 * HALO * FLAT, LANES),
            scratch(2 * HALO, packed * LANES),
            scratch(2 * HALO, packed * LANES),
            pltpu.SemaphoreType.DMA((4,)),
            pltpu.SemaphoreType.DMA((2,)),
        ],
        compiler_params=whole,
        name="pack_halo",
    )(layer_start, outer)
    up, down, potential_rest, outer = lax.optimization_barrier((up, down, potential, outer))
    v_rows, up_far, down_far = pl.pallas_call(
        pack_rest_kernel,
        out_shape=(f32(HALO - 1, packed, LANES), f32(2 * FLAT, LANES), f32(2 * FLAT, LANES)),
        in_specs=[SMEM_SPEC, HBM_SPEC, HBM_SPEC],
        out_specs=(VMEM_SPEC,) * 3,
        scratch_shapes=[
            scratch(SLOTS * FLAT, LANES),
            scratch(SLOTS * FLAT, LANES),
            scratch(layer_cap, plane),
            pltpu.SemaphoreType.DMA((5,)),
        ],
        compiler_params=whole,
        cost_estimate=pl.CostEstimate(flops=0, transcendentals=0, bytes_accessed=30_000_000),
        name="pack_rest",
    )(layer_start, potential_rest, outer)
    v_rows = lax.ppermute(
        v_rows,
        ("core", "domain"),
        [(source, source + 1) for source in range(domains - 1)]
        + [(domains + source + 1, domains + source) for source in range(domains - 1)],
    )
    below = from_behind(up, 1)
    above = from_behind(down, -1)
    below_far = from_behind(up_far, 2)
    above_far = from_behind(down_far, -2)
    v_rows, below_far, above_far = lax.optimization_barrier((v_rows, below_far, above_far))
    v_others = swapped(v_rows, "core")

    ions = pl.pallas_call(
        functools.partial(ions_kernel, count, length_cells),
        out_shape=f32(domains, SLOTS, width),
        in_specs=[SMEM_SPEC] + [VMEM_SPEC] * 4,
        out_specs=VMEM_SPEC,
        scratch_shapes=[
            scratch(SLOTS * FLAT, LANES),
            scratch(layer_cap * SIDE, WIDTH),
            scratch(SLOTS * SIDE, LANES),
            scratch(SLOTS * SIDE, LANES),
        ],
        compiler_params=params,
        name="ion_waves",
    )(layer_start, background, circle, into_y, table_z)
    ions = lax.all_to_all(ions, "domain", split_axis=0, concat_axis=0, tiled=True)
    ions, below = lax.optimization_barrier((ions, below))

    span = layer_cap + 2 * HALO
    fields = (2, span, TALL, WIDTH)
    psi, kept, sent = pl.pallas_call(
        functools.partial(propagate_kernel, count, length_cells),
        out_shape=(
            pltpu.HBM((2, layer_cap, SIDE, WIDTH), jnp.float32),
            f32(devices, SLOTS, width),
            f32(devices, SLOTS, width),
        ),
        in_specs=[SMEM_SPEC, SMEM_SPEC, VMEM_SPEC, VMEM_SPEC] + [HBM_SPEC] * 6 + [VMEM_SPEC] * 3,
        out_specs=(HBM_SPEC, VMEM_SPEC, VMEM_SPEC),
        scratch_shapes=[scratch(*fields)] * TERMS
        + [
            scratch(2, layer_cap, SIDE, WIDTH),
            scratch(span, SIDE, WIDTH),
            scratch(span, SIDE, WIDTH),
            scratch(SLOTS * FLAT, LANES),
            scratch(layer_cap * SIDE, WIDTH),
            scratch(SLOTS * SIDE, LANES),
            scratch(SLOTS * SIDE, LANES),
            scratch(SLOTS * FLAT, LANES),
            scratch(SLOTS * FLAT, LANES),
            scratch(SLOTS * FLAT, LANES),
            scratch(HALO - 1, packed, LANES),
            scratch(HALO - 1, packed, LANES),
            scratch(2 * HALO, packed * LANES),
            scratch(2 * HALO, packed * LANES),
            scratch(2 * FLAT, LANES),
            scratch(2 * FLAT, LANES),
            pltpu.SemaphoreType.DMA((6,)),
            pltpu.SemaphoreType.DMA,
        ],
        compiler_params=large,
        name="propagate",
    )(layer_start, occupation, layers, potential, below, above, below_far, above_far, v_rows, v_others,
      circle, into_y, table_z)
    waves = kept + swapped(sent, "core")
    waves, psi = lax.optimization_barrier((waves, psi))
    waves = lax.all_to_all(waves, ("row", "domain"), split_axis=0, concat_axis=0, tiled=True)
    orbitals_next, density_kept, density_sent = pl.pallas_call(
        unpack_kernel,
        out_shape=(
            f32(2, layer_cap, FLAT, LANES),
            f32(SLOTS // 2, FLAT, LANES),
            f32(SLOTS // 2, FLAT, LANES),
        ),
        in_specs=[SMEM_SPEC, VMEM_SPEC],
        out_specs=(VMEM_SPEC,) * 3,
        scratch_shapes=[scratch(SLOTS, FLAT, LANES)],
        compiler_params=params,
        name="unpack",
    )(occupation, psi)
    density = density_kept + swapped(density_sent, "core")
    waves, density = lax.optimization_barrier((waves, density))
    other_density = swapped(density, "row")
    waves = pl.pallas_call(
        functools.partial(coulomb_kernel, count, length_cells),
        out_shape=f32(devices, SLOTS, width),
        in_specs=[SMEM_SPEC] + [VMEM_SPEC] * 3,
        out_specs=VMEM_SPEC,
        compiler_params=params,
        name="coulomb",
    )(layer_start, waves, ions, table_x)
    waves = lax.all_to_all(waves, ("row", "domain"), split_axis=0, concat_axis=0, tiled=True)
    waves, other_density = lax.optimization_barrier((waves, other_density))
    density = density + other_density
    other_density = swapped(density, "core")
    other_waves = swapped(waves, "core")
    half = [scratch(SLOTS * SIDE // 2, LANES), scratch(SLOTS * SIDE // 2, LANES)]
    planes = pl.pallas_call(
        functools.partial(half_kernel, count),
        out_shape=f32(layer_cap * SIDE, WIDTH),
        in_specs=[VMEM_SPEC] * 3,
        out_specs=VMEM_SPEC,
        scratch_shapes=half,
        compiler_params=params,
        name="half_field",
    )(waves, out_of_y, table_z)
    potential_next = pl.pallas_call(
        functools.partial(field_kernel, count, length_cells),
        out_shape=f32(layer_cap, plane),
        in_specs=[SMEM_SPEC] + [VMEM_SPEC] * 7,
        out_specs=VMEM_SPEC,
        scratch_shapes=half + [scratch(layer_cap * SIDE, WIDTH), scratch(SLOTS * FLAT, LANES)],
        compiler_params=params,
        name="field",
    )(layer_start, other_waves, planes, density, other_density, flat_circle, out_of_y, table_z)
    return orbitals_next.reshape(orbitals.shape), potential_next


def solution(mesh):
    domains = mesh.shape["domain"]
    split = Mesh(mesh.devices.reshape(-1, 2, domains), ("row", "core", "domain"))
    states = ("row", "core")
    return jax.shard_map(
        shards,
        mesh=split,
        in_specs=(
            P(None, states, "domain", None),
            P(states),
            P("domain", None),
            P("domain", None),
            P(),
        ),
        out_specs=(P(None, states, "domain", None), P("domain", None)),
        check_vma=False,
    )
```

```python
import functools
import math

import jax
import jax.numpy as jnp
import ml_dtypes
import numpy as np
from jax import lax
from jax.experimental import pallas as pl
from jax.experimental.pallas import tpu as pltpu
from jax.sharding import Mesh, PartitionSpec as P

SIDE = 160
SLAB = 5
TERMS = 4

HALO = TERMS
LANES = 128
SLOTS = 8
RUN = SIDE // 8
FLAT = SIDE * SIDE // LANES
STRIDE = FLAT // 8
WIDTH = 2 * LANES
BLOCK = 32
TALL = SIDE + 16

time_step = 0.3
four_pi = 4.0 * math.pi
two_pi = 2.0 * math.pi
highest = lax.Precision.HIGHEST
MEBI = 1024 * 1024
SMEM_SPEC = pl.BlockSpec(memory_space=pltpu.SMEM)
VMEM_SPEC = pl.BlockSpec(memory_space=pltpu.VMEM)
HBM_SPEC = pl.BlockSpec(memory_space=pltpu.HBM)


def hartley_table(count_cells):
    index_run = np.arange(count_cells)
    angles = (index_run[:, None] * index_run[None, :] % count_cells) * (2.0 * np.pi / count_cells)
    return np.cos(angles) + np.sin(angles)


def plane_order():
    rows = np.arange(SIDE)
    return RUN * (rows % 8) + rows // 8


def two_parts(table):
    table = table.astype(np.float32)
    high = table.astype(ml_dtypes.bfloat16)
    low = (table - high.astype(np.float32)).astype(ml_dtypes.bfloat16)
    return high, low


def tables_of_side():
    table = hartley_table(SIDE)
    along_z = np.zeros((WIDTH, WIDTH))
    along_z[:SIDE, :SIDE] = table
    high, low = two_parts(along_z)
    along_z = np.concatenate([high, high, low], axis=0)
    high, low = two_parts(table[:, plane_order()])
    into_y = np.concatenate([high, high, low], axis=1).reshape(2, SIDE // 2, 3 * SIDE)
    high, low = two_parts(table[plane_order(), :])
    half = SIDE // 2
    halves = [slice(0, half), slice(half, SIDE)]
    out_of_y = np.stack([np.concatenate([high[:, at], high[:, at], low[:, at]], axis=1) for at in halves])
    return along_z, into_y, out_of_y


def circle_table():
    across = 2 * np.arange(SIDE, dtype=np.int64) - (SIDE - 1)
    return (across[:, None] ** 2 + across[None, :] ** 2).astype(np.int32)


def circle_plane():
    table = np.full((SIDE, WIDTH), 4 * SIDE * SIDE, np.int32)
    table[:, :SIDE] = circle_table()[plane_order()]
    return table


def mesh_points(x_row, circle, length_cells):
    room = ((length_cells - 2) ** 2 - (2 * x_row - (length_cells - 1)) ** 2) * (SIDE - 2) ** 2
    return (circle * (length_cells - 2) ** 2 <= room) & (circle < 4 * SIDE * SIDE)


def column_pieces(first, count):
    pieces = []
    column = first
    while column < first + count:
        row = column // SIDE
        stop = min((row + 1) * SIDE, first + count)
        pieces.append((row, column - row * SIDE, stop - row * SIDE))
        column = stop
    return pieces


def tile_rows(first, count):
    return pl.ds(first if isinstance(first, int) else pl.multiple_of(first, 8), count)


def eight(values):
    missing = jnp.zeros((SLOTS - values.shape[0], values.shape[1]), values.dtype)
    return jnp.concatenate([values, missing], axis=0)


def in_turns(first, last, size, body):
    turns = (last - first) // size
    if turns > 1:

        @pl.loop(0, turns)
        def _(turn):
            for index in range(size):
                body(first + turn * size + index)

        first += turns * size
    for index in range(first, last):
        body(index)


def to_plane(load, store):
    lane = lax.broadcasted_iota(jnp.int32, (8, LANES), 1)
    for step in range(RUN // 4):
        rows = [load(5 * step + part) for part in range(5)]
        store(4 * step, rows[0], rows[1])
        for part in range(1, 4):
            left = pltpu.roll(rows[part], LANES - 32 * part, 1)
            right = pltpu.roll(rows[part + 1], LANES - 32 * part, 1)
            store(4 * step + part, jnp.where(lane < LANES - 32 * part, left, right), right)


def to_flat(load, store):
    lane = lax.broadcasted_iota(jnp.int32, (8, LANES), 1)
    for step in range(RUN // 4):
        turned = []
        for part in range(4):
            low, high = load(4 * step + part)
            if part:
                low = pltpu.roll(low, 32 * part, 1)
                high = pltpu.roll(high, 32 * part, 1)
            turned.append((low, high))
        store(5 * step, turned[0][0])
        for part in range(1, 4):
            ended = 32 * (part - 1)
            values = jnp.where(lane < ended + 32, turned[part - 1][1], turned[part][0])
            if ended:
                values = jnp.where(lane < ended, turned[part - 1][0], values)
            store(5 * step + part, values)
        store(5 * step + 4, jnp.where(lane < 96, turned[3][0], turned[3][1]))


def chords():
    across = 2 * np.arange(SIDE, dtype=np.int64) - (SIDE - 1)
    room = (SIDE - 2) ** 2 - across**2
    return [max([w for w in range(1, SIDE // 2 + 1) if (2 * w - 1) ** 2 <= left], default=0) for left in room]


def chord_moves():
    moves = []
    packed = 0
    for row, half in enumerate(chords()):
        if half:
            moves.append((row * SIDE + SIDE // 2 - half, packed, 2 * half))
            packed += 2 * half
    return moves


def packed_tiles():
    _, start, length = chord_moves()[-1]
    return -(-(start + length) // LANES)


def move_lanes(moves, load, store):
    lane = lax.broadcasted_iota(jnp.int32, (8, LANES), 1)
    pieces = {}
    for source, target, length in moves:
        while length:
            size = min(length, LANES - source % LANES, LANES - target % LANES)
            pieces.setdefault(target // LANES, []).append((target % LANES, source // LANES, (target - source) % LANES))
            source, target, length = source + size, target + size, length - size
    loaded = {}
    turned = {}
    for tile in sorted(pieces):
        values = None
        for first, origin, shift in sorted(pieces[tile]):
            if origin not in loaded:
                loaded[origin] = load(origin)
            if (origin, shift) not in turned:
                turned[origin, shift] = pltpu.roll(loaded[origin], shift, 1) if shift else loaded[origin]
            piece = turned[origin, shift]
            values = piece if values is None else jnp.where(lane >= first, piece, values)
        store(tile, values)


def pack_chords(rows_ref, store):
    move_lanes(chord_moves(), lambda tile: rows_ref[pl.ds(tile, 8, stride=FLAT), :], store)


def unpack_chords(load, rows_ref):
    def store(tile, values):
        rows_ref[pl.ds(tile, 8, stride=FLAT), :] = values

    move_lanes([(target, source, length) for source, target, length in chord_moves()], load, store)


def parts_of(values):
    high = values.astype(jnp.bfloat16)
    low = (values - high.astype(jnp.float32)).astype(jnp.bfloat16)
    return high, low


def turn_z(values, table):
    high, low = parts_of(values)
    return jnp.dot(
        jnp.concatenate([high, low, high], axis=1), table, preferred_element_type=jnp.float32
    )


def turn_y(table, values):
    high, low = parts_of(values)
    return jnp.dot(
        table, jnp.concatenate([high, low, high], axis=0), preferred_element_type=jnp.float32
    )


def half_columns(along_z, slots, table_y, low_ref, high_ref):
    half = SIDE // 2
    for slot in range(slots):
        rows = slice(slot * half, (slot + 1) * half)
        waves = turn_y(table_y, along_z[slot * SIDE:(slot + 1) * SIDE])
        low_ref[rows, :] = waves[:, :LANES]
        high_ref[rows, :] = waves[:, LANES:]
    low_ref[slots * half:, :] = jnp.zeros(((SLOTS - slots) * half, LANES), jnp.float32)
    high_ref[slots * half:, :] = jnp.zeros(((SLOTS - slots) * half, LANES), jnp.float32)


def chunk_of(low_ref, high_ref, first_row, pieces, extra):
    parts = []
    for row, start, stop in pieces:
        at = pl.ds(first_row + row, SLOTS, stride=SIDE // 2)
        values = jnp.concatenate([low_ref[at, :], high_ref[at, :]], axis=1)
        parts.append(values[:, start:stop])
    return jnp.concatenate(parts + [extra], axis=1)


def layers_of(stored_ref, flat_ref):
    @pl.loop(0, FLAT // 8)
    def _(step):
        for part in range(8):
            lanes = pl.ds(pl.multiple_of((step * 8 + part) * LANES, LANES), LANES)
            flat_ref[pl.ds(step * 8 + part, SLOTS, stride=FLAT), :] = eight(stored_ref[:, lanes])


def place_of(start_ref):
    position = lax.axis_index("domain")
    return position, start_ref[position], start_ref[position + 1] - start_ref[position]


def started(sems, pairs):
    copies = [pltpu.make_async_copy(*pair, sems.at[index]) for index, pair in enumerate(pairs)]
    for made in copies:
        made.start()
    return copies


def layers_at(orbitals_ref, part, start, count):
    return orbitals_ref.at[part, pl.ds(pl.multiple_of(start * FLAT, 8), count * FLAT)]


def rows_at(ref, part, count):
    return ref.at[pl.ds(part * count * FLAT, count * FLAT)]


def pack_kernel(start_ref, orbitals_ref, up_ref, down_ref, up_rows_ref, down_rows_ref, up_buffer_ref,
                down_buffer_ref, in_sems, out_sems):
    _, _, thickness = place_of(start_ref)
    first = jnp.maximum(thickness - HALO, 0)
    arrivals = started(
        in_sems,
        [
            (layers_at(orbitals_ref, part, start, HALO), rows_at(rows_ref, part, HALO))
            for start, rows_ref in ((first, up_rows_ref), (0, down_rows_ref))
            for part in range(2)
        ],
    )
    departures = []
    for index, (rows_ref, buffer_ref, out_ref) in enumerate(
        ((up_rows_ref, up_buffer_ref, up_ref), (down_rows_ref, down_buffer_ref, down_ref))
    ):
        arrivals[2 * index].wait()
        arrivals[2 * index + 1].wait()

        def store(tile, values, buffer_ref=buffer_ref):
            buffer_ref[:, tile * LANES:(tile + 1) * LANES] = values

        pack_chords(rows_ref, store)
        departures.append(pltpu.make_async_copy(buffer_ref, out_ref, out_sems.at[index]))
        departures[-1].start()
    for made in departures:
        made.wait()


def pack_rest_kernel(start_ref, potential_ref, orbitals_ref, v_ref, up_far_ref, down_far_ref, flat_ref,
                     v_rows_ref, stored_ref, in_sems):
    _, _, thickness = place_of(start_ref)
    v_first = jnp.where(lax.axis_index("core") == 0, thickness - (HALO - 1), 0)
    arrivals = started(
        in_sems,
        [(potential_ref, stored_ref)]
        + [
            (layers_at(orbitals_ref, part, start, 1), rows_at(far_ref, part, 1))
            for start, far_ref in ((thickness - 1, up_far_ref), (0, down_far_ref))
            for part in range(2)
        ],
    )
    arrivals[0].wait()
    layers_of(stored_ref, flat_ref)
    for layer in range(HALO - 1):
        v_rows_ref[layer * FLAT:(layer + 1) * FLAT, :] = flat_ref[
            pl.ds(pl.multiple_of((v_first + layer) * FLAT, 8), FLAT), :
        ]

    def store_v(tile, values):
        for layer in range(HALO - 1):
            v_ref[layer, tile:tile + 1, :] = values[layer:layer + 1]

    pack_chords(v_rows_ref, store_v)
    for made in arrivals[1:]:
        made.wait()


def ions_kernel(count, length_cells, start_ref, background_ref, circle_ref, table_y_ref, table_z_ref,
                out_ref, flat_ref, planes_ref, low_ref, high_ref):
    _, own_start, thickness = place_of(start_ref)
    slots = background_ref.shape[0]
    groups, _, width = out_ref.shape
    layers_of(background_ref, flat_ref)

    def body(slot, total):
        def store(tile, low, high):
            rows = pl.ds(pl.multiple_of(slot * SIDE + tile * 8, 8), 8)
            planes_ref[rows, :LANES] = low
            planes_ref[rows, LANES:] = high

        to_plane(lambda k: flat_ref[pl.ds(slot * FLAT + k, 8, stride=STRIDE), :], store)
        rows = pl.ds(pl.multiple_of(slot * SIDE, 8), SIDE)
        inside = mesh_points(own_start + slot, circle_ref[...], length_cells) & (slot < thickness)
        values = jnp.where(inside, planes_ref[rows, :], 0.0)
        planes_ref[rows, :] = values
        return total + jnp.sum(values.reshape(RUN, 8, WIDTH), axis=0)

    total = lax.fori_loop(0, slots, body, jnp.zeros((8, WIDTH), jnp.float32))
    whole = jnp.broadcast_to(jnp.sum(total, keepdims=True), (SLOTS, LANES))[:, :width - count]
    along_z = turn_z(planes_ref[...], table_z_ref[...])
    half_columns(along_z, slots, table_y_ref[lax.axis_index("core")], low_ref, high_ref)
    first_row = lax.axis_index("row") * (SIDE // 2 // lax.axis_size("row"))
    for group in range(groups):
        out_ref[group] = chunk_of(low_ref, high_ref, first_row, column_pieces(group * count, count), whole)


def propagate_kernel(count, length_cells, start_ref, weight_ref, orbitals_ref, potential_ref, below_hbm_ref,
                     above_hbm_ref, below_far_hbm_ref, above_far_hbm_ref, v_hbm_ref, v_other_hbm_ref,
                     circle_ref, table_y_ref, table_z_ref, psi_ref, along_ref, whole_ref, sent_ref, first_ref, second_ref,
                     third_ref, fourth_ref, sum_ref, centre_ref, beside_ref, flat_ref, planes_ref, low_ref,
                     high_ref, below_rows_ref, above_rows_ref, v_rows_ref, v_ref, v_other_ref, below_ref,
                     above_ref, below_far_ref, above_far_ref, in_sems, out_sem):
    arrivals = started(
        in_sems,
        [
            (v_hbm_ref, v_ref),
            (v_other_hbm_ref, v_other_ref),
            (below_hbm_ref, below_ref),
            (above_hbm_ref, above_ref),
            (below_far_hbm_ref, below_far_ref),
            (above_far_hbm_ref, above_far_ref),
        ],
    )
    position, own_start, thickness = place_of(start_ref)
    domains = lax.axis_size("domain")
    before = start_ref[jnp.maximum(position - 1, 0)]
    after = start_ref[jnp.minimum(position + 2, domains)]
    short_below = ((position > 0) & (own_start - before < HALO)).astype(jnp.int32)
    short_above = (position < domains - 1) & (after - own_start - thickness < HALO)
    weight = weight_ref[0]
    core = lax.axis_index("core")
    slots = orbitals_ref.shape[1]
    layers = slots + 2 * HALO
    devices, _, width = sent_ref.shape
    field_refs = (first_ref, second_ref, third_ref, fourth_ref)

    def field_layer(part, x_row):
        def store(tile, low, high):
            first_ref[part, x_row, 8 + 8 * tile:16 + 8 * tile, :LANES] = low
            first_ref[part, x_row, 8 + 8 * tile:16 + 8 * tile, LANES:] = high

        return store

    def potential_layer(x_row):
        def store(tile, low, high):
            centre_ref[x_row, 8 * tile:8 * tile + 8, :LANES] = low
            centre_ref[x_row, 8 * tile:8 * tile + 8, LANES:] = high

        return store

    def rows_from(ref, *at):
        return lambda k: ref[(*at, pl.ds(k, 8, stride=STRIDE), slice(None))]

    def layer_of(rows_ref, layer):
        return lambda k: rows_ref[pl.ds(layer * FLAT + k, 8, stride=STRIDE), :]

    layers_of(potential_ref, flat_ref)

    for slot in range(slots):
        for part in range(2):
            to_plane(rows_from(orbitals_ref, part, slot), field_layer(part, HALO + slot))
        to_plane(layer_of(flat_ref, slot), potential_layer(HALO + slot))

    for made in arrivals:
        made.wait()
    for packed_ref, rows_ref in ((below_ref, below_rows_ref), (above_ref, above_rows_ref)):
        unpack_chords(
            lambda tile, packed_ref=packed_ref: packed_ref[:, tile * LANES:(tile + 1) * LANES], rows_ref
        )
    unpack_chords(
        lambda tile: eight(
            jnp.concatenate([ref[:, tile, :] for ref in (v_ref, v_other_ref)], axis=0)
        ),
        v_rows_ref,
    )

    for layer in range(HALO - 1):
        lower = 1 + layer
        upper = HALO + thickness + layer
        to_plane(layer_of(v_rows_ref, layer), potential_layer(jnp.where(core == 0, lower, upper)))
        to_plane(layer_of(v_rows_ref, HALO - 1 + layer), potential_layer(jnp.where(core == 0, upper, lower)))
        for part in range(2):
            to_plane(
                layer_of(below_rows_ref, part * HALO + 1 + layer - short_below), field_layer(part, 1 + layer)
            )
            to_plane(
                layer_of(above_rows_ref, part * HALO + layer), field_layer(part, HALO + thickness + layer)
            )

    @pl.loop(0, 2)
    def _(part):
        last = 2 * HALO - 1 + thickness

        @pl.when(short_below > 0)
        def _():
            to_plane(layer_of(below_far_ref, part), field_layer(part, 0))

        @pl.when(short_below == 0)
        def _():
            to_plane(layer_of(below_rows_ref, part * HALO), field_layer(part, 0))

        @pl.when(short_above)
        def _():
            to_plane(layer_of(above_far_ref, part), field_layer(part, last))

        @pl.when(jnp.logical_not(short_above))
        def _():
            to_plane(layer_of(above_rows_ref, part * HALO + HALO - 1), field_layer(part, last))

    def wrap(field_ref, part, x_row, first, final):
        field_ref[part, x_row, :8, :] = pltpu.roll(final, 1, 0)
        field_ref[part, x_row, SIDE + 8:, :] = pltpu.roll(first, 7, 0)

    blocks = SIDE // BLOCK

    def confine(x_row):
        known = x_row < thickness + 2 * HALO
        ends = {}
        for block in range(blocks):
            rows = slice(block * BLOCK, (block + 1) * BLOCK)
            inner = slice(8 + block * BLOCK, 8 + (block + 1) * BLOCK)
            inside = mesh_points(own_start - HALO + x_row, circle_ref[rows, :], length_cells) & known
            centre_ref[x_row, rows, :] = jnp.where(
                inside, (3.0 + centre_ref[x_row, rows, :]) * time_step, 0.0
            )
            beside_ref[x_row, rows, :] = jnp.where(inside, 0.5 * time_step, 0.0)
            for part in range(2):
                field = jnp.where(inside, first_ref[part, x_row, inner, :], 0.0)
                first_ref[part, x_row, inner, :] = field
                ends[part, block] = field
        for part in range(2):
            wrap(first_ref, part, x_row, ends[part, 0][:8], ends[part, blocks - 1][BLOCK - 8:])

    in_turns(0, layers, 5, confine)

    def hamilton(term, part, x_row, block, centre, beside):
        field_ref = field_refs[term]
        tall = field_ref[part, x_row, block * BLOCK:block * BLOCK + BLOCK + 16, :]
        inner = slice(8 + block * BLOCK, 8 + (block + 1) * BLOCK)
        field = tall[8:8 + BLOCK]
        around = field_ref[part, x_row - 1, inner, :] + field_ref[part, x_row + 1, inner, :]
        around = around + (tall[:BLOCK] + tall[16:])
        around = around + (pltpu.roll(field, 1, 1) + pltpu.roll(field, WIDTH - 1, 1))
        return centre * field - beside * around

    for term in range(1, TERMS):

        def step(x_row, term=term):
            ends = {}
            for block in range(blocks):
                rows = slice(block * BLOCK, (block + 1) * BLOCK)
                inner = slice(8 + block * BLOCK, 8 + (block + 1) * BLOCK)
                centre = centre_ref[x_row, rows, :]
                beside = beside_ref[x_row, rows, :]
                for part in range(2):
                    field = hamilton(term - 1, part, x_row, block, centre, beside)
                    field_refs[term][part, x_row, inner, :] = field
                    ends[part, block] = field
            for part in range(2):
                wrap(field_refs[term], part, x_row, ends[part, 0][:8], ends[part, blocks - 1][BLOCK - 8:])

        in_turns(term, layers - term, 4, step)

    def finish(slot, total):
        x_row = HALO + slot
        owned = slot < thickness
        for block in range(SIDE // BLOCK):
            rows = slice(block * BLOCK, (block + 1) * BLOCK)
            inner = slice(8 + block * BLOCK, 8 + (block + 1) * BLOCK)
            centre = centre_ref[x_row, rows, :]
            beside = beside_ref[x_row, rows, :]
            density = jnp.zeros((BLOCK, WIDTH), jnp.float32)
            for part, sign in ((0, 1.0), (1, -1.0)):
                summed = first_ref[part, x_row, inner, :]
                summed = summed + sign * second_ref[1 - part, x_row, inner, :]
                summed = summed - (1.0 / 2.0) * third_ref[part, x_row, inner, :]
                summed = summed - (sign / 6.0) * fourth_ref[1 - part, x_row, inner, :]
                summed = summed + (1.0 / 24.0) * hamilton(3, part, x_row, block, centre, beside)
                summed = jnp.where(owned, summed, 0.0)
                sum_ref[part, slot, rows, :] = summed
                density = density + summed * summed
            density = weight * density
            planes_ref[tile_rows(slot * SIDE + block * BLOCK, BLOCK), :] = density
            total = total + jnp.sum(density.reshape(BLOCK // 8, 8, WIDTH), axis=0)

        return total

    total = lax.fori_loop(
        0, slots // 2, lambda pair, total: finish(2 * pair + 1, finish(2 * pair, total)), jnp.zeros((8, WIDTH), jnp.float32)
    )
    for slot in range(slots // 2 * 2, slots):
        total = finish(slot, total)
    departure = pltpu.make_async_copy(sum_ref, psi_ref, out_sem)
    departure.start()
    whole = jnp.broadcast_to(jnp.sum(total, keepdims=True), (SLOTS, LANES))
    whole_ref[...] = whole
    along_z = turn_z(planes_ref[...], table_z_ref[...])
    along_ref[...] = along_z
    half_columns(along_z, slots, table_y_ref[1 - core], low_ref, high_ref)
    for device in range(devices):
        sent_ref[device] = chunk_of(
            low_ref, high_ref, 0, column_pieces(device * count, count), whole[:, :width - count]
        )
    departure.wait()


def kept_kernel(count, along_ref, whole_ref, table_y_ref, kept_ref, low_ref, high_ref):
    devices, _, width = kept_ref.shape
    slots = along_ref.shape[0] // SIDE
    half_columns(along_ref[...], slots, table_y_ref[lax.axis_index("core")], low_ref, high_ref)
    whole = whole_ref[...][:, :width - count]
    for device in range(devices):
        kept_ref[device] = chunk_of(low_ref, high_ref, 0, column_pieces(device * count, count), whole)


def unpack_kernel(weight_ref, psi_ref, next_ref, density_kept_ref, density_sent_ref, density_ref):
    core = lax.axis_index("core")
    weight = weight_ref[0]
    slots = psi_ref.shape[1]

    def unpack(slot):
        for part in range(2):

            def load(tile, part=part):
                tall = psi_ref[part, slot, 8 * tile:8 * tile + 8, :]
                return tall[:, :LANES], tall[:, LANES:]

            def store(k, values, part=part):
                next_ref[part, slot, pl.ds(k, 8, stride=STRIDE), :] = values

            to_flat(load, store)
        real = next_ref[0, slot]
        imag = next_ref[1, slot]
        density_ref[slot] = weight * (real * real + imag * imag)

    in_turns(0, slots, 2, unpack)
    for slot in range(slots, SLOTS):
        density_ref[slot] = jnp.zeros((FLAT, LANES), jnp.float32)

    @pl.loop(0, SLOTS // 2)
    def _(slot):
        density_kept_ref[slot] = density_ref[core * (SLOTS // 2) + slot]
        density_sent_ref[slot] = density_ref[(1 - core) * (SLOTS // 2) + slot]


def wave_squared(index, count_cells):
    folded = jnp.where(2 * index <= count_cells, index, index - count_cells)
    wave_number = folded.astype(jnp.float32) * (two_pi / count_cells)
    return wave_number * wave_number


def coulomb_kernel(count, length_cells, start_ref, charge_ref, ions_ref, table_ref, out_ref):
    domains, _, width = ions_ref.shape
    states = charge_ref.shape[0] // domains
    device = (lax.axis_index("core") * states + lax.axis_index("row")) * domains + lax.axis_index("domain")
    charge = charge_ref[:domains]
    for state in range(1, states):
        charge = charge + charge_ref[state * domains:(state + 1) * domains]
    charge = charge.reshape(domains * SLOTS, width)
    ions = ions_ref[...].reshape(domains * SLOTS, width)
    first = lax.broadcasted_iota(jnp.int32, (domains * SLOTS, width), 0) % SLOTS == 0
    lane = lax.broadcasted_iota(jnp.int32, (domains * SLOTS, width), 1)
    chosen = first & (lane == count)
    electrons = jnp.sum(jnp.where(chosen, charge, 0.0), keepdims=True)
    ionic = jnp.sum(jnp.where(chosen, ions, 0.0), keepdims=True)
    charge = charge - (electrons / ionic) * ions
    layer = lax.broadcasted_iota(jnp.int32, (length_cells, domains * SLOTS), 0)
    place = lax.broadcasted_iota(jnp.int32, (length_cells, domains * SLOTS), 1)
    chosen_layer = jnp.full(layer.shape, -1, jnp.int32)
    for domain in range(domains):
        slot = place - domain * SLOTS
        here = (slot >= 0) & (slot < start_ref[domain + 1] - start_ref[domain])
        chosen_layer = jnp.where(here, start_ref[domain] + slot, chosen_layer)
    pick = (layer == chosen_layer).astype(jnp.float32)
    table = jnp.dot(table_ref[...], pick, precision=highest, preferred_element_type=jnp.float32)
    waves = jnp.dot(table, charge, precision=highest, preferred_element_type=jnp.float32)
    wave_x = lax.broadcasted_iota(jnp.int32, waves.shape, 0)
    column = device * count + lax.broadcasted_iota(jnp.int32, waves.shape, 1)
    wave_y = ((column.astype(jnp.float32) + 0.5) * (1.0 / SIDE)).astype(jnp.int32)
    wave_z = column - wave_y * SIDE
    squared = (
        wave_squared(wave_x, length_cells) + wave_squared(wave_y, SIDE) + wave_squared(wave_z, SIDE)
    )
    gain = jnp.where(squared > 0, four_pi / jnp.where(squared > 0, squared, 1.0), 0.0)
    waves = waves * (gain * (1.0 / (length_cells * SIDE * SIDE)))
    back = lax.dot_general(
        table, waves, (((0,), (0,)), ((), ())), precision=highest, preferred_element_type=jnp.float32
    )
    back = back.reshape(domains, SLOTS, width)
    for state in range(states):
        out_ref[state * domains:(state + 1) * domains] = back


def half_planes(count, source_ref, table_y, table_z, low_ref, high_ref, slots):
    half = SIDE // 2
    pieces = []
    for device in range(source_ref.shape[0]):
        column = 0
        for row, start, stop in column_pieces(device * count, count):
            values = source_ref[device, :, column:column + stop - start]
            column += stop - start
            if start > 0:
                pieces.append(values)
                values = jnp.concatenate(pieces, axis=1)
            if stop < SIDE:
                pieces = [values]
                continue
            pieces = []
            at = pl.ds(row, SLOTS, stride=half)
            low_ref[at, :] = values[:, :LANES]
            high_ref[at, :] = jnp.concatenate(
                [values[:, LANES:], jnp.zeros((SLOTS, WIDTH - SIDE), jnp.float32)], axis=1
            )
    used = slice(0, slots * half)
    along_z = turn_z(jnp.concatenate([low_ref[used, :], high_ref[used, :]], axis=1), table_z)
    return [turn_y(table_y, along_z[slot * half:(slot + 1) * half]) for slot in range(slots)]


def half_kernel(count, waves_ref, table_y_ref, table_z_ref, out_ref, low_ref, high_ref):
    table_y = table_y_ref[lax.axis_index("core")]
    slots = out_ref.shape[0] // SIDE
    planes = half_planes(count, waves_ref, table_y, table_z_ref[...], low_ref, high_ref, slots)
    for slot, plane in enumerate(planes):
        out_ref[slot * SIDE:(slot + 1) * SIDE, :] = plane


def field_kernel(count, length_cells, start_ref, others_ref, half_ref, density_ref, other_ref, circle_ref,
                 table_y_ref, table_z_ref, out_ref, low_ref, high_ref, planes_ref, flat_ref):
    _, own_start, thickness = place_of(start_ref)
    slots = out_ref.shape[0]
    core = lax.axis_index("core")
    planes = half_planes(count, others_ref, table_y_ref[1 - core], table_z_ref[...], low_ref, high_ref, slots)
    for slot, plane in enumerate(planes):
        rows = slice(slot * SIDE, (slot + 1) * SIDE)
        planes_ref[rows, :] = half_ref[rows, :] + plane

    def field(slot):
        def load(tile):
            tall = planes_ref[tile_rows(slot * SIDE + tile * 8, 8), :]
            return tall[:, :LANES], tall[:, LANES:]

        def store(k, values):
            flat_ref[pl.ds(slot * FLAT + k, 8, stride=STRIDE), :] = values

        to_flat(load, store)
        rows = tile_rows(slot * FLAT, FLAT)
        here = slot // (SLOTS // 2) == core
        kept_slot = slot % (SLOTS // 2)
        content = jnp.where(here, density_ref[kept_slot], other_ref[kept_slot]) * (3.0 / math.pi)
        positive = jnp.where(content > 0, content, 1.0)
        root = jnp.exp(jnp.log(positive) * (1.0 / 3.0))
        root = root - (root - positive / (root * root)) * (1.0 / 3.0)
        root = jnp.where(content > 0, root, 0.0)
        inside = mesh_points(own_start + slot, circle_ref[...], length_cells) & (slot < thickness)
        flat_ref[rows, :] = jnp.where(inside, flat_ref[rows, :] - root, 0.0)

    in_turns(0, slots, 4, field)

    @pl.loop(0, FLAT // 8)
    def _(step):
        for part in range(8):
            lanes = pl.ds(pl.multiple_of((step * 8 + part) * LANES, LANES), LANES)
            out_ref[:, lanes] = flat_ref[pl.ds(step * 8 + part, SLOTS, stride=FLAT), :][:slots]


def from_behind(value, steps):
    count = lax.axis_size("domain")
    leading, last = (max(0, -steps), min(count, count - steps))
    return lax.ppermute(value, "domain", [(source, source + steps) for source in range(leading, last)])


def swapped(value, axis):
    return lax.ppermute(value, axis, [(0, 1), (1, 0)])


def shards(orbitals, occupation, potential, background, layer_start):
    domains = lax.axis_size("domain")
    rows = lax.axis_size("row")
    devices = domains * rows
    length_cells = SLAB * domains
    layer_cap, plane = potential.shape
    count = plane // (2 * devices)
    width = -(-(count + 1) // LANES) * LANES
    circle = jnp.asarray(circle_plane())
    flat_circle = jnp.asarray(circle_table().reshape(FLAT, LANES))
    table_z, into_y, out_of_y = (jnp.asarray(table) for table in tables_of_side())
    table_x = jnp.asarray(hartley_table(length_cells).astype(np.float32))
    params = pltpu.CompilerParams(vmem_limit_bytes=16 * MEBI)
    large = pltpu.CompilerParams(vmem_limit_bytes=44 * MEBI)
    whole = pltpu.CompilerParams(vmem_limit_bytes=56 * MEBI)

    def f32(*shape):
        return jax.ShapeDtypeStruct(shape, jnp.float32)

    def scratch(*shape):
        return pltpu.VMEM(shape, jnp.float32)

    layers = orbitals.reshape(2, layer_cap, FLAT, LANES)
    packed = packed_tiles()
    outer = orbitals.reshape(2, layer_cap * FLAT, LANES)
    up, down = pl.pallas_call(
        pack_kernel,
        out_shape=(f32(2 * HALO, packed * LANES), f32(2 * HALO, packed * LANES)),
        in_specs=[SMEM_SPEC, HBM_SPEC],
        out_specs=(HBM_SPEC, HBM_SPEC),
        scratch_shapes=[
            scratch(2 * HALO * FLAT, LANES),
            scratch(2 * HALO * FLAT, LANES),
            scratch(2 * HALO, packed * LANES),
            scratch(2 * HALO, packed * LANES),
            pltpu.SemaphoreType.DMA((4,)),
            pltpu.SemaphoreType.DMA((2,)),
        ],
        compiler_params=whole,
        name="pack_halo",
    )(layer_start, outer)
    up, down, potential_rest, outer = lax.optimization_barrier((up, down, potential, outer))
    v_rows, up_far, down_far = pl.pallas_call(
        pack_rest_kernel,
        out_shape=(f32(HALO - 1, packed, LANES), f32(2 * FLAT, LANES), f32(2 * FLAT, LANES)),
        in_specs=[SMEM_SPEC, HBM_SPEC, HBM_SPEC],
        out_specs=(VMEM_SPEC,) * 3,
        scratch_shapes=[
            scratch(SLOTS * FLAT, LANES),
            scratch(SLOTS * FLAT, LANES),
            scratch(layer_cap, plane),
            pltpu.SemaphoreType.DMA((5,)),
        ],
        compiler_params=whole,
        cost_estimate=pl.CostEstimate(flops=0, transcendentals=0, bytes_accessed=30_000_000),
        name="pack_rest",
    )(layer_start, potential_rest, outer)
    v_rows = lax.ppermute(
        v_rows,
        ("core", "domain"),
        [(source, source + 1) for source in range(domains - 1)]
        + [(domains + source + 1, domains + source) for source in range(domains - 1)],
    )
    below = from_behind(up, 1)
    above = from_behind(down, -1)
    below_far = from_behind(up_far, 2)
    above_far = from_behind(down_far, -2)
    v_rows, below_far, above_far = lax.optimization_barrier((v_rows, below_far, above_far))
    v_others = swapped(v_rows, "core")

    ions = pl.pallas_call(
        functools.partial(ions_kernel, count, length_cells),
        out_shape=f32(domains, SLOTS, width),
        in_specs=[SMEM_SPEC] + [VMEM_SPEC] * 4,
        out_specs=VMEM_SPEC,
        scratch_shapes=[
            scratch(SLOTS * FLAT, LANES),
            scratch(layer_cap * SIDE, WIDTH),
            scratch(SLOTS * SIDE // 2, LANES),
            scratch(SLOTS * SIDE // 2, LANES),
        ],
        compiler_params=params,
        name="ion_waves",
    )(layer_start, background, circle, into_y, table_z)
    ions = lax.all_to_all(ions, "domain", split_axis=0, concat_axis=0, tiled=True)
    ions, below = lax.optimization_barrier((ions, below))

    span = layer_cap + 2 * HALO
    fields = (2, span, TALL, WIDTH)
    psi, along_z, whole_sum, sent = pl.pallas_call(
        functools.partial(propagate_kernel, count, length_cells),
        out_shape=(
            pltpu.HBM((2, layer_cap, SIDE, WIDTH), jnp.float32),
            f32(layer_cap * SIDE, WIDTH),
            f32(SLOTS, LANES),
            f32(devices, SLOTS, width),
        ),
        in_specs=[SMEM_SPEC, SMEM_SPEC, VMEM_SPEC, VMEM_SPEC] + [HBM_SPEC] * 6 + [VMEM_SPEC] * 3,
        out_specs=(HBM_SPEC, VMEM_SPEC, VMEM_SPEC, VMEM_SPEC),
        scratch_shapes=[scratch(*fields)] * TERMS
        + [
            scratch(2, layer_cap, SIDE, WIDTH),
            scratch(span, SIDE, WIDTH),
            scratch(span, SIDE, WIDTH),
            scratch(SLOTS * FLAT, LANES),
            scratch(layer_cap * SIDE, WIDTH),
            scratch(SLOTS * SIDE // 2, LANES),
            scratch(SLOTS * SIDE // 2, LANES),
            scratch(SLOTS * FLAT, LANES),
            scratch(SLOTS * FLAT, LANES),
            scratch(SLOTS * FLAT, LANES),
            scratch(HALO - 1, packed, LANES),
            scratch(HALO - 1, packed, LANES),
            scratch(2 * HALO, packed * LANES),
            scratch(2 * HALO, packed * LANES),
            scratch(2 * FLAT, LANES),
            scratch(2 * FLAT, LANES),
            pltpu.SemaphoreType.DMA((6,)),
            pltpu.SemaphoreType.DMA,
        ],
        compiler_params=large,
        name="propagate",
    )(layer_start, occupation, layers, potential, below, above, below_far, above_far, v_rows, v_others,
      circle, into_y, table_z)
    half = [scratch(SLOTS * SIDE // 2, LANES), scratch(SLOTS * SIDE // 2, LANES)]
    kept = pl.pallas_call(
        functools.partial(kept_kernel, count),
        out_shape=f32(devices, SLOTS, width),
        in_specs=[VMEM_SPEC] * 3,
        out_specs=VMEM_SPEC,
        scratch_shapes=half,
        compiler_params=params,
        name="kept_waves",
    )(along_z, whole_sum, into_y)
    waves = kept + swapped(sent, "core")
    waves, psi = lax.optimization_barrier((waves, psi))
    waves = lax.all_to_all(waves, ("row", "domain"), split_axis=0, concat_axis=0, tiled=True)
    orbitals_next, density_kept, density_sent = pl.pallas_call(
        unpack_kernel,
        out_shape=(
            f32(2, layer_cap, FLAT, LANES),
            f32(SLOTS // 2, FLAT, LANES),
            f32(SLOTS // 2, FLAT, LANES),
        ),
        in_specs=[SMEM_SPEC, VMEM_SPEC],
        out_specs=(VMEM_SPEC,) * 3,
        scratch_shapes=[scratch(SLOTS, FLAT, LANES)],
        compiler_params=params,
        name="unpack",
    )(occupation, psi)
    density = density_kept + swapped(density_sent, "core")
    waves, density = lax.optimization_barrier((waves, density))
    other_density = swapped(density, "row")
    waves = pl.pallas_call(
        functools.partial(coulomb_kernel, count, length_cells),
        out_shape=f32(devices, SLOTS, width),
        in_specs=[SMEM_SPEC] + [VMEM_SPEC] * 3,
        out_specs=VMEM_SPEC,
        compiler_params=params,
        name="coulomb",
    )(layer_start, waves, ions, table_x)
    waves = lax.all_to_all(waves, ("row", "domain"), split_axis=0, concat_axis=0, tiled=True)
    waves, other_density = lax.optimization_barrier((waves, other_density))
    density = density + other_density
    other_density = swapped(density, "core")
    other_waves = swapped(waves, "core")
    planes = pl.pallas_call(
        functools.partial(half_kernel, count),
        out_shape=f32(layer_cap * SIDE, WIDTH),
        in_specs=[VMEM_SPEC] * 3,
        out_specs=VMEM_SPEC,
        scratch_shapes=half,
        compiler_params=params,
        name="half_field",
    )(waves, out_of_y, table_z)
    potential_next = pl.pallas_call(
        functools.partial(field_kernel, count, length_cells),
        out_shape=f32(layer_cap, plane),
        in_specs=[SMEM_SPEC] + [VMEM_SPEC] * 7,
        out_specs=VMEM_SPEC,
        scratch_shapes=half + [scratch(layer_cap * SIDE, WIDTH), scratch(SLOTS * FLAT, LANES)],
        compiler_params=params,
        name="field",
    )(layer_start, other_waves, planes, density, other_density, flat_circle, out_of_y, table_z)
    return orbitals_next.reshape(orbitals.shape), potential_next


def solution(mesh):
    domains = mesh.shape["domain"]
    split = Mesh(mesh.devices.reshape(-1, 2, domains), ("row", "core", "domain"))
    states = ("row", "core")
    return jax.shard_map(
        shards,
        mesh=split,
        in_specs=(
            P(None, states, "domain", None),
            P(states),
            P("domain", None),
            P("domain", None),
            P(),
        ),
        out_specs=(P(None, states, "domain", None), P("domain", None)),
        check_vma=False,
    )
```

```python
import functools
import math

import jax
import jax.numpy as jnp
import ml_dtypes
import numpy as np
from jax import lax
from jax.experimental import pallas as pl
from jax.experimental.pallas import tpu as pltpu
from jax.sharding import Mesh, PartitionSpec as P

SIDE = 160
SLAB = 5
TERMS = 4

HALO = TERMS
LANES = 128
SLOTS = 8
RUN = SIDE // 8
FLAT = SIDE * SIDE // LANES
STRIDE = FLAT // 8
WIDTH = 2 * LANES
BLOCK = 40
TALL = SIDE + 16

time_step = 0.3
four_pi = 4.0 * math.pi
two_pi = 2.0 * math.pi
highest = lax.Precision.HIGHEST
MEBI = 1024 * 1024
SMEM_SPEC = pl.BlockSpec(memory_space=pltpu.SMEM)
VMEM_SPEC = pl.BlockSpec(memory_space=pltpu.VMEM)
HBM_SPEC = pl.BlockSpec(memory_space=pltpu.HBM)


def hartley_table(count_cells):
    index_run = np.arange(count_cells)
    angles = (index_run[:, None] * index_run[None, :] % count_cells) * (2.0 * np.pi / count_cells)
    return np.cos(angles) + np.sin(angles)


def plane_order():
    rows = np.arange(SIDE)
    return RUN * (rows % 8) + rows // 8


def two_parts(table):
    table = table.astype(np.float32)
    high = table.astype(ml_dtypes.bfloat16)
    low = (table - high.astype(np.float32)).astype(ml_dtypes.bfloat16)
    return high, low


def tables_of_side():
    table = hartley_table(SIDE)
    along_z = np.zeros((WIDTH, WIDTH))
    along_z[:SIDE, :SIDE] = table
    high, low = two_parts(along_z)
    along_z = np.concatenate([high, high, low], axis=0)
    high, low = two_parts(table[:, plane_order()])
    into_y = np.concatenate([high, high, low], axis=1).reshape(2, SIDE // 2, 3 * SIDE)
    high, low = two_parts(table[plane_order(), :])
    half = SIDE // 2
    halves = [slice(0, half), slice(half, SIDE)]
    out_of_y = np.stack([np.concatenate([high[:, at], high[:, at], low[:, at]], axis=1) for at in halves])
    return along_z, into_y, out_of_y


def circle_table():
    across = 2 * np.arange(SIDE, dtype=np.int64) - (SIDE - 1)
    return (across[:, None] ** 2 + across[None, :] ** 2).astype(np.int32)


def circle_plane():
    table = np.full((SIDE, WIDTH), 4 * SIDE * SIDE, np.int32)
    table[:, :SIDE] = circle_table()[plane_order()]
    return table


def mesh_points(x_row, circle, length_cells):
    room = ((length_cells - 2) ** 2 - (2 * x_row - (length_cells - 1)) ** 2) * (SIDE - 2) ** 2
    return (circle * (length_cells - 2) ** 2 <= room) & (circle < 4 * SIDE * SIDE)


def column_pieces(first, count):
    pieces = []
    column = first
    while column < first + count:
        row = column // SIDE
        stop = min((row + 1) * SIDE, first + count)
        pieces.append((row, column - row * SIDE, stop - row * SIDE))
        column = stop
    return pieces


def tile_rows(first, count):
    return pl.ds(first if isinstance(first, int) else pl.multiple_of(first, 8), count)


def eight(values):
    missing = jnp.zeros((SLOTS - values.shape[0], values.shape[1]), values.dtype)
    return jnp.concatenate([values, missing], axis=0)


def in_turns(first, last, size, body):
    turns = (last - first) // size
    if turns > 1:

        @pl.loop(0, turns)
        def _(turn):
            for index in range(size):
                body(first + turn * size + index)

        first += turns * size
    for index in range(first, last):
        body(index)


def to_plane(load, store):
    lane = lax.broadcasted_iota(jnp.int32, (8, LANES), 1)
    for step in range(RUN // 4):
        rows = [load(5 * step + part) for part in range(5)]
        store(4 * step, rows[0], rows[1])
        for part in range(1, 4):
            left = pltpu.roll(rows[part], LANES - 32 * part, 1)
            right = pltpu.roll(rows[part + 1], LANES - 32 * part, 1)
            store(4 * step + part, jnp.where(lane < LANES - 32 * part, left, right), right)


def to_flat(load, store):
    lane = lax.broadcasted_iota(jnp.int32, (8, LANES), 1)
    for step in range(RUN // 4):
        turned = []
        for part in range(4):
            low, high = load(4 * step + part)
            if part:
                low = pltpu.roll(low, 32 * part, 1)
                high = pltpu.roll(high, 32 * part, 1)
            turned.append((low, high))
        store(5 * step, turned[0][0])
        for part in range(1, 4):
            ended = 32 * (part - 1)
            values = jnp.where(lane < ended + 32, turned[part - 1][1], turned[part][0])
            if ended:
                values = jnp.where(lane < ended, turned[part - 1][0], values)
            store(5 * step + part, values)
        store(5 * step + 4, jnp.where(lane < 96, turned[3][0], turned[3][1]))


def chords():
    across = 2 * np.arange(SIDE, dtype=np.int64) - (SIDE - 1)
    room = (SIDE - 2) ** 2 - across**2
    return [max([w for w in range(1, SIDE // 2 + 1) if (2 * w - 1) ** 2 <= left], default=0) for left in room]


def chord_moves():
    moves = []
    packed = 0
    for row, half in enumerate(chords()):
        if half:
            moves.append((row * SIDE + SIDE // 2 - half, packed, 2 * half))
            packed += 2 * half
    return moves


def packed_tiles():
    _, start, length = chord_moves()[-1]
    return -(-(start + length) // LANES)


def move_lanes(moves, load, store):
    lane = lax.broadcasted_iota(jnp.int32, (8, LANES), 1)
    pieces = {}
    for source, target, length in moves:
        while length:
            size = min(length, LANES - source % LANES, LANES - target % LANES)
            pieces.setdefault(target // LANES, []).append((target % LANES, source // LANES, (target - source) % LANES))
            source, target, length = source + size, target + size, length - size
    loaded = {}
    turned = {}
    for tile in sorted(pieces):
        values = None
        for first, origin, shift in sorted(pieces[tile]):
            if origin not in loaded:
                loaded[origin] = load(origin)
            if (origin, shift) not in turned:
                turned[origin, shift] = pltpu.roll(loaded[origin], shift, 1) if shift else loaded[origin]
            piece = turned[origin, shift]
            values = piece if values is None else jnp.where(lane >= first, piece, values)
        store(tile, values)


def pack_chords(rows_ref, store):
    move_lanes(chord_moves(), lambda tile: rows_ref[pl.ds(tile, 8, stride=FLAT), :], store)


def unpack_chords(load, rows_ref):
    def store(tile, values):
        rows_ref[pl.ds(tile, 8, stride=FLAT), :] = values

    move_lanes([(target, source, length) for source, target, length in chord_moves()], load, store)


def parts_of(values):
    high = values.astype(jnp.bfloat16)
    low = (values - high.astype(jnp.float32)).astype(jnp.bfloat16)
    return high, low


def turn_z(values, table):
    high, low = parts_of(values)
    return jnp.dot(
        jnp.concatenate([high, low, high], axis=1), table, preferred_element_type=jnp.float32
    )


def turn_y(table, values):
    high, low = parts_of(values)
    return jnp.dot(
        table, jnp.concatenate([high, low, high], axis=0), preferred_element_type=jnp.float32
    )


def half_columns(along_z, slots, table_y, low_ref, high_ref):
    half = SIDE // 2
    for slot in range(slots):
        rows = slice(slot * half, (slot + 1) * half)
        waves = turn_y(table_y, along_z[slot * SIDE:(slot + 1) * SIDE])
        low_ref[rows, :] = waves[:, :LANES]
        high_ref[rows, :] = waves[:, LANES:]
    low_ref[slots * half:, :] = jnp.zeros(((SLOTS - slots) * half, LANES), jnp.float32)
    high_ref[slots * half:, :] = jnp.zeros(((SLOTS - slots) * half, LANES), jnp.float32)


def chunk_of(low_ref, high_ref, first_row, pieces, extra):
    parts = []
    for row, start, stop in pieces:
        at = pl.ds(first_row + row, SLOTS, stride=SIDE // 2)
        values = jnp.concatenate([low_ref[at, :], high_ref[at, :]], axis=1)
        parts.append(values[:, start:stop])
    return jnp.concatenate(parts + [extra], axis=1)


def layers_of(stored_ref, flat_ref):
    @pl.loop(0, FLAT // 8)
    def _(step):
        for part in range(8):
            lanes = pl.ds(pl.multiple_of((step * 8 + part) * LANES, LANES), LANES)
            flat_ref[pl.ds(step * 8 + part, SLOTS, stride=FLAT), :] = eight(stored_ref[:, lanes])


def place_of(start_ref):
    position = lax.axis_index("domain")
    return position, start_ref[position], start_ref[position + 1] - start_ref[position]


def started(sems, pairs):
    copies = [pltpu.make_async_copy(*pair, sems.at[index]) for index, pair in enumerate(pairs)]
    for made in copies:
        made.start()
    return copies


def layers_at(orbitals_ref, part, start, count):
    return orbitals_ref.at[part, pl.ds(pl.multiple_of(start * FLAT, 8), count * FLAT)]


def rows_at(ref, part, count):
    return ref.at[pl.ds(part * count * FLAT, count * FLAT)]


def pack_kernel(start_ref, orbitals_ref, up_ref, down_ref, up_rows_ref, down_rows_ref, up_buffer_ref,
                down_buffer_ref, in_sems, out_sems):
    _, _, thickness = place_of(start_ref)
    first = jnp.maximum(thickness - HALO, 0)
    arrivals = started(
        in_sems,
        [
            (layers_at(orbitals_ref, part, start, HALO), rows_at(rows_ref, part, HALO))
            for start, rows_ref in ((first, up_rows_ref), (0, down_rows_ref))
            for part in range(2)
        ],
    )
    departures = []
    for index, (rows_ref, buffer_ref, out_ref) in enumerate(
        ((up_rows_ref, up_buffer_ref, up_ref), (down_rows_ref, down_buffer_ref, down_ref))
    ):
        arrivals[2 * index].wait()
        arrivals[2 * index + 1].wait()

        def store(tile, values, buffer_ref=buffer_ref):
            buffer_ref[:, tile * LANES:(tile + 1) * LANES] = values

        pack_chords(rows_ref, store)
        departures.append(pltpu.make_async_copy(buffer_ref, out_ref, out_sems.at[index]))
        departures[-1].start()
    for made in departures:
        made.wait()


def pack_rest_kernel(start_ref, potential_ref, orbitals_ref, v_ref, up_far_ref, down_far_ref, flat_ref,
                     v_rows_ref, stored_ref, in_sems):
    _, _, thickness = place_of(start_ref)
    v_first = jnp.where(lax.axis_index("core") == 0, thickness - (HALO - 1), 0)
    arrivals = started(
        in_sems,
        [(potential_ref, stored_ref)]
        + [
            (layers_at(orbitals_ref, part, start, 1), rows_at(far_ref, part, 1))
            for start, far_ref in ((thickness - 1, up_far_ref), (0, down_far_ref))
            for part in range(2)
        ],
    )
    arrivals[0].wait()
    layers_of(stored_ref, flat_ref)
    for layer in range(HALO - 1):
        v_rows_ref[layer * FLAT:(layer + 1) * FLAT, :] = flat_ref[
            pl.ds(pl.multiple_of((v_first + layer) * FLAT, 8), FLAT), :
        ]

    def store_v(tile, values):
        for layer in range(HALO - 1):
            v_ref[layer, tile:tile + 1, :] = values[layer:layer + 1]

    pack_chords(v_rows_ref, store_v)
    for made in arrivals[1:]:
        made.wait()


def ions_kernel(count, length_cells, start_ref, background_ref, circle_ref, table_y_ref, table_z_ref,
                out_ref, flat_ref, planes_ref, low_ref, high_ref):
    _, own_start, thickness = place_of(start_ref)
    slots = background_ref.shape[0]
    groups, _, width = out_ref.shape
    layers_of(background_ref, flat_ref)

    def body(slot, total):
        def store(tile, low, high):
            rows = pl.ds(pl.multiple_of(slot * SIDE + tile * 8, 8), 8)
            planes_ref[rows, :LANES] = low
            planes_ref[rows, LANES:] = high

        to_plane(lambda k: flat_ref[pl.ds(slot * FLAT + k, 8, stride=STRIDE), :], store)
        rows = pl.ds(pl.multiple_of(slot * SIDE, 8), SIDE)
        inside = mesh_points(own_start + slot, circle_ref[...], length_cells) & (slot < thickness)
        values = jnp.where(inside, planes_ref[rows, :], 0.0)
        planes_ref[rows, :] = values
        return total + jnp.sum(values.reshape(RUN, 8, WIDTH), axis=0)

    total = lax.fori_loop(0, slots, body, jnp.zeros((8, WIDTH), jnp.float32))
    whole = jnp.broadcast_to(jnp.sum(total, keepdims=True), (SLOTS, LANES))[:, :width - count]
    along_z = turn_z(planes_ref[...], table_z_ref[...])
    half_columns(along_z, slots, table_y_ref[lax.axis_index("core")], low_ref, high_ref)
    first_row = lax.axis_index("row") * (SIDE // 2 // lax.axis_size("row"))
    for group in range(groups):
        out_ref[group] = chunk_of(low_ref, high_ref, first_row, column_pieces(group * count, count), whole)


def propagate_kernel(count, length_cells, start_ref, weight_ref, orbitals_ref, potential_ref, below_hbm_ref,
                     above_hbm_ref, below_far_hbm_ref, above_far_hbm_ref, v_hbm_ref, v_other_hbm_ref,
                     circle_ref, table_y_ref, table_z_ref, psi_ref, along_ref, whole_ref, sent_ref, first_ref, second_ref,
                     third_ref, fourth_ref, sum_ref, centre_ref, beside_ref, flat_ref, planes_ref, low_ref,
                     high_ref, below_rows_ref, above_rows_ref, v_rows_ref, v_ref, v_other_ref, below_ref,
                     above_ref, below_far_ref, above_far_ref, in_sems, out_sem):
    arrivals = started(
        in_sems,
        [
            (v_hbm_ref, v_ref),
            (v_other_hbm_ref, v_other_ref),
            (below_hbm_ref, below_ref),
            (above_hbm_ref, above_ref),
            (below_far_hbm_ref, below_far_ref),
            (above_far_hbm_ref, above_far_ref),
        ],
    )
    position, own_start, thickness = place_of(start_ref)
    domains = lax.axis_size("domain")
    before = start_ref[jnp.maximum(position - 1, 0)]
    after = start_ref[jnp.minimum(position + 2, domains)]
    short_below = ((position > 0) & (own_start - before < HALO)).astype(jnp.int32)
    short_above = (position < domains - 1) & (after - own_start - thickness < HALO)
    weight = weight_ref[0]
    core = lax.axis_index("core")
    slots = orbitals_ref.shape[1]
    layers = slots + 2 * HALO
    devices, _, width = sent_ref.shape
    field_refs = (first_ref, second_ref, third_ref, fourth_ref)

    def field_layer(part, x_row):
        def store(tile, low, high):
            first_ref[part, x_row, 8 + 8 * tile:16 + 8 * tile, :LANES] = low
            first_ref[part, x_row, 8 + 8 * tile:16 + 8 * tile, LANES:] = high

        return store

    def potential_layer(x_row):
        def store(tile, low, high):
            centre_ref[x_row, 8 * tile:8 * tile + 8, :LANES] = low
            centre_ref[x_row, 8 * tile:8 * tile + 8, LANES:] = high

        return store

    def rows_from(ref, *at):
        return lambda k: ref[(*at, pl.ds(k, 8, stride=STRIDE), slice(None))]

    def layer_of(rows_ref, layer):
        return lambda k: rows_ref[pl.ds(layer * FLAT + k, 8, stride=STRIDE), :]

    layers_of(potential_ref, flat_ref)

    for slot in range(slots):
        for part in range(2):
            to_plane(rows_from(orbitals_ref, part, slot), field_layer(part, HALO + slot))
        to_plane(layer_of(flat_ref, slot), potential_layer(HALO + slot))

    for made in arrivals:
        made.wait()
    for packed_ref, rows_ref in ((below_ref, below_rows_ref), (above_ref, above_rows_ref)):
        unpack_chords(
            lambda tile, packed_ref=packed_ref: packed_ref[:, tile * LANES:(tile + 1) * LANES], rows_ref
        )
    unpack_chords(
        lambda tile: eight(
            jnp.concatenate([ref[:, tile, :] for ref in (v_ref, v_other_ref)], axis=0)
        ),
        v_rows_ref,
    )

    for layer in range(HALO - 1):
        lower = 1 + layer
        upper = HALO + thickness + layer
        to_plane(layer_of(v_rows_ref, layer), potential_layer(jnp.where(core == 0, lower, upper)))
        to_plane(layer_of(v_rows_ref, HALO - 1 + layer), potential_layer(jnp.where(core == 0, upper, lower)))
        for part in range(2):
            to_plane(
                layer_of(below_rows_ref, part * HALO + 1 + layer - short_below), field_layer(part, 1 + layer)
            )
            to_plane(
                layer_of(above_rows_ref, part * HALO + layer), field_layer(part, HALO + thickness + layer)
            )

    @pl.loop(0, 2)
    def _(part):
        last = 2 * HALO - 1 + thickness

        @pl.when(short_below > 0)
        def _():
            to_plane(layer_of(below_far_ref, part), field_layer(part, 0))

        @pl.when(short_below == 0)
        def _():
            to_plane(layer_of(below_rows_ref, part * HALO), field_layer(part, 0))

        @pl.when(short_above)
        def _():
            to_plane(layer_of(above_far_ref, part), field_layer(part, last))

        @pl.when(jnp.logical_not(short_above))
        def _():
            to_plane(layer_of(above_rows_ref, part * HALO + HALO - 1), field_layer(part, last))

    def wrap(field_ref, part, x_row, first, final):
        field_ref[part, x_row, :8, :] = pltpu.roll(final, 1, 0)
        field_ref[part, x_row, SIDE + 8:, :] = pltpu.roll(first, 7, 0)

    blocks = SIDE // BLOCK

    def confine(x_row):
        known = x_row < thickness + 2 * HALO
        ends = {}
        for block in range(blocks):
            rows = slice(block * BLOCK, (block + 1) * BLOCK)
            inner = slice(8 + block * BLOCK, 8 + (block + 1) * BLOCK)
            inside = mesh_points(own_start - HALO + x_row, circle_ref[rows, :], length_cells) & known
            centre_ref[x_row, rows, :] = jnp.where(
                inside, (3.0 + centre_ref[x_row, rows, :]) * time_step, 0.0
            )
            beside_ref[x_row, rows, :] = jnp.where(inside, 0.5 * time_step, 0.0)
            for part in range(2):
                field = jnp.where(inside, first_ref[part, x_row, inner, :], 0.0)
                first_ref[part, x_row, inner, :] = field
                ends[part, block] = field
        for part in range(2):
            wrap(first_ref, part, x_row, ends[part, 0][:8], ends[part, blocks - 1][BLOCK - 8:])

    in_turns(0, layers, 5, confine)

    def hamilton(term, part, x_row, block, centre, beside):
        field_ref = field_refs[term]
        tall = field_ref[part, x_row, block * BLOCK:block * BLOCK + BLOCK + 16, :]
        inner = slice(8 + block * BLOCK, 8 + (block + 1) * BLOCK)
        field = tall[8:8 + BLOCK]
        around = field_ref[part, x_row - 1, inner, :] + field_ref[part, x_row + 1, inner, :]
        around = around + (tall[:BLOCK] + tall[16:])
        around = around + (pltpu.roll(field, 1, 1) + pltpu.roll(field, WIDTH - 1, 1))
        return centre * field - beside * around

    for term in range(1, TERMS):

        def step(x_row, term=term):
            ends = {}
            for block in range(blocks):
                rows = slice(block * BLOCK, (block + 1) * BLOCK)
                inner = slice(8 + block * BLOCK, 8 + (block + 1) * BLOCK)
                centre = centre_ref[x_row, rows, :]
                beside = beside_ref[x_row, rows, :]
                for part in range(2):
                    field = hamilton(term - 1, part, x_row, block, centre, beside)
                    field_refs[term][part, x_row, inner, :] = field
                    ends[part, block] = field
            for part in range(2):
                wrap(field_refs[term], part, x_row, ends[part, 0][:8], ends[part, blocks - 1][BLOCK - 8:])

        in_turns(term, layers - term, 6, step)

    def finish(slot, total):
        x_row = HALO + slot
        owned = slot < thickness
        for block in range(SIDE // BLOCK):
            rows = slice(block * BLOCK, (block + 1) * BLOCK)
            inner = slice(8 + block * BLOCK, 8 + (block + 1) * BLOCK)
            centre = centre_ref[x_row, rows, :]
            beside = beside_ref[x_row, rows, :]
            density = jnp.zeros((BLOCK, WIDTH), jnp.float32)
            for part, sign in ((0, 1.0), (1, -1.0)):
                summed = first_ref[part, x_row, inner, :]
                summed = summed + sign * second_ref[1 - part, x_row, inner, :]
                summed = summed - (1.0 / 2.0) * third_ref[part, x_row, inner, :]
                summed = summed - (sign / 6.0) * fourth_ref[1 - part, x_row, inner, :]
                summed = summed + (1.0 / 24.0) * hamilton(3, part, x_row, block, centre, beside)
                summed = jnp.where(owned, summed, 0.0)
                sum_ref[part, slot, rows, :] = summed
                density = density + summed * summed
            density = weight * density
            planes_ref[tile_rows(slot * SIDE + block * BLOCK, BLOCK), :] = density
            total = total + jnp.sum(density.reshape(BLOCK // 8, 8, WIDTH), axis=0)

        return total

    total = jnp.zeros((8, WIDTH), jnp.float32)
    for slot in range(slots):
        total = finish(slot, total)
    departure = pltpu.make_async_copy(sum_ref, psi_ref, out_sem)
    departure.start()
    whole = jnp.broadcast_to(jnp.sum(total, keepdims=True), (SLOTS, LANES))
    whole_ref[...] = whole
    along_z = turn_z(planes_ref[...], table_z_ref[...])
    along_ref[...] = along_z
    half_columns(along_z, slots, table_y_ref[1 - core], low_ref, high_ref)
    for device in range(devices):
        sent_ref[device] = chunk_of(
            low_ref, high_ref, 0, column_pieces(device * count, count), whole[:, :width - count]
        )
    departure.wait()


def kept_kernel(count, along_ref, whole_ref, table_y_ref, kept_ref, low_ref, high_ref):
    devices, _, width = kept_ref.shape
    slots = along_ref.shape[0] // SIDE
    half_columns(along_ref[...], slots, table_y_ref[lax.axis_index("core")], low_ref, high_ref)
    whole = whole_ref[...][:, :width - count]
    for device in range(devices):
        kept_ref[device] = chunk_of(low_ref, high_ref, 0, column_pieces(device * count, count), whole)


def unpack_kernel(weight_ref, psi_ref, next_ref, density_kept_ref, density_sent_ref, density_ref):
    core = lax.axis_index("core")
    weight = weight_ref[0]
    slots = psi_ref.shape[1]

    def unpack(slot):
        for part in range(2):

            def load(tile, part=part):
                tall = psi_ref[part, slot, 8 * tile:8 * tile + 8, :]
                return tall[:, :LANES], tall[:, LANES:]

            def store(k, values, part=part):
                next_ref[part, slot, pl.ds(k, 8, stride=STRIDE), :] = values

            to_flat(load, store)
        real = next_ref[0, slot]
        imag = next_ref[1, slot]
        density_ref[slot] = weight * (real * real + imag * imag)

    in_turns(0, slots, 2, unpack)
    for slot in range(slots, SLOTS):
        density_ref[slot] = jnp.zeros((FLAT, LANES), jnp.float32)

    @pl.loop(0, SLOTS // 2)
    def _(slot):
        density_kept_ref[slot] = density_ref[core * (SLOTS // 2) + slot]
        density_sent_ref[slot] = density_ref[(1 - core) * (SLOTS // 2) + slot]


def wave_squared(index, count_cells):
    folded = jnp.where(2 * index <= count_cells, index, index - count_cells)
    wave_number = folded.astype(jnp.float32) * (two_pi / count_cells)
    return wave_number * wave_number


def coulomb_kernel(count, length_cells, start_ref, charge_ref, ions_ref, table_ref, out_ref):
    domains, _, width = ions_ref.shape
    states = charge_ref.shape[0] // domains
    device = (lax.axis_index("core") * states + lax.axis_index("row")) * domains + lax.axis_index("domain")
    charge = charge_ref[:domains]
    for state in range(1, states):
        charge = charge + charge_ref[state * domains:(state + 1) * domains]
    charge = charge.reshape(domains * SLOTS, width)
    ions = ions_ref[...].reshape(domains * SLOTS, width)
    first = lax.broadcasted_iota(jnp.int32, (domains * SLOTS, width), 0) % SLOTS == 0
    lane = lax.broadcasted_iota(jnp.int32, (domains * SLOTS, width), 1)
    chosen = first & (lane == count)
    electrons = jnp.sum(jnp.where(chosen, charge, 0.0), keepdims=True)
    ionic = jnp.sum(jnp.where(chosen, ions, 0.0), keepdims=True)
    charge = charge - (electrons / ionic) * ions
    layer = lax.broadcasted_iota(jnp.int32, (length_cells, domains * SLOTS), 0)
    place = lax.broadcasted_iota(jnp.int32, (length_cells, domains * SLOTS), 1)
    chosen_layer = jnp.full(layer.shape, -1, jnp.int32)
    for domain in range(domains):
        slot = place - domain * SLOTS
        here = (slot >= 0) & (slot < start_ref[domain + 1] - start_ref[domain])
        chosen_layer = jnp.where(here, start_ref[domain] + slot, chosen_layer)
    pick = (layer == chosen_layer).astype(jnp.float32)
    table = jnp.dot(table_ref[...], pick, precision=highest, preferred_element_type=jnp.float32)
    waves = jnp.dot(table, charge, precision=highest, preferred_element_type=jnp.float32)
    wave_x = lax.broadcasted_iota(jnp.int32, waves.shape, 0)
    column = device * count + lax.broadcasted_iota(jnp.int32, waves.shape, 1)
    wave_y = ((column.astype(jnp.float32) + 0.5) * (1.0 / SIDE)).astype(jnp.int32)
    wave_z = column - wave_y * SIDE
    squared = (
        wave_squared(wave_x, length_cells) + wave_squared(wave_y, SIDE) + wave_squared(wave_z, SIDE)
    )
    gain = jnp.where(squared > 0, four_pi / jnp.where(squared > 0, squared, 1.0), 0.0)
    waves = waves * (gain * (1.0 / (length_cells * SIDE * SIDE)))
    back = lax.dot_general(
        table, waves, (((0,), (0,)), ((), ())), precision=highest, preferred_element_type=jnp.float32
    )
    back = back.reshape(domains, SLOTS, width)
    for state in range(states):
        out_ref[state * domains:(state + 1) * domains] = back


def half_planes(count, source_ref, table_y, table_z, low_ref, high_ref, slots):
    half = SIDE // 2
    pieces = []
    for device in range(source_ref.shape[0]):
        column = 0
        for row, start, stop in column_pieces(device * count, count):
            values = source_ref[device, :, column:column + stop - start]
            column += stop - start
            if start > 0:
                pieces.append(values)
                values = jnp.concatenate(pieces, axis=1)
            if stop < SIDE:
                pieces = [values]
                continue
            pieces = []
            at = pl.ds(row, SLOTS, stride=half)
            low_ref[at, :] = values[:, :LANES]
            high_ref[at, :] = jnp.concatenate(
                [values[:, LANES:], jnp.zeros((SLOTS, WIDTH - SIDE), jnp.float32)], axis=1
            )
    used = slice(0, slots * half)
    along_z = turn_z(jnp.concatenate([low_ref[used, :], high_ref[used, :]], axis=1), table_z)
    return [turn_y(table_y, along_z[slot * half:(slot + 1) * half]) for slot in range(slots)]


def half_kernel(count, waves_ref, table_y_ref, table_z_ref, out_ref, low_ref, high_ref):
    table_y = table_y_ref[lax.axis_index("core")]
    slots = out_ref.shape[0] // SIDE
    planes = half_planes(count, waves_ref, table_y, table_z_ref[...], low_ref, high_ref, slots)
    for slot, plane in enumerate(planes):
        out_ref[slot * SIDE:(slot + 1) * SIDE, :] = plane


def field_kernel(count, length_cells, start_ref, others_ref, half_ref, density_ref, other_ref, circle_ref,
                 table_y_ref, table_z_ref, out_ref, low_ref, high_ref, planes_ref, flat_ref):
    _, own_start, thickness = place_of(start_ref)
    slots = out_ref.shape[0]
    core = lax.axis_index("core")
    planes = half_planes(count, others_ref, table_y_ref[1 - core], table_z_ref[...], low_ref, high_ref, slots)
    for slot, plane in enumerate(planes):
        rows = slice(slot * SIDE, (slot + 1) * SIDE)
        planes_ref[rows, :] = half_ref[rows, :] + plane

    def field(slot):
        def load(tile):
            tall = planes_ref[tile_rows(slot * SIDE + tile * 8, 8), :]
            return tall[:, :LANES], tall[:, LANES:]

        def store(k, values):
            flat_ref[pl.ds(slot * FLAT + k, 8, stride=STRIDE), :] = values

        to_flat(load, store)
        rows = tile_rows(slot * FLAT, FLAT)
        here = slot // (SLOTS // 2) == core
        kept_slot = slot % (SLOTS // 2)
        content = jnp.where(here, density_ref[kept_slot], other_ref[kept_slot]) * (3.0 / math.pi)
        positive = jnp.where(content > 0, content, 1.0)
        root = jnp.exp(jnp.log(positive) * (1.0 / 3.0))
        root = root - (root - positive / (root * root)) * (1.0 / 3.0)
        root = jnp.where(content > 0, root, 0.0)
        inside = mesh_points(own_start + slot, circle_ref[...], length_cells) & (slot < thickness)
        flat_ref[rows, :] = jnp.where(inside, flat_ref[rows, :] - root, 0.0)

    in_turns(0, slots, 4, field)

    @pl.loop(0, FLAT // 8)
    def _(step):
        for part in range(8):
            lanes = pl.ds(pl.multiple_of((step * 8 + part) * LANES, LANES), LANES)
            out_ref[:, lanes] = flat_ref[pl.ds(step * 8 + part, SLOTS, stride=FLAT), :][:slots]


def from_behind(value, steps):
    count = lax.axis_size("domain")
    leading, last = (max(0, -steps), min(count, count - steps))
    return lax.ppermute(value, "domain", [(source, source + steps) for source in range(leading, last)])


def swapped(value, axis):
    return lax.ppermute(value, axis, [(0, 1), (1, 0)])


def shards(orbitals, occupation, potential, background, layer_start):
    domains = lax.axis_size("domain")
    rows = lax.axis_size("row")
    devices = domains * rows
    length_cells = SLAB * domains
    layer_cap, plane = potential.shape
    count = plane // (2 * devices)
    width = -(-(count + 1) // LANES) * LANES
    circle = jnp.asarray(circle_plane())
    flat_circle = jnp.asarray(circle_table().reshape(FLAT, LANES))
    table_z, into_y, out_of_y = (jnp.asarray(table) for table in tables_of_side())
    table_x = jnp.asarray(hartley_table(length_cells).astype(np.float32))
    params = pltpu.CompilerParams(vmem_limit_bytes=16 * MEBI)
    large = pltpu.CompilerParams(vmem_limit_bytes=44 * MEBI)
    whole = pltpu.CompilerParams(vmem_limit_bytes=56 * MEBI)

    def f32(*shape):
        return jax.ShapeDtypeStruct(shape, jnp.float32)

    def scratch(*shape):
        return pltpu.VMEM(shape, jnp.float32)

    layers = orbitals.reshape(2, layer_cap, FLAT, LANES)
    packed = packed_tiles()
    outer = orbitals.reshape(2, layer_cap * FLAT, LANES)
    up, down = pl.pallas_call(
        pack_kernel,
        out_shape=(f32(2 * HALO, packed * LANES), f32(2 * HALO, packed * LANES)),
        in_specs=[SMEM_SPEC, HBM_SPEC],
        out_specs=(HBM_SPEC, HBM_SPEC),
        scratch_shapes=[
            scratch(2 * HALO * FLAT, LANES),
            scratch(2 * HALO * FLAT, LANES),
            scratch(2 * HALO, packed * LANES),
            scratch(2 * HALO, packed * LANES),
            pltpu.SemaphoreType.DMA((4,)),
            pltpu.SemaphoreType.DMA((2,)),
        ],
        compiler_params=whole,
        name="pack_halo",
    )(layer_start, outer)
    up, down, potential_rest, outer = lax.optimization_barrier((up, down, potential, outer))
    v_rows, up_far, down_far = pl.pallas_call(
        pack_rest_kernel,
        out_shape=(f32(HALO - 1, packed, LANES), f32(2 * FLAT, LANES), f32(2 * FLAT, LANES)),
        in_specs=[SMEM_SPEC, HBM_SPEC, HBM_SPEC],
        out_specs=(VMEM_SPEC,) * 3,
        scratch_shapes=[
            scratch(SLOTS * FLAT, LANES),
            scratch(SLOTS * FLAT, LANES),
            scratch(layer_cap, plane),
            pltpu.SemaphoreType.DMA((5,)),
        ],
        compiler_params=whole,
        cost_estimate=pl.CostEstimate(flops=0, transcendentals=0, bytes_accessed=30_000_000),
        name="pack_rest",
    )(layer_start, potential_rest, outer)
    v_rows = lax.ppermute(
        v_rows,
        ("core", "domain"),
        [(source, source + 1) for source in range(domains - 1)]
        + [(domains + source + 1, domains + source) for source in range(domains - 1)],
    )
    below = from_behind(up, 1)
    above = from_behind(down, -1)
    below_far = from_behind(up_far, 2)
    above_far = from_behind(down_far, -2)
    v_rows, below_far, above_far = lax.optimization_barrier((v_rows, below_far, above_far))
    v_others = swapped(v_rows, "core")

    ions = pl.pallas_call(
        functools.partial(ions_kernel, count, length_cells),
        out_shape=f32(domains, SLOTS, width),
        in_specs=[SMEM_SPEC] + [VMEM_SPEC] * 4,
        out_specs=VMEM_SPEC,
        scratch_shapes=[
            scratch(SLOTS * FLAT, LANES),
            scratch(layer_cap * SIDE, WIDTH),
            scratch(SLOTS * SIDE // 2, LANES),
            scratch(SLOTS * SIDE // 2, LANES),
        ],
        compiler_params=params,
        name="ion_waves",
    )(layer_start, background, circle, into_y, table_z)
    ions = lax.all_to_all(ions, "domain", split_axis=0, concat_axis=0, tiled=True)
    ions, below = lax.optimization_barrier((ions, below))

    span = layer_cap + 2 * HALO
    fields = (2, span, TALL, WIDTH)
    psi, along_z, whole_sum, sent = pl.pallas_call(
        functools.partial(propagate_kernel, count, length_cells),
        out_shape=(
            pltpu.HBM((2, layer_cap, SIDE, WIDTH), jnp.float32),
            f32(layer_cap * SIDE, WIDTH),
            f32(SLOTS, LANES),
            f32(devices, SLOTS, width),
        ),
        in_specs=[SMEM_SPEC, SMEM_SPEC, VMEM_SPEC, VMEM_SPEC] + [HBM_SPEC] * 6 + [VMEM_SPEC] * 3,
        out_specs=(HBM_SPEC, VMEM_SPEC, VMEM_SPEC, VMEM_SPEC),
        scratch_shapes=[scratch(*fields)] * TERMS
        + [
            scratch(2, layer_cap, SIDE, WIDTH),
            scratch(span, SIDE, WIDTH),
            scratch(span, SIDE, WIDTH),
            scratch(SLOTS * FLAT, LANES),
            scratch(layer_cap * SIDE, WIDTH),
            scratch(SLOTS * SIDE // 2, LANES),
            scratch(SLOTS * SIDE // 2, LANES),
            scratch(SLOTS * FLAT, LANES),
            scratch(SLOTS * FLAT, LANES),
            scratch(SLOTS * FLAT, LANES),
            scratch(HALO - 1, packed, LANES),
            scratch(HALO - 1, packed, LANES),
            scratch(2 * HALO, packed * LANES),
            scratch(2 * HALO, packed * LANES),
            scratch(2 * FLAT, LANES),
            scratch(2 * FLAT, LANES),
            pltpu.SemaphoreType.DMA((6,)),
            pltpu.SemaphoreType.DMA,
        ],
        compiler_params=large,
        name="propagate",
    )(layer_start, occupation, layers, potential, below, above, below_far, above_far, v_rows, v_others,
      circle, into_y, table_z)
    half = [scratch(SLOTS * SIDE // 2, LANES), scratch(SLOTS * SIDE // 2, LANES)]
    kept = pl.pallas_call(
        functools.partial(kept_kernel, count),
        out_shape=f32(devices, SLOTS, width),
        in_specs=[VMEM_SPEC] * 3,
        out_specs=VMEM_SPEC,
        scratch_shapes=half,
        compiler_params=params,
        name="kept_waves",
    )(along_z, whole_sum, into_y)
    waves = kept + swapped(sent, "core")
    waves, psi = lax.optimization_barrier((waves, psi))
    waves = lax.all_to_all(waves, ("row", "domain"), split_axis=0, concat_axis=0, tiled=True)
    orbitals_next, density_kept, density_sent = pl.pallas_call(
        unpack_kernel,
        out_shape=(
            f32(2, layer_cap, FLAT, LANES),
            f32(SLOTS // 2, FLAT, LANES),
            f32(SLOTS // 2, FLAT, LANES),
        ),
        in_specs=[SMEM_SPEC, VMEM_SPEC],
        out_specs=(VMEM_SPEC,) * 3,
        scratch_shapes=[scratch(SLOTS, FLAT, LANES)],
        compiler_params=params,
        name="unpack",
    )(occupation, psi)
    density = density_kept + swapped(density_sent, "core")
    waves, density = lax.optimization_barrier((waves, density))
    other_density = swapped(density, "row")
    waves = pl.pallas_call(
        functools.partial(coulomb_kernel, count, length_cells),
        out_shape=f32(devices, SLOTS, width),
        in_specs=[SMEM_SPEC] + [VMEM_SPEC] * 3,
        out_specs=VMEM_SPEC,
        compiler_params=params,
        name="coulomb",
    )(layer_start, waves, ions, table_x)
    waves = lax.all_to_all(waves, ("row", "domain"), split_axis=0, concat_axis=0, tiled=True)
    waves, other_density = lax.optimization_barrier((waves, other_density))
    density = density + other_density
    other_density = swapped(density, "core")
    other_waves = swapped(waves, "core")
    planes = pl.pallas_call(
        functools.partial(half_kernel, count),
        out_shape=f32(layer_cap * SIDE, WIDTH),
        in_specs=[VMEM_SPEC] * 3,
        out_specs=VMEM_SPEC,
        scratch_shapes=half,
        compiler_params=params,
        name="half_field",
    )(waves, out_of_y, table_z)
    potential_next = pl.pallas_call(
        functools.partial(field_kernel, count, length_cells),
        out_shape=f32(layer_cap, plane),
        in_specs=[SMEM_SPEC] + [VMEM_SPEC] * 7,
        out_specs=VMEM_SPEC,
        scratch_shapes=half + [scratch(layer_cap * SIDE, WIDTH), scratch(SLOTS * FLAT, LANES)],
        compiler_params=params,
        name="field",
    )(layer_start, other_waves, planes, density, other_density, flat_circle, out_of_y, table_z)
    return orbitals_next.reshape(orbitals.shape), potential_next


def solution(mesh):
    domains = mesh.shape["domain"]
    split = Mesh(mesh.devices.reshape(-1, 2, domains), ("row", "core", "domain"))
    states = ("row", "core")
    return jax.shard_map(
        shards,
        mesh=split,
        in_specs=(
            P(None, states, "domain", None),
            P(states),
            P("domain", None),
            P("domain", None),
            P(),
        ),
        out_specs=(P(None, states, "domain", None), P("domain", None)),
        check_vma=False,
    )
```
